32 devices in a mesh: win: 16 (over z, y, core), tp: 2 (over x).
Axes of the slice: x: 2, y: 2, z: 4, core: 2. Of those that a mesh axis runs over, the one named last changes fastest.
Arguments:
- tokens: bfloat16 [16, 56, 28, 384], P('win', 'tp'), may hold values from -6 to 6
- crop_ids: int32 [16, 56, 28], P('win'), may hold values from 0 to 5, as said below
- cotangent: bfloat16 [16, 56, 28, 384], P('win', 'tp'), may hold values from -6 to 6
- norm_gain: float32 [2, 2, 384], replicated, may hold values from 0.25 to 1.75
- norm_bias: float32 [2, 2, 384], replicated, may hold values from -1.75 to 1.75
- qkv_weight: bfloat16 [2, 384, 3, 384], P(None, None, None, 'tp'), may hold values from -0.3125 to 0.3125
- qv_bias: float32 [2, 2, 384], P(None, None, 'tp'), may hold values from -1.75 to 1.75
- proj_weight: bfloat16 [2, 384, 384], P(None, 'tp'), may hold values from -0.875 to 0.875
- proj_bias: float32 [2, 384], replicated, may hold values from -1.75 to 1.75
- fc1_weight: bfloat16 [2, 384, 1536], P(None, None, 'tp'), may hold values from -0.3125 to 0.3125
- fc1_bias: float32 [2, 1536], P(None, 'tp'), may hold values from -1.75 to 1.75
- fc2_weight: bfloat16 [2, 1536, 384], P(None, 'tp'), may hold values from -0.15625 to 0.15625
- fc2_bias: float32 [2, 384], replicated, may hold values from -1.75 to 1.75
- pos_table: float32 [2, 169, 12], P(None, None, 'tp'), may hold values from -6 to 6
Outputs:
- layer_out: bfloat16 [16, 56, 28, 384], P('win', 'tp')
- grad_tokens: float32 [16, 56, 28, 384], P('win', 'tp')
- grad_norm_gain: float32 [2, 2, 384], replicated
- grad_norm_bias: float32 [2, 2, 384], replicated
- grad_qkv_weight: float32 [2, 384, 3, 384], P(None, None, None, 'tp')
- grad_qv_bias: float32 [2, 2, 384], P(None, None, 'tp')
- grad_proj_weight: float32 [2, 384, 384], P(None, 'tp')
- grad_proj_bias: float32 [2, 384], replicated
- grad_fc1_weight: float32 [2, 384, 1536], P(None, None, 'tp')
- grad_fc1_bias: float32 [2, 1536], P(None, 'tp')
- grad_fc2_weight: float32 [2, 1536, 384], P(None, 'tp')
- grad_fc2_bias: float32 [2, 384], replicated
- grad_pos_table: float32 [2, 169, 12], P(None, None, 'tp')
The draws below stay inside these ranges and needn't reach their ends.
Inputs may be any that keep to these rules, and one draw needn't show every extreme that they name: `crop_ids`: in each canvas the ids form a grid of three bands of rows by two bands of columns, numbered band of rows * 2 + band of columns; the middle band of rows holds rows 14 to 41 and more; every id occurs in every canvas.
All inputs are finite; a program needn't handle non-finite values.
Results may differ from the reference program's by a relative error of at most 0.024.
Values may be sent and summed in bfloat16 or wider, within the bound.
No kernel may reach another device: no remote copies, remote signals or barrier semaphores. Data moves between devices by JAX's collectives and lax.ppermute only.
A program may use at most 192 MiB of HBM per device.

```python
import jax
import jax.numpy as jnp
from jax import lax

C = 384
HEADS = 12
FF = 1536
WIN = 7
SHIFT = 3
LAYERS = 2
HD = 32
HH = 56
WW = 28
CANV = 16
TABLE = 169


def draw_crop_ids(key, part):
    key = jax.random.fold_in(key, 7)
    canvas_keys = jax.random.split(key, CANV)

    def one_canvas(canvas_key):
        first_key, second_key, third_key = jax.random.split(canvas_key, 3)
        top_cut = jax.random.randint(first_key, (), 1, HH // 4 + 1)
        bottom_cut = jax.random.randint(second_key, (), HH - HH // 4, HH)
        column_cut = jax.random.randint(third_key, (), 3, WW - 3)
        row_ids = jnp.arange(HH, dtype=jnp.int32)[:, None]
        col_ids = jnp.arange(WW, dtype=jnp.int32)[None, :]
        band = (row_ids >= top_cut).astype(jnp.int32) + (row_ids >= bottom_cut).astype(jnp.int32)
        return (band * 2 + (col_ids >= column_cut).astype(jnp.int32)).astype(jnp.int32)
    return jax.vmap(one_canvas)(canvas_keys)


def shard_levels(rng, extent, shards, smallest, largest):
    gain = 1.0
    for dim, parts in shards:
        heights = jax.random.uniform(jax.random.fold_in(jax.random.fold_in(rng, 6), dim), (parts,), jnp.float32, smallest / len(shards), largest / len(shards))
        gain = gain * jnp.repeat(jnp.exp(heights), extent[dim] // parts).reshape((-1,) + (1,) * (len(extent) - 1 - dim))
    return gain


def gaussian(stream_key, extent, scale, reach, shards=(), kind=jnp.bfloat16):
    drawn = jax.random.normal(stream_key, extent, jnp.float32) * scale
    if len(shards) > 0:
        drawn = shard_levels(stream_key, extent, shards, -0.22, 0.18) * drawn
    return jnp.clip(drawn, min=-reach, max=reach).astype(kind)


def setup_inputs(seed: int = 0) -> dict:
    seeds = jax.random.split(jax.random.key(seed), 15)
    tokens = gaussian(seeds[0], (CANV, HH, WW, C), 1.0, 6.0, ((0, 16), (1, 2)))
    crop_ids = draw_crop_ids(jax.random.fold_in(seeds[14], 71), 0)
    cotangent = gaussian(seeds[2], (CANV, HH, WW, C), 1.0, 6.0, ((0, 16), (1, 2)))
    norm_gain = jnp.clip(1.0 + 0.15 * jax.random.normal(seeds[3], (LAYERS, 2, C), jnp.float32), 0.25, 1.75)
    norm_bias = gaussian(seeds[4], (LAYERS, 2, C), 0.3, 1.75, (), jnp.float32)
    qkv_weight = gaussian(seeds[5], (LAYERS, C, 3, C), C ** -0.5, 0.3125, ((3, 2),))
    qv_bias = gaussian(seeds[6], (LAYERS, 2, C), 0.3, 1.75, ((2, 2),), jnp.float32)
    proj_weight = gaussian(seeds[7], (LAYERS, C, C), (C // 8) ** -0.5, 0.875, ((1, 2),))
    proj_bias = gaussian(seeds[8], (LAYERS, C), 0.3, 1.75, (), jnp.float32)
    fc1_weight = gaussian(seeds[9], (LAYERS, C, FF), C ** -0.5, 0.3125, ((2, 2),))
    fc1_bias = gaussian(seeds[10], (LAYERS, FF), 0.3, 1.75, ((1, 2),), jnp.float32)
    fc2_weight = gaussian(seeds[11], (LAYERS, FF, C), FF ** -0.5, 0.15625, ((1, 2),))
    fc2_bias = gaussian(seeds[12], (LAYERS, C), 0.3, 1.75, (), jnp.float32)
    pos_table = gaussian(seeds[13], (LAYERS, TABLE, HEADS), 1.0, 6.0, ((2, 2),), jnp.float32)
    return {"tokens": tokens, "crop_ids": crop_ids, "cotangent": cotangent, "norm_gain": norm_gain, "norm_bias": norm_bias, "qkv_weight": qkv_weight, "qv_bias": qv_bias, "proj_weight": proj_weight, "proj_bias": proj_bias, "fc1_weight": fc1_weight, "fc1_bias": fc1_bias, "fc2_weight": fc2_weight, "fc2_bias": fc2_bias, "pos_table": pos_table}


@jax.custom_vjp
def low(v):
    return lax.optimization_barrier(v.astype(jnp.bfloat16)).astype(jnp.float32)

@jax.custom_vjp
def low_back(v):
    return v

def low_keep(v):
    return (low(v), None)

def low_pass(kept, grad):
    return (grad,)

def back_keep(v):
    return (v, None)

def back_low(kept, grad):
    return (low(grad),)
low.defvjp(low_keep, low_pass)
low_back.defvjp(back_keep, back_low)
negative_fill = -1000000000.0
norm_eps = 1e-05

def layer_norm(values, gain_row, offset):
    average = lax.optimization_barrier(jnp.mean(values, -1, keepdims=True))
    centred = values - average
    spread = lax.optimization_barrier(jnp.mean(centred * centred, -1, keepdims=True))
    return centred * lax.rsqrt(spread + norm_eps) * gain_row + offset

def to_windows(canvas):
    height, across = (canvas.shape[0], canvas.shape[1])
    blocks = canvas.reshape(height // WIN, WIN, across // WIN, WIN, -1)
    return blocks.transpose(0, 2, 1, 3, 4).reshape(-1, WIN * WIN, canvas.shape[-1])

def from_windows(blocks, height, across):
    tiles = blocks.reshape(height // WIN, across // WIN, WIN, WIN, -1)
    return tiles.transpose(0, 2, 1, 3, 4).reshape(height, across, -1)

def relative_index():
    places = jnp.arange(WIN * WIN, dtype=jnp.int32)
    row_of = places // WIN
    col_of = places % WIN
    return ((row_of[:, None] - row_of[None, :] + WIN - 1) * (2 * WIN - 1) + (col_of[:, None] - col_of[None, :] + WIN - 1)).astype(jnp.int32)

def window_mask(crop_grid, shifted):
    height, across = crop_grid.shape
    amount = SHIFT if shifted else 0
    rolled = jnp.roll(crop_grid, (-amount, -amount), (0, 1))
    if shifted:
        row_ids = jnp.arange(height, dtype=jnp.int32)
        col_ids = jnp.arange(across, dtype=jnp.int32)
        row_zone = (row_ids >= height - WIN).astype(jnp.int32) + (row_ids >= height - SHIFT).astype(jnp.int32)
        col_zone = (col_ids >= across - WIN).astype(jnp.int32) + (col_ids >= across - SHIFT).astype(jnp.int32)
        rolled = rolled * 9 + row_zone[:, None] * 3 + col_zone[None, :]
    labels = to_windows(rolled[:, :, None])[:, :, 0]
    return labels[:, :, None] == labels[:, None, :]

def block(canvas, crop_grid, weights, shifted):
    gain_pair, offsets, qkv_w, qv_b, proj_w, proj_b, fc1_w, fc1_b, fc2_w, fc2_b, rel_table = weights
    highest = lax.Precision.HIGHEST
    amount = SHIFT if shifted else 0
    query_scale = HD ** (-0.5)
    normed = low(layer_norm(canvas, gain_pair[0], offsets[0]))
    windows = to_windows(jnp.roll(normed, (-amount, -amount), (0, 1)))
    count = windows.shape[0]
    flat_rows = windows.reshape(-1, C)
    projected = jnp.einsum('tc,cjd->tjd', flat_rows, qkv_w, precision=highest)
    queries = low_back(low((projected[:, 0] + qv_b[0]) * query_scale)).reshape(count, WIN * WIN, HEADS, HD)
    key_rows = low_back(low(projected[:, 1])).reshape(count, WIN * WIN, HEADS, HD)
    value_rows = low_back(low(projected[:, 2] + qv_b[1])).reshape(count, WIN * WIN, HEADS, HD)
    scores = low_back(jnp.einsum('wqhd,wkhd->whqk', queries, key_rows, precision=highest))
    bias_map = rel_table[relative_index()].transpose(2, 0, 1)
    allowed = window_mask(crop_grid, shifted)
    scores = jnp.where(allowed[:, None], scores + bias_map[None], negative_fill)
    row_peak = lax.optimization_barrier(jnp.max(scores, -1, keepdims=True))
    exp_scores = jnp.exp(scores - row_peak)
    attn_probs = low(exp_scores / lax.optimization_barrier(jnp.sum(exp_scores, -1, keepdims=True)))
    mixed_heads = low_back(low(jnp.einsum('whqk,wkhd->wqhd', attn_probs, value_rows, precision=highest))).reshape(-1, C)
    branch = low_back(jnp.dot(mixed_heads, proj_w, precision=highest) + proj_b)
    branch = jnp.roll(from_windows(branch.reshape(count, WIN * WIN, C), HH, WW), (amount, amount), (0, 1))
    hidden_rows = canvas + branch
    normed_two = low(layer_norm(hidden_rows, gain_pair[1], offsets[1])).reshape(-1, C)
    upper_rows = low_back(jnp.dot(normed_two, fc1_w, precision=highest) + fc1_b)
    active = low(jax.nn.gelu(upper_rows, approximate=False))
    result = low_back(jnp.dot(active, fc2_w, precision=highest) + fc2_b)
    return hidden_rows + result.reshape(canvas.shape)

def reference(tokens, crop_ids, cotangent, norm_gain, norm_bias, qkv_weight, qv_bias, proj_weight, proj_bias, fc1_weight, fc1_bias, fc2_weight, fc2_bias, pos_table):
    weights = tuple((item.astype(jnp.float32) for item in (norm_gain, norm_bias, qkv_weight, qv_bias, proj_weight, proj_bias, fc1_weight, fc1_bias, fc2_weight, fc2_bias, pos_table)))

    def forward(states, *params):

        def canvas_pass(pair):
            canvas, crop_grid = pair
            for number in range(LAYERS):
                canvas = block(canvas, crop_grid, tuple((item[number] for item in params)), number % 2 == 1)
            return canvas
        return lax.map(jax.checkpoint(canvas_pass), (states, crop_ids))
    outputs, pullback = jax.vjp(forward, tokens.astype(jnp.float32), *weights)
    grads = pullback(cotangent.astype(jnp.float32))
    return (outputs.astype(jnp.bfloat16), grads[0], grads[1], grads[2], grads[3], grads[4], grads[5], grads[6], grads[7], grads[8], grads[9], grads[10], grads[11])
```

```python
from functools import partial

import jax
import jax.numpy as jnp
import numpy as np
from jax import lax
from jax.experimental import pallas as pl
from jax.experimental.pallas import tpu as pltpu
from jax.sharding import PartitionSpec as P

C = 384
WIN = 7
SHIFT = 3
HD = 32
EPS = 1e-05
NEG = -1000000000.0
SCALE = HD**-0.5
F32 = jnp.float32
BF = jnp.bfloat16
SEG = 8
WROWS = WIN * SEG
WPAD = 64
VMEM_LIMIT = 56 * 2**20


def nn(a, b):
    return lax.dot_general(a, b, (((1,), (0,)), ((), ())), preferred_element_type=F32)


def nt(a, b):
    return lax.dot_general(a, b, (((1,), (1,)), ((), ())), preferred_element_type=F32)


def tn(a, b):
    return lax.dot_general(a, b, (((0,), (0,)), ((), ())), preferred_element_type=F32)


def norm_stats(x):
    mean = jnp.mean(x, -1, keepdims=True)
    cent = x - mean
    var = jnp.mean(cent * cent, -1, keepdims=True)
    rinv = lax.rsqrt(var + EPS)
    return cent * rinv, rinv


def norm_back(dz, xhat, rinv, gain):
    d = dz * gain
    return rinv * (
        d - jnp.mean(d, -1, keepdims=True) - xhat * jnp.mean(d * xhat, -1, keepdims=True)
    )


def tile_row(r, k, across):
    return (((r // WIN) * across + k) * WIN + r % WIN) * SEG


def zero_rows(n):
    return jnp.zeros((n, C), F32)


def head_mask():
    row = lax.broadcasted_iota(jnp.int32, (6 * WPAD, 6 * HD), 0) // WPAD
    col = lax.broadcasted_iota(jnp.int32, (6 * WPAD, 6 * HD), 1) // HD
    return (row == col).astype(BF)


def spread(x, mask):
    return jnp.concatenate([x] * 6, axis=0) * mask


def swap_heads(x):
    parts = []
    for i in range(3):
        t = x[:, 128 * i : 128 * (i + 1)].T
        parts.append(jnp.concatenate([t[:WPAD], t[WPAD:]], axis=1))
    return jnp.concatenate(parts, axis=1)


def shift_in(tile, x_ref, rows, across):
    for r in range(rows):
        for k in range(across):
            a = tile(r + SHIFT, k)
            b = tile(r + SHIFT, (k + 1) % across)
            x_ref[pl.ds(tile_row(r, k, across), SEG), :] = jnp.concatenate(
                [a[SHIFT:WIN], b[:SHIFT], zero_rows(1)], axis=0
            )


def shift_out(tile, x_ref, rows, across):
    for r in range(rows):
        for k in range(across):
            a = tile(r - SHIFT, (k - 1) % across)
            b = tile(r - SHIFT, k)
            x_ref[pl.ds(tile_row(r, k, across), SEG), :] = jnp.concatenate(
                [a[WIN - SHIFT : WIN], b[: WIN - SHIFT], zero_rows(1)], axis=0
            )


def attn_fwd_kernel(layer, rows, across, *refs):
    if layer == 0:
        (tok_ref, refs) = (refs[0], refs[1:])
    else:
        (st_ref, halo_ref, refs) = (refs[0], refs[1], refs[2:])
    (gain_ref, bias_ref, pb_ref, own_ref, oa_ref, ob_ref, qvb_ref, pos_ref, lq_ref, lk_ref) = refs[
        :10
    ]
    (x_ref, hid_ref, xn_ref, qkv_ref, p_ref, mix_ref, mask_ref) = refs[10:]
    wins = (rows // WIN) * across
    if layer == 0:
        for r in range(rows):
            row = tok_ref[r].astype(F32)
            for k in range(across):
                x_ref[pl.ds(tile_row(r, k, across), SEG), :] = jnp.concatenate(
                    [row[WIN * k : WIN * (k + 1)], zero_rows(1)], axis=0
                )
    else:

        def tile(r, k):
            if r < rows:
                return st_ref[pl.ds(tile_row(r, k, across), SEG), :]
            return halo_ref[k, r - rows]

        shift_in(tile, x_ref, rows, across)
    mask_ref[...] = head_mask()
    gain = gain_ref[layer, 0:1]
    bias = bias_ref[layer, 0:1]

    def norm_one(w, carry):
        x = x_ref[pl.ds(pl.multiple_of(w * WROWS, WROWS), WROWS), :]
        xhat, _ = norm_stats(x)
        xn = jnp.concatenate([xhat * gain + bias, zero_rows(WPAD - WROWS)], axis=0)
        xn_ref[pl.ds(pl.multiple_of(w * WPAD, WPAD), WPAD), :] = xn.astype(BF)
        return carry

    lax.fori_loop(0, wins, norm_one, 0)

    def weight(half, j):
        if half == 0:
            return jnp.concatenate(
                [own_ref[0, 96 * j : 96 * (j + 1)], own_ref[1, 96 * j : 96 * (j + 1)]], axis=0
            )
        return jnp.concatenate(
            [oa_ref[96 * j : 96 * (j + 1)], ob_ref[96 * j : 96 * (j + 1)]], axis=0
        )

    big = 4 * WPAD

    def project(i, carry):
        at = pl.ds(pl.multiple_of(i * big, big), big)
        xn = xn_ref[at, :]
        for half in range(2):
            q = nt(xn, weight(half, 0))
            qkv_ref[half, 0, at, :] = ((q + qvb_ref[half, 0:1]) * SCALE).astype(BF)
            qkv_ref[half, 1, at, :] = nt(xn, weight(half, 1)).astype(BF)
            v = nt(xn, weight(half, 2))
            qkv_ref[half, 2, at, :] = (v + qvb_ref[half, 1:2]).astype(BF)
        return carry

    lax.fori_loop(0, wins // 4, project, 0)

    def attend(w, carry):
        at = pl.ds(pl.multiple_of(w * WPAD, WPAD), WPAD)
        same = lk_ref[w] == lq_ref[pl.ds(w, 1), :]
        same = jnp.concatenate([same] * 3, axis=1)
        for half in range(2):
            q = qkv_ref[half, 0, at, :]
            k = qkv_ref[half, 1, at, :]
            v = qkv_ref[half, 2, at, :]
            s = nt(k, spread(q, mask_ref[...]))
            s = jnp.where(same, s + pos_ref[half], NEG)
            e = jnp.exp(s - jnp.max(s, 0, keepdims=True))
            p = (e / jnp.sum(e, 0, keepdims=True)).astype(BF)
            p_ref[half, w] = p
            mix_ref[half, at, :] = nn(swap_heads(p), spread(v, mask_ref[...])).astype(BF)
        return carry

    lax.fori_loop(0, wins, attend, 0)
    pb = pb_ref[layer : layer + 1]
    po = jnp.concatenate([own_ref[0, 288:384], own_ref[1, 288:384]], axis=0)
    pt = jnp.concatenate([oa_ref[288:384], ob_ref[288:384]], axis=0)

    def out(i, carry):
        at = pl.ds(pl.multiple_of(i * big, big), big)
        res = nn(mix_ref[0, at, :], po) + nn(mix_ref[1, at, :], pt) + pb
        for n in range(4):
            to = pl.ds(pl.multiple_of((i * 4 + n) * WROWS, WROWS), WROWS)
            hid_ref[to, :] = x_ref[to, :] + res[n * WPAD : n * WPAD + WROWS]
        return carry

    lax.fori_loop(0, wins // 4, out, 0)


BLK = 128


def mlp_fwd_kernel(
    layer,
    hid_ref,
    gain_ref,
    bias_ref,
    fb1_ref,
    fb2_ref,
    f1_ref,
    f2_ref,
    oa_ref,
    ob_ref,
    st_ref,
    act_ref,
    gp_ref,
):
    gain = gain_ref[layer, 1:2]
    bias = bias_ref[layer, 1:2]
    fb2 = fb2_ref[layer : layer + 1]

    def block(i, carry):
        at = pl.ds(pl.multiple_of(i * BLK, BLK), BLK)
        h = hid_ref[at, :]
        xhat, _ = norm_stats(h)
        n2 = (xhat * gain + bias).astype(BF)
        acc = h + fb2
        for q in range(4):
            w1, w2 = quarter(q, f1_ref, f2_ref, oa_ref, ob_ref)
            u = nn(n2, w1) + fb1_ref[q : q + 1]
            phi = 0.5 + 0.5 * lax.erf(u * (2.0**-0.5))
            act = (u * phi).astype(BF)
            act_ref[q, at, :] = act
            gp_ref[q, at, :] = (phi + u * (jnp.exp(-0.5 * u * u) * (2.0 * np.pi) ** -0.5)).astype(BF)
            acc = acc + nn(act, w2)
        st_ref[at, :] = acc
        return carry

    lax.fori_loop(0, hid_ref.shape[0] // BLK, block, 0)


def quarter(q, f1_ref, f2_ref, oa_ref, ob_ref):
    if q < 2:
        return f1_ref[:, C * q : C * (q + 1)], f2_ref[C * q : C * (q + 1), :]
    ref = oa_ref if q == 2 else ob_ref
    return ref[:C], ref[C:]


def mlp_bwd_kernel(layer, rows, across, *refs):
    (g_in_ref, halo_ref, hid_ref, act_ref, gp_ref, gain_ref, bias_ref) = refs[:7]
    (f1_ref, f2_ref, oa_ref, ob_ref, par_ref) = refs[7:12]
    (gh_ref, keep_ref, send_ref, fb1_ref, sh_ref) = refs[12:17]
    (g_ref, df_ref, n2_ref, du_ref) = refs[17:]
    if layer == 1:
        for r in range(rows):
            s = r + SHIFT
            row = (g_in_ref[s] if s < rows else halo_ref[s - rows]).astype(F32)
            for k in range(across):
                a = WIN * k + SHIFT
                if k < across - 1:
                    piece = [row[a : a + WIN]]
                else:
                    piece = [row[a:], row[:SHIFT]]
                g_ref[pl.ds(tile_row(r, k, across), SEG), :] = jnp.concatenate(
                    piece + [zero_rows(1)], axis=0
                )
    else:

        def tile(r, k):
            if r >= 0:
                return g_in_ref[pl.ds(tile_row(r, k, across), SEG), :]
            return halo_ref[k, r + SHIFT]

        shift_out(tile, g_ref, rows, across)
    gain = gain_ref[layer, 1:2]
    bias = bias_ref[layer, 1:2]

    def block(i, carry):
        sb, sg, sf, s1 = carry
        at = pl.ds(pl.multiple_of(i * BLK, BLK), BLK)
        g = g_ref[at, :]
        df = g.astype(BF)
        df_ref[at, :] = df
        sf = sf + jnp.sum(df.astype(F32), 0, keepdims=True)
        dz = None
        new = []
        for q in range(4):
            w1, w2 = quarter(q, f1_ref, f2_ref, oa_ref, ob_ref)
            du = (nt(df, w2) * gp_ref[q, at, :].astype(F32)).astype(BF)
            du_ref[q, at, :] = du
            new.append(s1[q] + jnp.sum(du.astype(F32), 0, keepdims=True))
            part = nt(du, w1)
            dz = part if dz is None else dz + part
        xhat, rinv = norm_stats(hid_ref[at, :])
        n2_ref[at, :] = (xhat * gain + bias).astype(BF)
        sg = sg + jnp.sum(dz * xhat, 0, keepdims=True)
        sb = sb + jnp.sum(dz, 0, keepdims=True)
        gh_ref[at, :] = g + norm_back(dz, xhat, rinv, gain)
        return sb, sg, sf, tuple(new)

    z = jnp.zeros((1, C), F32)
    sb, sg, sf, s1 = lax.fori_loop(
        0, hid_ref.shape[0] // BLK, block, (z, z, z, (z,) * 4)
    )
    for q in range(4):
        fb1_ref[q : q + 1] = s1[q]
    sh_ref[0:1] = sg
    sh_ref[1:2] = sb
    sh_ref[2:3] = sf
    par = par_ref[0]
    n2 = n2_ref[...]
    df = df_ref[...]
    for slot, ref in ((0, keep_ref), (1, send_ref)):
        for part in range(2):
            q = (par ^ slot) if part == 0 else 2 + slot
            ref[part, 0:C, :] = tn(n2, du_ref[q]).astype(BF)
            ref[part, C:, :] = tn(act_ref[q], df).astype(BF)


def attn_bwd_kernel(layer, rows, across, *refs):
    (gh_ref, x_ref, xn_ref, qkv_ref, p_ref, mix_ref, gain_ref) = refs[:7]
    (own_ref, oa_ref, ob_ref, par_ref) = refs[7:11]
    (gin_ref, keep_ref, send_ref, pos_ref, qvb_ref, sh_ref) = refs[11:17]
    (da_ref, do_ref, dqkv_ref, mask_ref, row_ref, gx_ref) = refs[17:]
    wins = (rows // WIN) * across
    gain = gain_ref[layer, 0:1]
    mask_ref[...] = head_mask()
    z = jnp.zeros((1, C), F32)

    def windowed(w, s):
        g = gh_ref[pl.ds(pl.multiple_of(w * WROWS, WROWS), WROWS), :]
        da = jnp.concatenate([g, zero_rows(WPAD - WROWS)], axis=0).astype(BF)
        da_ref[pl.ds(pl.multiple_of(w * WPAD, WPAD), WPAD), :] = da
        return s + jnp.sum(da.astype(F32), 0, keepdims=True)

    sh_ref[2:3] = lax.fori_loop(0, wins, windowed, z)
    big = 4 * WPAD
    po = jnp.concatenate([own_ref[0, 288:384], own_ref[1, 288:384]], axis=0)
    pt = jnp.concatenate([oa_ref[288:384], ob_ref[288:384]], axis=0)

    def mixed_grad(i, carry):
        at = pl.ds(pl.multiple_of(i * big, big), big)
        da = da_ref[at, :]
        do_ref[0, at, :] = nt(da, po).astype(BF)
        do_ref[1, at, :] = nt(da, pt).astype(BF)
        return carry

    lax.fori_loop(0, wins // 4, mixed_grad, 0)
    par = par_ref[0]

    def give(value, at, half):
        if half == 0:
            row_ref[...] = value
            one = row_ref[pl.ds(pl.multiple_of(par * 96, 96), 96), :]
            two = row_ref[pl.ds(pl.multiple_of((1 - par) * 96, 96), 96), :]
        else:
            one, two = value[:96], value[96:]
        keep_ref[half, at : at + 96, :] = one.astype(BF)
        send_ref[half, at : at + 96, :] = two.astype(BF)

    for half in range(2):
        give(tn(mix_ref[half], da_ref[...]), 288, half)
    pos_ref[...] = jnp.zeros_like(pos_ref)

    def attend(w, carry):
        at = pl.ds(pl.multiple_of(w * WPAD, WPAD), WPAD)
        for half in range(2):
            q = qkv_ref[half, 0, at, :]
            k = qkv_ref[half, 1, at, :]
            v = qkv_ref[half, 2, at, :]
            do = spread(do_ref[half, at, :], mask_ref[...])
            p = p_ref[half, w]
            pf = p.astype(F32)
            dp = nt(v, do)
            ds = pf * (dp - jnp.sum(pf * dp, 0, keepdims=True))
            pos_ref[half] += ds
            dsb = ds.astype(BF)
            dqkv_ref[half, 2, at, :] = nn(p, do).astype(BF)
            dqkv_ref[half, 1, at, :] = nn(dsb, spread(q, mask_ref[...])).astype(BF)
            dqkv_ref[half, 0, at, :] = nn(swap_heads(dsb), spread(k, mask_ref[...])).astype(BF)
        return carry

    lax.fori_loop(0, wins, attend, 0)

    def weight(half, j):
        if half == 0:
            return jnp.concatenate(
                [own_ref[0, 96 * j : 96 * (j + 1)], own_ref[1, 96 * j : 96 * (j + 1)]], axis=0
            )
        return jnp.concatenate(
            [oa_ref[96 * j : 96 * (j + 1)], ob_ref[96 * j : 96 * (j + 1)]], axis=0
        )

    def back(i, carry):
        sg, sb, sq = carry
        at = pl.ds(pl.multiple_of(i * big, big), big)
        dn = nn(dqkv_ref[0, 0, at, :], weight(0, 0)) + nn(dqkv_ref[1, 0, at, :], weight(1, 0))
        dn = dn * SCALE
        for half in range(2):
            for j in (1, 2):
                dn = dn + nn(dqkv_ref[half, j, at, :], weight(half, j))
        new = []
        for half in range(2):
            for n, j in enumerate((0, 2)):
                new.append(
                    sq[half * 2 + n]
                    + jnp.sum(dqkv_ref[half, j, at, :].astype(F32), 0, keepdims=True)
                )
        for n in range(4):
            to = pl.ds(pl.multiple_of((i * 4 + n) * WROWS, WROWS), WROWS)
            d = dn[n * WPAD : n * WPAD + WROWS]
            xhat, rinv = norm_stats(x_ref[to, :])
            sg = sg + jnp.sum(d * xhat, 0, keepdims=True)
            sb = sb + jnp.sum(d, 0, keepdims=True)
            gx_ref[to, :] = gh_ref[to, :] + norm_back(d, xhat, rinv, gain)
        return sg, sb, tuple(new)

    zq = jnp.zeros((1, 6 * HD), F32)
    sg, sb, sq = lax.fori_loop(0, wins // 4, back, (z, z, (zq,) * 4))
    sh_ref[0:1] = sg
    sh_ref[1:2] = sb
    for half in range(2):
        qvb_ref[half, 0:1] = sq[half * 2] * SCALE
        qvb_ref[half, 1:2] = sq[half * 2 + 1]
    xn = xn_ref[...]
    for half in range(2):
        for j in range(3):
            grad = tn(dqkv_ref[half, j], xn)
            give(grad * SCALE if j == 0 else grad, 96 * j, half)
    if layer == 1:
        gin_ref[...] = gx_ref[...]
    else:
        for r in range(rows):
            parts = [
                gx_ref[pl.ds(tile_row(r, k, across), SEG), :][:WIN] for k in range(across)
            ]
            gin_ref[r] = jnp.concatenate(parts, axis=0)


def out_kernel(rows, across, st_ref, halo_ref, o_ref):
    for r in range(rows):
        parts = []
        for k in range(across):
            if r >= SHIFT:
                t = st_ref[pl.ds(tile_row(r - SHIFT, k, across), SEG), :]
            else:
                t = halo_ref[k, r]
            parts.append(t[:WIN])
        last = parts[-1]
        parts = [last[WIN - SHIFT :]] + parts[:-1] + [last[: WIN - SHIFT]]
        o_ref[r] = jnp.concatenate(parts, axis=0).astype(BF)


def whole(x):
    return pl.BlockSpec(x.shape, lambda i, n=len(x.shape): (0,) * n)


def layer_of(x, layer):
    return pl.BlockSpec(
        (None,) + x.shape[1:], lambda i, n=len(x.shape): (layer,) + (0,) * (n - 1)
    )


SMEM = pl.BlockSpec(memory_space=pltpu.SMEM)


def call(kernel, name, operands, outs, scratch=()):
    args = []
    specs = []
    for op in operands:
        if isinstance(op, tuple):
            args.append(op[0])
            specs.append(op[1])
        else:
            args.append(op)
            specs.append(whole(op))
    shapes = [jax.ShapeDtypeStruct(s, d) for s, d in outs]
    return pl.pallas_call(
        kernel,
        name=name,
        grid=(1,),
        in_specs=specs,
        out_specs=[whole(s) for s in shapes],
        out_shape=shapes,
        scratch_shapes=list(scratch),
        compiler_params=pltpu.CompilerParams(vmem_limit_bytes=VMEM_LIMIT),
    )(*args)


def labels(crop_grid, shifted, tp_index, rows):
    height, across = crop_grid.shape
    grid = crop_grid
    if shifted:
        grid = jnp.roll(crop_grid, (-SHIFT, -SHIFT), (0, 1))
        row_ids = jnp.arange(height, dtype=jnp.int32)
        col_ids = jnp.arange(across, dtype=jnp.int32)
        zr = (row_ids >= height - WIN).astype(jnp.int32) + (row_ids >= height - SHIFT)
        zc = (col_ids >= across - WIN).astype(jnp.int32) + (col_ids >= across - SHIFT)
        grid = grid * 9 + zr[:, None] * 3 + zc[None, :]
    grid = lax.dynamic_slice(grid, (tp_index * rows, 0), (rows, across))
    lab = grid.reshape(rows // WIN, WIN, across // WIN, WIN).transpose(0, 2, 1, 3)
    lab = lab.reshape(-1, WIN, WIN)
    lab = jnp.pad(lab, ((0, 0), (0, 1), (0, 1)), constant_values=-1).reshape(-1, WPAD)
    return jnp.concatenate([lab, lab], 1), jnp.broadcast_to(lab[:, :, None], lab.shape + (128,))


def table_onehot():
    p = np.arange(WPAD)
    y, x = p // 8, p % 8
    dy = y[None, :] - y[:, None]
    dx = x[None, :] - x[:, None]
    real = (y < WIN) & (x < WIN)
    idx = (dy + WIN - 1) * (2 * WIN - 1) + dx + WIN - 1
    ok = real[None, :] & real[:, None]
    idx = np.where(ok, idx, -1).reshape(-1)
    return jnp.asarray(idx, jnp.int32)


def on_device(n_win, *args):
    (
        tokens,
        crop_ids,
        cotangent,
        norm_gain,
        norm_bias,
        qkv_weight,
        qv_bias,
        proj_weight,
        proj_bias,
        fc1_weight,
        fc1_bias,
        fc2_weight,
        fc2_bias,
        pos_table,
    ) = args
    rows, cols = tokens.shape[1:3]
    across = cols // WIN
    wins = (rows // WIN) * across
    ntok = wins * WROWS
    npad = wins * WPAD
    win = lax.axis_index("win")
    tp = lax.axis_index("tp")
    par = win % 2
    par_arr = par.astype(jnp.int32).reshape(1)
    bits = n_win.bit_length() - 1

    def to_tp(x):
        return lax.ppermute(x, "tp", [(0, 1), (1, 0)])

    def to_win(x, bit):
        return lax.ppermute(x, "win", [(i, i ^ (1 << bit)) for i in range(n_win)])

    qkv_t = qkv_weight.transpose(0, 2, 3, 1).reshape(2, 3, 2, 96, C).transpose(0, 2, 1, 3, 4)
    own_attn = jnp.concatenate(
        [qkv_t.reshape(2, 2, 288, C), proj_weight.reshape(2, 2, 96, C)], axis=2
    )
    attn_q = lax.dynamic_index_in_dim(own_attn, par, 1, keepdims=False)
    fc1_q = lax.dynamic_slice(fc1_weight, (0, 0, par * C), (2, C, C))
    fc2_q = lax.dynamic_slice(fc2_weight, (0, par * C, 0), (2, C, C))
    mlp_q = jnp.concatenate([fc1_q, fc2_q], axis=1)
    attn_a, attn_b, mlp_a, mlp_b = [], [], [], []
    for layer in range(2):
        a = to_tp(attn_q[layer])
        m = to_tp(mlp_q[layer])
        attn_a.append(a)
        mlp_a.append(m)
        attn_b.append(to_win(a, 0))
        mlp_b.append(to_win(m, 0))

    small = jnp.concatenate(
        [
            qv_bias.reshape(2, 2, 2, 96).transpose(2, 0, 1, 3).reshape(2, -1),
            fc1_bias.reshape(2, 2, C).transpose(1, 0, 2).reshape(2, -1),
            pos_table.transpose(2, 0, 1).reshape(2, -1),
        ],
        axis=1,
    )
    other = to_tp(small)
    other = jnp.where(par == 0, other, other[::-1])
    both = jnp.stack([small, other])
    n1, n2 = 2 * 2 * 96, 2 * C
    qvb = both[:, :, :n1].reshape(2, 2, 2, 2, 96).transpose(2, 0, 3, 1, 4).reshape(2, 2, 2, 192)
    fb1 = both[:, :, n1 : n1 + n2].reshape(2, 2, 2, C).transpose(2, 0, 1, 3).reshape(2, 4, C)
    table = both[:, :, n1 + n2 :].reshape(2, 2, 3, 2, -1)
    table = table.transpose(3, 0, 1, 2, 4).reshape(24, -1)
    onehot = (
        jnp.arange(table.shape[1], dtype=jnp.int32)[:, None] == table_onehot()[None, :]
    ).astype(F32)
    pos = jnp.dot(table, onehot, precision=lax.Precision.HIGHEST)
    pos = pos.reshape(2, 2, 6, WPAD, WPAD).transpose(0, 1, 3, 2, 4).reshape(2, 2, WPAD, 6 * WPAD)

    labs = [labels(crop_ids[0], layer == 1, tp, rows) for layer in range(2)]
    cot_halo = to_tp(cotangent[0, :SHIFT])

    tiles = (rows // WIN, across, WIN, SEG, C)

    saved = []
    src = (tokens[0],)
    for layer in range(2):
        lq, lk = labs[layer]
        own = (own_attn, layer_of(own_attn, layer))
        x, hid, xn, qkv, p, mix = call(
            partial(attn_fwd_kernel, layer, rows, across),
            "attn_fwd_%d" % layer,
            src
            + (norm_gain, norm_bias, proj_bias, own, attn_a[layer], attn_b[layer])
            + (qvb[layer], pos[layer], lq, lk),
            [
                ((ntok, C), F32),
                ((ntok, C), F32),
                ((npad, C), BF),
                ((2, 3, npad, 192), BF),
                ((2, wins, WPAD, 384), BF),
                ((2, npad, 192), BF),
            ],
            [pltpu.VMEM((6 * WPAD, 6 * HD), BF)],
        )
        f1 = (fc1_weight, layer_of(fc1_weight, layer))
        f2 = (fc2_weight, layer_of(fc2_weight, layer))
        st, act, gp = call(
            partial(mlp_fwd_kernel, layer),
            "mlp_fwd_%d" % layer,
            (hid, norm_gain, norm_bias, fb1[layer], fc2_bias, f1, f2, mlp_a[layer], mlp_b[layer]),
            [((ntok, C), F32), ((4, ntok, C), BF), ((4, ntok, C), BF)],
        )
        saved.append((x, hid, xn, qkv, p, mix, act, gp, own, f1, f2))
        if layer == 0:
            src = (st, to_tp(st.reshape(tiles)[0, :, :SHIFT]))
    halo = to_tp(st.reshape(tiles)[-1, :, WIN - SHIFT :])
    (layer_out,) = call(
        partial(out_kernel, rows, across), "layer_out", (st, halo), [((rows, cols, C), BF)]
    )

    def reduce_chunk(keep, send):
        got = to_win(send, 0)
        s = (keep.astype(F32) + got.astype(F32)).astype(BF)
        t = to_tp(s[1])
        acc = (s[0].astype(F32) + t.astype(F32)).astype(BF)
        for bit in range(1, bits):
            n = acc.shape[0] // 2
            b = (win >> bit) & 1
            mine = lax.dynamic_slice_in_dim(acc, b * n, n)
            away = lax.dynamic_slice_in_dim(acc, (1 - b) * n, n)
            acc = (mine.astype(F32) + to_win(away, bit).astype(F32)).astype(BF)
        for bit in reversed(range(1, bits)):
            b = (win >> bit) & 1
            got = to_win(acc, bit)
            acc = jnp.where(b == 0, jnp.concatenate([acc, got]), jnp.concatenate([got, acc]))
        return acc, to_win(acc, 0)

    g = (cotangent[0], cot_halo)
    chunks = [None, None]
    smalls = [None, None]
    for layer in (1, 0):
        x, hid, xn, qkv, p, mix, act, gp, own, f1, f2 = saved[layer]
        gh, keep_m, send_m, gfb1, sh2 = call(
            partial(mlp_bwd_kernel, layer, rows, across),
            "mlp_bwd_%d" % layer,
            g
            + (hid, act, gp, norm_gain, norm_bias, f1, f2, mlp_a[layer], mlp_b[layer])
            + ((par_arr, SMEM),),
            [
                ((ntok, C), F32),
                ((2, 2 * C, C), BF),
                ((2, 2 * C, C), BF),
                ((4, C), F32),
                ((3, C), F32),
            ],
            [
                pltpu.VMEM((ntok, C), F32),
                pltpu.VMEM((ntok, C), BF),
                pltpu.VMEM((ntok, C), BF),
                pltpu.VMEM((4, ntok, C), BF),
            ],
        )
        gin_shape = (ntok, C) if layer == 1 else (rows, cols, C)
        gin, keep_a, send_a, gpos, gqvb, sh1 = call(
            partial(attn_bwd_kernel, layer, rows, across),
            "attn_bwd_%d" % layer,
            (gh, x, xn, qkv, p, mix, norm_gain, own, attn_a[layer], attn_b[layer])
            + ((par_arr, SMEM),),
            [
                (gin_shape, F32),
                ((2, C, C), BF),
                ((2, C, C), BF),
                ((2, WPAD, 384), F32),
                ((2, 2, 192), F32),
                ((3, C), F32),
            ],
            [
                pltpu.VMEM((npad, C), BF),
                pltpu.VMEM((2, npad, 192), BF),
                pltpu.VMEM((2, 3, npad, 192), BF),
                pltpu.VMEM((6 * WPAD, 6 * HD), BF),
                pltpu.VMEM((192, C), F32),
                pltpu.VMEM((ntok, C), F32),
            ],
        )
        if layer == 1:
            g = (gin, to_tp(gin.reshape(tiles)[-1, :, WIN - SHIFT :]))
        chunks[layer] = (reduce_chunk(keep_m, send_m), reduce_chunk(keep_a, send_a))
        smalls[layer] = (gfb1, sh2, gpos, gqvb, sh1)

    gpos = jnp.stack([s[2] for s in smalls])
    gpos = gpos.reshape(2, 2, WPAD, 6, WPAD).transpose(0, 1, 3, 2, 4).reshape(24, -1)
    gtab = lax.dot_general(
        gpos, onehot, (((1,), (1,)), ((), ())), precision=lax.Precision.HIGHEST
    ).reshape(2, 2, 2, 3, -1)
    gqvb = jnp.stack([s[3] for s in smalls]).reshape(2, 2, 2, 2, 96).transpose(0, 1, 3, 2, 4)
    gfb1 = jnp.stack([s[0] for s in smalls]).reshape(2, 2, 2, C)
    pack = jnp.concatenate(
        [
            gqvb.transpose(1, 2, 0, 3, 4).reshape(2, 2, -1),
            gfb1.transpose(1, 2, 0, 3).reshape(2, 2, -1),
            gtab.transpose(1, 2, 0, 3, 4).reshape(2, 2, -1),
        ],
        axis=2,
    )
    theirs = jnp.where(par == 0, pack[1], pack[1][::-1])
    shared = jnp.stack([jnp.concatenate([s[4], s[1]]) for s in smalls])
    shared = shared + to_tp(shared)
    mine = pack[0] + to_tp(theirs)
    flat = jnp.concatenate([shared.reshape(-1), mine.reshape(-1)])
    size = flat.shape[0]
    flat = jnp.pad(flat, (0, -size % 1024)).reshape(-1, 128)
    for bit in range(bits):
        flat = flat + to_win(flat, bit)
    flat = flat.reshape(-1)[:size]
    shared = flat[: 12 * C].reshape(2, 6, C)
    mine = flat[12 * C :].reshape(2, -1)
    m1, m2 = 2 * 2 * 96, 2 * C
    out_qvb = mine[:, :m1].reshape(2, 2, 2, 96).transpose(1, 2, 0, 3).reshape(2, 2, 192)
    out_fb1 = mine[:, m1 : m1 + m2].reshape(2, 2, C).transpose(1, 0, 2).reshape(2, 2 * C)
    out_tab = mine[:, m1 + m2 :].reshape(2, 2, 3, -1).transpose(1, 3, 0, 2)
    out_tab = out_tab.reshape(2, -1, 6)

    def halves(pair):
        a, b = pair
        return jnp.where(par == 0, a, b).astype(F32), jnp.where(par == 0, b, a).astype(F32)

    gq, gp_, g1, g2 = [], [], [], []
    for layer in range(2):
        m0, m1 = halves(chunks[layer][0])
        a0, a1 = halves(chunks[layer][1])
        g1.append(jnp.concatenate([m0[:C], m1[:C]], axis=1))
        g2.append(jnp.concatenate([m0[C:], m1[C:]], axis=0))
        gp_.append(jnp.concatenate([a0[288:], a1[288:]], axis=0))
        q = jnp.stack([a0[:288].reshape(3, 96, C), a1[:288].reshape(3, 96, C)], axis=1)
        gq.append(q.reshape(3, 192, C).transpose(2, 0, 1))
    return (
        layer_out[None],
        gin[None],
        jnp.stack([shared[:, 0], shared[:, 3]], axis=1),
        jnp.stack([shared[:, 1], shared[:, 4]], axis=1),
        jnp.stack(gq),
        out_qvb,
        jnp.stack(gp_),
        shared[:, 2],
        jnp.stack(g1),
        out_fb1,
        jnp.stack(g2),
        shared[:, 5],
        out_tab,
    )


def solution(mesh):
    return jax.shard_map(
        partial(on_device, mesh.shape["win"]),
        mesh=mesh,
        in_specs=(
            P("win", "tp", None, None),
            P("win", None, None),
            P("win", "tp", None, None),
            P(),
            P(),
            P(None, None, None, "tp"),
            P(None, None, "tp"),
            P(None, "tp", None),
            P(),
            P(None, None, "tp"),
            P(None, "tp"),
            P(None, "tp", None),
            P(),
            P(None, None, "tp"),
        ),
        out_specs=(
            P("win", "tp", None, None),
            P("win", "tp", None, None),
            P(),
            P(),
            P(None, None, None, "tp"),
            P(None, None, "tp"),
            P(None, "tp", None),
            P(),
            P(None, None, "tp"),
            P(None, "tp"),
            P(None, "tp", None),
            P(),
            P(None, None, "tp"),
        ),
        check_vma=False,
    )
```

```python
from functools import partial

import jax
import jax.numpy as jnp
import numpy as np
from jax import lax
from jax.experimental import pallas as pl
from jax.experimental.pallas import tpu as pltpu
from jax.sharding import PartitionSpec as P

C = 384
WIN = 7
SHIFT = 3
HD = 32
EPS = 1e-05
NEG = -1000000000.0
SCALE = HD**-0.5
F32 = jnp.float32
BF = jnp.bfloat16
SEG = 8
WROWS = WIN * SEG
WPAD = 64


def nn(a, b):
    return lax.dot_general(a, b, (((1,), (0,)), ((), ())), preferred_element_type=F32)


def nt(a, b):
    return lax.dot_general(a, b, (((1,), (1,)), ((), ())), preferred_element_type=F32)


def tn(a, b):
    return lax.dot_general(a, b, (((0,), (0,)), ((), ())), preferred_element_type=F32)


def norm_stats(x):
    mean = jnp.mean(x, -1, keepdims=True)
    cent = x - mean
    var = jnp.mean(cent * cent, -1, keepdims=True)
    rinv = lax.rsqrt(var + EPS)
    return cent * rinv, rinv


def norm_back(dz, xhat, rinv, gain):
    d = dz * gain
    return rinv * (
        d - jnp.mean(d, -1, keepdims=True) - xhat * jnp.mean(d * xhat, -1, keepdims=True)
    )


def tile_row(r, k, across):
    return (((r // WIN) * across + k) * WIN + r % WIN) * SEG


def zero_rows(n):
    return jnp.zeros((n, C), F32)


def head_mask():
    row = lax.broadcasted_iota(jnp.int32, (6 * WPAD, 6 * HD), 0) // WPAD
    col = lax.broadcasted_iota(jnp.int32, (6 * WPAD, 6 * HD), 1) // HD
    return (row == col).astype(BF)


def spread(x, mask):
    return jnp.concatenate([x] * 6, axis=0) * mask


def fold(o):
    lane = lax.broadcasted_iota(jnp.int32, (WPAD, 128), 1)

    def of(h, a, b):
        return o[WPAD * h : WPAD * (h + 1), a:b]

    one = jnp.where(lane < 96, of(2, 0, 128), of(3, 0, 128))
    one = jnp.where(lane < 64, of(1, 0, 128), one)
    one = jnp.where(lane < 32, of(0, 0, 128), one)
    two = jnp.where(lane[:, :64] < 32, of(4, 128, 192), of(5, 128, 192))
    return jnp.concatenate([one, two], axis=1)


def rows_at(i, n):
    return pl.ds(pl.multiple_of(i * n, n), n)


def iota(shape, dim):
    return lax.broadcasted_iota(jnp.int32, shape, dim)


def exact(a, b, ca, cb):
    return lax.dot_general(
        a,
        b,
        (((ca,), (cb,)), ((), ())),
        precision=lax.Precision.HIGHEST,
        preferred_element_type=F32,
    )


def offset_rows():
    return (12 - iota((16, 169), 0) == iota((16, 169), 1) // 13).astype(F32)


def offset_cols():
    return (iota((96, 169), 0) % 16 == iota((96, 169), 1) % 13).astype(F32)


def column_pick(kx):
    r = iota((96, 6 * WPAD), 0)
    c = iota((96, 6 * WPAD), 1)
    qx = c % 8
    return ((r // 16 == c // WPAD) & (r % 16 == qx - kx + WIN - 1) & (qx < WIN)).astype(F32)


def table_to_map(t, pos_ref):
    pos_ref[...] = jnp.zeros_like(pos_ref)
    group = (iota((8, 6 * WPAD), 1) % WPAD) // 8
    for kx in range(WIN):
        h = exact(t, column_pick(kx), 1, 0)
        g = jnp.zeros((8, 6 * WPAD), F32)
        for j in range(WIN):
            g = jnp.where(group == j, h[6 - j : 14 - j], g)
        for i in range(3):
            pos_ref[i, pl.ds(kx, 8, stride=8), :] = g[:, 128 * i : 128 * (i + 1)]


def map_to_table(pos_ref):
    group = (iota((16, 6 * WPAD), 1) % WPAD) // 8
    total = jnp.zeros((16, 96), F32)
    for kx in range(WIN):
        r = jnp.concatenate([pos_ref[i, pl.ds(kx, 8, stride=8), :] for i in range(3)], axis=1)
        h = jnp.zeros((16, 6 * WPAD), F32)
        for j in range(WIN):
            parts = [r, jnp.zeros((2 + j, 6 * WPAD), F32)]
            if j < 6:
                parts = [jnp.zeros((6 - j, 6 * WPAD), F32)] + parts
            h = jnp.where(group == j, jnp.concatenate(parts, axis=0), h)
        total = total + exact(h, column_pick(kx), 1, 1)
    return total


def shift_in(tile, x_ref, rows, across):
    for r in range(rows):
        for k in range(across):
            a = tile(r + SHIFT, k)
            b = tile(r + SHIFT, (k + 1) % across)
            x_ref[pl.ds(tile_row(r, k, across), SEG), :] = jnp.concatenate(
                [a[SHIFT:WIN], b[:SHIFT], zero_rows(1)], axis=0
            )


def shift_out(tile, x_ref, rows, across):
    for r in range(rows):
        for k in range(across):
            a = tile(r - SHIFT, (k - 1) % across)
            b = tile(r - SHIFT, k)
            x_ref[pl.ds(tile_row(r, k, across), SEG), :] = jnp.concatenate(
                [a[WIN - SHIFT : WIN], b[: WIN - SHIFT], zero_rows(1)], axis=0
            )

SMALL = 32


def prep_kernel(
    rows, across, tab_ref, qvb_ref, fb1_ref, crop_ref, info_ref, small_ref, lq_ref, lk_ref, pos_ref, c_ref
):
    tp = info_ref[1]
    cols = across * WIN
    height = crop_ref.shape[2]
    small_ref[...] = jnp.zeros_like(small_ref)
    for layer in range(2):
        tab = tab_ref[:, layer, :]
        wide = jnp.concatenate([jnp.broadcast_to(tab[h : h + 1], (16, 169)) for h in range(6)])
        t = exact(offset_rows(), wide * offset_cols(), 1, 1)
        small_ref[layer, 0:16, 0:96] = t
        small_ref[layer, 16:17, :] = fb1_ref[layer : layer + 1, 0:C]
        small_ref[layer, 17:18, :] = fb1_ref[layer : layer + 1, C:]
        small_ref[layer, 18:20, 0:192] = qvb_ref[layer]
        table_to_map(t, pos_ref.at[layer])
    c_ref[...] = jnp.zeros_like(c_ref)
    c_ref[0:cols, 0:height] = crop_ref[:, 0, :].astype(F32)
    crops = c_ref[...].astype(BF)
    row = iota((32, 128), 0)
    lane = iota((32, 128), 1)
    for layer in range(2):
        shift = SHIFT if layer == 1 else 0
        src = rows * tp + row + shift
        src = jnp.where(src >= height, src - height, src)
        grid = nt((src == lane).astype(BF), crops).astype(BF)
        for wc in range(across):
            qx = iota((128, 128), 1) % 8
            col = qx + (WIN * wc + shift)
            col = jnp.where(col >= cols, col - cols, col)
            pick = ((col == iota((128, 128), 0)) & (qx < WIN)).astype(BF)
            lab = nn(grid, pick)
            if layer == 1:
                g = rows * tp + row
                zr = (g >= height - WIN).astype(F32) + (g >= height - SHIFT).astype(F32)
                here = lane % 8 + WIN * wc
                zc = (here >= cols - WIN).astype(F32) + (here >= cols - SHIFT).astype(F32)
                lab = lab * 9.0 + zr * 3.0 + zc
            real = (iota((1, 128), 1) % 8 < WIN) & (iota((1, 128), 1) % WPAD < WROWS)
            for wr in range(rows // WIN):
                w = wr * across + wc
                mine = row == (lane % WPAD) // 8 + WIN * wr
                line = jnp.sum(jnp.where(mine, lab, 0.0), 0, keepdims=True)
                line = jnp.where(real, line, -1.0)
                lq_ref[layer, w : w + 1, :] = line
                lk_ref[layer, w] = jnp.broadcast_to(line, (128, 128)).T[:WPAD]


def qkv_weight_of(half, j, layer, qkvw_ref, a_ref, b_ref):
    if half == 0:
        return qkvw_ref[layer, j]
    return jnp.concatenate([a_ref[96 * j : 96 * (j + 1)], b_ref[96 * j : 96 * (j + 1)]], axis=0)


def proj_weight_of(half, layer, projw_ref, a_ref, b_ref):
    if half == 0:
        return projw_ref[layer]
    return jnp.concatenate([a_ref[288:384], b_ref[288:384]], axis=0)


def norm_windows(layer, wins, x_ref, xn_ref, gain_ref, bias_ref):
    gain = gain_ref[layer, 0:1]
    bias = bias_ref[layer, 0:1]

    def four(i, carry):
        xhat, _ = norm_stats(x_ref[rows_at(i, 4 * WROWS), :])
        xn = xhat * gain + bias
        for n in range(4):
            part = jnp.concatenate(
                [xn[n * WROWS : (n + 1) * WROWS], zero_rows(WPAD - WROWS)], axis=0
            )
            xn_ref[rows_at(4 * i + n, WPAD), :] = part.astype(BF)
        return carry

    lax.fori_loop(0, wins // 4, four, 0)


def project_half(xn_ref, qkv_ref, weight, qb, vb):
    n = xn_ref.shape[0] // 2

    def part(i, carry):
        at = rows_at(i, n)
        xn = xn_ref[at, :]
        q = nt(xn, weight(0))
        k = nt(xn, weight(1))
        v = nt(xn, weight(2))
        qkv_ref[0, at, :] = ((q + qb) * SCALE).astype(BF)
        qkv_ref[1, at, :] = k.astype(BF)
        qkv_ref[2, at, :] = (v + vb).astype(BF)
        return carry

    lax.fori_loop(0, 2, part, 0)


def attend_forward(halves, wins, group, layer, lq_ref, lk_ref, mask_ref):
    def body(i, carry):
        units = [(i * group + u, h) for u in range(group) for h in halves]
        scores = []
        for w, (qkv_ref, _, _, _) in units:
            at = rows_at(w, WPAD)
            scores.append(nt(qkv_ref[1, at, :], spread(qkv_ref[0, at, :], mask_ref[...])))
        probs = []
        for (w, (_, pos, p_ref, _)), s in zip(units, scores):
            same = lk_ref[layer, w] == lq_ref[layer, pl.ds(w, 1), :]
            same = jnp.concatenate([same] * 3, axis=1)
            s = jnp.where(same, s + jnp.concatenate([pos[n] for n in range(3)], axis=1), NEG)
            e = jnp.exp(s - jnp.max(s, 0, keepdims=True))
            p = (e * (1.0 / jnp.sum(e, 0, keepdims=True))).astype(BF)
            p_ref[w] = p
            probs.append(p)
        for (w, (qkv_ref, _, _, mix_ref)), p in zip(units, probs):
            at = rows_at(w, WPAD)
            mix_ref[at, :] = fold(tn(p, qkv_ref[2, at, :])).astype(BF)
        return carry

    lax.fori_loop(0, wins // group, body, 0)


def add_branch(wins, mixes, weights, bias, x_ref, hid_ref):
    n = 8

    def part(i, carry):
        res = bias
        for m_ref, w in zip(mixes, weights):
            res = res + nn(m_ref[rows_at(i, n * WPAD), :], w)
        for k in range(n):
            to = rows_at(i * n + k, WROWS)
            hid_ref[to, :] = x_ref[to, :] + res[k * WPAD : k * WPAD + WROWS]
        return carry

    lax.fori_loop(0, wins // n, part, 0)


def attn_own_kernel(rows, across, *refs):
    (tok_ref, gain_ref, bias_ref, pb_ref, qvb_ref, qkvw_ref, projw_ref) = refs[:7]
    (pos_ref, lq_ref, lk_ref) = refs[7:10]
    (x_ref, xn_ref, hid_ref, qkv_ref, p_ref, mix_ref, mask_ref) = refs[10:]
    wins = (rows // WIN) * across
    for r in range(rows):
        row = tok_ref[r].astype(F32)
        for k in range(across):
            x_ref[pl.ds(tile_row(r, k, across), SEG), :] = jnp.concatenate(
                [row[WIN * k : WIN * (k + 1)], zero_rows(1)], axis=0
            )
    mask_ref[...] = head_mask()
    norm_windows(0, wins, x_ref, xn_ref, gain_ref, bias_ref)
    project_half(
        xn_ref, qkv_ref, lambda j: qkvw_ref[0, j], qvb_ref[0, 0:1], qvb_ref[0, 1:2]
    )
    attend_forward(
        [(qkv_ref, pos_ref.at[0], p_ref, mix_ref)], wins, 8, 0, lq_ref, lk_ref, mask_ref
    )
    add_branch(wins, [mix_ref], [projw_ref[0]], pb_ref[0:1], x_ref, hid_ref)


def attn_other_kernel(rows, across, *refs):
    (part_ref, xn_ref, small_ref, a_ref, b_ref, lq_ref, lk_ref, info_ref) = refs[:8]
    (hid_ref, qkv_ref, p_ref, mix_ref, mask_ref, pos_ref, t_ref) = refs[8:]
    wins = (rows // WIN) * across
    mask_ref[...] = head_mask()
    bias = other_small(small_ref, 0, info_ref[0], t_ref, pos_ref)
    project_half(
        xn_ref,
        qkv_ref,
        lambda j: qkv_weight_of(1, j, 0, None, a_ref, b_ref),
        bias[0:1],
        bias[1:2],
    )
    attend_forward([(qkv_ref, pos_ref, p_ref, mix_ref)], wins, 8, 0, lq_ref, lk_ref, mask_ref)
    add_branch(
        wins, [mix_ref], [proj_weight_of(1, 0, None, a_ref, b_ref)], 0.0, part_ref, hid_ref
    )


def other_small(small_ref, layer, par, t_ref, pos_ref):
    first = par == 0

    def swapped(v, n):
        return jnp.where(first, v, jnp.concatenate([v[:, n : 2 * n], v[:, :n]], axis=1))

    t = swapped(small_ref[layer, 0:16, 0:96], 48)
    table_to_map(t, pos_ref)
    return swapped(small_ref[layer, 18:20, 0:192], 96)


def attn_both_kernel(rows, across, *refs):
    (st_ref, halo_ref, gain_ref, bias_ref, pb_ref, qvb_ref, qkvw_ref, projw_ref) = refs[:8]
    (pos_ref, small_ref, a_ref, b_ref, lq_ref, lk_ref, info_ref) = refs[8:15]
    (x_ref, xn_ref, hid_ref, qkv0_ref, p0_ref, mix0_ref) = refs[15:21]
    (qkv1_ref, p1_ref, mix1_ref, mask_ref, pos1_ref, t_ref) = refs[21:]
    wins = (rows // WIN) * across

    def tile(r, k):
        if r < rows:
            return st_ref[pl.ds(tile_row(r, k, across), SEG), :]
        return halo_ref[k, r - rows]

    shift_in(tile, x_ref, rows, across)
    mask_ref[...] = head_mask()
    bias = other_small(small_ref, 1, info_ref[0], t_ref, pos1_ref)
    norm_windows(1, wins, x_ref, xn_ref, gain_ref, bias_ref)
    project_half(
        xn_ref, qkv0_ref, lambda j: qkvw_ref[1, j], qvb_ref[1, 0:1], qvb_ref[1, 1:2]
    )
    project_half(
        xn_ref,
        qkv1_ref,
        lambda j: qkv_weight_of(1, j, 1, None, a_ref, b_ref),
        bias[0:1],
        bias[1:2],
    )
    attend_forward(
        [(qkv0_ref, pos_ref.at[1], p0_ref, mix0_ref), (qkv1_ref, pos1_ref, p1_ref, mix1_ref)],
        wins,
        4,
        1,
        lq_ref,
        lk_ref,
        mask_ref,
    )
    add_branch(
        wins,
        [mix0_ref, mix1_ref],
        [projw_ref[1], proj_weight_of(1, 1, None, a_ref, b_ref)],
        pb_ref[1:2],
        x_ref,
        hid_ref,
    )


def up_weight(part, layer, base, f1_ref, a_ref, b_ref):
    if part == 0:
        return f1_ref[layer]
    return jnp.concatenate([a_ref[base : base + C], b_ref[base : base + C]], axis=1)


def down_weight(part, layer, base, f2_ref, a_ref, b_ref):
    if part == 0:
        return f2_ref[layer]
    return jnp.concatenate([a_ref[base + C : base + 2 * C], b_ref[base + C : base + 2 * C]], axis=0)


def up_biases(layer, par, fb1_ref, small_ref):
    own = fb1_ref[layer : layer + 1]
    one, two = small_ref[layer, 16:17], small_ref[layer, 17:18]
    first = par == 0
    return own, jnp.concatenate(
        [jnp.where(first, one, two), jnp.where(first, two, one)], axis=1
    )


def gelu_pair(u):
    phi = 0.5 + 0.5 * lax.erf(u * (2.0**-0.5))
    slope = phi + u * (jnp.exp(-0.5 * u * u) * (2.0 * np.pi) ** -0.5)
    return (u * phi).astype(BF), slope.astype(BF)


def mlp_fwd_kernel(
    layer, base, hid_ref, gain_ref, bias_ref, fb1_ref, small_ref, fb2_ref, f1_ref, f2_ref, a_ref,
    b_ref, info_ref, st_ref, act_ref, gp_ref
):
    h = hid_ref[...]
    xhat, _ = norm_stats(h)
    n2 = (xhat * gain_ref[layer, 1:2] + bias_ref[layer, 1:2]).astype(BF)
    biases = up_biases(layer, info_ref[0], fb1_ref, small_ref)
    ups = [
        nn(n2, up_weight(p, layer, base, f1_ref, a_ref, b_ref)) + biases[p] for p in range(2)
    ]
    acts = []
    for p in range(2):
        act, slope = gelu_pair(ups[p])
        acts.append(act)
        for z in range(2):
            act_ref[2 * p + z] = act[:, C * z : C * (z + 1)]
            gp_ref[2 * p + z] = slope[:, C * z : C * (z + 1)]
    down = nn(acts[0], down_weight(0, layer, base, f2_ref, a_ref, b_ref)) + nn(
        acts[1], down_weight(1, layer, base, f2_ref, a_ref, b_ref)
    )
    st_ref[...] = h + fb2_ref[layer : layer + 1] + down


def mlp_back_rows(
    layer, base, at, g, h, slopes, gain, bias, f1_ref, f2_ref, a_ref, b_ref, refs, carry
):
    (gh_ref, df_ref, n2_ref, du_ref) = refs
    (sb, sg, sf, s1) = carry
    df = g.astype(BF)
    df_ref[at, :] = df
    sf = sf + jnp.sum(df.astype(F32), 0, keepdims=True)
    grads = [nt(df, down_weight(p, layer, base, f2_ref, a_ref, b_ref)) for p in range(2)]
    new = []
    parts = []
    for p in range(2):
        du = [
            (grads[p][:, C * z : C * (z + 1)] * slopes(2 * p + z).astype(F32)).astype(BF)
            for z in range(2)
        ]
        for z in range(2):
            du_ref[2 * p + z, at, :] = du[z]
            new.append(s1[2 * p + z] + jnp.sum(du[z].astype(F32), 0, keepdims=True))
        parts.append(jnp.concatenate(du, axis=1))
    dz = nt(parts[0], up_weight(0, layer, base, f1_ref, a_ref, b_ref)) + nt(
        parts[1], up_weight(1, layer, base, f1_ref, a_ref, b_ref)
    )
    xhat, rinv = norm_stats(h)
    n2_ref[at, :] = (xhat * gain + bias).astype(BF)
    sg = sg + jnp.sum(dz * xhat, 0, keepdims=True)
    sb = sb + jnp.sum(dz, 0, keepdims=True)
    gh_ref[at, :] = g + norm_back(dz, xhat, rinv, gain)
    return sb, sg, sf, tuple(new)


def mlp_weight_grads(par, n2_ref, df_ref, du_ref, act_ref, keep_ref, send_ref):
    n2 = n2_ref[...]
    df = df_ref[...]
    for slot, ref in ((1, send_ref), (0, keep_ref)):
        for part in range(2):
            q = (par ^ slot) if part == 0 else 2 + slot
            ref[part, 0:C, :] = tn(n2, du_ref[q]).astype(BF)
            ref[part, C:, :] = tn(act_ref[q], df).astype(BF)


def mlp_sums(carry, fb1_ref, sh_ref):
    sb, sg, sf, s1 = carry
    for q in range(4):
        fb1_ref[q : q + 1] = s1[q]
    sh_ref[0:1] = sg
    sh_ref[1:2] = sb
    sh_ref[2:3] = sf


def zero_sums():
    z = jnp.zeros((1, C), F32)
    return z, z, z, (z,) * 4


def mlp_both_kernel(rows, across, base, *refs):
    (cot_ref, halo_ref, hid_ref, gain_ref, bias_ref, fb1b_ref, small_ref, fb2_ref) = refs[:8]
    (f1_ref, f2_ref, a_ref, b_ref, info_ref) = refs[8:13]
    (st_ref, gh_ref, keep_ref, send_ref, fb1_ref, sh_ref) = refs[13:19]
    (g_ref, df_ref, n2_ref, du_ref, act_ref) = refs[19:]
    layer = 1
    for r in range(rows):
        s = r + SHIFT
        row = (cot_ref[s] if s < rows else halo_ref[s - rows]).astype(F32)
        for k in range(across):
            a = WIN * k + SHIFT
            if k < across - 1:
                piece = [row[a : a + WIN]]
            else:
                piece = [row[a:], row[:SHIFT]]
            g_ref[pl.ds(tile_row(r, k, across), SEG), :] = jnp.concatenate(
                piece + [zero_rows(1)], axis=0
            )
    gain = gain_ref[layer, 1:2]
    bias = bias_ref[layer, 1:2]
    par = info_ref[0]
    biases = up_biases(layer, par, fb1b_ref, small_ref)
    n = hid_ref.shape[0] // 2

    def block(i, carry):
        at = rows_at(i, n)
        h = hid_ref[at, :]
        xhat, _ = norm_stats(h)
        n2 = (xhat * gain + bias).astype(BF)
        ups = [
            nn(n2, up_weight(p, layer, base, f1_ref, a_ref, b_ref)) + biases[p] for p in range(2)
        ]
        acts = []
        slopes = []
        for p in range(2):
            act, slope = gelu_pair(ups[p])
            acts.append(act)
            for z in range(2):
                act_ref[2 * p + z, at, :] = act[:, C * z : C * (z + 1)]
                slopes.append(slope[:, C * z : C * (z + 1)])
        down = nn(acts[0], down_weight(0, layer, base, f2_ref, a_ref, b_ref)) + nn(
            acts[1], down_weight(1, layer, base, f2_ref, a_ref, b_ref)
        )
        st_ref[at, :] = h + fb2_ref[layer : layer + 1] + down
        return mlp_back_rows(
            layer, base, at, g_ref[at, :], h, lambda q: slopes[q], gain, bias, f1_ref, f2_ref,
            a_ref, b_ref, (gh_ref, df_ref, n2_ref, du_ref), carry
        )

    mlp_sums(lax.fori_loop(0, 2, block, zero_sums()), fb1_ref, sh_ref)
    mlp_weight_grads(par, n2_ref, df_ref, du_ref, act_ref, keep_ref, send_ref)


def mlp_bwd_kernel(rows, across, base, n_dep, *refs):
    (gin_ref, halo_ref, hid_ref, act_ref, gp_ref, gain_ref, bias_ref) = refs[:7]
    (f1_ref, f2_ref, a_ref, b_ref, info_ref) = refs[7:12]
    refs = refs[12 + n_dep :]
    (gh_ref, keep_ref, send_ref, fb1_ref, sh_ref) = refs[:5]
    (g_ref, df_ref, n2_ref, du_ref) = refs[5:]
    layer = 0

    def tile(r, k):
        if r >= 0:
            return gin_ref[pl.ds(tile_row(r, k, across), SEG), :]
        return halo_ref[k, r + SHIFT]

    shift_out(tile, g_ref, rows, across)
    gain = gain_ref[layer, 1:2]
    bias = bias_ref[layer, 1:2]
    n = hid_ref.shape[0] // 2

    def block(i, carry):
        at = rows_at(i, n)
        return mlp_back_rows(
            layer, base, at, g_ref[at, :], hid_ref[at, :], lambda q: gp_ref[q, at, :], gain, bias,
            f1_ref, f2_ref, a_ref, b_ref, (gh_ref, df_ref, n2_ref, du_ref), carry
        )

    mlp_sums(lax.fori_loop(0, 2, block, zero_sums()), fb1_ref, sh_ref)
    mlp_weight_grads(info_ref[0], n2_ref, df_ref, du_ref, act_ref, keep_ref, send_ref)


def window_grads(wins, gh_ref, da_ref):
    def four(i, s):
        g = gh_ref[rows_at(i, 4 * WROWS), :]
        for n in range(4):
            part = jnp.concatenate(
                [g[n * WROWS : (n + 1) * WROWS], zero_rows(WPAD - WROWS)], axis=0
            ).astype(BF)
            da_ref[rows_at(4 * i + n, WPAD), :] = part
            s = s + jnp.sum(part.astype(F32), 0, keepdims=True)
        return s

    return lax.fori_loop(0, wins // 4, four, jnp.zeros((1, C), F32))


def attend_backward(halves, wins, group, mask_ref):
    def body(i, carry):
        units = [(i * group + u, h) for u in range(group) for h in halves]
        first = []
        for w, (qkv_ref, p_ref, do_ref, dqkv_ref, _) in units:
            at = rows_at(w, WPAD)
            do = spread(do_ref[at, :], mask_ref[...])
            first.append(nt(qkv_ref[2, at, :], do))
            dqkv_ref[2, at, :] = nn(p_ref[w], do).astype(BF)
        second = []
        for (w, (_, p_ref, _, _, acc_ref)), dp in zip(units, first):
            p = p_ref[w].astype(F32)
            ds = p * (dp - jnp.sum(p * dp, 0, keepdims=True))
            for n in range(3):
                acc_ref[n] += ds[:, 128 * n : 128 * (n + 1)]
            second.append(ds.astype(BF))
        for (w, (qkv_ref, _, _, dqkv_ref, _)), ds in zip(units, second):
            at = rows_at(w, WPAD)
            dqkv_ref[1, at, :] = nn(ds, spread(qkv_ref[0, at, :], mask_ref[...])).astype(BF)
            dqkv_ref[0, at, :] = fold(tn(ds, qkv_ref[1, at, :])).astype(BF)
        return carry

    lax.fori_loop(0, wins // group, body, 0)


def half_grads(half, par, xn_ref, da_ref, mix_ref, dqkv_ref, row_ref, give):
    def put(value, at):
        if half == 0:
            row_ref[...] = value
            one = row_ref[pl.ds(pl.multiple_of(par * 96, 96), 96), :]
            two = row_ref[pl.ds(pl.multiple_of((1 - par) * 96, 96), 96), :]
        else:
            one, two = value[:96], value[96:]
        give(at, one.astype(BF), two.astype(BF))

    xn = xn_ref[...]
    for j in range(3):
        grad = tn(dqkv_ref[j], xn)
        put(grad * SCALE if j == 0 else grad, 96 * j)
    put(tn(mix_ref[...], da_ref[...]), 288)


def normed_grads(layer, wins, dqkvs, weights, gh_ref, x_ref, gain_ref, gx_ref):
    gain = gain_ref[layer, 0:1]
    n = 8

    def part(i, carry):
        sg, sb, sq = carry
        at = rows_at(i, n * WPAD)
        dn = nn(dqkvs[0][0, at, :], weights[0](0)) + nn(dqkvs[1][0, at, :], weights[1](0))
        dn = dn * SCALE
        for half in range(2):
            for j in (1, 2):
                dn = dn + nn(dqkvs[half][j, at, :], weights[half](j))
        new = []
        for half in range(2):
            for m, j in enumerate((0, 2)):
                new.append(
                    sq[half * 2 + m] + jnp.sum(dqkvs[half][j, at, :].astype(F32), 0, keepdims=True)
                )
        d = jnp.concatenate([dn[k * WPAD : k * WPAD + WROWS] for k in range(n)], axis=0)
        to = rows_at(i, n * WROWS)
        xhat, rinv = norm_stats(x_ref[to, :])
        sg = sg + jnp.sum(d * xhat, 0, keepdims=True)
        sb = sb + jnp.sum(d, 0, keepdims=True)
        gx_ref[to, :] = gh_ref[to, :] + norm_back(d, xhat, rinv, gain)
        return sg, sb, tuple(new)

    z = jnp.zeros((1, C), F32)
    zq = jnp.zeros((1, 6 * HD), F32)
    return lax.fori_loop(0, wins // n, part, (z, z, (zq,) * 4))


def small_grads(par, sums, projb, fb1_ref, sh_ref, accs, sm_ref):
    sg, sb, sq = sums
    sm_ref[...] = jnp.zeros_like(sm_ref)
    tables = [map_to_table(a) for a in accs]
    for q in range(4):
        half, z = q // 2, q % 2
        sm_ref[q, 0:1] = sg
        sm_ref[q, 1:2] = sb
        sm_ref[q, 2:3] = projb
        sm_ref[q, 3:6] = sh_ref[...]
        sm_ref[q, 6:7] = fb1_ref[q : q + 1]
        sm_ref[q, 7:8, 0:96] = sq[2 * half][:, 96 * z : 96 * (z + 1)] * SCALE
        sm_ref[q, 7:8, 128:224] = sq[2 * half + 1][:, 96 * z : 96 * (z + 1)]
        sm_ref[q, 8:24, 0:48] = tables[half][:, 48 * z : 48 * (z + 1)]


def attn_bwd_kernel(rows, across, n_dep, *refs):
    (gh_ref, x_ref, xn_ref, gain_ref, qkvw_ref, projw_ref, a_ref, b_ref, info_ref) = refs[:9]
    (fb1_ref, sh_ref, qkv0_ref, p0_ref, mix0_ref, qkv1_ref, p1_ref, mix1_ref) = refs[9:17]
    refs = refs[17 + n_dep :]
    (gin_ref, keep_ref, send_ref) = refs[:3]
    (da_ref, do_ref, dqkv0_ref, dqkv1_ref, acc_ref, mask_ref, row_ref, sm_ref) = refs[3:]
    layer = 1
    par = info_ref[0]
    wins = (rows // WIN) * across
    mask_ref[...] = head_mask()
    acc_ref[...] = jnp.zeros_like(acc_ref)
    projb = window_grads(wins, gh_ref, da_ref)
    for half in range(2):
        do_ref[half] = nt(
            da_ref[...], proj_weight_of(half, layer, projw_ref, a_ref, b_ref)
        ).astype(BF)
    attend_backward(
        [
            (qkv0_ref, p0_ref, do_ref.at[0], dqkv0_ref, acc_ref.at[0]),
            (qkv1_ref, p1_ref, do_ref.at[1], dqkv1_ref, acc_ref.at[1]),
        ],
        wins,
        4,
        mask_ref,
    )
    for half, mix_ref, dqkv_ref in ((1, mix1_ref, dqkv1_ref), (0, mix0_ref, dqkv0_ref)):

        def give(at, one, two, half=half):
            keep_ref[half, at : at + 96, :] = one
            send_ref[half, at : at + 96, :] = two

        half_grads(half, par, xn_ref, da_ref, mix_ref, dqkv_ref, row_ref, give)
    weights = [
        lambda j, half=half: qkv_weight_of(half, j, layer, qkvw_ref, a_ref, b_ref)
        for half in range(2)
    ]
    sums = normed_grads(
        layer, wins, [dqkv0_ref, dqkv1_ref], weights, gh_ref, x_ref, gain_ref, gin_ref
    )
    small_grads(par, sums, projb, fb1_ref, sh_ref, [acc_ref.at[0], acc_ref.at[1]], sm_ref)
    keep_ref[0, C:, :] = sm_ref[par].astype(BF)
    send_ref[0, C:, :] = sm_ref[1 - par].astype(BF)
    keep_ref[1, C:, :] = sm_ref[2].astype(BF)
    send_ref[1, C:, :] = sm_ref[3].astype(BF)


def attn_bwd_other_kernel(rows, across, n_dep, *refs):
    (gh_ref, xn_ref, projw_ref, a_ref, b_ref, qkv_ref, p_ref, mix_ref) = refs[:8]
    refs = refs[8 + n_dep :]
    (da_ref, do_ref, dqkv_ref, acc_ref, pb_ref, keep_ref, send_ref) = refs[:7]
    (do1_ref, mask_ref) = refs[7:]
    wins = (rows // WIN) * across
    mask_ref[...] = head_mask()
    acc_ref[...] = jnp.zeros_like(acc_ref)
    pb_ref[...] = window_grads(wins, gh_ref, da_ref)
    da = da_ref[...]
    do1_ref[...] = nt(da, proj_weight_of(1, 0, projw_ref, a_ref, b_ref)).astype(BF)
    do_ref[...] = nt(da, proj_weight_of(0, 0, projw_ref, a_ref, b_ref)).astype(BF)
    attend_backward([(qkv_ref, p_ref, do1_ref, dqkv_ref, acc_ref)], wins, 8, mask_ref)

    def give(at, one, two):
        keep_ref[at : at + 96, :] = one
        send_ref[at : at + 96, :] = two

    half_grads(1, None, xn_ref, da_ref, mix_ref, dqkv_ref, None, give)


def attn_bwd_own_kernel(rows, across, n_dep, *refs):
    (gh_ref, x_ref, xn_ref, gain_ref, qkvw_ref, a_ref, b_ref, info_ref) = refs[:8]
    (fb1_ref, sh_ref, da_ref, do_ref, dqkv1_ref, acc1_ref, pb_ref) = refs[8:15]
    (qkv_ref, p_ref, mix_ref) = refs[15:18]
    refs = refs[18 + n_dep :]
    (out_ref, keep_ref, send_ref) = refs[:3]
    (dqkv_ref, acc_ref, gx_ref, mask_ref, row_ref, sm_ref) = refs[3:]
    par = info_ref[0]
    wins = (rows // WIN) * across
    mask_ref[...] = head_mask()
    acc_ref[...] = jnp.zeros_like(acc_ref)
    attend_backward([(qkv_ref, p_ref, do_ref, dqkv_ref, acc_ref)], wins, 8, mask_ref)

    def give(at, one, two):
        keep_ref[at : at + 96, :] = one
        send_ref[at : at + 96, :] = two

    half_grads(0, par, xn_ref, da_ref, mix_ref, dqkv_ref, row_ref, give)
    weights = [
        lambda j, half=half: qkv_weight_of(half, j, 0, qkvw_ref, a_ref, b_ref)
        for half in range(2)
    ]
    sums = normed_grads(
        0, wins, [dqkv_ref, dqkv1_ref], weights, gh_ref, x_ref, gain_ref, gx_ref
    )
    small_grads(par, sums, pb_ref[...], fb1_ref, sh_ref, [acc_ref, acc1_ref], sm_ref)
    keep_ref[C : C + SMALL, :] = sm_ref[par].astype(BF)
    send_ref[C : C + SMALL, :] = sm_ref[1 - par].astype(BF)
    keep_ref[C + SMALL :, :] = sm_ref[2].astype(BF)
    send_ref[C + SMALL :, :] = sm_ref[3].astype(BF)
    for r in range(rows):
        parts = [gx_ref[pl.ds(tile_row(r, k, across), SEG), :][:WIN] for k in range(across)]
        out_ref[r] = jnp.concatenate(parts, axis=0)


def out_kernel(rows, across, st_ref, halo_ref, o_ref):
    for r in range(rows):
        parts = []
        for k in range(across):
            if r >= SHIFT:
                t = st_ref[pl.ds(tile_row(r - SHIFT, k, across), SEG), :]
            else:
                t = halo_ref[k, r]
            parts.append(t[:WIN])
        last = parts[-1]
        parts = [last[WIN - SHIFT :]] + parts[:-1] + [last[: WIN - SHIFT]]
        o_ref[r] = jnp.concatenate(parts, axis=0).astype(BF)


def final_kernel(*refs):
    (c0_ref, c1_ref, m0_ref, m1_ref, a0_ref, a1_ref, info_ref) = refs[:7]
    (qkv_ref, proj_ref, f1_ref, f2_ref, gain_ref, bias_ref, pb_ref, fb2_ref) = refs[7:15]
    (qvb_ref, fb1_ref, tab_ref) = refs[15:]
    first = info_ref[0] == 0

    def pair(mine, theirs, a, b):
        x = mine[a:b, :].astype(F32)
        y = theirs[a:b, :].astype(F32)
        return jnp.where(first, x, y), jnp.where(first, y, x)

    for layer in range(2):
        if layer == 1:
            mlp, attn, base = (c0_ref, c1_ref), (c0_ref, c1_ref), 2 * C
        else:
            mlp, attn, base = (m0_ref, m1_ref), (a0_ref, a1_ref), 0
        x, y = pair(*mlp, 0, C)
        f1_ref[layer, :, 0:C] = x
        f1_ref[layer, :, C:] = y
        x, y = pair(*mlp, C, 2 * C)
        f2_ref[layer, 0:C, :] = x
        f2_ref[layer, C:, :] = y
        for j in range(4):
            x, y = pair(*attn, base + 96 * j, base + 96 * (j + 1))
            if j < 3:
                qkv_ref[layer, j, 0:96, :] = x
                qkv_ref[layer, j, 96:, :] = y
            else:
                proj_ref[layer, 0:96, :] = x
                proj_ref[layer, 96:, :] = y
        x, y = pair(*attn, base + C, base + C + SMALL)
        gain_ref[layer, 0:1] = x[0:1]
        gain_ref[layer, 1:2] = x[3:4]
        bias_ref[layer, 0:1] = x[1:2]
        bias_ref[layer, 1:2] = x[4:5]
        pb_ref[layer : layer + 1] = x[2:3]
        fb2_ref[layer : layer + 1] = x[5:6]
        fb1_ref[layer : layer + 1, 0:C] = x[6:7]
        fb1_ref[layer : layer + 1, C:] = y[6:7]
        for n in range(2):
            qvb_ref[layer, n : n + 1, 0:96] = x[7:8, 128 * n : 128 * n + 96]
            qvb_ref[layer, n : n + 1, 96:192] = y[7:8, 128 * n : 128 * n + 96]
        t = jnp.concatenate([x[8:24, 0:48], y[8:24, 0:48]], axis=1)
        wide = exact(t, offset_rows(), 0, 0) * offset_cols()
        for h in range(6):
            tab_ref[h, layer : layer + 1, :] = jnp.sum(
                wide[16 * h : 16 * (h + 1)], 0, keepdims=True
            )


SMEM = pl.BlockSpec(memory_space=pltpu.SMEM)
VMEM = pl.BlockSpec(memory_space=pltpu.VMEM)
ANY = pl.BlockSpec(memory_space=pl.ANY)


def call(kernel, name, us, limit, operands, outs, scratch=()):
    args = []
    specs = []
    for op in operands:
        args.append(op[0] if isinstance(op, tuple) else op)
        specs.append(op[1] if isinstance(op, tuple) else VMEM)
    shapes = [jax.ShapeDtypeStruct(s, d) for s, d in outs]
    return pl.pallas_call(
        kernel,
        name=name,
        in_specs=specs,
        out_specs=[VMEM for s in shapes],
        out_shape=shapes,
        scratch_shapes=[pltpu.VMEM(s, d) for s, d in scratch],
        cost_estimate=pl.CostEstimate(
            flops=int(us * 1e9), bytes_accessed=1000000, transcendentals=0
        ),
        compiler_params=pltpu.CompilerParams(vmem_limit_bytes=limit * 2**20),
    )(*args)


def on_device(n_win, *args):
    (
        tokens,
        crop_ids,
        cotangent,
        norm_gain,
        norm_bias,
        qkv_weight,
        qv_bias,
        proj_weight,
        proj_bias,
        fc1_weight,
        fc1_bias,
        fc2_weight,
        fc2_bias,
        pos_table,
    ) = args
    rows, cols = tokens.shape[1:3]
    across = cols // WIN
    wins = (rows // WIN) * across
    ntok = wins * WROWS
    npad = wins * WPAD
    win = lax.axis_index("win")
    tp = lax.axis_index("tp")
    par = win % 2
    info = (jnp.stack([par, tp]).astype(jnp.int32), SMEM)
    bits = n_win.bit_length() - 1

    def to_tp(x):
        return lax.ppermute(x, "tp", [(0, 1), (1, 0)])

    def to_win(x, bit):
        return lax.ppermute(x, "win", [(i, i ^ (1 << bit)) for i in range(n_win)])

    qkv_t = qkv_weight.transpose(0, 2, 3, 1)

    def attn_quarter(layer):
        q = lax.dynamic_slice(qkv_t[layer], (0, par * 96, 0), (3, 96, C)).reshape(288, C)
        return jnp.concatenate([q, lax.dynamic_slice(proj_weight[layer], (par * 96, 0), (96, C))])

    def mlp_quarter(layer):
        return jnp.concatenate(
            [
                lax.dynamic_slice(fc1_weight[layer], (0, par * C), (C, C)),
                lax.dynamic_slice(fc2_weight[layer], (par * C, 0), (C, C)),
            ]
        )

    a0 = to_tp(attn_quarter(0))
    small, lq, lk, pos = call(
        partial(prep_kernel, rows, across),
        "prep",
        4,
        8,
        (pos_table.transpose(2, 0, 1), qv_bias, fc1_bias, crop_ids.transpose(2, 0, 1), info),
        [
            ((2, 24, C), F32),
            ((2, wins, 128), F32),
            ((2, wins, WPAD, 128), F32),
            ((2, 3, WPAD, 128), F32),
        ],
        [((128, 128), F32)],
    )
    small_o = to_tp(small)
    m0 = to_tp(mlp_quarter(0))
    w1 = to_tp(jnp.concatenate([attn_quarter(1), mlp_quarter(1)]))
    a0s = to_win(a0, 0)
    m0s = to_win(m0, 0)
    w1s = to_win(w1, 0)
    cot_halo = to_tp(cotangent[0, :SHIFT])
    tiles = (rows // WIN, across, WIN, SEG, C)
    mask = ((6 * WPAD, 6 * HD), BF)
    half_outs = [((3, npad, 192), BF), ((wins, WPAD, 6 * WPAD), BF), ((npad, 192), BF)]
    tok_f = ((ntok, C), F32)

    x0, xn0, part, qkv00, p00, mix00 = call(
        partial(attn_own_kernel, rows, across),
        "attn_own_0",
        8,
        12,
        (tokens[0], norm_gain, norm_bias, proj_bias, qv_bias, qkv_t, proj_weight, pos, lq, lk),
        [tok_f, ((npad, C), BF), tok_f] + half_outs,
        [mask],
    )
    hid0, qkv01, p01, mix01 = call(
        partial(attn_other_kernel, rows, across),
        "attn_other_0",
        7,
        12,
        (part, xn0, small_o, a0, a0s, lq, lk, info),
        [tok_f] + half_outs,
        [mask, ((3, WPAD, 128), F32), ((16, 96), F32)],
    )
    st0, act0, gp0 = call(
        partial(mlp_fwd_kernel, 0, 0),
        "mlp_fwd_0",
        7,
        24,
        (hid0, norm_gain, norm_bias, fc1_bias, small_o, fc2_bias, fc1_weight, fc2_weight, m0, m0s, info),
        [tok_f, ((4, ntok, C), BF), ((4, ntok, C), BF)],
    )
    halo = to_tp(st0.reshape(tiles)[0, :, :SHIFT])
    x1, xn1, hid1, qkv10, p10, mix10, qkv11, p11, mix11 = call(
        partial(attn_both_kernel, rows, across),
        "attn_fwd_1",
        12,
        14,
        (st0, halo, norm_gain, norm_bias, proj_bias, qv_bias, qkv_t, proj_weight)
        + (pos, small_o, w1, w1s, lq, lk, info),
        [tok_f, ((npad, C), BF), tok_f] + half_outs + half_outs,
        [mask, ((3, WPAD, 128), F32), ((16, 96), F32)],
    )
    mlp_outs = [((2, 2 * C, C), BF), ((2, 2 * C, C), BF), ((4, C), F32), ((3, C), F32)]
    mlp_scratch = [tok_f, ((ntok, C), BF), ((ntok, C), BF), ((4, ntok, C), BF)]
    st1, gh1, keep_m1, send_m1, gfb1, gsh1 = call(
        partial(mlp_both_kernel, rows, across, C),
        "mlp_both_1",
        18,
        30,
        (cotangent[0], cot_halo, hid1, norm_gain, norm_bias, fc1_bias, small_o, fc2_bias)
        + (fc1_weight, fc2_weight, w1, w1s, info),
        [tok_f, tok_f] + mlp_outs,
        mlp_scratch + [((4, ntok, C), BF)],
    )

    def add(a, b):
        return (a.astype(F32) + b.astype(F32)).astype(BF)

    m1_got = to_win(send_m1, 0)
    gin1, keep_a1, send_a1 = call(
        partial(attn_bwd_kernel, rows, across, 0),
        "attn_bwd_1",
        15,
        16,
        (gh1, x1, xn1, norm_gain, qkv_t, proj_weight, w1, w1s, info)
        + (gfb1, gsh1, qkv10, p10, mix10, qkv11, p11, mix11),
        [tok_f, ((2, C + SMALL, C), BF), ((2, C + SMALL, C), BF)],
        [
            ((npad, C), BF),
            ((2, npad, 192), BF),
            ((3, npad, 192), BF),
            ((3, npad, 192), BF),
            ((2, 3, WPAD, 128), F32),
            mask,
            ((192, C), F32),
            ((4, SMALL, C), F32),
        ],
    )
    halo = to_tp(gin1.reshape(tiles)[-1, :, WIN - SHIFT :])
    m1_sum = add(keep_m1, m1_got)
    a1_sum = add(keep_a1, to_win(send_a1, 0))
    m1_t = to_tp(m1_sum[1])
    a1_t = to_tp(a1_sum[1])
    gh0, keep_m0, send_m0, gfb0, gsh0 = call(
        partial(mlp_bwd_kernel, rows, across, 0, 2),
        "mlp_bwd_0",
        11,
        24,
        (gin1, halo, hid0, act0, gp0, norm_gain, norm_bias, fc1_weight, fc2_weight, m0, m0s, info)
        + ((m1_sum, ANY), (a1_sum, ANY)),
        [tok_f] + mlp_outs,
        mlp_scratch,
    )

    def split(acc, bit):
        n = acc.shape[0] // 2
        b = (win >> bit) & 1
        return (
            lax.dynamic_slice_in_dim(acc, b * n, n),
            lax.dynamic_slice_in_dim(acc, (1 - b) * n, n),
        )

    def join(acc, got, bit):
        b = (win >> bit) & 1
        return jnp.where(b == 0, jnp.concatenate([acc, got]), jnp.concatenate([got, acc]))

    m0_got = to_win(send_m0, 0)
    c1 = jnp.concatenate([add(m1_sum[0], m1_t), add(a1_sum[0], a1_t)])
    m0_sum = add(keep_m0, m0_got)
    c1_mine, c1_away = split(c1, 1)
    c1_y = to_win(c1_away, 1)
    m0_t = to_tp(m0_sum[1])
    da, do, dqkv1, acc1, pb0, keep_o0, send_o0 = call(
        partial(attn_bwd_other_kernel, rows, across, 3),
        "attn_bwd_other_0",
        8,
        16,
        (gh0, xn0, proj_weight, a0, a0s, qkv01, p01, mix01)
        + ((c1_mine, ANY), (c1_away, ANY), (m0_sum, ANY)),
        [
            ((npad, C), BF),
            ((npad, 192), BF),
            ((3, npad, 192), BF),
            ((3, WPAD, 128), F32),
            ((1, C), F32),
            ((C, C), BF),
            ((C, C), BF),
        ],
        [((npad, 192), BF), mask],
    )
    c1 = add(c1_mine, c1_y)
    o0_sum = add(keep_o0, to_win(send_o0, 0))
    o0_t = to_tp(o0_sum)
    m0_acc = add(m0_sum[0], m0_t)
    m0_mine, m0_away = split(m0_acc, 1)
    m0_y = to_win(m0_away, 1)
    c1_mine, c1_away = split(c1, 2)
    c1_z = to_win(c1_away, 2)
    grad_tokens, keep_a0, send_a0 = call(
        partial(attn_bwd_own_kernel, rows, across, 4),
        "attn_bwd_own_0",
        10,
        16,
        (gh0, x0, xn0, norm_gain, qkv_t, a0, a0s, info)
        + (gfb0, gsh0, da, do, dqkv1, acc1, pb0, qkv00, p00, mix00)
        + ((o0_sum, ANY), (m0_away, ANY), (m0_mine, ANY), (c1_away, ANY)),
        [((rows, cols, C), F32), ((C + 2 * SMALL, C), BF), ((C + 2 * SMALL, C), BF)],
        [
            ((3, npad, 192), BF),
            ((3, WPAD, 128), F32),
            tok_f,
            mask,
            ((192, C), F32),
            ((4, SMALL, C), F32),
        ],
    )
    a0_sum = add(keep_a0, to_win(send_a0, 0))
    small_t = to_tp(a0_sum[C + SMALL :])
    acc = jnp.concatenate(
        [add(a0_sum[:C], o0_t), add(a0_sum[C : C + SMALL], small_t)]
    )
    m0_acc = add(m0_mine, m0_y)
    c1 = add(c1_mine, c1_z)
    mine, away = split(acc, 1)
    acc = add(mine, to_win(away, 1))
    for bit in range(2, bits):
        acc = add(acc, to_win(acc, bit))
        m0_acc = add(m0_acc, to_win(m0_acc, bit))
        if bit > 2:
            c1 = add(c1, to_win(c1, bit))
    m0_acc = join(m0_acc, to_win(m0_acc, 1), 1)
    acc = join(acc, to_win(acc, 1), 1)
    c1 = join(c1, to_win(c1, 2), 2)
    c1 = join(c1, to_win(c1, 1), 1)
    halo = to_tp(st1.reshape(tiles)[-1, :, WIN - SHIFT :])
    (layer_out,) = call(
        partial(out_kernel, rows, across), "layer_out", 2, 8, (st1, halo), [((rows, cols, C), BF)]
    )
    outs = call(
        final_kernel,
        "final",
        4,
        12,
        (c1, to_win(c1, 0), m0_acc, to_win(m0_acc, 0), acc, to_win(acc, 0), info),
        [
            ((2, 3, 192, C), F32),
            ((2, 192, C), F32),
            ((2, C, 2 * C), F32),
            ((2, 2 * C, C), F32),
            ((2, 2, C), F32),
            ((2, 2, C), F32),
            ((2, C), F32),
            ((2, C), F32),
            ((2, 2, 192), F32),
            ((2, 2 * C), F32),
            ((6, 2, 169), F32),
        ],
    )
    (g_qkv, g_proj, g_f1, g_f2, g_gain, g_bias, g_pb, g_fb2, g_qvb, g_fb1, g_tab) = outs
    return (
        layer_out[None],
        grad_tokens[None],
        g_gain,
        g_bias,
        g_qkv.transpose(0, 3, 1, 2),
        g_qvb,
        g_proj,
        g_pb,
        g_f1,
        g_fb1,
        g_f2,
        g_fb2,
        g_tab.transpose(1, 2, 0),
    )


def solution(mesh):
    return jax.shard_map(
        partial(on_device, mesh.shape["win"]),
        mesh=mesh,
        in_specs=(
            P("win", "tp", None, None),
            P("win", None, None),
            P("win", "tp", None, None),
            P(),
            P(),
            P(None, None, None, "tp"),
            P(None, None, "tp"),
            P(None, "tp", None),
            P(),
            P(None, None, "tp"),
            P(None, "tp"),
            P(None, "tp", None),
            P(),
            P(None, None, "tp"),
        ),
        out_specs=(
            P("win", "tp", None, None),
            P("win", "tp", None, None),
            P(),
            P(),
            P(None, None, None, "tp"),
            P(None, None, "tp"),
            P(None, "tp", None),
            P(),
            P(None, None, "tp"),
            P(None, "tp"),
            P(None, "tp", None),
            P(),
            P(None, None, "tp"),
        ),
        check_vma=False,
    )
```

```python
from functools import partial

import jax
import jax.numpy as jnp
import numpy as np
from jax import lax
from jax.experimental import pallas as pl
from jax.experimental.pallas import tpu as pltpu
from jax.sharding import PartitionSpec as P

C = 384
WIN = 7
SHIFT = 3
HD = 32
EPS = 1e-05
NEG = -1000000000.0
SCALE = HD**-0.5
F32 = jnp.float32
BF = jnp.bfloat16
SEG = 8
WROWS = WIN * SEG
WPAD = 64


def nn(a, b):
    return lax.dot_general(a, b, (((1,), (0,)), ((), ())), preferred_element_type=F32)


def nt(a, b):
    return lax.dot_general(a, b, (((1,), (1,)), ((), ())), preferred_element_type=F32)


def tn(a, b):
    return lax.dot_general(a, b, (((0,), (0,)), ((), ())), preferred_element_type=F32)


def norm_stats(x):
    mean = jnp.mean(x, -1, keepdims=True)
    cent = x - mean
    var = jnp.mean(cent * cent, -1, keepdims=True)
    rinv = lax.rsqrt(var + EPS)
    return cent * rinv, rinv


def norm_back(dz, xhat, rinv, gain):
    d = dz * gain
    return rinv * (
        d - jnp.mean(d, -1, keepdims=True) - xhat * jnp.mean(d * xhat, -1, keepdims=True)
    )


def tile_row(r, k, across):
    return (((r // WIN) * across + k) * WIN + r % WIN) * SEG


def zero_rows(n):
    return jnp.zeros((n, C), F32)


def head_mask():
    row = lax.broadcasted_iota(jnp.int32, (6 * WPAD, 6 * HD), 0) // WPAD
    col = lax.broadcasted_iota(jnp.int32, (6 * WPAD, 6 * HD), 1) // HD
    return (row == col).astype(BF)


def spread(x, mask):
    return jnp.concatenate([x] * 6, axis=0) * mask


def fold(o):
    lane = lax.broadcasted_iota(jnp.int32, (WPAD, 128), 1)

    def of(h, a, b):
        return o[WPAD * h : WPAD * (h + 1), a:b]

    one = jnp.where(lane < 96, of(2, 0, 128), of(3, 0, 128))
    one = jnp.where(lane < 64, of(1, 0, 128), one)
    one = jnp.where(lane < 32, of(0, 0, 128), one)
    two = jnp.where(lane[:, :64] < 32, of(4, 128, 192), of(5, 128, 192))
    return jnp.concatenate([one, two], axis=1)


def rows_at(i, n):
    return pl.ds(pl.multiple_of(i * n, n), n)


def iota(shape, dim):
    return lax.broadcasted_iota(jnp.int32, shape, dim)


def exact(a, b, ca, cb):
    return lax.dot_general(
        a,
        b,
        (((ca,), (cb,)), ((), ())),
        precision=lax.Precision.HIGHEST,
        preferred_element_type=F32,
    )


def offset_rows():
    return (12 - iota((16, 169), 0) == iota((16, 169), 1) // 13).astype(F32)


def offset_cols():
    return (iota((96, 169), 0) % 16 == iota((96, 169), 1) % 13).astype(F32)


def column_pick(kx):
    r = iota((96, 6 * WPAD), 0)
    c = iota((96, 6 * WPAD), 1)
    qx = c % 8
    return ((r // 16 == c // WPAD) & (r % 16 == qx - kx + WIN - 1) & (qx < WIN)).astype(F32)


def table_to_map(t, pos_ref):
    pos_ref[...] = jnp.zeros_like(pos_ref)
    group = (iota((8, 6 * WPAD), 1) % WPAD) // 8
    for kx in range(WIN):
        h = exact(t, column_pick(kx), 1, 0)
        g = jnp.zeros((8, 6 * WPAD), F32)
        for j in range(WIN):
            g = jnp.where(group == j, h[6 - j : 14 - j], g)
        for i in range(3):
            pos_ref[i, pl.ds(kx, 8, stride=8), :] = g[:, 128 * i : 128 * (i + 1)]


def map_to_table(pos_ref):
    group = (iota((16, 6 * WPAD), 1) % WPAD) // 8
    total = jnp.zeros((16, 96), F32)
    for kx in range(WIN):
        r = jnp.concatenate([pos_ref[i, pl.ds(kx, 8, stride=8), :] for i in range(3)], axis=1)
        h = jnp.zeros((16, 6 * WPAD), F32)
        for j in range(WIN):
            parts = [r, jnp.zeros((2 + j, 6 * WPAD), F32)]
            if j < 6:
                parts = [jnp.zeros((6 - j, 6 * WPAD), F32)] + parts
            h = jnp.where(group == j, jnp.concatenate(parts, axis=0), h)
        total = total + exact(h, column_pick(kx), 1, 1)
    return total


def shift_in(tile, x_ref, rows, across):
    for r in range(rows):
        for k in range(across):
            a = tile(r + SHIFT, k)
            b = tile(r + SHIFT, (k + 1) % across)
            x_ref[pl.ds(tile_row(r, k, across), SEG), :] = jnp.concatenate(
                [a[SHIFT:WIN], b[:SHIFT], zero_rows(1)], axis=0
            )


def shift_out(tile, x_ref, rows, across):
    for r in range(rows):
        for k in range(across):
            a = tile(r - SHIFT, (k - 1) % across)
            b = tile(r - SHIFT, k)
            x_ref[pl.ds(tile_row(r, k, across), SEG), :] = jnp.concatenate(
                [a[WIN - SHIFT : WIN], b[: WIN - SHIFT], zero_rows(1)], axis=0
            )

SMALL = 32


def pack_kernel(
    qkvw_ref, projw_ref, f1_ref, f2_ref, tab_ref, qvb_ref, fb1_ref, info_ref,
    a0_ref, m0_ref, a1_ref, m1_ref, small_ref, tab_v, qvb_v, fb1_v, sems
):
    par = info_ref[0]
    of_heads = pl.ds(pl.multiple_of(par * 96, 96), 96)
    of_units = pl.ds(pl.multiple_of(par * C, C), C)
    copies = [(tab_ref, tab_v), (qvb_ref, qvb_v), (fb1_ref, fb1_v)]
    for layer, (a_ref, m_ref) in enumerate(((a0_ref, m0_ref), (a1_ref, m1_ref))):
        for j in range(3):
            copies.append((qkvw_ref.at[layer, j, of_heads, :], a_ref.at[pl.ds(96 * j, 96), :]))
        copies.append((projw_ref.at[layer, of_heads, :], a_ref.at[pl.ds(288, 96), :]))
        copies.append((f1_ref.at[layer, :, of_units], m_ref.at[pl.ds(0, C), :]))
        copies.append((f2_ref.at[layer, of_units, :], m_ref.at[pl.ds(C, C), :]))
    copies = [pltpu.make_async_copy(x, y, sems.at[n]) for n, (x, y) in enumerate(copies)]
    for copy in copies:
        copy.start()
    small_ref[...] = jnp.zeros_like(small_ref)
    for copy in copies[:3]:
        copy.wait()
    for layer in range(2):
        tab = tab_v[:, layer, :]
        wide = jnp.concatenate([jnp.broadcast_to(tab[h : h + 1], (16, 169)) for h in range(6)])
        small_ref[layer, 0:16, 0:96] = exact(offset_rows(), wide * offset_cols(), 1, 1)
        small_ref[layer, 16:17, :] = fb1_v[layer : layer + 1, 0:C]
        small_ref[layer, 17:18, :] = fb1_v[layer : layer + 1, C:]
        small_ref[layer, 18:20, 0:192] = qvb_v[layer]
        high = small_ref[layer].astype(BF).astype(F32)
        rows = jnp.concatenate([high, small_ref[layer] - high, zero_rows(16)], axis=0)
        a0_ref[C + 64 * layer : C + 64 * (layer + 1), :] = rows.astype(BF)
    for copy in copies[3:]:
        copy.wait()


def prep_kernel(rows, across, crop_ref, small_ref, info_ref, lq_ref, lk_ref, pos_ref, c_ref):
    tp = info_ref[1]
    cols = across * WIN
    height = crop_ref.shape[2]
    for layer in range(2):
        table_to_map(small_ref[layer, 0:16, 0:96], pos_ref.at[layer])
    c_ref[...] = jnp.zeros_like(c_ref)
    c_ref[0:cols, 0:height] = crop_ref[:, 0, :].astype(F32)
    crops = c_ref[...].astype(BF)
    row = iota((32, 128), 0)
    lane = iota((32, 128), 1)
    for layer in range(2):
        shift = SHIFT if layer == 1 else 0
        src = rows * tp + row + shift
        src = jnp.where(src >= height, src - height, src)
        grid = nt((src == lane).astype(BF), crops).astype(BF)
        for wc in range(across):
            qx = iota((128, 128), 1) % 8
            col = qx + (WIN * wc + shift)
            col = jnp.where(col >= cols, col - cols, col)
            pick = ((col == iota((128, 128), 0)) & (qx < WIN)).astype(BF)
            lab = nn(grid, pick)
            if layer == 1:
                g = rows * tp + row
                zr = (g >= height - WIN).astype(F32) + (g >= height - SHIFT).astype(F32)
                here = lane % 8 + WIN * wc
                zc = (here >= cols - WIN).astype(F32) + (here >= cols - SHIFT).astype(F32)
                lab = lab * 9.0 + zr * 3.0 + zc
            real = (iota((1, 128), 1) % 8 < WIN) & (iota((1, 128), 1) % WPAD < WROWS)
            for wr in range(rows // WIN):
                w = wr * across + wc
                mine = row == (lane % WPAD) // 8 + WIN * wr
                line = jnp.sum(jnp.where(mine, lab, 0.0), 0, keepdims=True)
                line = jnp.where(real, line, -1.0)
                lq_ref[layer, w : w + 1, :] = line
                lk_ref[layer, w] = jnp.broadcast_to(line, (128, 128)).T[:WPAD]


def qkv_weight_of(half, j, layer, qkvw_ref, a_ref, b_ref):
    if half == 0:
        return qkvw_ref[layer, j]
    return jnp.concatenate([a_ref[96 * j : 96 * (j + 1)], b_ref[96 * j : 96 * (j + 1)]], axis=0)


def proj_weight_of(half, layer, projw_ref, a_ref, b_ref):
    if half == 0:
        return projw_ref[layer]
    return jnp.concatenate([a_ref[288:384], b_ref[288:384]], axis=0)


def norm_windows(layer, wins, x_ref, xn_ref, gain_ref, bias_ref):
    gain = gain_ref[layer, 0:1]
    bias = bias_ref[layer, 0:1]

    def four(i, carry):
        xhat, _ = norm_stats(x_ref[rows_at(i, 4 * WROWS), :])
        xn = xhat * gain + bias
        for n in range(4):
            part = jnp.concatenate(
                [xn[n * WROWS : (n + 1) * WROWS], zero_rows(WPAD - WROWS)], axis=0
            )
            xn_ref[rows_at(4 * i + n, WPAD), :] = part.astype(BF)
        return carry

    lax.fori_loop(0, wins // 4, four, 0)


def project_half(xn_ref, qkv_ref, weight, qb, vb):
    n = xn_ref.shape[0] // 2

    def part(i, carry):
        at = rows_at(i, n)
        xn = xn_ref[at, :]
        q = nt(xn, weight(0))
        k = nt(xn, weight(1))
        v = nt(xn, weight(2))
        qkv_ref[0, at, :] = ((q + qb) * SCALE).astype(BF)
        qkv_ref[1, at, :] = k.astype(BF)
        qkv_ref[2, at, :] = (v + vb).astype(BF)
        return carry

    lax.fori_loop(0, 2, part, 0)


def attend_forward(halves, wins, group, layer, lq_ref, lk_ref, mask_ref):
    def body(i, carry):
        units = [(i * group + u, h) for u in range(group) for h in halves]
        scores = []
        for w, (qkv_ref, _, _, _) in units:
            at = rows_at(w, WPAD)
            scores.append(nt(qkv_ref[1, at, :], spread(qkv_ref[0, at, :], mask_ref[...])))
        probs = []
        for (w, (_, pos, p_ref, _)), s in zip(units, scores):
            same = lk_ref[layer, w] == lq_ref[layer, pl.ds(w, 1), :]
            same = jnp.concatenate([same] * 3, axis=1)
            s = jnp.where(same, s + jnp.concatenate([pos[n] for n in range(3)], axis=1), NEG)
            e = jnp.exp(s - jnp.max(s, 0, keepdims=True))
            p = (e * (1.0 / jnp.sum(e, 0, keepdims=True))).astype(BF)
            p_ref[w] = p
            probs.append(p)
        for (w, (qkv_ref, _, _, mix_ref)), p in zip(units, probs):
            at = rows_at(w, WPAD)
            mix_ref[at, :] = fold(tn(p, qkv_ref[2, at, :])).astype(BF)
        return carry

    lax.fori_loop(0, wins // group, body, 0)


def add_branch(wins, mixes, weights, bias, x_ref, hid_ref):
    n = 8

    def part(i, carry):
        res = bias
        for m_ref, w in zip(mixes, weights):
            res = res + nn(m_ref[rows_at(i, n * WPAD), :], w)
        for k in range(n):
            to = rows_at(i * n + k, WROWS)
            hid_ref[to, :] = x_ref[to, :] + res[k * WPAD : k * WPAD + WROWS]
        return carry

    lax.fori_loop(0, wins // n, part, 0)


def attn_own_kernel(rows, across, *refs):
    (tok_ref, gain_ref, bias_ref, pb_ref, qvb_ref, qkvw_ref, projw_ref) = refs[:7]
    (pos_ref, lq_ref, lk_ref) = refs[7:10]
    (x_ref, xn_ref, hid_ref, qkv_ref, p_ref, mix_ref, mask_ref) = refs[10:]
    wins = (rows // WIN) * across
    for r in range(rows):
        row = tok_ref[r].astype(F32)
        for k in range(across):
            x_ref[pl.ds(tile_row(r, k, across), SEG), :] = jnp.concatenate(
                [row[WIN * k : WIN * (k + 1)], zero_rows(1)], axis=0
            )
    mask_ref[...] = head_mask()
    norm_windows(0, wins, x_ref, xn_ref, gain_ref, bias_ref)
    project_half(
        xn_ref, qkv_ref, lambda j: qkvw_ref[0, j], qvb_ref[0, 0:1], qvb_ref[0, 1:2]
    )
    attend_forward(
        [(qkv_ref, pos_ref.at[0], p_ref, mix_ref)], wins, 8, 0, lq_ref, lk_ref, mask_ref
    )
    add_branch(wins, [mix_ref], [projw_ref[0]], pb_ref[0:1], x_ref, hid_ref)


def attn_other_kernel(rows, across, *refs):
    (part_ref, xn_ref, a_ref, b_ref, lq_ref, lk_ref, info_ref) = refs[:7]
    (hid_ref, qkv_ref, p_ref, mix_ref, small_ref, mask_ref, pos_ref, t_ref) = refs[7:]
    for layer in range(2):
        rows_of = a_ref[C + 64 * layer : C + 64 * (layer + 1), :].astype(F32)
        small_ref[layer] = rows_of[0:24] + rows_of[24:48]
    wins = (rows // WIN) * across
    mask_ref[...] = head_mask()
    bias = other_small(small_ref, 0, info_ref[0], t_ref, pos_ref)
    project_half(
        xn_ref,
        qkv_ref,
        lambda j: qkv_weight_of(1, j, 0, None, a_ref, b_ref),
        bias[0:1],
        bias[1:2],
    )
    attend_forward([(qkv_ref, pos_ref, p_ref, mix_ref)], wins, 8, 0, lq_ref, lk_ref, mask_ref)
    add_branch(
        wins, [mix_ref], [proj_weight_of(1, 0, None, a_ref, b_ref)], 0.0, part_ref, hid_ref
    )


def other_small(small_ref, layer, par, t_ref, pos_ref):
    first = par == 0

    def swapped(v, n):
        return jnp.where(first, v, jnp.concatenate([v[:, n : 2 * n], v[:, :n]], axis=1))

    t = swapped(small_ref[layer, 0:16, 0:96], 48)
    table_to_map(t, pos_ref)
    return swapped(small_ref[layer, 18:20, 0:192], 96)


def attn_both_kernel(rows, across, *refs):
    (st_ref, halo_ref, gain_ref, bias_ref, pb_ref, qvb_ref, qkvw_ref, projw_ref) = refs[:8]
    (pos_ref, small_ref, a_ref, b_ref, lq_ref, lk_ref, info_ref) = refs[8:15]
    (x_ref, xn_ref, hid_ref, qkv0_ref, p0_ref, mix0_ref) = refs[15:21]
    (qkv1_ref, p1_ref, mix1_ref, mask_ref, pos1_ref, t_ref) = refs[21:]
    wins = (rows // WIN) * across

    def tile(r, k):
        if r < rows:
            return st_ref[pl.ds(tile_row(r, k, across), SEG), :]
        return halo_ref[k, r - rows]

    shift_in(tile, x_ref, rows, across)
    mask_ref[...] = head_mask()
    bias = other_small(small_ref, 1, info_ref[0], t_ref, pos1_ref)
    norm_windows(1, wins, x_ref, xn_ref, gain_ref, bias_ref)
    project_half(
        xn_ref, qkv0_ref, lambda j: qkvw_ref[1, j], qvb_ref[1, 0:1], qvb_ref[1, 1:2]
    )
    project_half(
        xn_ref,
        qkv1_ref,
        lambda j: qkv_weight_of(1, j, 1, None, a_ref, b_ref),
        bias[0:1],
        bias[1:2],
    )
    attend_forward(
        [(qkv0_ref, pos_ref.at[1], p0_ref, mix0_ref), (qkv1_ref, pos1_ref, p1_ref, mix1_ref)],
        wins,
        4,
        1,
        lq_ref,
        lk_ref,
        mask_ref,
    )
    add_branch(
        wins,
        [mix0_ref, mix1_ref],
        [projw_ref[1], proj_weight_of(1, 1, None, a_ref, b_ref)],
        pb_ref[1:2],
        x_ref,
        hid_ref,
    )


def up_weight(part, layer, base, f1_ref, a_ref, b_ref):
    if part == 0:
        return f1_ref[layer]
    return jnp.concatenate([a_ref[base : base + C], b_ref[base : base + C]], axis=1)


def down_weight(part, layer, base, f2_ref, a_ref, b_ref):
    if part == 0:
        return f2_ref[layer]
    return jnp.concatenate([a_ref[base + C : base + 2 * C], b_ref[base + C : base + 2 * C]], axis=0)


def up_biases(layer, par, fb1_ref, small_ref):
    own = fb1_ref[layer : layer + 1]
    one, two = small_ref[layer, 16:17], small_ref[layer, 17:18]
    first = par == 0
    return own, jnp.concatenate(
        [jnp.where(first, one, two), jnp.where(first, two, one)], axis=1
    )


def gelu_pair(u):
    phi = 0.5 + 0.5 * lax.erf(u * (2.0**-0.5))
    slope = phi + u * (jnp.exp(-0.5 * u * u) * (2.0 * np.pi) ** -0.5)
    return (u * phi).astype(BF), slope.astype(BF)


def mlp_fwd_kernel(
    layer, base, hid_ref, gain_ref, bias_ref, fb1_ref, small_ref, fb2_ref, f1_ref, f2_ref, a_ref,
    b_ref, info_ref, st_ref, act_ref, gp_ref
):
    h = hid_ref[...]
    xhat, _ = norm_stats(h)
    n2 = (xhat * gain_ref[layer, 1:2] + bias_ref[layer, 1:2]).astype(BF)
    biases = up_biases(layer, info_ref[0], fb1_ref, small_ref)
    ups = [
        nn(n2, up_weight(p, layer, base, f1_ref, a_ref, b_ref)) + biases[p] for p in range(2)
    ]
    acts = []
    for p in range(2):
        act, slope = gelu_pair(ups[p])
        acts.append(act)
        for z in range(2):
            act_ref[2 * p + z] = act[:, C * z : C * (z + 1)]
            gp_ref[2 * p + z] = slope[:, C * z : C * (z + 1)]
    down = nn(acts[0], down_weight(0, layer, base, f2_ref, a_ref, b_ref)) + nn(
        acts[1], down_weight(1, layer, base, f2_ref, a_ref, b_ref)
    )
    st_ref[...] = h + fb2_ref[layer : layer + 1] + down


def mlp_back_rows(
    layer, base, at, g, df, h, slopes, gain, bias, f1_ref, f2_ref, a_ref, b_ref, refs, carry
):
    (gh_ref, n2_ref, du_ref) = refs
    (sb, sg, sf, s1) = carry
    sf = sf + jnp.sum(df.astype(F32), 0, keepdims=True)
    grads = [nt(df, down_weight(p, layer, base, f2_ref, a_ref, b_ref)) for p in range(2)]
    new = []
    parts = []
    for p in range(2):
        du = [
            (grads[p][:, C * z : C * (z + 1)] * slopes(2 * p + z).astype(F32)).astype(BF)
            for z in range(2)
        ]
        for z in range(2):
            du_ref[2 * p + z, at, :] = du[z]
            new.append(s1[2 * p + z] + jnp.sum(du[z].astype(F32), 0, keepdims=True))
        parts.append(jnp.concatenate(du, axis=1))
    dz = nt(parts[0], up_weight(0, layer, base, f1_ref, a_ref, b_ref)) + nt(
        parts[1], up_weight(1, layer, base, f1_ref, a_ref, b_ref)
    )
    xhat, rinv = norm_stats(h)
    n2_ref[at, :] = (xhat * gain + bias).astype(BF)
    sg = sg + jnp.sum(dz * xhat, 0, keepdims=True)
    sb = sb + jnp.sum(dz, 0, keepdims=True)
    gh_ref[at, :] = g + norm_back(dz, xhat, rinv, gain)
    return sb, sg, sf, tuple(new)


def quarter_of(par, slot, part):
    return (par ^ slot) if part == 0 else 2 + slot


def mlp_sums(carry, fb1_ref, sh_ref):
    sb, sg, sf, s1 = carry
    for q in range(4):
        fb1_ref[q : q + 1] = s1[q]
    sh_ref[0:1] = sg
    sh_ref[1:2] = sb
    sh_ref[2:3] = sf


def zero_sums():
    z = jnp.zeros((1, C), F32)
    return z, z, z, (z,) * 4


def mlp_both_kernel(rows, across, base, *refs):
    (cot_ref, halo_ref, hid_ref, gain_ref, bias_ref, fb1b_ref, small_ref, fb2_ref) = refs[:8]
    (f1_ref, f2_ref, a_ref, b_ref, info_ref) = refs[8:13]
    (st_ref, gh_ref, df_ref, n2_ref, du_ref, act_ref, send_ref, fb1_ref, sh_ref) = refs[13:22]
    (g_ref,) = refs[22:]
    layer = 1
    for r in range(rows):
        s = r + SHIFT
        row = (cot_ref[s] if s < rows else halo_ref[s - rows]).astype(F32)
        for k in range(across):
            a = WIN * k + SHIFT
            if k < across - 1:
                piece = [row[a : a + WIN]]
            else:
                piece = [row[a:], row[:SHIFT]]
            g_ref[pl.ds(tile_row(r, k, across), SEG), :] = jnp.concatenate(
                piece + [zero_rows(1)], axis=0
            )
    gain = gain_ref[layer, 1:2]
    bias = bias_ref[layer, 1:2]
    par = info_ref[0]
    biases = up_biases(layer, par, fb1b_ref, small_ref)
    n = hid_ref.shape[0] // 2

    def block(i, carry):
        at = rows_at(i, n)
        h = hid_ref[at, :]
        xhat, _ = norm_stats(h)
        n2 = (xhat * gain + bias).astype(BF)
        ups = [
            nn(n2, up_weight(p, layer, base, f1_ref, a_ref, b_ref)) + biases[p] for p in range(2)
        ]
        acts = []
        slopes = []
        for p in range(2):
            act, slope = gelu_pair(ups[p])
            acts.append(act)
            for z in range(2):
                act_ref[2 * p + z, at, :] = act[:, C * z : C * (z + 1)]
                slopes.append(slope[:, C * z : C * (z + 1)])
        down = nn(acts[0], down_weight(0, layer, base, f2_ref, a_ref, b_ref)) + nn(
            acts[1], down_weight(1, layer, base, f2_ref, a_ref, b_ref)
        )
        st_ref[at, :] = h + fb2_ref[layer : layer + 1] + down
        g = g_ref[at, :]
        df = g.astype(BF)
        df_ref[at, :] = df
        return mlp_back_rows(
            layer, base, at, g, df, h, lambda q: slopes[q], gain, bias, f1_ref, f2_ref,
            a_ref, b_ref, (gh_ref, n2_ref, du_ref), carry
        )

    mlp_sums(lax.fori_loop(0, 2, block, zero_sums()), fb1_ref, sh_ref)
    n2 = n2_ref[...]
    df = df_ref[...]
    for part in range(2):
        q = quarter_of(par, 1, part)
        send_ref[part, 0:C, :] = tn(n2, du_ref[q]).astype(BF)
        send_ref[part, C:, :] = tn(act_ref[q], df).astype(BF)


def mlp_keep_kernel(n2_ref, df_ref, du_ref, act_ref, got_ref, info_ref, own_ref, oth_ref):
    n2 = n2_ref[...]
    df = df_ref[...]
    for part, ref in ((1, oth_ref), (0, own_ref)):
        q = quarter_of(info_ref[0], 0, part)
        ref[0:C, :] = (tn(n2, du_ref[q]) + got_ref[part, 0:C, :].astype(F32)).astype(BF)
        ref[C:, :] = (tn(act_ref[q], df) + got_ref[part, C:, :].astype(F32)).astype(BF)


def up_keep_kernel(n2_ref, du_ref, got_ref, info_ref, own_ref, oth_ref):
    n2 = n2_ref[...]
    for part, ref in ((1, oth_ref), (0, own_ref)):
        q = quarter_of(info_ref[0], 0, part)
        ref[...] = (tn(n2, du_ref[q]) + got_ref[part].astype(F32)).astype(BF)


def down_grad_kernel(rows, across, gin_ref, halo_ref, act_ref, info_ref, g_ref, df_ref, keep_ref, send_ref):
    def tile(r, k):
        if r >= 0:
            return gin_ref[pl.ds(tile_row(r, k, across), SEG), :]
        return halo_ref[k, r + SHIFT]

    shift_out(tile, g_ref, rows, across)
    df = g_ref[...].astype(BF)
    df_ref[...] = df
    for slot, ref in ((1, send_ref), (0, keep_ref)):
        for part in range(2):
            ref[part] = tn(act_ref[quarter_of(info_ref[0], slot, part)], df).astype(BF)


def mlp_bwd_kernel(base, *refs):
    (g_ref, df_ref, hid_ref, gp_ref, gain_ref, bias_ref) = refs[:6]
    (f1_ref, f2_ref, a_ref, b_ref, info_ref) = refs[6:11]
    (gh_ref, n2_ref, du_ref, send_ref, fb1_ref, sh_ref) = refs[11:]
    layer = 0
    gain = gain_ref[layer, 1:2]
    bias = bias_ref[layer, 1:2]
    n = hid_ref.shape[0] // 2

    def block(i, carry):
        at = rows_at(i, n)
        return mlp_back_rows(
            layer, base, at, g_ref[at, :], df_ref[at, :], hid_ref[at, :],
            lambda q: gp_ref[q, at, :], gain, bias,
            f1_ref, f2_ref, a_ref, b_ref, (gh_ref, n2_ref, du_ref), carry
        )

    mlp_sums(lax.fori_loop(0, 2, block, zero_sums()), fb1_ref, sh_ref)
    n2 = n2_ref[...]
    for part in range(2):
        send_ref[part] = tn(n2, du_ref[quarter_of(info_ref[0], 1, part)]).astype(BF)


def window_grads(wins, gh_ref, da_ref):
    def four(i, s):
        g = gh_ref[rows_at(i, 4 * WROWS), :]
        for n in range(4):
            part = jnp.concatenate(
                [g[n * WROWS : (n + 1) * WROWS], zero_rows(WPAD - WROWS)], axis=0
            ).astype(BF)
            da_ref[rows_at(4 * i + n, WPAD), :] = part
            s = s + jnp.sum(part.astype(F32), 0, keepdims=True)
        return s

    return lax.fori_loop(0, wins // 4, four, jnp.zeros((1, C), F32))


def attend_backward(halves, wins, group, mask_ref):
    def body(i, carry):
        units = [(i * group + u, h) for u in range(group) for h in halves]
        first = []
        for w, (qkv_ref, p_ref, do_ref, dqkv_ref, _) in units:
            at = rows_at(w, WPAD)
            do = spread(do_ref[at, :], mask_ref[...])
            first.append(nt(qkv_ref[2, at, :], do))
            dqkv_ref[2, at, :] = nn(p_ref[w], do).astype(BF)
        second = []
        for (w, (_, p_ref, _, _, acc_ref)), dp in zip(units, first):
            p = p_ref[w].astype(F32)
            ds = p * (dp - jnp.sum(p * dp, 0, keepdims=True))
            for n in range(3):
                acc_ref[n] += ds[:, 128 * n : 128 * (n + 1)]
            second.append(ds.astype(BF))
        for (w, (qkv_ref, _, _, dqkv_ref, _)), ds in zip(units, second):
            at = rows_at(w, WPAD)
            dqkv_ref[1, at, :] = nn(ds, spread(qkv_ref[0, at, :], mask_ref[...])).astype(BF)
            dqkv_ref[0, at, :] = fold(tn(ds, qkv_ref[1, at, :])).astype(BF)
        return carry

    lax.fori_loop(0, wins // group, body, 0)


def half_grads(half, par, xn_ref, da_ref, mix_ref, dqkv_ref, row_ref, give):
    def put(value, at):
        if half == 0:
            row_ref[...] = value
            one = row_ref[pl.ds(pl.multiple_of(par * 96, 96), 96), :]
            two = row_ref[pl.ds(pl.multiple_of((1 - par) * 96, 96), 96), :]
        else:
            one, two = value[:96], value[96:]
        give(at, one.astype(BF), two.astype(BF))

    xn = xn_ref[...]
    for j in range(3):
        grad = tn(dqkv_ref[j], xn)
        put(grad * SCALE if j == 0 else grad, 96 * j)
    put(tn(mix_ref[...], da_ref[...]), 288)


def normed_grads(layer, wins, dqkvs, weights, gh_ref, x_ref, gain_ref, gx_ref):
    gain = gain_ref[layer, 0:1]
    n = 8

    def part(i, carry):
        sg, sb, sq = carry
        at = rows_at(i, n * WPAD)
        dn = nn(dqkvs[0][0, at, :], weights[0](0)) + nn(dqkvs[1][0, at, :], weights[1](0))
        dn = dn * SCALE
        for half in range(2):
            for j in (1, 2):
                dn = dn + nn(dqkvs[half][j, at, :], weights[half](j))
        new = []
        for half in range(2):
            for m, j in enumerate((0, 2)):
                new.append(
                    sq[half * 2 + m] + jnp.sum(dqkvs[half][j, at, :].astype(F32), 0, keepdims=True)
                )
        d = jnp.concatenate([dn[k * WPAD : k * WPAD + WROWS] for k in range(n)], axis=0)
        to = rows_at(i, n * WROWS)
        xhat, rinv = norm_stats(x_ref[to, :])
        sg = sg + jnp.sum(d * xhat, 0, keepdims=True)
        sb = sb + jnp.sum(d, 0, keepdims=True)
        gx_ref[to, :] = gh_ref[to, :] + norm_back(d, xhat, rinv, gain)
        return sg, sb, tuple(new)

    z = jnp.zeros((1, C), F32)
    zq = jnp.zeros((1, 6 * HD), F32)
    return lax.fori_loop(0, wins // n, part, (z, z, (zq,) * 4))


def small_rows(ref, z, sq, fb1, table, shared):
    ref[...] = jnp.zeros_like(ref)
    if shared is not None:
        sg, sb, projb, sh_ref = shared
        ref[0:1] = sg
        ref[1:2] = sb
        ref[2:3] = projb
        ref[3:6] = sh_ref[...]
    ref[6:7] = fb1
    ref[7:8, 0:96] = sq[0][:, 96 * z : 96 * (z + 1)] * SCALE
    ref[7:8, 128:224] = sq[1][:, 96 * z : 96 * (z + 1)]
    ref[8:24, 0:48] = table[:, 48 * z : 48 * (z + 1)]


def attn_bwd_kernel(rows, across, *refs):
    (gh_ref, x_ref, xn_ref, gain_ref, qkvw_ref, projw_ref, a_ref, b_ref, info_ref) = refs[:9]
    (fb1_ref, sh_ref, qkv0_ref, p0_ref, mix0_ref, qkv1_ref, p1_ref, mix1_ref) = refs[9:17]
    (gin_ref, keep_ref, send_ref) = refs[17:20]
    (da_ref, do_ref, dqkv0_ref, dqkv1_ref, acc_ref, mask_ref, row_ref, sm_ref) = refs[20:]
    layer = 1
    par = info_ref[0]
    wins = (rows // WIN) * across
    mask_ref[...] = head_mask()
    acc_ref[...] = jnp.zeros_like(acc_ref)
    projb = window_grads(wins, gh_ref, da_ref)
    for half in range(2):
        do_ref[half] = nt(
            da_ref[...], proj_weight_of(half, layer, projw_ref, a_ref, b_ref)
        ).astype(BF)
    attend_backward(
        [
            (qkv0_ref, p0_ref, do_ref.at[0], dqkv0_ref, acc_ref.at[0]),
            (qkv1_ref, p1_ref, do_ref.at[1], dqkv1_ref, acc_ref.at[1]),
        ],
        wins,
        4,
        mask_ref,
    )
    for half, mix_ref, dqkv_ref in ((1, mix1_ref, dqkv1_ref), (0, mix0_ref, dqkv0_ref)):

        def give(at, one, two, half=half):
            keep_ref[half, at : at + 96, :] = one
            send_ref[half, at : at + 96, :] = two

        half_grads(half, par, xn_ref, da_ref, mix_ref, dqkv_ref, row_ref, give)
    weights = [
        lambda j, half=half: qkv_weight_of(half, j, layer, qkvw_ref, a_ref, b_ref)
        for half in range(2)
    ]
    sg, sb, sq = normed_grads(
        layer, wins, [dqkv0_ref, dqkv1_ref], weights, gh_ref, x_ref, gain_ref, gin_ref
    )
    for half in range(2):
        table = map_to_table(acc_ref.at[half])
        for z in range(2):
            q = 2 * half + z
            small_rows(
                sm_ref.at[q], z, sq[2 * half : 2 * half + 2], fb1_ref[q : q + 1], table,
                (sg, sb, projb, sh_ref)
            )
    keep_ref[0, C:, :] = sm_ref[par].astype(BF)
    send_ref[0, C:, :] = sm_ref[1 - par].astype(BF)
    keep_ref[1, C:, :] = sm_ref[2].astype(BF)
    send_ref[1, C:, :] = sm_ref[3].astype(BF)


def column_sum(ref):
    return jnp.sum(ref[...].astype(F32), 0, keepdims=True)


def attn_bwd_other_kernel(rows, across, *refs):
    (gh_ref, xn_ref, projw_ref, a_ref, b_ref, fb1_ref, qkv_ref, p_ref, mix_ref) = refs[:9]
    (da_ref, do_ref, dqkv_ref, pb_ref, keep_ref, send_ref) = refs[9:15]
    (do1_ref, mask_ref, acc_ref, sm_ref) = refs[15:]
    wins = (rows // WIN) * across
    mask_ref[...] = head_mask()
    acc_ref[...] = jnp.zeros_like(acc_ref)
    pb_ref[...] = window_grads(wins, gh_ref, da_ref)
    da = da_ref[...]
    do1_ref[...] = nt(da, proj_weight_of(1, 0, projw_ref, a_ref, b_ref)).astype(BF)
    do_ref[...] = nt(da, proj_weight_of(0, 0, projw_ref, a_ref, b_ref)).astype(BF)
    attend_backward([(qkv_ref, p_ref, do1_ref, dqkv_ref, acc_ref)], wins, 8, mask_ref)

    def give(at, one, two):
        keep_ref[at : at + 96, :] = one
        send_ref[at : at + 96, :] = two

    half_grads(1, None, xn_ref, da_ref, mix_ref, dqkv_ref, None, give)
    table = map_to_table(acc_ref)
    sq = (column_sum(dqkv_ref.at[0]), column_sum(dqkv_ref.at[2]))
    for z, ref in ((0, keep_ref), (1, send_ref)):
        small_rows(sm_ref, z, sq, fb1_ref[2 + z : 3 + z], table, None)
        ref[C:, :] = sm_ref[...].astype(BF)


def attn_bwd_own_kernel(rows, across, *refs):
    (gh_ref, x_ref, xn_ref, gain_ref, qkvw_ref, a_ref, b_ref, info_ref) = refs[:8]
    (fb1_ref, sh_ref, da_ref, do_ref, dqkv1_ref, pb_ref) = refs[8:14]
    (qkv_ref, p_ref, mix_ref) = refs[14:17]
    (out_ref, keep_ref, send_ref) = refs[17:20]
    (dqkv_ref, acc_ref, gx_ref, mask_ref, row_ref, sm_ref) = refs[20:]
    par = info_ref[0]
    wins = (rows // WIN) * across
    mask_ref[...] = head_mask()
    acc_ref[...] = jnp.zeros_like(acc_ref)
    attend_backward([(qkv_ref, p_ref, do_ref, dqkv_ref, acc_ref)], wins, 8, mask_ref)

    def give(at, one, two):
        keep_ref[at : at + 96, :] = one
        send_ref[at : at + 96, :] = two

    half_grads(0, par, xn_ref, da_ref, mix_ref, dqkv_ref, row_ref, give)
    weights = [
        lambda j, half=half: qkv_weight_of(half, j, 0, qkvw_ref, a_ref, b_ref)
        for half in range(2)
    ]
    sg, sb, sq = normed_grads(
        0, wins, [dqkv_ref, dqkv1_ref], weights, gh_ref, x_ref, gain_ref, gx_ref
    )
    table = map_to_table(acc_ref)
    for z in range(2):
        small_rows(
            sm_ref.at[z], z, sq[0:2], fb1_ref[z : z + 1], table, (sg, sb, pb_ref[...], sh_ref)
        )
    keep_ref[C:, :] = sm_ref[par].astype(BF)
    send_ref[C:, :] = sm_ref[1 - par].astype(BF)
    for r in range(rows):
        parts = [gx_ref[pl.ds(tile_row(r, k, across), SEG), :][:WIN] for k in range(across)]
        out_ref[r] = jnp.concatenate(parts, axis=0)


def pair_kernel(keep_ref, got_ref, own_ref, oth_ref):
    own_ref[...] = (keep_ref[0].astype(F32) + got_ref[0].astype(F32)).astype(BF)
    oth_ref[...] = (keep_ref[1].astype(F32) + got_ref[1].astype(F32)).astype(BF)


def combine_kernel(parts, bit, n_in, *refs):
    ins = refs[:n_in]
    info_ref = refs[n_in]
    outs = refs[n_in + 1 :]
    at = 0
    for rows, terms, split in parts:

        def total(first, n):
            acc = None
            for i, base in terms:
                x = ins[i][pl.ds(base + first, n), :].astype(F32)
                acc = x if acc is None else acc + x
            return acc.astype(BF)

        if bit is None or not split:
            whole = total(0, rows)
            for out in outs:
                out[at : at + rows, :] = whole
            at += rows
        else:
            n = rows // 2
            b = (info_ref[2] >> bit) & 1
            outs[0][at : at + n, :] = total(pl.multiple_of(b * n, n), n)
            outs[1][at : at + n, :] = total(pl.multiple_of((1 - b) * n, n), n)
            at += n


def join_kernel(halves, bit, mine_ref, got_ref, info_ref, out_ref):
    b = (info_ref[2] >> bit) & 1
    at = 0
    for n in halves:
        for ref, place in ((mine_ref, b), (got_ref, 1 - b)):
            to = pl.multiple_of(2 * at + place * n, 16)
            out_ref[pl.ds(to, n), :] = ref[at : at + n, :]
        at += n
    if at < mine_ref.shape[0]:
        out_ref[2 * at :, :] = mine_ref[at:, :]


def out_kernel(rows, across, st_ref, halo_ref, o_ref):
    for r in range(rows):
        parts = []
        for k in range(across):
            if r >= SHIFT:
                t = st_ref[pl.ds(tile_row(r - SHIFT, k, across), SEG), :]
            else:
                t = halo_ref[k, r]
            parts.append(t[:WIN])
        last = parts[-1]
        parts = [last[WIN - SHIFT :]] + parts[:-1] + [last[: WIN - SHIFT]]
        o_ref[r] = jnp.concatenate(parts, axis=0).astype(BF)


def final_kernel(*refs):
    pieces = refs[:12]
    (shared_ref, info_ref) = refs[12:14]
    (qkv_ref, proj_ref, f1_ref, f2_ref, gain_ref, bias_ref, pb_ref, fb2_ref) = refs[14:22]
    (qvb_ref, fb1_ref, tab_ref, asm_ref) = refs[22:]
    n = C // 2
    for layer in range(2):
        for i in range(4):
            core = info_ref[0] ^ (i // 2)
            half = ((info_ref[2] >> 1) & 1) ^ (i % 2)
            if layer == 1:
                mlp, attn, base = pieces[i], pieces[i], C
            else:
                mlp, attn, base = pieces[4 + i], pieces[8 + i], 0
            rows = pl.ds(pl.multiple_of(half * n, n), n)
            cols = pl.ds(pl.multiple_of(core * C, C), C)
            f1_ref[layer, rows, cols] = mlp[0:n, :].astype(F32)
            rows = pl.ds(pl.multiple_of(core * C + half * n, n), n)
            f2_ref[layer, rows, :] = mlp[n:C, :].astype(F32)
            rows = pl.ds(pl.multiple_of(half * n, n), n)
            asm_ref[core, rows, :] = attn[base : base + n, :].astype(F32)
            if i % 2 == 0:
                asm_ref[core, C:, :] = attn[base + n :, :].astype(F32)
        x_ref, y_ref = asm_ref.at[0], asm_ref.at[1]
        for j in range(4):
            for core, ref in enumerate((x_ref, y_ref)):
                to = pl.ds(96 * core, 96)
                if j < 3:
                    qkv_ref[layer, j, to, :] = ref[96 * j : 96 * (j + 1), :]
                else:
                    proj_ref[layer, to, :] = ref[96 * j : 96 * (j + 1), :]
        x = x_ref[C:, :]
        y = y_ref[C:, :]
        shared = x[0:6]
        if layer == 0:
            shared = asm_ref[info_ref[0], pl.ds(C, 6), :] + shared_ref[0:6].astype(F32)
        gain_ref[layer, 0:1] = shared[0:1]
        gain_ref[layer, 1:2] = shared[3:4]
        bias_ref[layer, 0:1] = shared[1:2]
        bias_ref[layer, 1:2] = shared[4:5]
        pb_ref[layer : layer + 1] = shared[2:3]
        fb2_ref[layer : layer + 1] = shared[5:6]
        fb1_ref[layer : layer + 1, 0:C] = x[6:7]
        fb1_ref[layer : layer + 1, C:] = y[6:7]
        for k in range(2):
            qvb_ref[layer, k : k + 1, 0:96] = x[7:8, 128 * k : 128 * k + 96]
            qvb_ref[layer, k : k + 1, 96:192] = y[7:8, 128 * k : 128 * k + 96]
        t = jnp.concatenate([x[8:24, 0:48], y[8:24, 0:48]], axis=1)
        wide = exact(t, offset_rows(), 0, 0) * offset_cols()
        for h in range(6):
            tab_ref[h, layer : layer + 1, :] = jnp.sum(
                wide[16 * h : 16 * (h + 1)], 0, keepdims=True
            )


SMEM = pl.BlockSpec(memory_space=pltpu.SMEM)
VMEM = pl.BlockSpec(memory_space=pltpu.VMEM)
HBM = pl.BlockSpec(memory_space=pltpu.HBM)


def call(kernel, name, us, limit, operands, outs, scratch=()):
    args = []
    specs = []
    for op in operands:
        args.append(op[0] if isinstance(op, tuple) else op)
        specs.append(op[1] if isinstance(op, tuple) else VMEM)
    shapes = [jax.ShapeDtypeStruct(s, d) for s, d in outs]
    return pl.pallas_call(
        kernel,
        name=name,
        in_specs=specs,
        out_specs=[VMEM for s in shapes],
        out_shape=shapes,
        scratch_shapes=[s if not isinstance(s, tuple) else pltpu.VMEM(*s) for s in scratch],
        cost_estimate=pl.CostEstimate(
            flops=int(us * 1e10), bytes_accessed=1000000, transcendentals=0
        ),
        compiler_params=pltpu.CompilerParams(vmem_limit_bytes=limit * 2**20),
    )(*args)


def on_device(n_win, *args):
    (
        tokens,
        crop_ids,
        cotangent,
        norm_gain,
        norm_bias,
        qkv_weight,
        qv_bias,
        proj_weight,
        proj_bias,
        fc1_weight,
        fc1_bias,
        fc2_weight,
        fc2_bias,
        pos_table,
    ) = args
    rows, cols = tokens.shape[1:3]
    across = cols // WIN
    wins = (rows // WIN) * across
    ntok = wins * WROWS
    npad = wins * WPAD
    win = lax.axis_index("win")
    tp = lax.axis_index("tp")
    par = win % 2
    info = (jnp.stack([par, tp, win]).astype(jnp.int32), SMEM)
    bits = n_win.bit_length() - 1
    assert n_win == 1 << bits and bits >= 3

    def to_tp(x, name):
        with jax.named_scope(name + "_tp"):
            return lax.ppermute(x, "tp", [(0, 1), (1, 0)])

    def to_win(x, bit, name):
        with jax.named_scope("%s_win%d" % (name, bit)):
            return lax.ppermute(x, "win", [(i, i ^ (1 << bit)) for i in range(n_win)])

    def after(x, *others):
        return lax.optimization_barrier((x,) + others)[0]

    def combine(parts, bit, ins, name):
        total = sum(rows // 2 if split and bit is not None else rows for rows, _, split in parts)
        outs = [((total, C), BF)] * (1 if bit is None else 2)
        return call(
            partial(combine_kernel, parts, bit, len(ins)), name, 1, 8, tuple(ins) + (info,), outs
        )

    def join(halves, bit, mine, got, name):
        return call(
            partial(join_kernel, halves, bit), name, 1, 8, (mine, got, info),
            [((mine.shape[0] + sum(halves), C), BF)],
        )[0]

    qkv_t = qkv_weight.transpose(0, 2, 3, 1)
    table = pos_table.transpose(2, 0, 1)
    raw = (qkv_t, proj_weight, fc1_weight, fc2_weight, table, qv_bias, fc1_bias)
    a0q, m0q, a1q, m1q, small = call(
        pack_kernel,
        "pack",
        2,
        8,
        tuple((x, HBM) for x in raw) + (info,),
        [((C + 128, C), BF), ((2 * C, C), BF), ((C, C), BF), ((2 * C, C), BF), ((2, 24, C), F32)],
        [(table.shape, F32), (qv_bias.shape, F32), (fc1_bias.shape, F32), pltpu.SemaphoreType.DMA((15,))],
    )
    a0 = to_tp(a0q, "a0")
    m0 = to_tp(m0q, "m0")
    a1 = to_tp(a1q, "a1")
    lq, lk, pos = call(
        partial(prep_kernel, rows, across),
        "prep",
        3,
        8,
        (crop_ids.transpose(2, 0, 1), small, info),
        [
            ((2, wins, 128), F32),
            ((2, wins, WPAD, 128), F32),
            ((2, 3, WPAD, 128), F32),
        ],
        [((128, 128), F32)],
    )
    tiles = (rows // WIN, across, WIN, SEG, C)
    mask = ((6 * WPAD, 6 * HD), BF)
    half_outs = [((3, npad, 192), BF), ((wins, WPAD, 6 * WPAD), BF), ((npad, 192), BF)]
    tok_f = ((ntok, C), F32)
    tok_b = ((ntok, C), BF)
    hid_b = ((4, ntok, C), BF)
    other_scratch = [mask, ((3, WPAD, 128), F32), ((16, 96), F32)]

    x0, xn0, part, qkv00, p00, mix00 = call(
        partial(attn_own_kernel, rows, across),
        "attn_own_0",
        5,
        12,
        (tokens[0], norm_gain, norm_bias, proj_bias, qv_bias, qkv_t, proj_weight, pos, lq, lk),
        [tok_f, ((npad, C), BF), tok_f] + half_outs,
        [mask],
    )
    cot_halo = to_tp(after(cotangent[0, :SHIFT], part), "cot")
    a0 = after(a0, part)
    a0s = to_win(a0[:C], 0, "a0")
    hid0, qkv01, p01, mix01, small_o = call(
        partial(attn_other_kernel, rows, across),
        "attn_other_0",
        0.1,
        12,
        (part, xn0, a0, a0s, lq, lk, info),
        [tok_f] + half_outs + [((2, 24, C), F32)],
        other_scratch,
    )
    m0 = after(m0, hid0)
    m0s = to_win(m0, 0, "m0")
    st0, act0, gp0 = call(
        partial(mlp_fwd_kernel, 0, 0),
        "mlp_fwd_0",
        5,
        20,
        (after(hid0, cot_halo), norm_gain, norm_bias, fc1_bias, small_o, fc2_bias)
        + (fc1_weight, fc2_weight, m0, m0s, info),
        [tok_f, hid_b, hid_b],
    )
    edge = st0.reshape(tiles)[0, :, :SHIFT]
    halo = to_tp(edge, "edge0")
    a1 = after(a1, edge)
    a1s = to_win(a1, 0, "a1")
    m1 = to_tp(after(m1q, edge), "m1")
    x1, xn1, hid1, qkv10, p10, mix10, qkv11, p11, mix11 = call(
        partial(attn_both_kernel, rows, across),
        "attn_fwd_1",
        10,
        14,
        (st0, halo, norm_gain, norm_bias, proj_bias, qv_bias, qkv_t, proj_weight)
        + (pos, small_o, a1, a1s, lq, lk, info),
        [tok_f, ((npad, C), BF), tok_f] + half_outs + half_outs,
        other_scratch,
    )
    m1 = after(m1, hid1)
    m1s = to_win(m1, 0, "m1")
    sums = [((4, C), F32), ((3, C), F32)]
    st1, gh1, df1, n21, du1, act1, send_m1, gfb1, gsh1 = call(
        partial(mlp_both_kernel, rows, across, 0),
        "mlp_both_1",
        10,
        20,
        (cotangent[0], cot_halo, hid1, norm_gain, norm_bias, fc1_bias, small_o, fc2_bias)
        + (fc1_weight, fc2_weight, m1, m1s, info),
        [tok_f, tok_f, tok_b, tok_b, hid_b, hid_b, ((2, 2 * C, C), BF)] + sums,
        [tok_f],
    )

    m1_core = to_win(send_m1, 0, "gm1")
    out_edge = after(st1.reshape(tiles)[-1, :, WIN - SHIFT :], send_m1)
    out_halo = to_tp(out_edge, "out")
    m1_own, m1_oth = call(
        mlp_keep_kernel, "mlp_keep_1", 2, 12, (n21, df1, du1, act1, after(m1_core, out_edge), info),
        [((2 * C, C), BF)] * 2,
    )
    m1_t = to_tp(m1_oth, "gm1")
    gin1, keep_a1, send_a1 = call(
        partial(attn_bwd_kernel, rows, across),
        "attn_bwd_1",
        14,
        16,
        (after(gh1, m1_oth), x1, xn1, norm_gain, qkv_t, proj_weight, a1, a1s, info)
        + (gfb1, gsh1, qkv10, p10, mix10, qkv11, p11, mix11),
        [tok_f, ((2, C + SMALL, C), BF), ((2, C + SMALL, C), BF)],
        [
            ((npad, C), BF),
            ((2, npad, 192), BF),
            ((3, npad, 192), BF),
            ((3, npad, 192), BF),
            ((2, 3, WPAD, 128), F32),
            mask,
            ((192, C), F32),
            ((4, SMALL, C), F32),
        ],
    )
    gin1, keep_a1, send_a1, m1_t = lax.optimization_barrier((gin1, keep_a1, send_a1, m1_t))
    edge = gin1.reshape(tiles)[-1, :, WIN - SHIFT :]
    halo = to_tp(edge, "edge1")
    a1_core = to_win(after(send_a1, edge), 0, "ga1")
    (layer_out,) = call(
        partial(out_kernel, rows, across), "layer_out", 1, 8, (after(st1, edge), out_halo),
        [((rows, cols, C), BF)],
    )
    a1_own, a1_oth = call(
        pair_kernel, "pair_a1", 1, 8, (keep_a1, after(a1_core, layer_out)), [((C + SMALL, C), BF)] * 2
    )
    a1_t = to_tp(a1_oth, "ga1")
    g0, df0, keep_f2, send_f2 = call(
        partial(down_grad_kernel, rows, across),
        "down_grad_0",
        4,
        8,
        (gin1, after(halo, a1_oth), act0, info),
        [tok_f, tok_b, ((2, C, C), BF), ((2, C, C), BF)],
    )
    f2_core = to_win(send_f2, 0, "gf2")
    m1_mine, m1_away = combine(
        [(C, [(0, 0), (1, 0)], True), (C, [(0, C), (1, C)], True)],
        1,
        (m1_own, after(m1_t, send_f2)),
        "m1_y",
    )
    m1_y = to_win(m1_away, 1, "gm1")
    f2_own, f2_oth = call(
        pair_kernel, "pair_f2", 1, 8, (keep_f2, after(f2_core, m1_away)), [((C, C), BF)] * 2
    )
    f2_t = to_tp(f2_oth, "gf2")
    gh0, n20, du0, send_f1, gfb0, gsh0 = call(
        partial(mlp_bwd_kernel, 0),
        "mlp_bwd_0",
        6,
        16,
        (after(g0, f2_oth), df0, hid0, gp0, norm_gain, norm_bias, fc1_weight, fc2_weight, m0, m0s, info),
        [tok_f, tok_b, hid_b, ((2, C, C), BF)] + sums,
    )
    f1_core = to_win(send_f1, 0, "gf1")
    na = C + SMALL
    a1_mine, a1_away = combine(
        [(C, [(0, 0), (1, 0)], True), (SMALL, [(0, C), (1, C)], False)],
        1,
        (a1_own, after(a1_t, send_f1)),
        "a1_y",
    )
    a1_y = to_win(a1_away, 1, "ga1")
    f1_own, f1_oth = call(
        up_keep_kernel, "up_keep_0", 1, 8, (n20, du0, after(f1_core, a1_away), info),
        [((C, C), BF)] * 2,
    )
    f1_t = to_tp(f1_oth, "gf1")
    da, do, dqkv1, pb0, keep_o0, send_o0 = call(
        partial(attn_bwd_other_kernel, rows, across),
        "attn_bwd_other_0",
        6,
        16,
        (after(gh0, f1_oth), xn0, proj_weight, a0, a0s, gfb0, qkv01, p01, mix01),
        [
            ((npad, C), BF),
            ((npad, 192), BF),
            ((3, npad, 192), BF),
            ((1, C), F32),
            ((na, C), BF),
            ((na, C), BF),
        ],
        [((npad, 192), BF), mask, ((3, WPAD, 128), F32), ((SMALL, C), F32)],
    )
    o0_core = to_win(send_o0, 0, "go0")
    n = C // 2
    c1_mine, c1_away = combine(
        [
            (n, [(0, 0), (1, 0)], True),
            (n, [(0, n), (1, n)], True),
            (n, [(2, 0), (3, 0)], True),
            (SMALL, [(2, n), (3, n)], False),
        ],
        2,
        (m1_mine, after(m1_y, send_o0), a1_mine, after(a1_y, send_o0)),
        "c1_z",
    )
    c1_z = to_win(c1_away, 2, "gc1")
    (o0_sum,) = combine([(na, [(0, 0), (1, 0)], True)], None, (keep_o0, after(o0_core, c1_away)), "o0")
    o0_t = to_tp(o0_sum, "go0")
    m0_mine, m0_away = combine(
        [(C, [(0, 0), (1, 0)], True), (C, [(2, 0), (3, 0)], True)],
        1,
        (f1_own, after(f1_t, o0_sum), f2_own, after(f2_t, o0_sum)),
        "m0_y",
    )
    m0_y = to_win(m0_away, 1, "gm0")
    grad_tokens, keep_a0, send_a0 = call(
        partial(attn_bwd_own_kernel, rows, across),
        "attn_bwd_own_0",
        9,
        16,
        (gh0, x0, xn0, norm_gain, qkv_t, a0, a0s, info)
        + (gfb0, gsh0, da, do, dqkv1, pb0, qkv00, p00, after(mix00, m0_away)),
        [((rows, cols, C), F32), ((na, C), BF), ((na, C), BF)],
        [
            ((3, npad, 192), BF),
            ((3, WPAD, 128), F32),
            tok_f,
            mask,
            ((192, C), F32),
            ((2, SMALL, C), F32),
        ],
    )

    a0_core = to_win(send_a0, 0, "ga0")
    def plus(x, y, name):
        return combine([(x.shape[0], [(0, 0), (1, 0)], True)], None, (x, y), name)[0]

    c1 = plus(c1_mine, after(c1_z, send_a0), "c1_z2")
    a0_mine, a0_away = combine(
        [(C, [(0, 0), (1, 0), (2, 0)], True), (SMALL, [(0, C), (1, C), (2, C)], False)],
        1,
        (keep_a0, a0_core, after(o0_t, c1)),
        "a0_y",
    )
    a0_y = to_win(a0_away, 1, "ga0")
    c1_z2 = to_win(after(c1, a0_away), 3, "gc1")
    m0_mine, m0_away = combine(
        [(n, [(0, 0), (1, 0)], True), (n, [(0, n), (1, n)], True)],
        2,
        (m0_mine, after(m0_y, a0_away)),
        "m0_z",
    )
    m0_z = to_win(m0_away, 2, "gm0")
    a0 = plus(a0_mine, a0_y, "a0_z")
    a0_z = to_win(a0, 2, "ga0")
    m0 = plus(m0_mine, after(m0_z, a0), "m0_z2")
    a0 = plus(a0, a0_z, "a0_z2")
    for bit in range(3, bits):
        a0_b = to_win(a0, bit, "ga0")
        m0_b = to_win(after(m0, a0), bit, "gm0")
        c1_b = c1_z2 if bit == 3 else to_win(c1, bit, "gc1")
        c1 = plus(c1, c1_b, "c1_s")
        m0 = plus(m0, m0_b, "m0_s")
        a0 = plus(a0, a0_b, "a0_s")
    pieces = []
    c1 = join([n // 2] * 3, 2, c1, to_win(c1, 2, "gc1_back"), "c1_join")
    m0 = join([n // 2] * 2, 2, m0, to_win(m0, 2, "gm0_back"), "m0_join")
    for name, x in (("gc1", c1), ("gm0", m0), ("ga0", a0)):
        y = to_win(x, 1, name + "_back")
        pieces += [x, y, to_win(x, 0, name + "_mine"), to_win(y, 0, name + "_theirs")]
    shared = to_tp(a0[n : n + 16], "shared")
    outs = call(
        final_kernel,
        "final",
        4,
        12,
        tuple(pieces) + (shared, info),
        [
            ((2, 3, 192, C), F32),
            ((2, 192, C), F32),
            ((2, C, 2 * C), F32),
            ((2, 2 * C, C), F32),
            ((2, 2, C), F32),
            ((2, 2, C), F32),
            ((2, C), F32),
            ((2, C), F32),
            ((2, 2, 192), F32),
            ((2, 2 * C), F32),
            ((6, 2, 169), F32),
        ],
        [((2, na, C), F32)],
    )
    (g_qkv, g_proj, g_f1, g_f2, g_gain, g_bias, g_pb, g_fb2, g_qvb, g_fb1, g_tab) = outs
    return (
        layer_out[None],
        grad_tokens[None],
        g_gain,
        g_bias,
        g_qkv.transpose(0, 3, 1, 2),
        g_qvb,
        g_proj,
        g_pb,
        g_f1,
        g_fb1,
        g_f2,
        g_fb2,
        g_tab.transpose(1, 2, 0),
    )


def solution(mesh):
    return jax.shard_map(
        partial(on_device, mesh.shape["win"]),
        mesh=mesh,
        in_specs=(
            P("win", "tp", None, None),
            P("win", None, None),
            P("win", "tp", None, None),
            P(),
            P(),
            P(None, None, None, "tp"),
            P(None, None, "tp"),
            P(None, "tp", None),
            P(),
            P(None, None, "tp"),
            P(None, "tp"),
            P(None, "tp", None),
            P(),
            P(None, None, "tp"),
        ),
        out_specs=(
            P("win", "tp", None, None),
            P("win", "tp", None, None),
            P(),
            P(),
            P(None, None, None, "tp"),
            P(None, None, "tp"),
            P(None, "tp", None),
            P(),
            P(None, None, "tp"),
            P(None, "tp"),
            P(None, "tp", None),
            P(),
            P(None, None, "tp"),
        ),
        check_vma=False,
    )
```

```python
from functools import partial

import jax
import jax.numpy as jnp
import numpy as np
from jax import lax
from jax.experimental import pallas as pl
from jax.experimental.pallas import tpu as pltpu
from jax.sharding import PartitionSpec as P

C = 384
WIN = 7
SHIFT = 3
HD = 32
EPS = 1e-05
NEG = -1000000000.0
SCALE = HD**-0.5
F32 = jnp.float32
BF = jnp.bfloat16
SEG = 8
WROWS = WIN * SEG
WPAD = 64


def nn(a, b):
    return lax.dot_general(a, b, (((1,), (0,)), ((), ())), preferred_element_type=F32)


def nt(a, b):
    return lax.dot_general(a, b, (((1,), (1,)), ((), ())), preferred_element_type=F32)


def tn(a, b):
    return lax.dot_general(a, b, (((0,), (0,)), ((), ())), preferred_element_type=F32)


def norm_stats(x):
    mean = jnp.mean(x, -1, keepdims=True)
    cent = x - mean
    var = jnp.mean(cent * cent, -1, keepdims=True)
    rinv = lax.rsqrt(var + EPS)
    return cent * rinv, rinv


def norm_back(dz, xhat, rinv, gain):
    d = dz * gain
    return rinv * (
        d - jnp.mean(d, -1, keepdims=True) - xhat * jnp.mean(d * xhat, -1, keepdims=True)
    )


def tile_row(r, k, across):
    return (((r // WIN) * across + k) * WIN + r % WIN) * SEG


def zero_rows(n):
    return jnp.zeros((n, C), F32)


def head_mask():
    row = lax.broadcasted_iota(jnp.int32, (6 * WPAD, 6 * HD), 0) // WPAD
    col = lax.broadcasted_iota(jnp.int32, (6 * WPAD, 6 * HD), 1) // HD
    return (row == col).astype(BF)


def spread(x, mask):
    return jnp.concatenate([x] * 6, axis=0) * mask


def fold(o):
    lane = lax.broadcasted_iota(jnp.int32, (WPAD, 128), 1)

    def of(h, a, b):
        return o[WPAD * h : WPAD * (h + 1), a:b]

    one = jnp.where(lane < 96, of(2, 0, 128), of(3, 0, 128))
    one = jnp.where(lane < 64, of(1, 0, 128), one)
    one = jnp.where(lane < 32, of(0, 0, 128), one)
    two = jnp.where(lane[:, :64] < 32, of(4, 128, 192), of(5, 128, 192))
    return jnp.concatenate([one, two], axis=1)


def rows_at(i, n):
    return pl.ds(pl.multiple_of(i * n, n), n)


def iota(shape, dim):
    return lax.broadcasted_iota(jnp.int32, shape, dim)


def exact(a, b, ca, cb):
    return lax.dot_general(
        a,
        b,
        (((ca,), (cb,)), ((), ())),
        precision=lax.Precision.HIGHEST,
        preferred_element_type=F32,
    )


def offset_rows():
    return (12 - iota((16, 169), 0) == iota((16, 169), 1) // 13).astype(F32)


def offset_cols():
    return (iota((96, 169), 0) % 16 == iota((96, 169), 1) % 13).astype(F32)


def column_pick(kx):
    r = iota((96, 6 * WPAD), 0)
    c = iota((96, 6 * WPAD), 1)
    qx = c % 8
    return ((r // 16 == c // WPAD) & (r % 16 == qx - kx + WIN - 1) & (qx < WIN)).astype(BF)


def table_to_map(t, pick_ref, pos_ref):
    pos_ref[...] = jnp.zeros_like(pos_ref)
    group = (iota((8, 6 * WPAD), 1) % WPAD) // 8
    high = t.astype(BF)
    low = (t - high.astype(F32)).astype(BF)
    both = jnp.concatenate([high, low], axis=0)
    for kx in range(WIN):
        h = nn(both, pick_ref[kx])
        h = h[:16] + h[16:]
        g = jnp.zeros((8, 6 * WPAD), F32)
        for j in range(WIN):
            g = jnp.where(group == j, h[6 - j : 14 - j], g)
        for i in range(3):
            pos_ref[i, pl.ds(kx, 8, stride=8), :] = g[:, 128 * i : 128 * (i + 1)]


def map_to_table(pos_ref, pick_ref):
    group = (iota((16, 6 * WPAD), 1) % WPAD) // 8
    total = jnp.zeros((16, 96), F32)
    for kx in range(WIN):
        r = jnp.concatenate([pos_ref[i, pl.ds(kx, 8, stride=8), :] for i in range(3)], axis=1)
        h = jnp.zeros((16, 6 * WPAD), F32)
        for j in range(WIN):
            parts = [r, jnp.zeros((2 + j, 6 * WPAD), F32)]
            if j < 6:
                parts = [jnp.zeros((6 - j, 6 * WPAD), F32)] + parts
            h = jnp.where(group == j, jnp.concatenate(parts, axis=0), h)
        total = total + nt(h.astype(BF), pick_ref[kx])
    return total


def shift_in(tile, x_ref, rows, across):
    for r in range(rows):
        for k in range(across):
            a = tile(r + SHIFT, k)
            b = tile(r + SHIFT, (k + 1) % across)
            x_ref[pl.ds(tile_row(r, k, across), SEG), :] = jnp.concatenate(
                [a[SHIFT:WIN], b[:SHIFT], zero_rows(1)], axis=0
            )


def shift_out(tile, x_ref, rows, across):
    for r in range(rows):
        for k in range(across):
            a = tile(r - SHIFT, (k - 1) % across)
            b = tile(r - SHIFT, k)
            x_ref[pl.ds(tile_row(r, k, across), SEG), :] = jnp.concatenate(
                [a[WIN - SHIFT : WIN], b[: WIN - SHIFT], zero_rows(1)], axis=0
            )

EDGE_ROWS = 96
SMALL = 32


SMALL_ROWS = 24


def copies_of(pairs, sems):
    copies = [pltpu.make_async_copy(x, y, sems.at[n]) for n, (x, y) in enumerate(pairs)]
    for copy in copies:
        copy.start()
    return copies


def attn_copies(layer, par, qkvw_ref, projw_ref, a_ref):
    of_heads = pl.ds(pl.multiple_of(par * 96, 96), 96)
    pairs = [
        (qkvw_ref.at[layer, j, of_heads, :], a_ref.at[pl.ds(96 * j, 96), :]) for j in range(3)
    ]
    return pairs + [(projw_ref.at[layer, of_heads, :], a_ref.at[pl.ds(288, 96), :])]


def mlp_copies(layer, par, f1_ref, f2_ref, m_ref):
    of_units = pl.ds(pl.multiple_of(par * C, C), C)
    return [
        (f1_ref.at[layer, :, of_units], m_ref.at[pl.ds(0, C), :]),
        (f2_ref.at[layer, of_units, :], m_ref.at[pl.ds(C, C), :]),
    ]


def high_low(x):
    high = x.astype(BF).astype(F32)
    return jnp.concatenate([high, x - high], axis=0).astype(BF)


def pack_first_kernel(
    qkvw_ref, projw_ref, tab_ref, qvb_ref, fb1_ref, info_ref,
    a0_ref, small_ref, tab_v, qvb_v, fb1_v, sems
):
    pairs = [(tab_ref, tab_v), (qvb_ref, qvb_v), (fb1_ref, fb1_v)]
    copies = copies_of(pairs + attn_copies(0, info_ref[0], qkvw_ref, projw_ref, a0_ref), sems)
    small_ref[...] = jnp.zeros_like(small_ref)
    for copy in copies[:3]:
        copy.wait()
    for layer in range(2):
        tab = tab_v[:, layer, :]
        wide = jnp.concatenate([jnp.broadcast_to(tab[h : h + 1], (16, 169)) for h in range(6)])
        small_ref[layer, 0:16, 0:96] = exact(offset_rows(), wide * offset_cols(), 1, 1)
        small_ref[layer, 16:17, :] = fb1_v[layer : layer + 1, 0:C]
        small_ref[layer, 17:18, :] = fb1_v[layer : layer + 1, C:]
        small_ref[layer, 18:20, 0:192] = qvb_v[layer]
    a0_ref[C:, :] = high_low(small_ref[0])
    for copy in copies[3:]:
        copy.wait()


def pack_kernel(
    qkvw_ref, projw_ref, f1_ref, f2_ref, cot_ref, small_ref, info_ref,
    m0_ref, a1_ref, m1_ref, cot_v, sems
):
    par = info_ref[0]
    pairs = [(cot_ref.at[pl.ds(0, SHIFT)], cot_v)]
    pairs += mlp_copies(0, par, f1_ref, f2_ref, m0_ref)
    pairs += attn_copies(1, par, qkvw_ref, projw_ref, a1_ref)
    pairs += mlp_copies(1, par, f1_ref, f2_ref, m1_ref)
    copies = copies_of(pairs, sems)
    a1_ref[C:, :] = high_low(small_ref[1])
    copies[0].wait()
    edge = [cot_v[r].astype(F32) for r in range(SHIFT)]
    n = EDGE_ROWS - SHIFT * cot_v.shape[1]
    m1_ref[2 * C :, :] = jnp.concatenate(edge + [zero_rows(n)], axis=0).astype(BF)
    for copy in copies[1:]:
        copy.wait()


def small_of(a_ref):
    rows = a_ref[C : C + 2 * SMALL_ROWS, :].astype(F32)
    return rows[0:SMALL_ROWS] + rows[SMALL_ROWS:]


def edge_tile(edge, k, r):
    at = (k * SHIFT + r) * SEG
    return edge[at : at + SEG]


def edge_rows(ref, across, rows):
    tiles = [ref[pl.ds(tile_row(r, k, across), SEG), :] for k in range(across) for r in rows]
    return jnp.concatenate(tiles, axis=0).astype(BF)


def prep_kernel(layer, rows, across, *refs):
    (crop_ref, small_ref, info_ref) = refs[:3]
    if layer == 0:
        (lq_ref, lk_ref, pos_ref, pick_ref, c_ref) = refs[3:]
        for kx in range(WIN):
            pick_ref[kx] = column_pick(kx)
    else:
        (pick_ref, lq_ref, lk_ref, pos_ref, c_ref) = refs[3:]
    tp = info_ref[1]
    cols = across * WIN
    height = crop_ref.shape[2]
    table_to_map(small_ref[layer, 0:16, 0:96], pick_ref, pos_ref)
    c_ref[...] = jnp.zeros_like(c_ref)
    c_ref[0:cols, 0:height] = crop_ref[:, 0, :].astype(F32)
    crops = c_ref[...].astype(BF)
    row = iota((32, 128), 0)
    lane = iota((32, 128), 1)
    shift = SHIFT if layer == 1 else 0
    src = rows * tp + row + shift
    src = jnp.where(src >= height, src - height, src)
    grid = nt((src == lane).astype(BF), crops).astype(BF)
    labs = []
    for wc in range(across):
        qx = iota((128, 128), 1) % 8
        col = qx + (WIN * wc + shift)
        col = jnp.where(col >= cols, col - cols, col)
        pick = ((col == iota((128, 128), 0)) & (qx < WIN)).astype(BF)
        lab = nn(grid, pick)
        if layer == 1:
            g = rows * tp + row
            zr = (g >= height - WIN).astype(F32) + (g >= height - SHIFT).astype(F32)
            here = lane % 8 + WIN * wc
            zc = (here >= cols - WIN).astype(F32) + (here >= cols - SHIFT).astype(F32)
            lab = lab * 9.0 + zr * 3.0 + zc
        labs.append(lab)
    real = (iota((1, 128), 1) % 8 < WIN) & (iota((1, 128), 1) % WPAD < WROWS)
    for wr in range(rows // WIN):
        lines = []
        for wc in range(across):
            w = wr * across + wc
            mine = row == (lane % WPAD) // 8 + WIN * wr
            line = jnp.sum(jnp.where(mine, labs[wc], 0.0), 0, keepdims=True)
            line = jnp.where(real, line, -1.0)
            lq_ref[w : w + 1, :] = line
            lines.append(line)
        for wc in range(0, across, 2):
            w = wr * across + wc
            both = jnp.where(iota((1, 128), 1) < WPAD, lines[wc], lines[wc + 1])
            both = jnp.broadcast_to(both, (128, 128)).T
            lk_ref[w] = both[:WPAD]
            lk_ref[w + 1] = both[WPAD:]


def qkv_weight_of(half, j, layer, qkvw_ref, a_ref, b_ref):
    if half == 0:
        return qkvw_ref[layer, j]
    return jnp.concatenate([a_ref[96 * j : 96 * (j + 1)], b_ref[96 * j : 96 * (j + 1)]], axis=0)


def proj_weight_of(half, layer, projw_ref, a_ref, b_ref):
    if half == 0:
        return projw_ref[layer]
    return jnp.concatenate([a_ref[288:384], b_ref[288:384]], axis=0)


def norm_windows(layer, wins, x_ref, xn_ref, gain_ref, bias_ref):
    gain = gain_ref[layer, 0:1]
    bias = bias_ref[layer, 0:1]

    def four(i, carry):
        xhat, _ = norm_stats(x_ref[rows_at(i, 4 * WROWS), :])
        xn = xhat * gain + bias
        for n in range(4):
            part = jnp.concatenate(
                [xn[n * WROWS : (n + 1) * WROWS], zero_rows(WPAD - WROWS)], axis=0
            )
            xn_ref[rows_at(4 * i + n, WPAD), :] = part.astype(BF)
        return carry

    lax.fori_loop(0, wins // 4, four, 0)


def project_half(xn_ref, qkv_ref, weight, qb, vb):
    n = xn_ref.shape[0] // 2

    def part(i, carry):
        at = rows_at(i, n)
        xn = xn_ref[at, :]
        q = nt(xn, weight(0))
        k = nt(xn, weight(1))
        v = nt(xn, weight(2))
        qkv_ref[0, at, :] = ((q + qb) * SCALE).astype(BF)
        qkv_ref[1, at, :] = k.astype(BF)
        qkv_ref[2, at, :] = (v + vb).astype(BF)
        return carry

    lax.fori_loop(0, 2, part, 0)


def attend_forward(halves, wins, group, lq_ref, lk_ref, mask_ref):
    def body(i, carry):
        units = [(i * group + u, h) for u in range(group) for h in halves]
        scores = []
        for w, (qkv_ref, _, _, _) in units:
            at = rows_at(w, WPAD)
            scores.append(nt(qkv_ref[1, at, :], spread(qkv_ref[0, at, :], mask_ref[...])))
        probs = []
        for (w, (_, pos, p_ref, _)), s in zip(units, scores):
            same = lk_ref[w] == lq_ref[pl.ds(w, 1), :]
            same = jnp.concatenate([same] * 3, axis=1)
            s = jnp.where(same, s + jnp.concatenate([pos[n] for n in range(3)], axis=1), NEG)
            e = jnp.exp(s - jnp.max(s, 0, keepdims=True))
            p = (e * (1.0 / jnp.sum(e, 0, keepdims=True))).astype(BF)
            p_ref[w] = p
            probs.append(p)
        for (w, (qkv_ref, _, _, mix_ref)), p in zip(units, probs):
            at = rows_at(w, WPAD)
            mix_ref[at, :] = fold(tn(p, qkv_ref[2, at, :])).astype(BF)
        return carry

    lax.fori_loop(0, wins // group, body, 0)


def add_branch(wins, mixes, weights, bias, x_ref, hid_ref):
    n = 8

    def part(i, carry):
        res = bias
        for m_ref, w in zip(mixes, weights):
            res = res + nn(m_ref[rows_at(i, n * WPAD), :], w)
        for k in range(n):
            to = rows_at(i * n + k, WROWS)
            hid_ref[to, :] = x_ref[to, :] + res[k * WPAD : k * WPAD + WROWS]
        return carry

    lax.fori_loop(0, wins // n, part, 0)


def attn_own_kernel(rows, across, *refs):
    (tok_ref, gain_ref, bias_ref, pb_ref, qvb_ref, qkvw_ref, projw_ref) = refs[:7]
    (pos_ref, lq_ref, lk_ref) = refs[7:10]
    (x_ref, xn_ref, hid_ref, qkv_ref, p_ref, mix_ref, mask_ref) = refs[10:]
    wins = (rows // WIN) * across
    for r in range(rows):
        row = tok_ref[r].astype(F32)
        for k in range(across):
            x_ref[pl.ds(tile_row(r, k, across), SEG), :] = jnp.concatenate(
                [row[WIN * k : WIN * (k + 1)], zero_rows(1)], axis=0
            )
    mask_ref[...] = head_mask()
    norm_windows(0, wins, x_ref, xn_ref, gain_ref, bias_ref)
    project_half(
        xn_ref, qkv_ref, lambda j: qkvw_ref[0, j], qvb_ref[0, 0:1], qvb_ref[0, 1:2]
    )
    attend_forward(
        [(qkv_ref, pos_ref, p_ref, mix_ref)], wins, 8, lq_ref, lk_ref, mask_ref
    )
    add_branch(wins, [mix_ref], [projw_ref[0]], pb_ref[0:1], x_ref, hid_ref)


def attn_other_kernel(rows, across, *refs):
    (part_ref, xn_ref, a_ref, b_ref, lq_ref, lk_ref, pick_ref, info_ref) = refs[:8]
    (hid_ref, qkv_ref, p_ref, mix_ref, small_ref, mask_ref, pos_ref) = refs[8:]
    small_ref[...] = small_of(a_ref)
    wins = (rows // WIN) * across
    mask_ref[...] = head_mask()
    bias = other_small(small_ref, info_ref[0], pick_ref, pos_ref)
    project_half(
        xn_ref,
        qkv_ref,
        lambda j: qkv_weight_of(1, j, 0, None, a_ref, b_ref),
        bias[0:1],
        bias[1:2],
    )
    attend_forward([(qkv_ref, pos_ref, p_ref, mix_ref)], wins, 8, lq_ref, lk_ref, mask_ref)
    add_branch(
        wins, [mix_ref], [proj_weight_of(1, 0, None, a_ref, b_ref)], 0.0, part_ref, hid_ref
    )


def other_small(small_ref, par, pick_ref, pos_ref):
    first = par == 0

    def swapped(v, n):
        return jnp.where(first, v, jnp.concatenate([v[:, n : 2 * n], v[:, :n]], axis=1))

    t = swapped(small_ref[0:16, 0:96], 48)
    table_to_map(t, pick_ref, pos_ref)
    return swapped(small_ref[18:20, 0:192], 96)


def norm_kernel(rows, across, *refs):
    (st_ref, halo_ref, gain_ref, bias_ref, qvb_ref, qkvw_ref) = refs[:6]
    (x_ref, xn_ref, qkv_ref) = refs[6:]

    def tile(r, k):
        if r < rows:
            return st_ref[pl.ds(tile_row(r, k, across), SEG), :]
        return edge_tile(halo, k, r - rows)

    halo = halo_ref[...].astype(F32)
    shift_in(tile, x_ref, rows, across)
    norm_windows(1, (rows // WIN) * across, x_ref, xn_ref, gain_ref, bias_ref)
    project_half(
        xn_ref, qkv_ref, lambda j: qkvw_ref[1, j], qvb_ref[1, 0:1], qvb_ref[1, 1:2]
    )


def attn_both_kernel(rows, across, *refs):
    (xn_ref, qkv0_ref, pos_ref, a_ref, b_ref) = refs[:5]
    (lq_ref, lk_ref, pick_ref, info_ref) = refs[5:9]
    (p0_ref, mix0_ref, qkv1_ref, p1_ref, mix1_ref, small_ref, mask_ref, pos1_ref) = refs[9:]
    wins = (rows // WIN) * across
    mask_ref[...] = head_mask()
    small_ref[...] = small_of(a_ref)
    bias = other_small(small_ref, info_ref[0], pick_ref, pos1_ref)
    project_half(
        xn_ref,
        qkv1_ref,
        lambda j: qkv_weight_of(1, j, 1, None, a_ref, b_ref),
        bias[0:1],
        bias[1:2],
    )
    attend_forward(
        [(qkv0_ref, pos_ref, p0_ref, mix0_ref), (qkv1_ref, pos1_ref, p1_ref, mix1_ref)],
        wins,
        4,
        lq_ref,
        lk_ref,
        mask_ref,
    )


def branch_kernel(wins, x_ref, mix0_ref, mix1_ref, projw_ref, a_ref, b_ref, pb_ref, hid_ref):
    add_branch(
        wins,
        [mix0_ref, mix1_ref],
        [projw_ref[1], proj_weight_of(1, 1, None, a_ref, b_ref)],
        pb_ref[1:2],
        x_ref,
        hid_ref,
    )


def up_weight(part, layer, base, f1_ref, a_ref, b_ref):
    if part == 0:
        return f1_ref[layer]
    return jnp.concatenate([a_ref[base : base + C], b_ref[base : base + C]], axis=1)


def down_weight(part, layer, base, f2_ref, a_ref, b_ref):
    if part == 0:
        return f2_ref[layer]
    return jnp.concatenate([a_ref[base + C : base + 2 * C], b_ref[base + C : base + 2 * C]], axis=0)


def up_biases(layer, par, fb1_ref, small_ref):
    own = fb1_ref[layer : layer + 1]
    one, two = small_ref[16:17], small_ref[17:18]
    first = par == 0
    return own, jnp.concatenate(
        [jnp.where(first, one, two), jnp.where(first, two, one)], axis=1
    )


def gelu_pair(u):
    phi = 0.5 + 0.5 * lax.erf(u * (2.0**-0.5))
    slope = phi + u * (jnp.exp(-0.5 * u * u) * (2.0 * np.pi) ** -0.5)
    return (u * phi).astype(BF), slope.astype(BF)


def mlp_own_kernel(hid_ref, gain_ref, bias_ref, fb1_ref, fb2_ref, f1_ref, f2_ref, st_ref, n2_ref, act_ref, gp_ref):
    h = hid_ref[...]
    xhat, _ = norm_stats(h)
    n2 = (xhat * gain_ref[0, 1:2] + bias_ref[0, 1:2]).astype(BF)
    n2_ref[...] = n2
    act, slope = gelu_pair(nn(n2, f1_ref[0]) + fb1_ref[0:1])
    for z in range(2):
        act_ref[z] = act[:, C * z : C * (z + 1)]
        gp_ref[z] = slope[:, C * z : C * (z + 1)]
    st_ref[...] = h + fb2_ref[0:1] + nn(act, f2_ref[0])


def mlp_other_kernel(
    across, part_ref, n2_ref, fb1_ref, small_ref, a_ref, b_ref, info_ref, st_ref, act_ref, gp_ref,
    edge_ref
):
    _, bias = up_biases(0, info_ref[0], fb1_ref, small_ref)
    act, slope = gelu_pair(nn(n2_ref[...], up_weight(1, 0, 0, None, a_ref, b_ref)) + bias)
    for z in range(2):
        act_ref[z] = act[:, C * z : C * (z + 1)]
        gp_ref[z] = slope[:, C * z : C * (z + 1)]
    st_ref[...] = part_ref[...] + nn(act, down_weight(1, 0, 0, None, a_ref, b_ref))
    edge_ref[...] = edge_rows(st_ref, across, range(SHIFT))


def mlp_back_rows(
    layer, base, at, g, df, h, slopes, gain, bias, f1_ref, f2_ref, a_ref, b_ref, refs, carry
):
    (gh_ref, n2_ref, du_ref) = refs
    (sb, sg, sf, s1) = carry
    sf = sf + jnp.sum(df.astype(F32), 0, keepdims=True)
    grads = [nt(df, down_weight(p, layer, base, f2_ref, a_ref, b_ref)) for p in range(2)]
    new = []
    parts = []
    for p in range(2):
        du = [
            (grads[p][:, C * z : C * (z + 1)] * slopes(2 * p + z).astype(F32)).astype(BF)
            for z in range(2)
        ]
        for z in range(2):
            du_ref[2 * p + z, at, :] = du[z]
            new.append(s1[2 * p + z] + jnp.sum(du[z].astype(F32), 0, keepdims=True))
        parts.append(jnp.concatenate(du, axis=1))
    dz = nt(parts[0], up_weight(0, layer, base, f1_ref, a_ref, b_ref)) + nt(
        parts[1], up_weight(1, layer, base, f1_ref, a_ref, b_ref)
    )
    xhat, rinv = norm_stats(h)
    n2_ref[at, :] = (xhat * gain + bias).astype(BF)
    sg = sg + jnp.sum(dz * xhat, 0, keepdims=True)
    sb = sb + jnp.sum(dz, 0, keepdims=True)
    gh_ref[at, :] = g + norm_back(dz, xhat, rinv, gain)
    return sb, sg, sf, tuple(new)


def quarter_of(par, slot, part):
    return (par ^ slot) if part == 0 else 2 + slot


def mlp_sums(carry, fb1_ref, sh_ref):
    sb, sg, sf, s1 = carry
    for q in range(4):
        fb1_ref[q : q + 1] = s1[q]
    sh_ref[0:1] = sg
    sh_ref[1:2] = sb
    sh_ref[2:3] = sf


def zero_sums():
    z = jnp.zeros((1, C), F32)
    return z, z, z, (z,) * 4


def mlp_both_kernel(rows, across, base, *refs):
    (cot_ref, hid_ref, gain_ref, bias_ref, fb1b_ref, small_ref, fb2_ref) = refs[:7]
    (f1_ref, f2_ref, a_ref, b_ref, info_ref) = refs[7:12]
    (st_ref, gh_ref, df_ref, n2_ref, du_ref, act_ref, send_ref, fb1_ref, sh_ref) = refs[12:21]
    (edge_ref, g_ref) = refs[21:]
    layer = 1
    cot_edge = a_ref[2 * C :, :].astype(F32)
    cols = across * WIN
    for r in range(rows):
        s = r + SHIFT
        if s < rows:
            row = cot_ref[s].astype(F32)
        else:
            row = cot_edge[(s - rows) * cols : (s - rows + 1) * cols]
        for k in range(across):
            a = WIN * k + SHIFT
            if k < across - 1:
                piece = [row[a : a + WIN]]
            else:
                piece = [row[a:], row[:SHIFT]]
            g_ref[pl.ds(tile_row(r, k, across), SEG), :] = jnp.concatenate(
                piece + [zero_rows(1)], axis=0
            )
    gain = gain_ref[layer, 1:2]
    bias = bias_ref[layer, 1:2]
    par = info_ref[0]
    biases = up_biases(layer, par, fb1b_ref, small_ref)
    n = hid_ref.shape[0] // 2

    def block(i, carry):
        at = rows_at(i, n)
        h = hid_ref[at, :]
        xhat, _ = norm_stats(h)
        n2 = (xhat * gain + bias).astype(BF)
        ups = [
            nn(n2, up_weight(p, layer, base, f1_ref, a_ref, b_ref)) + biases[p] for p in range(2)
        ]
        acts = []
        slopes = []
        for p in range(2):
            act, slope = gelu_pair(ups[p])
            acts.append(act)
            for z in range(2):
                act_ref[2 * p + z, at, :] = act[:, C * z : C * (z + 1)]
                slopes.append(slope[:, C * z : C * (z + 1)])
        down = nn(acts[0], down_weight(0, layer, base, f2_ref, a_ref, b_ref)) + nn(
            acts[1], down_weight(1, layer, base, f2_ref, a_ref, b_ref)
        )
        st_ref[at, :] = h + fb2_ref[layer : layer + 1] + down
        g = g_ref[at, :]
        df = g.astype(BF)
        df_ref[at, :] = df
        return mlp_back_rows(
            layer, base, at, g, df, h, lambda q: slopes[q], gain, bias, f1_ref, f2_ref,
            a_ref, b_ref, (gh_ref, n2_ref, du_ref), carry
        )

    mlp_sums(lax.fori_loop(0, 2, block, zero_sums()), fb1_ref, sh_ref)
    edge_ref[...] = edge_rows(st_ref, across, range(rows - SHIFT, rows))
    n2 = n2_ref[...]
    df = df_ref[...]
    for part in range(2):
        q = quarter_of(par, 1, part)
        send_ref[part, 0:C, :] = tn(n2, du_ref[q]).astype(BF)
        send_ref[part, C:, :] = tn(act_ref[q], df).astype(BF)


def mlp_keep_kernel(n2_ref, df_ref, du_ref, act_ref, got_ref, info_ref, own_ref, oth_ref):
    n2 = n2_ref[...]
    df = df_ref[...]
    for part, ref in ((1, oth_ref), (0, own_ref)):
        q = quarter_of(info_ref[0], 0, part)
        ref[0:C, :] = (tn(n2, du_ref[q]) + got_ref[part, 0:C, :].astype(F32)).astype(BF)
        ref[C:, :] = (tn(act_ref[q], df) + got_ref[part, C:, :].astype(F32)).astype(BF)


def up_keep_kernel(n2_ref, du_ref, got_ref, info_ref, own_ref, oth_ref):
    n2 = n2_ref[...]
    for part, ref in ((1, oth_ref), (0, own_ref)):
        q = quarter_of(info_ref[0], 0, part)
        ref[...] = (tn(n2, du_ref[q]) + got_ref[part].astype(F32)).astype(BF)


def down_grad_kernel(rows, across, *refs):
    (gin_ref, halo_ref, act0_ref, act1_ref, info_ref, g_ref, df_ref, keep_ref, send_ref) = refs

    def tile(r, k):
        if r >= 0:
            return gin_ref[pl.ds(tile_row(r, k, across), SEG), :]
        return edge_tile(halo, k, r + SHIFT)

    halo = halo_ref[...].astype(F32)
    shift_out(tile, g_ref, rows, across)
    df = g_ref[...].astype(BF)
    df_ref[...] = df
    for slot, ref in ((1, send_ref), (0, keep_ref)):
        ref[1] = tn(act1_ref[slot], df).astype(BF)
        ref[0] = tn(act0_ref[info_ref[0] ^ slot], df).astype(BF)


def mlp_bwd_kernel(base, *refs):
    (g_ref, df_ref, hid_ref, gp0_ref, gp1_ref, gain_ref, bias_ref) = refs[:7]
    (f1_ref, f2_ref, a_ref, b_ref, info_ref) = refs[7:12]
    (gh_ref, n2_ref, du_ref, send_ref, fb1_ref, sh_ref) = refs[12:]
    layer = 0
    gain = gain_ref[layer, 1:2]
    bias = bias_ref[layer, 1:2]
    n = hid_ref.shape[0] // 2

    def block(i, carry):
        at = rows_at(i, n)
        return mlp_back_rows(
            layer, base, at, g_ref[at, :], df_ref[at, :], hid_ref[at, :],
            lambda q: (gp0_ref if q < 2 else gp1_ref)[q % 2, at, :], gain, bias,
            f1_ref, f2_ref, a_ref, b_ref, (gh_ref, n2_ref, du_ref), carry
        )

    mlp_sums(lax.fori_loop(0, 2, block, zero_sums()), fb1_ref, sh_ref)
    n2 = n2_ref[...]
    for part in range(2):
        send_ref[part] = tn(n2, du_ref[quarter_of(info_ref[0], 1, part)]).astype(BF)


def window_grads(wins, gh_ref, da_ref):
    def four(i, s):
        g = gh_ref[rows_at(i, 4 * WROWS), :]
        for n in range(4):
            part = jnp.concatenate(
                [g[n * WROWS : (n + 1) * WROWS], zero_rows(WPAD - WROWS)], axis=0
            ).astype(BF)
            da_ref[rows_at(4 * i + n, WPAD), :] = part
            s = s + jnp.sum(part.astype(F32), 0, keepdims=True)
        return s

    return lax.fori_loop(0, wins // 4, four, jnp.zeros((1, C), F32))


def attend_backward(halves, wins, group, mask_ref):
    def body(i, carry):
        units = [(i * group + u, h) for u in range(group) for h in halves]
        first = []
        for w, (qkv_ref, p_ref, do_ref, dqkv_ref, _) in units:
            at = rows_at(w, WPAD)
            do = spread(do_ref[at, :], mask_ref[...])
            first.append(nt(qkv_ref[2, at, :], do))
            dqkv_ref[2, at, :] = nn(p_ref[w], do).astype(BF)
        second = []
        for (w, (_, p_ref, _, _, acc_ref)), dp in zip(units, first):
            p = p_ref[w].astype(F32)
            ds = p * (dp - jnp.sum(p * dp, 0, keepdims=True))
            for n in range(3):
                acc_ref[n] += ds[:, 128 * n : 128 * (n + 1)]
            second.append(ds.astype(BF))
        for (w, (qkv_ref, _, _, dqkv_ref, _)), ds in zip(units, second):
            at = rows_at(w, WPAD)
            dqkv_ref[1, at, :] = nn(ds, spread(qkv_ref[0, at, :], mask_ref[...])).astype(BF)
            dqkv_ref[0, at, :] = fold(tn(ds, qkv_ref[1, at, :])).astype(BF)
        return carry

    lax.fori_loop(0, wins // group, body, 0)


def half_grads(half, par, xn_ref, da_ref, mix_ref, dqkv_ref, row_ref, give):
    def put(value, at):
        if half == 0:
            row_ref[...] = value
            one = row_ref[pl.ds(pl.multiple_of(par * 96, 96), 96), :]
            two = row_ref[pl.ds(pl.multiple_of((1 - par) * 96, 96), 96), :]
        else:
            one, two = value[:96], value[96:]
        give(at, one.astype(BF), two.astype(BF))

    xn = xn_ref[...]
    for j in range(3):
        grad = tn(dqkv_ref[j], xn)
        put(grad * SCALE if j == 0 else grad, 96 * j)
    put(tn(mix_ref[...], da_ref[...]), 288)


def normed_grads(layer, wins, dqkvs, weights, gh_ref, x_ref, gain_ref, gx_ref):
    gain = gain_ref[layer, 0:1]
    n = 8

    def part(i, carry):
        sg, sb, sq = carry
        at = rows_at(i, n * WPAD)
        dn = nn(dqkvs[0][0, at, :], weights[0](0)) + nn(dqkvs[1][0, at, :], weights[1](0))
        dn = dn * SCALE
        for half in range(2):
            for j in (1, 2):
                dn = dn + nn(dqkvs[half][j, at, :], weights[half](j))
        new = []
        for half in range(2):
            for m, j in enumerate((0, 2)):
                new.append(
                    sq[half * 2 + m] + jnp.sum(dqkvs[half][j, at, :].astype(F32), 0, keepdims=True)
                )
        d = jnp.concatenate([dn[k * WPAD : k * WPAD + WROWS] for k in range(n)], axis=0)
        to = rows_at(i, n * WROWS)
        xhat, rinv = norm_stats(x_ref[to, :])
        sg = sg + jnp.sum(d * xhat, 0, keepdims=True)
        sb = sb + jnp.sum(d, 0, keepdims=True)
        gx_ref[to, :] = gh_ref[to, :] + norm_back(d, xhat, rinv, gain)
        return sg, sb, tuple(new)

    z = jnp.zeros((1, C), F32)
    zq = jnp.zeros((1, 6 * HD), F32)
    return lax.fori_loop(0, wins // n, part, (z, z, (zq,) * 4))


def small_rows(ref, z, sq, fb1, table, shared):
    ref[...] = jnp.zeros_like(ref)
    if shared is not None:
        sg, sb, projb, sh_ref = shared
        ref[0:1] = sg
        ref[1:2] = sb
        ref[2:3] = projb
        ref[3:6] = sh_ref[...]
    ref[6:7] = fb1
    ref[7:8, 0:96] = sq[0][:, 96 * z : 96 * (z + 1)] * SCALE
    ref[7:8, 128:224] = sq[1][:, 96 * z : 96 * (z + 1)]
    ref[8:24, 0:48] = table[:, 48 * z : 48 * (z + 1)]


def mixed_grad_kernel(wins, gh_ref, projw_ref, a_ref, b_ref, da_ref, do_ref, pb_ref):
    pb_ref[...] = window_grads(wins, gh_ref, da_ref)
    for half in range(2):
        do_ref[half] = nt(da_ref[...], proj_weight_of(half, 1, projw_ref, a_ref, b_ref)).astype(BF)


def attn_bwd_kernel(rows, across, *refs):
    (gh_ref, x_ref, xn_ref, gain_ref, qkvw_ref, a_ref, b_ref, info_ref) = refs[:8]
    (fb1_ref, sh_ref, qkv0_ref, p0_ref, mix0_ref, qkv1_ref, p1_ref, mix1_ref, pick_ref) = refs[8:17]
    (da_ref, do_ref, pb_ref) = refs[17:20]
    (gin_ref, keep_ref, send_ref, edge_ref) = refs[20:24]
    (dqkv0_ref, dqkv1_ref, acc_ref, mask_ref, row_ref, sm_ref) = refs[24:]
    layer = 1
    par = info_ref[0]
    wins = (rows // WIN) * across
    mask_ref[...] = head_mask()
    acc_ref[...] = jnp.zeros_like(acc_ref)
    projb = pb_ref[...]
    attend_backward(
        [
            (qkv0_ref, p0_ref, do_ref.at[0], dqkv0_ref, acc_ref.at[0]),
            (qkv1_ref, p1_ref, do_ref.at[1], dqkv1_ref, acc_ref.at[1]),
        ],
        wins,
        4,
        mask_ref,
    )
    for half, mix_ref, dqkv_ref in ((1, mix1_ref, dqkv1_ref), (0, mix0_ref, dqkv0_ref)):

        def give(at, one, two, half=half):
            keep_ref[half, at : at + 96, :] = one
            send_ref[half, at : at + 96, :] = two

        half_grads(half, par, xn_ref, da_ref, mix_ref, dqkv_ref, row_ref, give)
    weights = [
        lambda j, half=half: qkv_weight_of(half, j, layer, qkvw_ref, a_ref, b_ref)
        for half in range(2)
    ]
    sg, sb, sq = normed_grads(
        layer, wins, [dqkv0_ref, dqkv1_ref], weights, gh_ref, x_ref, gain_ref, gin_ref
    )
    edge_ref[...] = edge_rows(gin_ref, across, range(rows - SHIFT, rows))
    for half in range(2):
        table = map_to_table(acc_ref.at[half], pick_ref)
        for z in range(2):
            q = 2 * half + z
            small_rows(
                sm_ref.at[q], z, sq[2 * half : 2 * half + 2], fb1_ref[q : q + 1], table,
                (sg, sb, projb, sh_ref)
            )
    keep_ref[0, C:, :] = sm_ref[par].astype(BF)
    send_ref[0, C:, :] = sm_ref[1 - par].astype(BF)
    keep_ref[1, C:, :] = sm_ref[2].astype(BF)
    send_ref[1, C:, :] = sm_ref[3].astype(BF)


def column_sum(ref):
    return jnp.sum(ref[...].astype(F32), 0, keepdims=True)


def attn_bwd_other_kernel(rows, across, *refs):
    (gh_ref, xn_ref, projw_ref, a_ref, b_ref, fb1_ref, qkv_ref, p_ref, mix_ref, pick_ref) = refs[:10]
    (da_ref, do_ref, dqkv_ref, pb_ref, keep_ref, send_ref) = refs[10:16]
    (do1_ref, mask_ref, acc_ref, sm_ref) = refs[16:]
    wins = (rows // WIN) * across
    mask_ref[...] = head_mask()
    acc_ref[...] = jnp.zeros_like(acc_ref)
    pb_ref[...] = window_grads(wins, gh_ref, da_ref)
    da = da_ref[...]
    do1_ref[...] = nt(da, proj_weight_of(1, 0, projw_ref, a_ref, b_ref)).astype(BF)
    do_ref[...] = nt(da, proj_weight_of(0, 0, projw_ref, a_ref, b_ref)).astype(BF)
    attend_backward([(qkv_ref, p_ref, do1_ref, dqkv_ref, acc_ref)], wins, 8, mask_ref)

    def give(at, one, two):
        keep_ref[at : at + 96, :] = one
        send_ref[at : at + 96, :] = two

    half_grads(1, None, xn_ref, da_ref, mix_ref, dqkv_ref, None, give)
    table = map_to_table(acc_ref, pick_ref)
    sq = (column_sum(dqkv_ref.at[0]), column_sum(dqkv_ref.at[2]))
    for z, ref in ((0, keep_ref), (1, send_ref)):
        small_rows(sm_ref, z, sq, fb1_ref[2 + z : 3 + z], table, None)
        ref[C:, :] = sm_ref[...].astype(BF)


def attend_own_kernel(wins, qkv_ref, p_ref, do_ref, dqkv_ref, acc_ref, mask_ref):
    mask_ref[...] = head_mask()
    acc_ref[...] = jnp.zeros_like(acc_ref)
    attend_backward([(qkv_ref, p_ref, do_ref, dqkv_ref, acc_ref)], wins, 8, mask_ref)


def attn_bwd_own_kernel(rows, across, *refs):
    (gh_ref, x_ref, xn_ref, gain_ref, qkvw_ref, a_ref, b_ref, info_ref) = refs[:8]
    (fb1_ref, sh_ref, da_ref, dqkv_ref, acc_ref, dqkv1_ref, pb_ref, mix_ref, pick_ref) = refs[8:17]
    (out_ref, keep_ref, send_ref) = refs[17:20]
    (gx_ref, row_ref, sm_ref) = refs[20:]
    par = info_ref[0]
    wins = (rows // WIN) * across

    def give(at, one, two):
        keep_ref[at : at + 96, :] = one
        send_ref[at : at + 96, :] = two

    half_grads(0, par, xn_ref, da_ref, mix_ref, dqkv_ref, row_ref, give)
    weights = [
        lambda j, half=half: qkv_weight_of(half, j, 0, qkvw_ref, a_ref, b_ref)
        for half in range(2)
    ]
    sg, sb, sq = normed_grads(
        0, wins, [dqkv_ref, dqkv1_ref], weights, gh_ref, x_ref, gain_ref, gx_ref
    )
    table = map_to_table(acc_ref, pick_ref)
    for z in range(2):
        small_rows(
            sm_ref.at[z], z, sq[0:2], fb1_ref[z : z + 1], table, (sg, sb, pb_ref[...], sh_ref)
        )
    keep_ref[C:, :] = sm_ref[par].astype(BF)
    send_ref[C:, :] = sm_ref[1 - par].astype(BF)
    for r in range(rows):
        parts = [gx_ref[pl.ds(tile_row(r, k, across), SEG), :][:WIN] for k in range(across)]
        out_ref[r, :, 0, :] = jnp.concatenate(parts, axis=0)


def pair_kernel(keep_ref, got_ref, own_ref, oth_ref):
    own_ref[...] = (keep_ref[0].astype(F32) + got_ref[0].astype(F32)).astype(BF)
    oth_ref[...] = (keep_ref[1].astype(F32) + got_ref[1].astype(F32)).astype(BF)


def combine_kernel(parts, bit, n_in, *refs):
    ins = refs[:n_in]
    info_ref = refs[n_in]
    outs = refs[n_in + 1 :]
    at = 0
    for rows, terms, split in parts:

        def total(first, n):
            acc = None
            for i, base in terms:
                x = ins[i][pl.ds(base + first, n), :].astype(F32)
                acc = x if acc is None else acc + x
            return acc.astype(BF)

        if bit is None or not split:
            whole = total(0, rows)
            for out in outs:
                out[at : at + rows, :] = whole
            at += rows
        else:
            n = rows // 2
            b = (info_ref[2] >> bit) & 1
            outs[0][at : at + n, :] = total(pl.multiple_of(b * n, n), n)
            outs[1][at : at + n, :] = total(pl.multiple_of((1 - b) * n, n), n)
            at += n


def close_kernel(halves, bit, mine_ref, got_ref, info_ref, out_ref, small_ref):
    join_kernel(halves, bit, mine_ref.at[0 : sum(halves)], got_ref, info_ref, out_ref)
    at = sum(halves)
    rest = (mine_ref[at:, :].astype(F32) + got_ref[at:, :].astype(F32)).astype(BF)
    n = rest.shape[0] - SMALL
    out_ref[2 * at :, :] = rest[:n]
    small_ref[...] = rest[n:]


def join_kernel(halves, bit, mine_ref, got_ref, info_ref, out_ref):
    b = (info_ref[2] >> bit) & 1
    at = 0
    for n in halves:
        for ref, place in ((mine_ref, b), (got_ref, 1 - b)):
            to = pl.multiple_of(2 * at + place * n, 16)
            out_ref[pl.ds(to, n), :] = ref[at : at + n, :]
        at += n
    if at < mine_ref.shape[0]:
        out_ref[2 * at :, :] = mine_ref[at:, :]


def out_kernel(rows, across, st_ref, halo_ref, o_ref):
    halo = halo_ref[C + SMALL :, :].astype(F32)
    for r in range(rows):
        parts = []
        for k in range(across):
            if r >= SHIFT:
                t = st_ref[pl.ds(tile_row(r - SHIFT, k, across), SEG), :]
            else:
                t = edge_tile(halo, k, r)
            parts.append(t[:WIN])
        last = parts[-1]
        parts = [last[WIN - SHIFT :]] + parts[:-1] + [last[: WIN - SHIFT]]
        o_ref[r] = jnp.concatenate(parts, axis=0).astype(BF)


def place_of(i, info_ref):
    return info_ref[0] ^ (i // 2), ((info_ref[2] >> 1) & 1) ^ (i % 2)


def put_up(pieces, base, info_ref, ref):
    n = C // 2
    for i in range(4):
        core, half = place_of(i, info_ref)
        rows = pl.ds(pl.multiple_of(half * n, n), n)
        cols = pl.ds(pl.multiple_of(core * C, C), C)
        ref[rows, cols] = pieces[i][base : base + n, :].astype(F32)


def put_down(pieces, base, info_ref, ref):
    n = C // 2
    for i in range(4):
        core, half = place_of(i, info_ref)
        rows = pl.ds(pl.multiple_of(core * C + half * n, n), n)
        ref[rows, :] = pieces[i][base : base + n, :].astype(F32)


def put_attn(pieces, base, info_ref, asm_ref, qkv_ref, proj_ref):
    n = C // 2
    for i in range(4):
        core, half = place_of(i, info_ref)
        rows = pl.ds(pl.multiple_of(half * n, n), n)
        asm_ref[core, rows, :] = pieces[i][base : base + n, :].astype(F32)
    for core in range(2):
        to = pl.ds(96 * core, 96)
        for j in range(3):
            qkv_ref[j, to, :] = asm_ref[core, 96 * j : 96 * (j + 1), :]
        proj_ref[to, :] = asm_ref[core, 288:384, :]


def final_second_kernel(*refs):
    pieces = refs[:4]
    (info_ref, f1_ref, f2_ref, qkv_ref, proj_ref) = refs[4:9]
    (up_ref, down_ref, asm_ref, q_ref, p_ref, sems) = refs[9:]
    put_up(pieces, 0, info_ref, up_ref)
    put_down(pieces, C // 2, info_ref, down_ref)
    put_attn(pieces, C, info_ref, asm_ref, q_ref, p_ref)
    outs = [f1_ref, f2_ref, qkv_ref, proj_ref]
    for copy in copies_of([(x, y.at[1]) for x, y in zip((up_ref, down_ref, q_ref, p_ref), outs)], sems):
        copy.wait()


def final_mlp_kernel(*refs):
    pieces = refs[:4]
    (info_ref, _, _, f1_ref, f2_ref, up_ref, down_ref, sems) = refs[4:]
    put_up(pieces, 0, info_ref, up_ref)
    put_down(pieces, C // 2, info_ref, down_ref)
    for copy in copies_of([(up_ref, f1_ref.at[0]), (down_ref, f2_ref.at[0])], sems):
        copy.wait()


def final_kernel(*refs):
    attns, smalls = refs[:4], refs[4:6]
    (shared_ref, info_ref, _, _, qkv_ref, proj_ref) = refs[6:12]
    (gain_ref, bias_ref, pb_ref, fb2_ref, qvb_ref, fb1_ref, tab_ref) = refs[12:19]
    (asm_ref, q_ref, p_ref, sm_ref, sems) = refs[19:]
    put_attn(attns, 0, info_ref, asm_ref, q_ref, p_ref)
    copies = copies_of([(q_ref, qkv_ref.at[0]), (p_ref, proj_ref.at[0])], sems)
    n = C // 2
    par = info_ref[0]
    for layer in range(2):
        for i in range(2):
            x = smalls[i][...] if layer == 1 else attns[2 * i][n:, :]
            sm_ref[par ^ i] = x.astype(F32)
        x, y = sm_ref[0], sm_ref[1]
        shared = x[0:6]
        if layer == 0:
            shared = sm_ref[par, 0:6, :] + shared_ref[0:6].astype(F32)
        gain_ref[layer, 0:1] = shared[0:1]
        gain_ref[layer, 1:2] = shared[3:4]
        bias_ref[layer, 0:1] = shared[1:2]
        bias_ref[layer, 1:2] = shared[4:5]
        pb_ref[layer : layer + 1] = shared[2:3]
        fb2_ref[layer : layer + 1] = shared[5:6]
        fb1_ref[layer : layer + 1, 0:C] = x[6:7]
        fb1_ref[layer : layer + 1, C:] = y[6:7]
        for k in range(2):
            qvb_ref[layer, k : k + 1, 0:96] = x[7:8, 128 * k : 128 * k + 96]
            qvb_ref[layer, k : k + 1, 96:192] = y[7:8, 128 * k : 128 * k + 96]
        t = jnp.concatenate([x[8:24, 0:48], y[8:24, 0:48]], axis=1)
        wide = tn(t.astype(BF), offset_rows().astype(BF)) * offset_cols()
        for h in range(6):
            tab_ref[h, layer : layer + 1, :] = jnp.sum(
                wide[16 * h : 16 * (h + 1)], 0, keepdims=True
            )
    for copy in copies:
        copy.wait()


SMEM = pl.BlockSpec(memory_space=pltpu.SMEM)
VMEM = pl.BlockSpec(memory_space=pltpu.VMEM)
HBM = pl.BlockSpec(memory_space=pltpu.HBM)


def call(kernel, name, us, limit, operands, outs, scratch=(), aliases=None):
    args = []
    specs = []
    for op in operands:
        args.append(op[0] if isinstance(op, tuple) else op)
        specs.append(op[1] if isinstance(op, tuple) else VMEM)
    shapes = [jax.ShapeDtypeStruct(o[0], o[1]) for o in outs]
    return pl.pallas_call(
        kernel,
        name=name,
        in_specs=specs,
        out_specs=[o[2] if len(o) > 2 else VMEM for o in outs],
        input_output_aliases=aliases or {},
        out_shape=shapes,
        scratch_shapes=[s if not isinstance(s, tuple) else pltpu.VMEM(*s) for s in scratch],
        cost_estimate=pl.CostEstimate(
            flops=int(us * 1e10), bytes_accessed=1000000, transcendentals=0
        ),
        compiler_params=pltpu.CompilerParams(vmem_limit_bytes=limit * 2**20),
    )(*args)


def on_device(n_win, *args):
    (
        tokens,
        crop_ids,
        cotangent,
        norm_gain,
        norm_bias,
        qkv_weight,
        qv_bias,
        proj_weight,
        proj_bias,
        fc1_weight,
        fc1_bias,
        fc2_weight,
        fc2_bias,
        pos_table,
    ) = args
    rows, cols = tokens.shape[1:3]
    across = cols // WIN
    wins = (rows // WIN) * across
    ntok = wins * WROWS
    npad = wins * WPAD
    win = lax.axis_index("win")
    tp = lax.axis_index("tp")
    par = win % 2
    info = (jnp.stack([par, tp, win]).astype(jnp.int32), SMEM)
    bits = n_win.bit_length() - 1
    assert n_win == 1 << bits and bits >= 3

    def to_tp(x, name):
        with jax.named_scope(name + "_tp"):
            return lax.ppermute(x, "tp", [(0, 1), (1, 0)])

    def to_win(x, bit, name):
        if bit >= bits:
            return jnp.zeros_like(x)
        with jax.named_scope("%s_win%d" % (name, bit)):
            return lax.ppermute(x, "win", [(i, i ^ (1 << bit)) for i in range(n_win)])

    def after(x, *others):
        return lax.optimization_barrier((x,) + others)[0]

    def combine(parts, bit, ins, name):
        total = sum(rows // 2 if split and bit is not None else rows for rows, _, split in parts)
        outs = [((total, C), BF)] * (1 if bit is None else 2)
        return call(
            partial(combine_kernel, parts, bit, len(ins)), name, 1, 4, tuple(ins) + (info,), outs
        )

    def join(halves, bit, mine, got, name):
        return call(
            partial(join_kernel, halves, bit), name, 1, 4, (mine, got, info),
            [((mine.shape[0] + sum(halves), C), BF)],
        )[0]

    qkv_t = qkv_weight.transpose(0, 2, 3, 1)
    table = pos_table.transpose(2, 0, 1)
    na = C + SMALL
    n = C // 2
    edge_b = ((across * SHIFT * SEG, C), BF)
    a0q, small = call(
        pack_first_kernel,
        "pack_first",
        0.1,
        60,
        tuple((x, HBM) for x in (qkv_t, proj_weight, table, qv_bias, fc1_bias)) + (info,),
        [((C + 2 * SMALL_ROWS, C), BF), ((2, SMALL_ROWS, C), F32)],
        [
            (table.shape, F32),
            (qv_bias.shape, F32),
            (fc1_bias.shape, F32),
            pltpu.SemaphoreType.DMA((7,)),
        ],
    )
    a0 = to_tp(a0q, "a0")
    m0q, a1q, m1q = call(
        pack_kernel,
        "pack",
        0.1,
        60,
        tuple((x, HBM) for x in (qkv_t, proj_weight, fc1_weight, fc2_weight, cotangent[0]))
        + (after(small, a0q), info),
        [
            ((2 * C, C), BF),
            ((C + 2 * SMALL_ROWS, C), BF),
            ((2 * C + EDGE_ROWS, C), BF),
        ],
        [((SHIFT, cols, C), BF), pltpu.SemaphoreType.DMA((9,))],
    )
    m0 = to_tp(m0q, "m0")
    crops = crop_ids.transpose(2, 0, 1)
    label_outs = [((wins, 128), F32), ((wins, WPAD, 128), F32), ((3, WPAD, 128), F32)]
    lq0, lk0, pos0, pick = call(
        partial(prep_kernel, 0, rows, across),
        "prep_0",
        0.1,
        8,
        (crops, after(small, m0q), info),
        label_outs + [((WIN, 96, 6 * WPAD), BF)],
        [((128, 128), F32)],
    )
    tiles = (rows // WIN, across, WIN, SEG, C)
    mask = ((6 * WPAD, 6 * HD), BF)
    half_outs = [((3, npad, 192), BF), ((wins, WPAD, 6 * WPAD), BF), ((npad, 192), BF)]
    tok_f = ((ntok, C), F32)
    tok_b = ((ntok, C), BF)
    hid_b = ((4, ntok, C), BF)
    other_scratch = [mask, ((3, WPAD, 128), F32)]

    x0, xn0, part, qkv00, p00, mix00 = call(
        partial(attn_own_kernel, rows, across),
        "attn_own_0",
        0.1,
        8,
        (tokens[0], norm_gain, norm_bias, proj_bias, qv_bias, qkv_t, proj_weight, pos0, lq0, lk0),
        [tok_f, ((npad, C), BF), tok_f] + half_outs,
        [mask],
    )
    lq1, lk1, pos1 = call(
        partial(prep_kernel, 1, rows, across),
        "prep_1",
        0.1,
        8,
        (crops, after(small, part), info, pick),
        label_outs,
        [((128, 128), F32)],
    )
    a1 = to_tp(after(a1q, lq1), "a1")
    a0 = after(a0, lq1)
    a0s = to_win(a0, 0, "a0")
    hid0, qkv01, p01, mix01, small0 = call(
        partial(attn_other_kernel, rows, across),
        "attn_other_0",
        0.1,
        8,
        (part, xn0, a0, a0s, lq0, lk0, pick, info),
        [tok_f] + half_outs + [((SMALL_ROWS, C), F32)],
        other_scratch,
    )
    half_b = ((2, ntok, C), BF)
    st_own, n2f, act00, gp00 = call(
        mlp_own_kernel,
        "mlp_own_0",
        0.1,
        14,
        (hid0, norm_gain, norm_bias, fc1_bias, fc2_bias, fc1_weight, fc2_weight),
        [tok_f, tok_b, half_b, half_b],
    )
    m0 = after(m0, st_own)
    m0s = to_win(m0, 0, "m0")
    st0, act01, gp01, edge = call(
        partial(mlp_other_kernel, across),
        "mlp_other_0",
        3,
        14,
        (st_own, n2f, fc1_bias, small0, m0, m0s, info),
        [tok_f, half_b, half_b, edge_b],
    )
    halo = to_tp(edge, "edge0")
    a1 = after(a1, halo)
    a1s = to_win(a1, 0, "a1")
    m1 = to_tp(after(m1q, edge), "m1")
    x1, xn1, qkv10 = call(
        partial(norm_kernel, rows, across),
        "norm_1",
        2,
        6,
        (st0, halo, norm_gain, norm_bias, qv_bias, qkv_t),
        [tok_f, ((npad, C), BF), half_outs[0]],
    )
    p10, mix10, qkv11, p11, mix11, small1 = call(
        partial(attn_both_kernel, rows, across),
        "attn_fwd_1",
        10,
        9,
        (xn1, qkv10, pos1, a1, a1s, lq1, lk1, pick, info),
        half_outs[1:] + half_outs + [((SMALL_ROWS, C), F32)],
        other_scratch,
    )
    m1 = after(m1, mix11)
    m1s = to_win(m1, 0, "m1")
    (hid1,) = call(
        partial(branch_kernel, wins),
        "branch_1",
        1,
        8,
        (x1, after(mix10, m1), mix11, proj_weight, a1, a1s, proj_bias),
        [tok_f],
    )
    sums = [((4, C), F32), ((3, C), F32)]
    st1, gh1, df1, n21, du1, act1, send_m1, gfb1, gsh1, out_edge = call(
        partial(mlp_both_kernel, rows, across, 0),
        "mlp_both_1",
        10,
        16,
        (cotangent[0], hid1, norm_gain, norm_bias, fc1_bias, small1, fc2_bias)
        + (fc1_weight, fc2_weight, m1, m1s, info),
        [tok_f, tok_f, tok_b, tok_b, hid_b, hid_b, ((2, 2 * C, C), BF)] + sums + [edge_b],
        [tok_f],
    )

    def plus(x, y, name):
        return combine([(x.shape[0], [(0, 0), (1, 0)], True)], None, (x, y), name)[0]

    def pair(keep, got, name):
        shape = keep.shape[1:]
        return call(pair_kernel, name, 1, 4, (keep, got), [(shape, BF), (shape, BF)])

    m1_core = to_win(send_m1, 0, "gm1")
    da1, do1, pb1 = call(
        partial(mixed_grad_kernel, wins),
        "mixed_grad_1",
        2,
        4,
        (gh1, proj_weight, a1, a1s),
        [((npad, C), BF), ((2, npad, 192), BF), ((1, C), F32)],
    )
    m1_own, m1_oth = call(
        mlp_keep_kernel,
        "mlp_keep_1",
        2,
        6,
        (n21, df1, du1, act1, after(m1_core, da1), info),
        [((2 * C, C), BF)] * 2,
    )
    m1_t = to_tp(m1_oth, "gm1")
    gin1, keep_a1, send_a1, edge = call(
        partial(attn_bwd_kernel, rows, across),
        "attn_bwd_1",
        14,
        10,
        (after(gh1, m1_oth), x1, xn1, norm_gain, qkv_t, a1, a1s, info)
        + (gfb1, gsh1, qkv10, p10, mix10, qkv11, p11, mix11, pick, da1, do1, pb1),
        [tok_f, ((2, na, C), BF), ((2, na, C), BF), edge_b],
        [
            ((3, npad, 192), BF),
            ((3, npad, 192), BF),
            ((2, 3, WPAD, 128), F32),
            mask,
            ((192, C), F32),
            ((4, SMALL, C), F32),
        ],
    )
    halo = to_tp(edge, "edge1")
    a1_core = to_win(after(send_a1, edge), 0, "ga1")
    m1_mine, m1_away = combine(
        [(C, [(0, 0), (1, 0)], True), (C, [(0, C), (1, C)], True)],
        1,
        (m1_own, after(m1_t, edge)),
        "m1_y",
    )
    m1_y = to_win(m1_away, 1, "gm1")
    a1_own, a1_oth = pair(keep_a1, after(a1_core, m1_away), "pair_a1")
    a1_t = to_tp(a1_oth, "ga1")
    g0, df0, keep_f2, send_f2 = call(
        partial(down_grad_kernel, rows, across),
        "down_grad_0",
        4,
        6,
        (gin1, after(halo, a1_oth), act00, act01, info),
        [tok_f, tok_b, ((2, C, C), BF), ((2, C, C), BF)],
    )
    f2_core = to_win(send_f2, 0, "gf2")
    m1_mine, m1_away = combine(
        [(n, [(0, 0), (1, 0)], True), (n, [(0, n), (1, n)], True)],
        2,
        (m1_mine, after(m1_y, send_f2)),
        "m1_z",
    )
    m1_z = to_win(m1_away, 2, "gm1")
    f2_own, f2_oth = pair(keep_f2, after(f2_core, m1_away), "pair_f2")
    f2_t = to_tp(f2_oth, "gf2")
    a1_mine, a1_away = combine(
        [(C, [(0, 0), (1, 0)], True), (SMALL, [(0, C), (1, C)], False)],
        1,
        (a1_own, after(a1_t, f2_oth)),
        "a1_y",
    )
    a1_y = to_win(a1_away, 1, "ga1")
    gh0, n20, du0, send_f1, gfb0, gsh0 = call(
        partial(mlp_bwd_kernel, 0),
        "mlp_bwd_0",
        6,
        12,
        (after(g0, a1_away), df0, hid0, gp00, gp01, norm_gain, norm_bias, fc1_weight, fc2_weight)
        + (m0, m0s, info),
        [tok_f, tok_b, hid_b, ((2, C, C), BF)] + sums,
    )
    f1_core = to_win(send_f1, 0, "gf1")
    (c1,) = combine(
        [(n, [(0, 0), (1, 0)], True), (n + SMALL, [(2, 0), (3, 0)], True)],
        None,
        (m1_mine, after(m1_z, send_f1), a1_mine, after(a1_y, send_f1)),
        "c1",
    )
    c1_b = to_win(c1, 3, "gc1")
    f1_own, f1_oth = call(
        up_keep_kernel, "up_keep_0", 1, 8, (n20, du0, after(f1_core, c1), info),
        [((C, C), BF)] * 2,
    )
    f1_t = to_tp(f1_oth, "gf1")
    da, do, dqkv1, pb0, keep_o0, send_o0 = call(
        partial(attn_bwd_other_kernel, rows, across),
        "attn_bwd_other_0",
        6,
        8,
        (after(gh0, f1_oth, f2_t), xn0, proj_weight, a0, a0s, gfb0, qkv01, p01, mix01, pick),
        [
            ((npad, C), BF),
            ((npad, 192), BF),
            ((3, npad, 192), BF),
            ((1, C), F32),
            ((na, C), BF),
            ((na, C), BF),
        ],
        [((npad, 192), BF), mask, ((3, WPAD, 128), F32), ((SMALL, C), F32)],
    )
    o0_core = to_win(send_o0, 0, "go0")
    m0_mine, m0_away = combine(
        [(C, [(0, 0), (1, 0)], True), (C, [(2, 0), (3, 0)], True)],
        1,
        (f1_own, after(f1_t, send_o0), f2_own, f2_t),
        "m0_y",
    )
    m0_y = to_win(m0_away, 1, "gm0")
    (o0_sum,) = combine(
        [(na, [(0, 0), (1, 0)], True), (edge_b[0][0], [(2, 0)], True)],
        None,
        (keep_o0, after(o0_core, m0_away), out_edge),
        "o0",
    )
    o0_t = to_tp(o0_sum, "go0")
    dqkv0, acc0 = call(
        partial(attend_own_kernel, wins),
        "attend_own_0",
        0.1,
        8,
        (qkv00, p00, after(do, o0_sum)),
        [half_outs[0], ((3, WPAD, 128), F32)],
        [mask],
    )
    c1 = plus(c1, after(c1_b, dqkv0), "c1_sum")
    for bit in range(4, bits):
        c1 = plus(c1, to_win(c1, bit, "gc1"), "c1_sum")
    c1_b = to_win(c1, 2, "gc1")
    grad_tokens, keep_a0, send_a0 = call(
        partial(attn_bwd_own_kernel, rows, across),
        "attn_bwd_own_0",
        9,
        10,
        (gh0, x0, xn0, norm_gain, qkv_t, a0, a0s, info)
        + (gfb0, gsh0, da, dqkv0, acc0, dqkv1, pb0, after(mix00, c1), pick),
        [((rows, cols, 1, C), F32), ((na, C), BF), ((na, C), BF)],
        [tok_f, ((192, C), F32), ((2, SMALL, C), F32)],
    )

    a0_core = to_win(send_a0, 0, "ga0")
    m0_mine, m0_away = combine(
        [(n, [(0, 0), (1, 0)], True), (n, [(0, n), (1, n)], True)],
        2,
        (m0_mine, after(m0_y, send_a0)),
        "m0_z",
    )
    m0_z = to_win(m0_away, 2, "gm0")
    a0_mine, a0_away = combine(
        [(C, [(0, 0), (1, 0), (2, 0)], True), (SMALL, [(0, C), (1, C), (2, C)], False)],
        1,
        (keep_a0, after(a0_core, m0_away), o0_t),
        "a0_y",
    )
    a0_y = to_win(a0_away, 1, "ga0")
    c1, c1_small = call(
        partial(close_kernel, [n // 2] * 2, 2), "c1_close", 1, 8, (c1, after(c1_b, a0_away), info),
        [((3 * n, C), BF), ((SMALL, C), BF)],
    )
    c1_back = to_win(c1, 1, "gc1_back")
    c1_sib = to_win(c1, 0, "gc1_mine")
    c1_small_sib = to_win(c1_small, 0, "gc1_small")
    m0 = plus(m0_mine, after(m0_z, c1), "m0_z2")
    m0_b = to_win(m0, 3, "gm0")
    (layer_out,) = call(
        partial(out_kernel, rows, across), "layer_out", 1, 8, (after(st1, m0), o0_t),
        [((rows, cols, C), BF)],
    )
    a0 = plus(a0_mine, after(a0_y, layer_out), "a0_z")
    a0_z = to_win(a0, 2, "ga0")
    m0 = plus(m0, after(m0_b, a0), "m0_sum")
    for bit in range(4, bits):
        m0 = plus(m0, to_win(m0, bit, "gm0"), "m0_sum")
    m0_b = to_win(m0, 2, "gm0_back")
    a0 = plus(a0, after(a0_z, m0), "a0_z2")
    a0_b = to_win(a0, 3, "ga0")
    c1_back = after(c1_back, a0)
    c1_pieces = (c1, c1_back, c1_sib, to_win(c1_back, 0, "gc1_theirs"))
    m0 = join([n // 2] * 2, 2, m0, after(m0_b, c1_back), "m0_join")
    m0_back = to_win(m0, 1, "gm0_back")
    m0_sib = to_win(m0, 0, "gm0_mine")
    c1_small_sib, c1_pieces = after((c1_small_sib, c1_pieces), m0)
    f1_shape, f2_shape = (2, C, 2 * C), (2, 2 * C, C)
    qkv_shape, proj_shape = (2, 3, 192, C), (2, 192, C)
    whole = [(f1_shape, F32, HBM), (f2_shape, F32, HBM), (qkv_shape, F32, HBM), (proj_shape, F32, HBM)]
    parts = [(x[0][1:], F32) for x in whole]
    attn_parts = [((2, C, C), F32)] + parts[2:]
    g_f1, g_f2, g_qkv, g_proj = call(
        final_second_kernel, "final_second", 1, 20, c1_pieces + (info,), whole,
        parts[:2] + attn_parts + [pltpu.SemaphoreType.DMA((4,))],
    )
    a0 = plus(a0, after(a0_b, g_f1), "a0_sum")
    for bit in range(4, bits):
        a0 = plus(a0, to_win(a0, bit, "ga0"), "a0_sum")
    a0_back = to_win(a0, 1, "ga0_back")
    a0_sib = to_win(a0, 0, "ga0_mine")
    shared = to_tp(a0[n : n + 16], "shared")
    m0_back = after(m0_back, a0_sib, shared)
    m0_pieces = (m0, m0_back, m0_sib, to_win(m0_back, 0, "gm0_theirs"))
    g_f1, g_f2 = call(
        final_mlp_kernel, "final_mlp", 0.1, 20,
        after(m0_pieces, shared) + (info, (g_f1, HBM), (g_f2, HBM)), whole[:2],
        parts[:2] + [pltpu.SemaphoreType.DMA((2,))],
        aliases={5: 0, 6: 1},
    )
    outs = call(
        final_kernel,
        "final",
        0.1,
        16,
        (a0, a0_back, a0_sib, to_win(a0_back, 0, "ga0_theirs"), c1_small, c1_small_sib)
        + (shared, info, (g_qkv, HBM), (g_proj, HBM)),
        whole[2:]
        + [
            ((2, 2, C), F32),
            ((2, 2, C), F32),
            ((2, C), F32),
            ((2, C), F32),
            ((2, 2, 192), F32),
            ((2, 2 * C), F32),
            ((6, 2, 169), F32),
        ],
        attn_parts + [((2, SMALL, C), F32), pltpu.SemaphoreType.DMA((2,))],
        aliases={8: 0, 9: 1},
    )
    (g_qkv, g_proj, g_gain, g_bias, g_pb, g_fb2, g_qvb, g_fb1, g_tab) = outs
    return (
        layer_out[None],
        grad_tokens.transpose(2, 0, 1, 3),
        g_gain,
        g_bias,
        g_qkv.transpose(0, 3, 1, 2),
        g_qvb,
        g_proj,
        g_pb,
        g_f1,
        g_fb1,
        g_f2,
        g_fb2,
        g_tab.transpose(1, 2, 0),
    )


def solution(mesh):
    return jax.shard_map(
        partial(on_device, mesh.shape["win"]),
        mesh=mesh,
        in_specs=(
            P("win", "tp", None, None),
            P("win", None, None),
            P("win", "tp", None, None),
            P(),
            P(),
            P(None, None, None, "tp"),
            P(None, None, "tp"),
            P(None, "tp", None),
            P(),
            P(None, None, "tp"),
            P(None, "tp"),
            P(None, "tp", None),
            P(),
            P(None, None, "tp"),
        ),
        out_specs=(
            P("win", "tp", None, None),
            P("win", "tp", None, None),
            P(),
            P(),
            P(None, None, None, "tp"),
            P(None, None, "tp"),
            P(None, "tp", None),
            P(),
            P(None, None, "tp"),
            P(None, "tp"),
            P(None, "tp", None),
            P(),
            P(None, None, "tp"),
        ),
        check_vma=False,
    )
```

```python
from functools import partial

import jax
import jax.numpy as jnp
import numpy as np
from jax import lax
from jax.experimental import pallas as pl
from jax.experimental.pallas import tpu as pltpu
from jax.sharding import PartitionSpec as P

C = 384
WIN = 7
SHIFT = 3
HD = 32
EPS = 1e-05
NEG = -1000000000.0
SCALE = HD**-0.5
F32 = jnp.float32
BF = jnp.bfloat16
SEG = 8
WROWS = WIN * SEG
WPAD = 64


def nn(a, b):
    return lax.dot_general(a, b, (((1,), (0,)), ((), ())), preferred_element_type=F32)


def nt(a, b):
    return lax.dot_general(a, b, (((1,), (1,)), ((), ())), preferred_element_type=F32)


def tn(a, b):
    return lax.dot_general(a, b, (((0,), (0,)), ((), ())), preferred_element_type=F32)


def norm_stats(x):
    mean = jnp.mean(x, -1, keepdims=True)
    cent = x - mean
    var = jnp.mean(cent * cent, -1, keepdims=True)
    rinv = lax.rsqrt(var + EPS)
    return cent * rinv, rinv


def norm_back(dz, xhat, rinv, gain):
    d = dz * gain
    return rinv * (
        d - jnp.mean(d, -1, keepdims=True) - xhat * jnp.mean(d * xhat, -1, keepdims=True)
    )


def tile_row(r, k, across):
    return (((r // WIN) * across + k) * WIN + r % WIN) * SEG


def zero_rows(n):
    return jnp.zeros((n, C), F32)


def head_mask():
    row = lax.broadcasted_iota(jnp.int32, (6 * WPAD, 6 * HD), 0) // WPAD
    col = lax.broadcasted_iota(jnp.int32, (6 * WPAD, 6 * HD), 1) // HD
    return (row == col).astype(BF)


def spread(x, mask):
    return jnp.concatenate([x] * 6, axis=0) * mask


def fold(o):
    lane = lax.broadcasted_iota(jnp.int32, (WPAD, 128), 1)

    def of(h, a, b):
        return o[WPAD * h : WPAD * (h + 1), a:b]

    one = jnp.where(lane < 96, of(2, 0, 128), of(3, 0, 128))
    one = jnp.where(lane < 64, of(1, 0, 128), one)
    one = jnp.where(lane < 32, of(0, 0, 128), one)
    two = jnp.where(lane[:, :64] < 32, of(4, 128, 192), of(5, 128, 192))
    return jnp.concatenate([one, two], axis=1)


def rows_at(i, n):
    return pl.ds(i * n, n)


def repeat(n, body, carry):
    for i in range(n):
        carry = body(i, carry)
    return carry


def iota(shape, dim):
    return lax.broadcasted_iota(jnp.int32, shape, dim)


def exact(a, b, ca, cb):
    return lax.dot_general(
        a,
        b,
        (((ca,), (cb,)), ((), ())),
        precision=lax.Precision.HIGHEST,
        preferred_element_type=F32,
    )


def offset_rows():
    return (12 - iota((16, 169), 0) == iota((16, 169), 1) // 13).astype(F32)


def offset_cols():
    return (iota((96, 169), 0) % 16 == iota((96, 169), 1) % 13).astype(F32)


def column_pick(kx):
    r = iota((96, 6 * WPAD), 0)
    c = iota((96, 6 * WPAD), 1)
    qx = c % 8
    return ((r // 16 == c // WPAD) & (r % 16 == qx - kx + WIN - 1) & (qx < WIN)).astype(BF)


def table_to_map(t, pick_ref, pos_ref):
    pos_ref[...] = jnp.zeros_like(pos_ref)
    group = (iota((8, 6 * WPAD), 1) % WPAD) // 8
    high = t.astype(BF)
    low = (t - high.astype(F32)).astype(BF)
    both = jnp.concatenate([high, low], axis=0)
    for kx in range(WIN):
        h = nn(both, pick_ref[kx])
        h = h[:16] + h[16:]
        g = jnp.zeros((8, 6 * WPAD), F32)
        for j in range(WIN):
            g = jnp.where(group == j, h[6 - j : 14 - j], g)
        for i in range(3):
            pos_ref[i, pl.ds(kx, 8, stride=8), :] = g[:, 128 * i : 128 * (i + 1)]


def map_to_table(pos_ref, pick_ref):
    group = (iota((16, 6 * WPAD), 1) % WPAD) // 8
    total = jnp.zeros((16, 96), F32)
    for kx in range(WIN):
        r = jnp.concatenate([pos_ref[i, pl.ds(kx, 8, stride=8), :] for i in range(3)], axis=1)
        h = jnp.zeros((16, 6 * WPAD), F32)
        for j in range(WIN):
            parts = [r, jnp.zeros((2 + j, 6 * WPAD), F32)]
            if j < 6:
                parts = [jnp.zeros((6 - j, 6 * WPAD), F32)] + parts
            h = jnp.where(group == j, jnp.concatenate(parts, axis=0), h)
        total = total + nt(h.astype(BF), pick_ref[kx])
    return total


def shift_in(tile, x_ref, rows, across):
    for r in range(rows):
        for k in range(across):
            a = tile(r + SHIFT, k)
            b = tile(r + SHIFT, (k + 1) % across)
            x_ref[pl.ds(tile_row(r, k, across), SEG), :] = jnp.concatenate(
                [a[SHIFT:WIN], b[:SHIFT], zero_rows(1)], axis=0
            )


def shift_out(tile, x_ref, rows, across):
    for r in range(rows):
        for k in range(across):
            a = tile(r - SHIFT, (k - 1) % across)
            b = tile(r - SHIFT, k)
            x_ref[pl.ds(tile_row(r, k, across), SEG), :] = jnp.concatenate(
                [a[WIN - SHIFT : WIN], b[: WIN - SHIFT], zero_rows(1)], axis=0
            )

EDGE_ROWS = 96
SMALL = 32


SMALL_ROWS = 24
SENT_ROWS = 8


def copies_of(pairs, sems):
    copies = [pltpu.make_async_copy(x, y, sems.at[n]) for n, (x, y) in enumerate(pairs)]
    for copy in copies:
        copy.start()
    return copies


def attn_copies(layer, par, qkvw_ref, projw_ref, a_ref):
    of_heads = pl.ds(pl.multiple_of(par * 96, 96), 96)
    pairs = [
        (qkvw_ref.at[layer, j, of_heads, :], a_ref.at[pl.ds(96 * j, 96), :]) for j in range(3)
    ]
    return pairs + [(projw_ref.at[layer, of_heads, :], a_ref.at[pl.ds(288, 96), :])]


def mlp_copies(layer, par, f1_ref, f2_ref, m_ref):
    of_units = pl.ds(pl.multiple_of(par * C, C), C)
    return [
        (f1_ref.at[layer, :, of_units], m_ref.at[pl.ds(0, C), :]),
        (f2_ref.at[layer, of_units, :], m_ref.at[pl.ds(C, C), :]),
    ]


def high_low(x):
    rows = []
    for r in range(4):
        rows.append(jnp.concatenate([x[4 * r + k : 4 * r + k + 1, 0:96] for k in range(4)], axis=1))
    rows.append(x[16:18])
    rows.append(jnp.concatenate([x[18:19, 0:192], x[19:20, 0:192]], axis=1))
    rows.append(zero_rows(1))
    x = jnp.concatenate(rows, axis=0)
    high = x.astype(BF).astype(F32)
    return jnp.concatenate([high, x - high], axis=0).astype(BF)


def pack_first_kernel(
    qkvw_ref, projw_ref, tab_ref, qvb_ref, fb1_ref,
    a0_ref, small_ref, tab_v, qvb_v, fb1_v, sems
):
    pairs = [(tab_ref, tab_v), (qvb_ref, qvb_v), (fb1_ref, fb1_v)]
    copies = copies_of(pairs + attn_copies(0, lax.rem(lax.axis_index("win"), 2), qkvw_ref, projw_ref, a0_ref), sems)
    small_ref[...] = jnp.zeros_like(small_ref)
    for copy in copies[:3]:
        copy.wait()
    for layer in range(2):
        tab = tab_v[:, layer, :]
        wide = jnp.concatenate([jnp.broadcast_to(tab[h : h + 1], (16, 169)) for h in range(6)])
        small_ref[layer, 0:16, 0:96] = exact(offset_rows(), wide * offset_cols(), 1, 1)
        small_ref[layer, 16:17, :] = fb1_v[layer : layer + 1, 0:C]
        small_ref[layer, 17:18, :] = fb1_v[layer : layer + 1, C:]
        small_ref[layer, 18:20, 0:192] = qvb_v[layer]
    a0_ref[C:, :] = high_low(small_ref[0])
    for copy in copies[3:]:
        copy.wait()


def pack_kernel(
    qkvw_ref, projw_ref, f1_ref, f2_ref, cot_ref, small_ref, info_ref,
    m0_ref, a1_ref, m1_ref, edge_ref, cot_v, sems
):
    par = info_ref[0]
    pairs = [(cot_ref.at[pl.ds(0, SHIFT)], cot_v)]
    pairs += mlp_copies(0, par, f1_ref, f2_ref, m0_ref)
    pairs += attn_copies(1, par, qkvw_ref, projw_ref, a1_ref)
    pairs += mlp_copies(1, par, f1_ref, f2_ref, m1_ref)
    copies = copies_of(pairs, sems)
    a1_ref[C:, :] = high_low(small_ref[1])
    copies[0].wait()
    edge = [cot_v[r].astype(F32) for r in range(SHIFT)]
    n = EDGE_ROWS - SHIFT * cot_v.shape[1]
    edge_ref[...] = jnp.concatenate(edge + [zero_rows(n)], axis=0).astype(BF)
    for copy in copies[1:]:
        copy.wait()


def small_of(a_ref, small_ref):
    rows = a_ref[C : C + 2 * SENT_ROWS, :].astype(F32)
    x = rows[0:SENT_ROWS] + rows[SENT_ROWS:]
    small_ref[...] = jnp.zeros_like(small_ref)
    for r in range(4):
        for k in range(4):
            small_ref[4 * r + k : 4 * r + k + 1, 0:96] = x[r : r + 1, 96 * k : 96 * (k + 1)]
    small_ref[16:18, :] = x[4:6]
    small_ref[18:19, 0:192] = x[6:7, 0:192]
    small_ref[19:20, 0:192] = x[6:7, 192:384]


def edge_tile(edge, k, r):
    at = (k * SHIFT + r) * SEG
    return edge[at : at + SEG]


def edge_rows(ref, across, rows):
    tiles = [ref[pl.ds(tile_row(r, k, across), SEG), :] for k in range(across) for r in rows]
    return jnp.concatenate(tiles, axis=0).astype(BF)


def prep_kernel(layer, rows, across, *refs):
    (crop_ref, small_ref, info_ref) = refs[:3]
    if layer == 0:
        (lq_ref, lk_ref, pos_ref, pick_ref, c_ref) = refs[3:]
        for kx in range(WIN):
            pick_ref[kx] = column_pick(kx)
    else:
        (pick_ref, lq_ref, lk_ref, pos_ref, c_ref) = refs[3:]
    tp = info_ref[1]
    cols = across * WIN
    height = crop_ref.shape[2]
    table_to_map(small_ref[layer, 0:16, 0:96], pick_ref, pos_ref)
    c_ref[...] = jnp.zeros_like(c_ref)
    c_ref[0:cols, 0:height] = crop_ref[:, 0, :].astype(F32)
    crops = c_ref[...].astype(BF)
    row = iota((32, 128), 0)
    lane = iota((32, 128), 1)
    shift = SHIFT if layer == 1 else 0
    src = rows * tp + row + shift
    src = jnp.where(src >= height, src - height, src)
    grid = nt((src == lane).astype(BF), crops).astype(BF)
    labs = []
    for wc in range(across):
        qx = iota((128, 128), 1) % 8
        col = qx + (WIN * wc + shift)
        col = jnp.where(col >= cols, col - cols, col)
        pick = ((col == iota((128, 128), 0)) & (qx < WIN)).astype(BF)
        lab = nn(grid, pick)
        if layer == 1:
            g = rows * tp + row
            zr = (g >= height - WIN).astype(F32) + (g >= height - SHIFT).astype(F32)
            here = lane % 8 + WIN * wc
            zc = (here >= cols - WIN).astype(F32) + (here >= cols - SHIFT).astype(F32)
            lab = lab * 9.0 + zr * 3.0 + zc
        labs.append(lab)
    real = (iota((1, 128), 1) % 8 < WIN) & (iota((1, 128), 1) % WPAD < WROWS)
    for wr in range(rows // WIN):
        lines = []
        for wc in range(across):
            w = wr * across + wc
            mine = row == (lane % WPAD) // 8 + WIN * wr
            line = jnp.sum(jnp.where(mine, labs[wc], 0.0), 0, keepdims=True)
            line = jnp.where(real, line, -1.0)
            lq_ref[w : w + 1, :] = line
            lines.append(line)
        for wc in range(0, across, 2):
            w = wr * across + wc
            both = jnp.where(iota((1, 128), 1) < WPAD, lines[wc], lines[wc + 1])
            both = jnp.broadcast_to(both, (128, 128)).T
            lk_ref[w] = both[:WPAD]
            lk_ref[w + 1] = both[WPAD:]


def qkv_weight_of(half, j, layer, qkvw_ref, a_ref, b_ref):
    if half == 0:
        return qkvw_ref[layer, j]
    return jnp.concatenate([a_ref[96 * j : 96 * (j + 1)], b_ref[96 * j : 96 * (j + 1)]], axis=0)


def proj_weight_of(half, layer, projw_ref, a_ref, b_ref):
    if half == 0:
        return projw_ref[layer]
    return jnp.concatenate([a_ref[288:384], b_ref[288:384]], axis=0)


def norm_windows(layer, wins, x_ref, xn_ref, gain_ref, bias_ref):
    gain = gain_ref[layer, 0:1]
    bias = bias_ref[layer, 0:1]

    def four(i, carry):
        xhat, _ = norm_stats(x_ref[rows_at(i, 4 * WROWS), :])
        xn = xhat * gain + bias
        for n in range(4):
            part = jnp.concatenate(
                [xn[n * WROWS : (n + 1) * WROWS], zero_rows(WPAD - WROWS)], axis=0
            )
            xn_ref[rows_at(4 * i + n, WPAD), :] = part.astype(BF)
        return carry

    repeat(wins // 4, four, 0)


def project_half(xn_ref, qkv_ref, weight, qb, vb):
    n = xn_ref.shape[0]

    def part(i, carry):
        at = rows_at(i, n)
        xn = xn_ref[at, :]
        q = nt(xn, weight(0))
        k = nt(xn, weight(1))
        v = nt(xn, weight(2))
        qkv_ref[0, at, :] = ((q + qb) * SCALE).astype(BF)
        qkv_ref[1, at, :] = k.astype(BF)
        qkv_ref[2, at, :] = (v + vb).astype(BF)
        return carry

    repeat(1, part, 0)


def attend_forward(halves, wins, group, lq_ref, lk_ref, mask_ref):
    def body(i, carry):
        units = [(i * group + u, h) for u in range(group) for h in halves]
        scores = []
        for w, (qkv_ref, _, _, _) in units:
            at = rows_at(w, WPAD)
            scores.append(nt(qkv_ref[1, at, :], spread(qkv_ref[0, at, :], mask_ref[...])))
        probs = []
        for (w, (_, pos, p_ref, _)), s in zip(units, scores):
            same = lk_ref[w] == lq_ref[pl.ds(w, 1), :]
            same = jnp.concatenate([same] * 3, axis=1)
            s = jnp.where(same, s + jnp.concatenate([pos[n] for n in range(3)], axis=1), NEG)
            e = jnp.exp(s - jnp.max(s, 0, keepdims=True))
            p = (e * (1.0 / jnp.sum(e, 0, keepdims=True))).astype(BF)
            p_ref[w] = p
            probs.append(p)
        for (w, (qkv_ref, _, _, mix_ref)), p in zip(units, probs):
            at = rows_at(w, WPAD)
            mix_ref[at, :] = fold(tn(p, qkv_ref[2, at, :])).astype(BF)
        return carry

    repeat(wins // group, body, 0)


def add_branch(wins, mixes, weights, bias, x_ref, hid_ref):
    n = 8

    def part(i, carry):
        res = bias
        for m_ref, w in zip(mixes, weights):
            res = res + nn(m_ref[rows_at(i, n * WPAD), :], w)
        for k in range(n):
            to = rows_at(i * n + k, WROWS)
            hid_ref[to, :] = x_ref[to, :] + res[k * WPAD : k * WPAD + WROWS]
        return carry

    repeat(wins // n, part, 0)


def attn_own_kernel(rows, across, *refs):
    (tok_ref, gain_ref, bias_ref, pb_ref, qvb_ref, qkvw_ref, projw_ref) = refs[:7]
    (pos_ref, lq_ref, lk_ref) = refs[7:10]
    (x_ref, xn_ref, hid_ref, qkv_ref, p_ref, mix_ref, mask_ref) = refs[10:]
    wins = (rows // WIN) * across
    for r in range(rows):
        row = tok_ref[r].astype(F32)
        for k in range(across):
            x_ref[pl.ds(tile_row(r, k, across), SEG), :] = jnp.concatenate(
                [row[WIN * k : WIN * (k + 1)], zero_rows(1)], axis=0
            )
    mask_ref[...] = head_mask()
    norm_windows(0, wins, x_ref, xn_ref, gain_ref, bias_ref)
    project_half(
        xn_ref, qkv_ref, lambda j: qkvw_ref[0, j], qvb_ref[0, 0:1], qvb_ref[0, 1:2]
    )
    attend_forward(
        [(qkv_ref, pos_ref, p_ref, mix_ref)], wins, wins, lq_ref, lk_ref, mask_ref
    )
    add_branch(wins, [mix_ref], [projw_ref[0]], pb_ref[0:1], x_ref, hid_ref)


def attn_other_kernel(rows, across, *refs):
    (part_ref, xn_ref, a_ref, b_ref, lq_ref, lk_ref, pick_ref, info_ref) = refs[:8]
    (hid_ref, qkv_ref, p_ref, mix_ref, small_ref, mask_ref, pos_ref) = refs[8:]
    small_of(a_ref, small_ref)
    wins = (rows // WIN) * across
    mask_ref[...] = head_mask()
    bias = other_small(small_ref, info_ref[0], pick_ref, pos_ref)
    project_half(
        xn_ref,
        qkv_ref,
        lambda j: qkv_weight_of(1, j, 0, None, a_ref, b_ref),
        bias[0:1],
        bias[1:2],
    )
    attend_forward([(qkv_ref, pos_ref, p_ref, mix_ref)], wins, wins, lq_ref, lk_ref, mask_ref)
    add_branch(
        wins, [mix_ref], [proj_weight_of(1, 0, None, a_ref, b_ref)], 0.0, part_ref, hid_ref
    )


def other_small(small_ref, par, pick_ref, pos_ref):
    first = par == 0

    def swapped(v, n):
        return jnp.where(first, v, jnp.concatenate([v[:, n : 2 * n], v[:, :n]], axis=1))

    t = swapped(small_ref[0:16, 0:96], 48)
    table_to_map(t, pick_ref, pos_ref)
    return swapped(small_ref[18:20, 0:192], 96)


def norm_kernel(rows, across, *refs):
    (st_ref, halo_ref, gain_ref, bias_ref, qvb_ref, qkvw_ref) = refs[:6]
    (x_ref, xn_ref, qkv_ref) = refs[6:]

    def tile(r, k):
        if r < rows:
            return st_ref[pl.ds(tile_row(r, k, across), SEG), :]
        return edge_tile(halo, k, r - rows)

    halo = halo_ref[...].astype(F32)
    shift_in(tile, x_ref, rows, across)
    norm_windows(1, (rows // WIN) * across, x_ref, xn_ref, gain_ref, bias_ref)
    project_half(
        xn_ref, qkv_ref, lambda j: qkvw_ref[1, j], qvb_ref[1, 0:1], qvb_ref[1, 1:2]
    )


def attn_both_kernel(rows, across, *refs):
    (xn_ref, qkv0_ref, pos_ref, a_ref, b_ref) = refs[:5]
    (lq_ref, lk_ref, pick_ref, info_ref) = refs[5:9]
    (p0_ref, mix0_ref, qkv1_ref, p1_ref, mix1_ref, small_ref, mask_ref, pos1_ref) = refs[9:]
    wins = (rows // WIN) * across
    mask_ref[...] = head_mask()
    small_of(a_ref, small_ref)
    bias = other_small(small_ref, info_ref[0], pick_ref, pos1_ref)
    project_half(
        xn_ref,
        qkv1_ref,
        lambda j: qkv_weight_of(1, j, 1, None, a_ref, b_ref),
        bias[0:1],
        bias[1:2],
    )
    attend_forward(
        [(qkv0_ref, pos_ref, p0_ref, mix0_ref), (qkv1_ref, pos1_ref, p1_ref, mix1_ref)],
        wins,
        wins,
        lq_ref,
        lk_ref,
        mask_ref,
    )


def branch_kernel(wins, x_ref, mix0_ref, mix1_ref, projw_ref, a_ref, b_ref, pb_ref, hid_ref):
    add_branch(
        wins,
        [mix0_ref, mix1_ref],
        [projw_ref[1], proj_weight_of(1, 1, None, a_ref, b_ref)],
        pb_ref[1:2],
        x_ref,
        hid_ref,
    )


def up_weight(part, layer, base, f1_ref, a_ref, b_ref):
    if part == 0:
        return f1_ref[layer]
    return jnp.concatenate([a_ref[base : base + C], b_ref[base : base + C]], axis=1)


def down_weight(part, layer, base, f2_ref, a_ref, b_ref):
    if part == 0:
        return f2_ref[layer]
    return jnp.concatenate([a_ref[base + C : base + 2 * C], b_ref[base + C : base + 2 * C]], axis=0)


def up_biases(layer, par, fb1_ref, small_ref):
    own = fb1_ref[layer : layer + 1]
    one, two = small_ref[16:17], small_ref[17:18]
    first = par == 0
    return own, jnp.concatenate(
        [jnp.where(first, one, two), jnp.where(first, two, one)], axis=1
    )


def gelu_pair(u):
    phi = 0.5 + 0.5 * lax.erf(u * (2.0**-0.5))
    slope = phi + u * (jnp.exp(-0.5 * u * u) * (2.0 * np.pi) ** -0.5)
    return (u * phi).astype(BF), slope.astype(BF)


def mlp_own_kernel(hid_ref, gain_ref, bias_ref, fb1_ref, fb2_ref, f1_ref, f2_ref, st_ref, n2_ref, act_ref, gp_ref):
    h = hid_ref[...]
    xhat, _ = norm_stats(h)
    n2 = (xhat * gain_ref[0, 1:2] + bias_ref[0, 1:2]).astype(BF)
    n2_ref[...] = n2
    act, slope = gelu_pair(nn(n2, f1_ref[0]) + fb1_ref[0:1])
    for z in range(2):
        act_ref[z] = act[:, C * z : C * (z + 1)]
        gp_ref[z] = slope[:, C * z : C * (z + 1)]
    st_ref[...] = h + fb2_ref[0:1] + nn(act, f2_ref[0])


def mlp_other_kernel(
    across, part_ref, n2_ref, fb1_ref, small_ref, a_ref, b_ref, info_ref, st_ref, act_ref, gp_ref,
    edge_ref
):
    _, bias = up_biases(0, info_ref[0], fb1_ref, small_ref)
    act, slope = gelu_pair(nn(n2_ref[...], up_weight(1, 0, 0, None, a_ref, b_ref)) + bias)
    for z in range(2):
        act_ref[z] = act[:, C * z : C * (z + 1)]
        gp_ref[z] = slope[:, C * z : C * (z + 1)]
    st_ref[...] = part_ref[...] + nn(act, down_weight(1, 0, 0, None, a_ref, b_ref))
    edge_ref[...] = edge_rows(st_ref, across, range(SHIFT))


def mlp_back_rows(
    layer, base, at, g, df, h, slopes, gain, bias, f1_ref, f2_ref, a_ref, b_ref, refs, carry
):
    (gh_ref, n2_ref, du_ref) = refs
    (sb, sg, sf, s1) = carry
    sf = sf + jnp.sum(df.astype(F32), 0, keepdims=True)
    grads = [nt(df, down_weight(p, layer, base, f2_ref, a_ref, b_ref)) for p in range(2)]
    new = []
    parts = []
    for p in range(2):
        du = [
            (grads[p][:, C * z : C * (z + 1)] * slopes(2 * p + z).astype(F32)).astype(BF)
            for z in range(2)
        ]
        for z in range(2):
            du_ref[2 * p + z, at, :] = du[z]
            new.append(s1[2 * p + z] + jnp.sum(du[z].astype(F32), 0, keepdims=True))
        parts.append(jnp.concatenate(du, axis=1))
    dz = nt(parts[0], up_weight(0, layer, base, f1_ref, a_ref, b_ref)) + nt(
        parts[1], up_weight(1, layer, base, f1_ref, a_ref, b_ref)
    )
    xhat, rinv = norm_stats(h)
    n2_ref[at, :] = (xhat * gain + bias).astype(BF)
    sg = sg + jnp.sum(dz * xhat, 0, keepdims=True)
    sb = sb + jnp.sum(dz, 0, keepdims=True)
    gh_ref[at, :] = g + norm_back(dz, xhat, rinv, gain)
    return sb, sg, sf, tuple(new)


def quarter_of(par, slot, part):
    return (par ^ slot) if part == 0 else 2 + slot


def mlp_sums(carry, fb1_ref, sh_ref):
    sb, sg, sf, s1 = carry
    for q in range(4):
        fb1_ref[q : q + 1] = s1[q]
    sh_ref[0:1] = sg
    sh_ref[1:2] = sb
    sh_ref[2:3] = sf


def zero_sums():
    z = jnp.zeros((1, C), F32)
    return z, z, z, (z,) * 4


def half_sums(du, ref):
    for z in range(2):
        ref[z : z + 1] = jnp.sum(du[z].astype(F32), 0, keepdims=True)


def mlp_own_both_kernel(rows, across, *refs):
    (cot_ref, edge_ref, hid_ref, gain_ref, bias_ref, fb1_ref, fb2_ref, f1_ref, f2_ref) = refs[:9]
    (g_ref, df_ref, n2_ref, st_ref, dz_ref, du_ref, act_ref, sum_ref, sf_ref) = refs[9:]
    layer = 1
    cols = across * WIN
    cot_edge = edge_ref[...].astype(F32)
    for r in range(rows):
        s = r + SHIFT
        if s < rows:
            row = cot_ref[s].astype(F32)
        else:
            row = cot_edge[(s - rows) * cols : (s - rows + 1) * cols]
        for k in range(across):
            a = WIN * k + SHIFT
            if k < across - 1:
                piece = [row[a : a + WIN]]
            else:
                piece = [row[a:], row[:SHIFT]]
            g_ref[pl.ds(tile_row(r, k, across), SEG), :] = jnp.concatenate(
                piece + [zero_rows(1)], axis=0
            )
    h = hid_ref[...]
    xhat, _ = norm_stats(h)
    n2 = (xhat * gain_ref[layer, 1:2] + bias_ref[layer, 1:2]).astype(BF)
    n2_ref[...] = n2
    df = g_ref[...].astype(BF)
    df_ref[...] = df
    sf_ref[...] = jnp.sum(df.astype(F32), 0, keepdims=True)
    up = nn(n2, f1_ref[layer]) + fb1_ref[layer : layer + 1]
    grad = nt(df, f2_ref[layer])
    act, slope = gelu_pair(up)
    du = (grad * slope.astype(F32)).astype(BF)
    parts = [du[:, C * z : C * (z + 1)] for z in range(2)]
    for z in range(2):
        act_ref[z] = act[:, C * z : C * (z + 1)]
        du_ref[z] = parts[z]
    half_sums(parts, sum_ref)
    st_ref[...] = h + fb2_ref[layer : layer + 1] + nn(act, f2_ref[layer])
    dz_ref[...] = nt(du, f1_ref[layer])


def mlp_other_both_kernel(rows, across, *refs):
    (hid_ref, g_ref, df_ref, n2_ref, part_ref, dzp_ref, gain_ref, fb1_ref, small_ref) = refs[:9]
    (a_ref, b_ref, info_ref, duo_ref, acto_ref, sumo_ref, sf_ref) = refs[9:16]
    (st_ref, gh_ref, du_ref, act_ref, send_ref, sum_ref, sh_ref, edge_ref) = refs[16:]
    layer = 1
    par = info_ref[0]
    n2 = n2_ref[...]
    df = df_ref[...]
    _, bias = up_biases(layer, par, fb1_ref, small_ref)
    up = nn(n2, up_weight(1, layer, 0, None, a_ref, b_ref)) + bias
    grad = nt(df, down_weight(1, layer, 0, None, a_ref, b_ref))
    act, slope = gelu_pair(up)
    du = (grad * slope.astype(F32)).astype(BF)
    parts = [du[:, C * z : C * (z + 1)] for z in range(2)]
    for z in range(2):
        act_ref[z] = act[:, C * z : C * (z + 1)]
        du_ref[z] = parts[z]
    sum_ref[0:2] = sumo_ref[...]
    half_sums(parts, sum_ref.at[2:4])
    st_ref[...] = part_ref[...] + nn(act, down_weight(1, layer, 0, None, a_ref, b_ref))
    edge_ref[...] = edge_rows(st_ref, across, range(rows - SHIFT, rows))
    dz = dzp_ref[...] + nt(du, up_weight(1, layer, 0, None, a_ref, b_ref))
    xhat, rinv = norm_stats(hid_ref[...])
    sh_ref[0:1] = jnp.sum(dz * xhat, 0, keepdims=True)
    sh_ref[1:2] = jnp.sum(dz, 0, keepdims=True)
    sh_ref[2:3] = sf_ref[...]
    gh_ref[...] = g_ref[...] + norm_back(dz, xhat, rinv, gain_ref[layer, 1:2])
    send_ref[0, 0:C, :] = tn(n2, duo_ref[1 - par]).astype(BF)
    send_ref[0, C:, :] = tn(acto_ref[1 - par], df).astype(BF)
    send_ref[1, 0:C, :] = tn(n2, du_ref[1]).astype(BF)
    send_ref[1, C:, :] = tn(act_ref[1], df).astype(BF)


def mlp_keep_kernel(n2_ref, df_ref, duo_ref, acto_ref, du_ref, act_ref, info_ref, keep_ref):
    n2 = n2_ref[...]
    df = df_ref[...]
    for part in range(2):
        if part == 0:
            d, a = duo_ref[info_ref[0]], acto_ref[info_ref[0]]
        else:
            d, a = du_ref[0], act_ref[0]
        keep_ref[part, 0:C, :] = tn(n2, d).astype(BF)
        keep_ref[part, C:, :] = tn(a, df).astype(BF)


def up_keep_kernel(n2_ref, du_ref, got_ref, info_ref, own_ref, oth_ref):
    n2 = n2_ref[...]
    for part, ref in ((1, oth_ref), (0, own_ref)):
        q = quarter_of(info_ref[0], 0, part)
        ref[...] = (tn(n2, du_ref[q]) + got_ref[part].astype(F32)).astype(BF)


def down_grad_kernel(rows, across, *refs):
    (gin_ref, halo_ref, act0_ref, act1_ref, info_ref, g_ref, df_ref, keep_ref, send_ref) = refs

    def tile(r, k):
        if r >= 0:
            return gin_ref[pl.ds(tile_row(r, k, across), SEG), :]
        return edge_tile(halo, k, r + SHIFT)

    halo = halo_ref[...].astype(F32)
    shift_out(tile, g_ref, rows, across)
    df = g_ref[...].astype(BF)
    df_ref[...] = df
    for slot, ref in ((1, send_ref), (0, keep_ref)):
        ref[1] = tn(act1_ref[slot], df).astype(BF)
        ref[0] = tn(act0_ref[info_ref[0] ^ slot], df).astype(BF)


def mlp_bwd_kernel(base, *refs):
    (g_ref, df_ref, hid_ref, gp0_ref, gp1_ref, gain_ref, bias_ref) = refs[:7]
    (f1_ref, f2_ref, a_ref, b_ref, info_ref) = refs[7:12]
    (gh_ref, n2_ref, du_ref, send_ref, fb1_ref, sh_ref) = refs[12:]
    layer = 0
    gain = gain_ref[layer, 1:2]
    bias = bias_ref[layer, 1:2]
    n = hid_ref.shape[0]

    def block(i, carry):
        at = rows_at(i, n)
        return mlp_back_rows(
            layer, base, at, g_ref[at, :], df_ref[at, :], hid_ref[at, :],
            lambda q: (gp0_ref if q < 2 else gp1_ref)[q % 2, at, :], gain, bias,
            f1_ref, f2_ref, a_ref, b_ref, (gh_ref, n2_ref, du_ref), carry
        )

    mlp_sums(repeat(1, block, zero_sums()), fb1_ref, sh_ref)
    n2 = n2_ref[...]
    for part in range(2):
        send_ref[part] = tn(n2, du_ref[quarter_of(info_ref[0], 1, part)]).astype(BF)


def window_grads(wins, gh_ref, da_ref):
    def four(i, s):
        g = gh_ref[rows_at(i, 4 * WROWS), :]
        for n in range(4):
            part = jnp.concatenate(
                [g[n * WROWS : (n + 1) * WROWS], zero_rows(WPAD - WROWS)], axis=0
            ).astype(BF)
            da_ref[rows_at(4 * i + n, WPAD), :] = part
            s = s + jnp.sum(part.astype(F32), 0, keepdims=True)
        return s

    return repeat(wins // 4, four, jnp.zeros((1, C), F32))


def attend_backward(halves, wins, group, mask_ref):
    def body(i, carry):
        units = [(i * group + u, h) for u in range(group) for h in halves]
        first = []
        for w, (qkv_ref, p_ref, do_ref, dqkv_ref, _) in units:
            at = rows_at(w, WPAD)
            do = spread(do_ref[at, :], mask_ref[...])
            first.append(nt(qkv_ref[2, at, :], do))
            dqkv_ref[2, at, :] = nn(p_ref[w], do).astype(BF)
        second = []
        for (w, (_, p_ref, _, _, acc_ref)), dp in zip(units, first):
            p = p_ref[w].astype(F32)
            ds = p * (dp - jnp.sum(p * dp, 0, keepdims=True))
            for n in range(3):
                acc_ref[n] += ds[:, 128 * n : 128 * (n + 1)]
            second.append(ds.astype(BF))
        for (w, (qkv_ref, _, _, dqkv_ref, _)), ds in zip(units, second):
            at = rows_at(w, WPAD)
            dqkv_ref[1, at, :] = nn(ds, spread(qkv_ref[0, at, :], mask_ref[...])).astype(BF)
            dqkv_ref[0, at, :] = fold(tn(ds, qkv_ref[1, at, :])).astype(BF)
        return carry

    repeat(wins // group, body, 0)


def half_grads(half, par, xn_ref, da_ref, mix_ref, dqkv_ref, row_ref, give):
    def put(value, at):
        if half == 0:
            row_ref[...] = value
            one = row_ref[pl.ds(pl.multiple_of(par * 96, 96), 96), :]
            two = row_ref[pl.ds(pl.multiple_of((1 - par) * 96, 96), 96), :]
        else:
            one, two = value[:96], value[96:]
        give(at, one.astype(BF), two.astype(BF))

    xn = xn_ref[...]
    for j in range(3):
        grad = tn(dqkv_ref[j], xn)
        put(grad * SCALE if j == 0 else grad, 96 * j)
    put(tn(mix_ref[...], da_ref[...]), 288)


def normed_grads(layer, wins, dqkvs, weights, gh_ref, x_ref, gain_ref, gx_ref):
    gain = gain_ref[layer, 0:1]
    n = 8

    def part(i, carry):
        sg, sb, sq = carry
        at = rows_at(i, n * WPAD)
        dn = nn(dqkvs[0][0, at, :], weights[0](0)) + nn(dqkvs[1][0, at, :], weights[1](0))
        dn = dn * SCALE
        for half in range(2):
            for j in (1, 2):
                dn = dn + nn(dqkvs[half][j, at, :], weights[half](j))
        new = []
        for half in range(2):
            for m, j in enumerate((0, 2)):
                new.append(
                    sq[half * 2 + m] + jnp.sum(dqkvs[half][j, at, :].astype(F32), 0, keepdims=True)
                )
        d = jnp.concatenate([dn[k * WPAD : k * WPAD + WROWS] for k in range(n)], axis=0)
        to = rows_at(i, n * WROWS)
        xhat, rinv = norm_stats(x_ref[to, :])
        sg = sg + jnp.sum(d * xhat, 0, keepdims=True)
        sb = sb + jnp.sum(d, 0, keepdims=True)
        gx_ref[to, :] = gh_ref[to, :] + norm_back(d, xhat, rinv, gain)
        return sg, sb, tuple(new)

    z = jnp.zeros((1, C), F32)
    zq = jnp.zeros((1, 6 * HD), F32)
    return repeat(wins // n, part, (z, z, (zq,) * 4))


def small_rows(ref, z, sq, fb1, table, shared):
    ref[...] = jnp.zeros_like(ref)
    if shared is not None:
        sg, sb, projb, sh_ref = shared
        ref[0:1] = sg
        ref[1:2] = sb
        ref[2:3] = projb
        ref[3:6] = sh_ref[...]
    ref[6:7] = fb1
    ref[7:8, 0:96] = sq[0][:, 96 * z : 96 * (z + 1)] * SCALE
    ref[7:8, 128:224] = sq[1][:, 96 * z : 96 * (z + 1)]
    ref[8:24, 0:48] = table[:, 48 * z : 48 * (z + 1)]


def mixed_grad_kernel(wins, gh_ref, projw_ref, a_ref, b_ref, da_ref, do_ref, pb_ref):
    pb_ref[...] = window_grads(wins, gh_ref, da_ref)
    for half in range(2):
        do_ref[half] = nt(da_ref[...], proj_weight_of(half, 1, projw_ref, a_ref, b_ref)).astype(BF)


def attn_bwd_kernel(rows, across, *refs):
    (gh_ref, x_ref, xn_ref, gain_ref, qkvw_ref, a_ref, b_ref, info_ref) = refs[:8]
    (fb1_ref, sh_ref, qkv0_ref, p0_ref, mix0_ref, qkv1_ref, p1_ref, mix1_ref, pick_ref) = refs[8:17]
    (da_ref, do_ref, pb_ref) = refs[17:20]
    (gin_ref, keep_ref, send_ref, edge_ref) = refs[20:24]
    (dqkv0_ref, dqkv1_ref, acc_ref, mask_ref, row_ref, sm_ref) = refs[24:]
    layer = 1
    par = info_ref[0]
    wins = (rows // WIN) * across
    mask_ref[...] = head_mask()
    acc_ref[...] = jnp.zeros_like(acc_ref)
    projb = pb_ref[...]
    attend_backward(
        [
            (qkv0_ref, p0_ref, do_ref.at[0], dqkv0_ref, acc_ref.at[0]),
            (qkv1_ref, p1_ref, do_ref.at[1], dqkv1_ref, acc_ref.at[1]),
        ],
        wins,
        wins,
        mask_ref,
    )
    for half, mix_ref, dqkv_ref in ((1, mix1_ref, dqkv1_ref), (0, mix0_ref, dqkv0_ref)):

        def give(at, one, two, half=half):
            keep_ref[half, at : at + 96, :] = one
            send_ref[half, at : at + 96, :] = two

        half_grads(half, par, xn_ref, da_ref, mix_ref, dqkv_ref, row_ref, give)
    weights = [
        lambda j, half=half: qkv_weight_of(half, j, layer, qkvw_ref, a_ref, b_ref)
        for half in range(2)
    ]
    sg, sb, sq = normed_grads(
        layer, wins, [dqkv0_ref, dqkv1_ref], weights, gh_ref, x_ref, gain_ref, gin_ref
    )
    edge_ref[...] = edge_rows(gin_ref, across, range(rows - SHIFT, rows))
    for half in range(2):
        table = map_to_table(acc_ref.at[half], pick_ref)
        for z in range(2):
            q = 2 * half + z
            small_rows(
                sm_ref.at[q], z, sq[2 * half : 2 * half + 2], fb1_ref[q : q + 1], table,
                (sg, sb, projb, sh_ref)
            )
    keep_ref[0, C:, :] = sm_ref[par].astype(BF)
    send_ref[0, C:, :] = sm_ref[1 - par].astype(BF)
    keep_ref[1, C:, :] = sm_ref[2].astype(BF)
    send_ref[1, C:, :] = sm_ref[3].astype(BF)


def column_sum(ref):
    return jnp.sum(ref[...].astype(F32), 0, keepdims=True)


def attn_bwd_heads_kernel(rows, across, *refs):
    (gh_ref, xn_ref, projw_ref, a_ref, b_ref, fb1_ref) = refs[:6]
    (qkv0_ref, p0_ref, qkv1_ref, p1_ref, mix1_ref, pick_ref) = refs[6:12]
    (da_ref, dqkv0_ref, acc0_ref, dqkv1_ref, pb_ref, keep_ref, send_ref) = refs[12:19]
    (do_ref, mask_ref, acc1_ref, sm_ref) = refs[19:]
    wins = (rows // WIN) * across
    mask_ref[...] = head_mask()
    acc0_ref[...] = jnp.zeros_like(acc0_ref)
    acc1_ref[...] = jnp.zeros_like(acc1_ref)
    pb_ref[...] = window_grads(wins, gh_ref, da_ref)
    da = da_ref[...]
    for half in range(2):
        do_ref[half] = nt(da, proj_weight_of(half, 0, projw_ref, a_ref, b_ref)).astype(BF)
    attend_backward(
        [
            (qkv1_ref, p1_ref, do_ref.at[1], dqkv1_ref, acc1_ref),
            (qkv0_ref, p0_ref, do_ref.at[0], dqkv0_ref, acc0_ref),
        ],
        wins,
        wins,
        mask_ref,
    )

    def give(at, one, two):
        keep_ref[at : at + 96, :] = one
        send_ref[at : at + 96, :] = two

    half_grads(1, None, xn_ref, da_ref, mix1_ref, dqkv1_ref, None, give)
    table = map_to_table(acc1_ref, pick_ref)
    sq = (column_sum(dqkv1_ref.at[0]), column_sum(dqkv1_ref.at[2]))
    for z, ref in ((0, keep_ref), (1, send_ref)):
        small_rows(sm_ref, z, sq, fb1_ref[2 + z : 3 + z], table, None)
        ref[C:, :] = sm_ref[...].astype(BF)


def attn_bwd_own_kernel(rows, across, *refs):
    (gh_ref, x_ref, xn_ref, gain_ref, qkvw_ref, a_ref, b_ref, info_ref) = refs[:8]
    (fb1_ref, sh_ref, da_ref, dqkv_ref, acc_ref, dqkv1_ref, pb_ref, mix_ref, pick_ref) = refs[8:17]
    (out_ref, keep_ref, send_ref) = refs[17:20]
    (gx_ref, row_ref, sm_ref) = refs[20:]
    par = info_ref[0]
    wins = (rows // WIN) * across

    def give(at, one, two):
        keep_ref[at : at + 96, :] = one
        send_ref[at : at + 96, :] = two

    half_grads(0, par, xn_ref, da_ref, mix_ref, dqkv_ref, row_ref, give)
    weights = [
        lambda j, half=half: qkv_weight_of(half, j, 0, qkvw_ref, a_ref, b_ref)
        for half in range(2)
    ]
    sg, sb, sq = normed_grads(
        0, wins, [dqkv_ref, dqkv1_ref], weights, gh_ref, x_ref, gain_ref, gx_ref
    )
    table = map_to_table(acc_ref, pick_ref)
    for z in range(2):
        small_rows(
            sm_ref.at[z], z, sq[0:2], fb1_ref[z : z + 1], table, (sg, sb, pb_ref[...], sh_ref)
        )
    keep_ref[C:, :] = sm_ref[par].astype(BF)
    send_ref[C:, :] = sm_ref[1 - par].astype(BF)
    for r in range(rows):
        parts = [gx_ref[pl.ds(tile_row(r, k, across), SEG), :][:WIN] for k in range(across)]
        out_ref[r, :, 0, :] = jnp.concatenate(parts, axis=0)


def pair_kernel(keep_ref, got_ref, own_ref, oth_ref):
    own_ref[...] = (keep_ref[0].astype(F32) + got_ref[0].astype(F32)).astype(BF)
    oth_ref[...] = (keep_ref[1].astype(F32) + got_ref[1].astype(F32)).astype(BF)


def combine_kernel(parts, bit, n_in, *refs):
    ins = refs[:n_in]
    info_ref = refs[n_in]
    outs = refs[n_in + 1 :]
    at = 0
    for rows, terms, split in parts:

        def total(first, n):
            acc = None
            for i, base in terms:
                x = ins[i][pl.ds(base + first, n), :].astype(F32)
                acc = x if acc is None else acc + x
            return acc.astype(BF)

        if bit is None or not split:
            whole = total(0, rows)
            for out in outs:
                out[at : at + rows, :] = whole
            at += rows
        else:
            n = rows // 2
            b = (info_ref[2] >> bit) & 1
            outs[0][at : at + n, :] = total(pl.multiple_of(b * n, n), n)
            outs[1][at : at + n, :] = total(pl.multiple_of((1 - b) * n, n), n)
            at += n


def close_kernel(halves, bit, mine_ref, got_ref, info_ref, out_ref, small_ref):
    join_kernel(halves, bit, mine_ref.at[0 : sum(halves)], got_ref, info_ref, out_ref)
    at = sum(halves)
    rest = (mine_ref[at:, :].astype(F32) + got_ref[at:, :].astype(F32)).astype(BF)
    n = rest.shape[0] - SMALL
    out_ref[2 * at :, :] = rest[:n]
    small_ref[...] = rest[n:]


def join_kernel(halves, bit, mine_ref, got_ref, info_ref, out_ref):
    b = (info_ref[2] >> bit) & 1
    at = 0
    for n in halves:
        for ref, place in ((mine_ref, b), (got_ref, 1 - b)):
            to = pl.multiple_of(2 * at + place * n, 16)
            out_ref[pl.ds(to, n), :] = ref[at : at + n, :]
        at += n
    if at < mine_ref.shape[0]:
        out_ref[2 * at :, :] = mine_ref[at:, :]


def out_kernel(rows, across, st_ref, halo_ref, o_ref):
    halo = halo_ref[C + SMALL :, :].astype(F32)
    for r in range(rows):
        parts = []
        for k in range(across):
            if r >= SHIFT:
                t = st_ref[pl.ds(tile_row(r - SHIFT, k, across), SEG), :]
            else:
                t = edge_tile(halo, k, r)
            parts.append(t[:WIN])
        last = parts[-1]
        parts = [last[WIN - SHIFT :]] + parts[:-1] + [last[: WIN - SHIFT]]
        o_ref[r] = jnp.concatenate(parts, axis=0).astype(BF)


def place_of(i, info_ref):
    return info_ref[0] ^ (i // 2), ((info_ref[2] >> 1) & 1) ^ (i % 2)


def put_up(pieces, base, info_ref, ref):
    n = C // 2
    for i in range(4):
        core, half = place_of(i, info_ref)
        rows = pl.ds(pl.multiple_of(half * n, n), n)
        cols = pl.ds(pl.multiple_of(core * C, C), C)
        ref[rows, cols] = pieces[i][base : base + n, :].astype(F32)


def put_down(pieces, base, info_ref, ref):
    n = C // 2
    for i in range(4):
        core, half = place_of(i, info_ref)
        rows = pl.ds(pl.multiple_of(core * C + half * n, n), n)
        ref[rows, :] = pieces[i][base : base + n, :].astype(F32)


def put_attn(pieces, base, info_ref, asm_ref, qkv_ref, proj_ref):
    n = C // 2
    for i in range(4):
        core, half = place_of(i, info_ref)
        rows = pl.ds(pl.multiple_of(half * n, n), n)
        asm_ref[core, rows, :] = pieces[i][base : base + n, :].astype(F32)
    for core in range(2):
        to = pl.ds(96 * core, 96)
        for j in range(3):
            qkv_ref[j, to, :] = asm_ref[core, 96 * j : 96 * (j + 1), :]
        proj_ref[to, :] = asm_ref[core, 288:384, :]


def final_second_kernel(*refs):
    pieces = refs[:4]
    (info_ref, f1_ref, f2_ref, qkv_ref, proj_ref) = refs[4:9]
    (up_ref, down_ref, asm_ref, q_ref, p_ref, sems) = refs[9:]
    put_up(pieces, 0, info_ref, up_ref)
    put_down(pieces, C // 2, info_ref, down_ref)
    put_attn(pieces, C, info_ref, asm_ref, q_ref, p_ref)
    outs = [f1_ref, f2_ref, qkv_ref, proj_ref]
    for copy in copies_of([(x, y.at[1]) for x, y in zip((up_ref, down_ref, q_ref, p_ref), outs)], sems):
        copy.wait()


def final_kernel(*refs):
    mlps, attns, smalls = refs[:4], refs[4:8], refs[8:10]
    (shared_ref, info_ref) = refs[10:12]
    (f1_ref, f2_ref, qkv_ref, proj_ref) = refs[16:20]
    (gain_ref, bias_ref, pb_ref, fb2_ref, qvb_ref, fb1_ref, tab_ref) = refs[20:27]
    (up_ref, down_ref, asm_ref, q_ref, p_ref, sm_ref, sems) = refs[27:]
    put_up(mlps, 0, info_ref, up_ref)
    copies = copies_of([(up_ref, f1_ref.at[0])], sems)
    put_down(mlps, C // 2, info_ref, down_ref)
    copies += copies_of([(down_ref, f2_ref.at[0])], sems.at[1:2])
    put_attn(attns, 0, info_ref, asm_ref, q_ref, p_ref)
    copies += copies_of([(q_ref, qkv_ref.at[0]), (p_ref, proj_ref.at[0])], sems.at[2:4])
    n = C // 2
    par = info_ref[0]
    for layer in range(2):
        for i in range(2):
            x = smalls[i][...] if layer == 1 else attns[2 * i][n:, :]
            sm_ref[par ^ i] = x.astype(F32)
        x, y = sm_ref[0], sm_ref[1]
        shared = x[0:6]
        if layer == 0:
            shared = sm_ref[par, 0:6, :] + shared_ref[0:6].astype(F32)
        gain_ref[layer, 0:1] = shared[0:1]
        gain_ref[layer, 1:2] = shared[3:4]
        bias_ref[layer, 0:1] = shared[1:2]
        bias_ref[layer, 1:2] = shared[4:5]
        pb_ref[layer : layer + 1] = shared[2:3]
        fb2_ref[layer : layer + 1] = shared[5:6]
        fb1_ref[layer : layer + 1, 0:C] = x[6:7]
        fb1_ref[layer : layer + 1, C:] = y[6:7]
        for k in range(2):
            qvb_ref[layer, k : k + 1, 0:96] = x[7:8, 128 * k : 128 * k + 96]
            qvb_ref[layer, k : k + 1, 96:192] = y[7:8, 128 * k : 128 * k + 96]
        t = jnp.concatenate([x[8:24, 0:48], y[8:24, 0:48]], axis=1)
        wide = tn(t.astype(BF), offset_rows().astype(BF)) * offset_cols()
        for h in range(6):
            tab_ref[h, layer : layer + 1, :] = jnp.sum(
                wide[16 * h : 16 * (h + 1)], 0, keepdims=True
            )
    for copy in copies:
        copy.wait()


SMEM = pl.BlockSpec(memory_space=pltpu.SMEM)
VMEM = pl.BlockSpec(memory_space=pltpu.VMEM)
HBM = pl.BlockSpec(memory_space=pltpu.HBM)


def call(kernel, name, us, limit, operands, outs, scratch=(), aliases=None):
    args = []
    specs = []
    for op in operands:
        args.append(op[0] if isinstance(op, tuple) else op)
        specs.append(op[1] if isinstance(op, tuple) else VMEM)
    shapes = [jax.ShapeDtypeStruct(o[0], o[1]) for o in outs]
    return pl.pallas_call(
        kernel,
        name=name,
        in_specs=specs,
        out_specs=[o[2] if len(o) > 2 else VMEM for o in outs],
        input_output_aliases=aliases or {},
        out_shape=shapes,
        scratch_shapes=[s if not isinstance(s, tuple) else pltpu.VMEM(*s) for s in scratch],
        cost_estimate=pl.CostEstimate(
            flops=int(us * 1e10), bytes_accessed=1000000, transcendentals=0
        ),
        compiler_params=pltpu.CompilerParams(vmem_limit_bytes=limit * 2**20),
    )(*args)


def on_device(n_win, *args):
    (
        tokens,
        crop_ids,
        cotangent,
        norm_gain,
        norm_bias,
        qkv_weight,
        qv_bias,
        proj_weight,
        proj_bias,
        fc1_weight,
        fc1_bias,
        fc2_weight,
        fc2_bias,
        pos_table,
    ) = args
    rows, cols = tokens.shape[1:3]
    across = cols // WIN
    wins = (rows // WIN) * across
    ntok = wins * WROWS
    npad = wins * WPAD
    win = lax.axis_index("win")
    tp = lax.axis_index("tp")
    par = win % 2
    info = (jnp.stack([par, tp, win]).astype(jnp.int32), SMEM)
    bits = n_win.bit_length() - 1
    assert n_win == 1 << bits and bits >= 3

    def to_tp(x, name):
        with jax.named_scope(name + "_tp"):
            return lax.ppermute(x, "tp", [(0, 1), (1, 0)])

    def to_win(x, bit, name):
        if bit >= bits:
            return jnp.zeros_like(x)
        with jax.named_scope("%s_win%d" % (name, bit)):
            return lax.ppermute(x, "win", [(i, i ^ (1 << bit)) for i in range(n_win)])

    def after(x, *others):
        return lax.optimization_barrier((x,) + others)[0]

    def combine(parts, bit, ins, name):
        total = sum(rows // 2 if split and bit is not None else rows for rows, _, split in parts)
        outs = [((total, C), BF)] * (1 if bit is None else 2)
        return call(
            partial(combine_kernel, parts, bit, len(ins)), name, 1, 4, tuple(ins) + (info,), outs
        )

    def join(halves, bit, mine, got, name):
        return call(
            partial(join_kernel, halves, bit), name, 1, 4, (mine, got, info),
            [((mine.shape[0] + sum(halves), C), BF)],
        )[0]

    qkv_t = qkv_weight.transpose(0, 2, 3, 1)
    table = pos_table.transpose(2, 0, 1)
    na = C + SMALL
    n = C // 2
    edge_b = ((across * SHIFT * SEG, C), BF)
    a0q, small = call(
        pack_first_kernel,
        "pack_first",
        0.1,
        60,
        tuple((x, HBM) for x in (qkv_t, proj_weight, table, qv_bias, fc1_bias)),
        [((C + 2 * SENT_ROWS, C), BF), ((2, SMALL_ROWS, C), F32)],
        [
            (table.shape, F32),
            (qv_bias.shape, F32),
            (fc1_bias.shape, F32),
            pltpu.SemaphoreType.DMA((7,)),
        ],
    )
    a0 = to_tp(a0q, "a0")
    m0q, a1q, m1q, cot_edge = call(
        pack_kernel,
        "pack",
        0.1,
        60,
        tuple((x, HBM) for x in (qkv_t, proj_weight, fc1_weight, fc2_weight, cotangent[0]))
        + (after(small, a0q), info),
        [
            ((2 * C, C), BF),
            ((C + 2 * SENT_ROWS, C), BF),
            ((2 * C, C), BF),
            ((EDGE_ROWS, C), BF),
        ],
        [((SHIFT, cols, C), BF), pltpu.SemaphoreType.DMA((9,))],
    )
    m0 = to_tp(m0q, "m0")
    crops = crop_ids.transpose(2, 0, 1)
    label_outs = [((wins, 128), F32), ((wins, WPAD, 128), F32), ((3, WPAD, 128), F32)]
    lq0, lk0, pos0, pick = call(
        partial(prep_kernel, 0, rows, across),
        "prep_0",
        0.1,
        8,
        (crops, after(small, m0q), info),
        label_outs + [((WIN, 96, 6 * WPAD), BF)],
        [((128, 128), F32)],
    )
    tiles = (rows // WIN, across, WIN, SEG, C)
    mask = ((6 * WPAD, 6 * HD), BF)
    half_outs = [((3, npad, 192), BF), ((wins, WPAD, 6 * WPAD), BF), ((npad, 192), BF)]
    tok_f = ((ntok, C), F32)
    tok_b = ((ntok, C), BF)
    hid_b = ((4, ntok, C), BF)
    other_scratch = [mask, ((3, WPAD, 128), F32)]

    x0, xn0, part, qkv00, p00, mix00 = call(
        partial(attn_own_kernel, rows, across),
        "attn_own_0",
        0.1,
        8,
        (tokens[0], norm_gain, norm_bias, proj_bias, qv_bias, qkv_t, proj_weight, pos0, lq0, lk0),
        [tok_f, ((npad, C), BF), tok_f] + half_outs,
        [mask],
    )
    lq1, lk1, pos1 = call(
        partial(prep_kernel, 1, rows, across),
        "prep_1",
        0.1,
        8,
        (crops, after(small, part), info, pick),
        label_outs,
        [((128, 128), F32)],
    )
    a1 = to_tp(after(a1q, lq1), "a1")
    a0 = after(a0, lq1)
    a0s = to_win(a0, 0, "a0")
    hid0, qkv01, p01, mix01, small0 = call(
        partial(attn_other_kernel, rows, across),
        "attn_other_0",
        0.1,
        8,
        (part, xn0, a0, a0s, lq0, lk0, pick, info),
        [tok_f] + half_outs + [((SMALL_ROWS, C), F32)],
        other_scratch,
    )
    half_b = ((2, ntok, C), BF)
    st_own, n2f, act00, gp00 = call(
        mlp_own_kernel,
        "mlp_own_0",
        0.1,
        14,
        (hid0, norm_gain, norm_bias, fc1_bias, fc2_bias, fc1_weight, fc2_weight),
        [tok_f, tok_b, half_b, half_b],
    )
    m0 = after(m0, st_own)
    m0s = to_win(m0, 0, "m0")
    st0, act01, gp01, edge = call(
        partial(mlp_other_kernel, across),
        "mlp_other_0",
        3,
        14,
        (st_own, n2f, fc1_bias, small0, m0, m0s, info),
        [tok_f, half_b, half_b, edge_b],
    )
    halo = to_tp(edge, "edge0")
    a1 = after(a1, halo)
    a1s = to_win(a1, 0, "a1")
    cot_edge = to_tp(after(cot_edge, edge), "cot")
    m1 = to_tp(after(m1q, edge), "m1")
    x1, xn1, qkv10 = call(
        partial(norm_kernel, rows, across),
        "norm_1",
        2,
        6,
        (st0, halo, norm_gain, norm_bias, qv_bias, qkv_t),
        [tok_f, ((npad, C), BF), half_outs[0]],
    )
    p10, mix10, qkv11, p11, mix11, small1 = call(
        partial(attn_both_kernel, rows, across),
        "attn_fwd_1",
        10,
        9,
        (xn1, qkv10, pos1, a1, a1s, lq1, lk1, pick, info),
        half_outs[1:] + half_outs + [((SMALL_ROWS, C), F32)],
        other_scratch,
    )
    (hid1,) = call(
        partial(branch_kernel, wins),
        "branch_1",
        1,
        8,
        (x1, mix10, mix11, proj_weight, a1, a1s, proj_bias),
        [tok_f],
    )
    sums = [((4, C), F32), ((3, C), F32)]
    g1, df1, n21, st_own, dz_own, du10, act10, sum10, sf1 = call(
        partial(mlp_own_both_kernel, rows, across),
        "mlp_own_1",
        5,
        14,
        (cotangent[0], after(cot_edge, a1s), hid1, norm_gain, norm_bias, fc1_bias, fc2_bias)
        + (fc1_weight, fc2_weight),
        [tok_f, tok_b, tok_b, tok_f, tok_f, half_b, half_b, ((2, C), F32), ((1, C), F32)],
    )
    m1 = after(m1, dz_own)
    m1s = to_win(m1, 0, "m1")
    st1, gh1, du11, act11, send_m1, gfb1, gsh1, out_edge = call(
        partial(mlp_other_both_kernel, rows, across),
        "mlp_other_1",
        6,
        14,
        (hid1, g1, df1, n21, st_own, dz_own, norm_gain, fc1_bias, small1, m1, m1s, info)
        + (du10, act10, sum10, sf1),
        [tok_f, tok_f, half_b, half_b, ((2, 2 * C, C), BF)] + sums + [edge_b],
    )

    def plus(x, y, name):
        return combine([(x.shape[0], [(0, 0), (1, 0)], True)], None, (x, y), name)[0]

    def pair(keep, got, name):
        shape = keep.shape[1:]
        return call(pair_kernel, name, 1, 4, (keep, got), [(shape, BF), (shape, BF)])

    m1_core = to_win(send_m1, 0, "gm1")
    (keep_m1,) = call(
        mlp_keep_kernel,
        "mlp_keep_1",
        2,
        6,
        (n21, df1, du10, act10, du11, act11, info),
        [((2, 2 * C, C), BF)],
    )
    m1_own, m1_oth = pair(keep_m1, after(m1_core, keep_m1), "pair_m1")
    m1_t = to_tp(m1_oth, "gm1")
    da1, do1, pb1 = call(
        partial(mixed_grad_kernel, wins),
        "mixed_grad_1",
        0.1,
        4,
        (after(gh1, m1_oth), proj_weight, a1, a1s),
        [((npad, C), BF), ((2, npad, 192), BF), ((1, C), F32)],
    )
    gin1, keep_a1, send_a1, edge = call(
        partial(attn_bwd_kernel, rows, across),
        "attn_bwd_1",
        14,
        10,
        (gh1, x1, xn1, norm_gain, qkv_t, a1, a1s, info)
        + (gfb1, gsh1, qkv10, p10, mix10, qkv11, p11, mix11, pick, da1, do1, pb1),
        [tok_f, ((2, na, C), BF), ((2, na, C), BF), edge_b],
        [
            ((3, npad, 192), BF),
            ((3, npad, 192), BF),
            ((2, 3, WPAD, 128), F32),
            mask,
            ((192, C), F32),
            ((4, SMALL, C), F32),
        ],
    )
    halo = to_tp(edge, "edge1")
    a1_core = to_win(after(send_a1, edge), 0, "ga1")
    m1_mine, m1_away = combine(
        [(C, [(0, 0), (1, 0)], True), (C, [(0, C), (1, C)], True)],
        1,
        (m1_own, after(m1_t, edge)),
        "m1_y",
    )
    m1_y = to_win(m1_away, 1, "gm1")
    a1_own, a1_oth = pair(keep_a1, after(a1_core, m1_away), "pair_a1")
    a1_t = to_tp(a1_oth, "ga1")
    g0, df0, keep_f2, send_f2 = call(
        partial(down_grad_kernel, rows, across),
        "down_grad_0",
        4,
        6,
        (gin1, after(halo, a1_oth), act00, act01, info),
        [tok_f, tok_b, ((2, C, C), BF), ((2, C, C), BF)],
    )
    f2_core = to_win(send_f2, 0, "gf2")
    m1_mine, m1_away = combine(
        [(n, [(0, 0), (1, 0)], True), (n, [(0, n), (1, n)], True)],
        2,
        (m1_mine, after(m1_y, send_f2)),
        "m1_z",
    )
    m1_z = to_win(m1_away, 2, "gm1")
    f2_own, f2_oth = pair(keep_f2, after(f2_core, m1_away), "pair_f2")
    f2_t = to_tp(f2_oth, "gf2")
    a1_mine, a1_away = combine(
        [(C, [(0, 0), (1, 0)], True), (SMALL, [(0, C), (1, C)], False)],
        1,
        (a1_own, after(a1_t, f2_oth)),
        "a1_y",
    )
    a1_y = to_win(a1_away, 1, "ga1")
    gh0, n20, du0, send_f1, gfb0, gsh0 = call(
        partial(mlp_bwd_kernel, 0),
        "mlp_bwd_0",
        6,
        12,
        (after(g0, a1_away), df0, hid0, gp00, gp01, norm_gain, norm_bias, fc1_weight, fc2_weight)
        + (m0, m0s, info),
        [tok_f, tok_b, hid_b, ((2, C, C), BF)] + sums,
    )
    f1_core = to_win(send_f1, 0, "gf1")
    (c1,) = combine(
        [(n, [(0, 0), (1, 0)], True), (n + SMALL, [(2, 0), (3, 0)], True)],
        None,
        (m1_mine, after(m1_z, send_f1), a1_mine, after(a1_y, send_f1)),
        "c1",
    )
    c1_b = to_win(c1, 3, "gc1")
    f1_own, f1_oth = call(
        up_keep_kernel, "up_keep_0", 1, 8, (n20, du0, after(f1_core, c1), info),
        [((C, C), BF)] * 2,
    )
    f1_t = to_tp(f1_oth, "gf1")
    da, dqkv0, acc0, dqkv1, pb0, keep_o0, send_o0 = call(
        partial(attn_bwd_heads_kernel, rows, across),
        "attn_bwd_heads_0",
        8,
        12,
        (after(gh0, f1_oth, f2_t), xn0, proj_weight, a0, a0s, gfb0)
        + (qkv00, p00, qkv01, p01, mix01, pick),
        [
            ((npad, C), BF),
            ((3, npad, 192), BF),
            ((3, WPAD, 128), F32),
            ((3, npad, 192), BF),
            ((1, C), F32),
            ((na, C), BF),
            ((na, C), BF),
        ],
        [((2, npad, 192), BF), mask, ((3, WPAD, 128), F32), ((SMALL, C), F32)],
    )
    o0_core = to_win(send_o0, 0, "go0")
    m0_mine, m0_away = combine(
        [(C, [(0, 0), (1, 0)], True), (C, [(2, 0), (3, 0)], True)],
        1,
        (f1_own, after(f1_t, send_o0), f2_own, f2_t),
        "m0_y",
    )
    m0_y = to_win(m0_away, 1, "gm0")
    (o0_sum,) = combine(
        [(na, [(0, 0), (1, 0)], True), (edge_b[0][0], [(2, 0)], True)],
        None,
        (keep_o0, after(o0_core, m0_away), out_edge),
        "o0",
    )
    o0_t = to_tp(o0_sum, "go0")
    c1 = plus(c1, after(c1_b, o0_sum), "c1_sum")
    for bit in range(4, bits):
        c1 = plus(c1, to_win(c1, bit, "gc1"), "c1_sum")
    c1_b = to_win(c1, 2, "gc1")
    grad_tokens, keep_a0, send_a0 = call(
        partial(attn_bwd_own_kernel, rows, across),
        "attn_bwd_own_0",
        9,
        10,
        (gh0, x0, xn0, norm_gain, qkv_t, a0, a0s, info)
        + (gfb0, gsh0, da, dqkv0, acc0, dqkv1, pb0, after(mix00, c1), pick),
        [((rows, cols, 1, C), F32), ((na, C), BF), ((na, C), BF)],
        [tok_f, ((192, C), F32), ((2, SMALL, C), F32)],
    )

    a0_core = to_win(send_a0, 0, "ga0")
    m0_mine, m0_away = combine(
        [(n, [(0, 0), (1, 0)], True), (n, [(0, n), (1, n)], True)],
        2,
        (m0_mine, after(m0_y, send_a0)),
        "m0_z",
    )
    m0_z = to_win(m0_away, 2, "gm0")
    a0_mine, a0_away = combine(
        [(C, [(0, 0), (1, 0), (2, 0)], True), (SMALL, [(0, C), (1, C), (2, C)], False)],
        1,
        (keep_a0, after(a0_core, m0_away), o0_t),
        "a0_y",
    )
    a0_y = to_win(a0_away, 1, "ga0")
    c1, c1_small = call(
        partial(close_kernel, [n // 2] * 2, 2), "c1_close", 1, 8, (c1, after(c1_b, a0_away), info),
        [((3 * n, C), BF), ((SMALL, C), BF)],
    )
    c1_back = to_win(c1, 1, "gc1_back")
    c1_sib = to_win(c1, 0, "gc1_mine")
    c1_small_sib = to_win(c1_small, 0, "gc1_small")
    m0 = plus(m0_mine, after(m0_z, c1), "m0_z2")
    m0_b = to_win(m0, 3, "gm0")
    (layer_out,) = call(
        partial(out_kernel, rows, across), "layer_out", 1, 8, (after(st1, m0), o0_t),
        [((rows, cols, C), BF)],
    )
    a0 = plus(a0_mine, after(a0_y, layer_out), "a0_z")
    a0_z = to_win(a0, 2, "ga0")
    m0 = plus(m0, after(m0_b, a0), "m0_sum")
    for bit in range(4, bits):
        m0 = plus(m0, to_win(m0, bit, "gm0"), "m0_sum")
    m0_b = to_win(m0, 2, "gm0_back")
    a0 = plus(a0, after(a0_z, m0), "a0_z2")
    a0_b = to_win(a0, 3, "ga0")
    c1_back = after(c1_back, a0)
    c1_pieces = (c1, c1_back, c1_sib, to_win(c1_back, 0, "gc1_theirs"))
    m0 = join([n // 2] * 2, 2, m0, after(m0_b, c1_back), "m0_join")
    m0_back = to_win(m0, 1, "gm0_back")
    m0_sib = to_win(m0, 0, "gm0_mine")
    c1_small_sib, c1_pieces = after((c1_small_sib, c1_pieces), m0)
    f1_shape, f2_shape = (2, C, 2 * C), (2, 2 * C, C)
    qkv_shape, proj_shape = (2, 3, 192, C), (2, 192, C)
    whole = [(f1_shape, F32, HBM), (f2_shape, F32, HBM), (qkv_shape, F32, HBM), (proj_shape, F32, HBM)]
    parts = [(x[0][1:], F32) for x in whole]
    attn_parts = [((2, C, C), F32)] + parts[2:]
    g_f1, g_f2, g_qkv, g_proj = call(
        final_second_kernel, "final_second", 1, 20, c1_pieces + (info,), whole,
        parts[:2] + attn_parts + [pltpu.SemaphoreType.DMA((4,))],
    )
    a0 = plus(a0, after(a0_b, g_f1), "a0_sum")
    for bit in range(4, bits):
        a0 = plus(a0, to_win(a0, bit, "ga0"), "a0_sum")
    a0_back = to_win(a0, 1, "ga0_back")
    a0_sib = to_win(a0, 0, "ga0_mine")
    shared = to_tp(a0[n : n + 16], "shared")
    m0_back = after(m0_back, a0_sib)
    m0_pieces = (m0, m0_back, m0_sib, to_win(m0_back, 0, "gm0_theirs"))
    outs = call(
        final_kernel,
        "final",
        0.1,
        16,
        m0_pieces
        + (a0, a0_back, a0_sib, to_win(after(a0_back, shared), 0, "ga0_theirs"), c1_small, c1_small_sib)
        + (shared, info, (g_f1, HBM), (g_f2, HBM), (g_qkv, HBM), (g_proj, HBM)),
        whole
        + [
            ((2, 2, C), F32),
            ((2, 2, C), F32),
            ((2, C), F32),
            ((2, C), F32),
            ((2, 2, 192), F32),
            ((2, 2 * C), F32),
            ((6, 2, 169), F32),
        ],
        parts[:2] + attn_parts + [((2, SMALL, C), F32), pltpu.SemaphoreType.DMA((4,))],
        aliases={12: 0, 13: 1, 14: 2, 15: 3},
    )
    (g_f1, g_f2, g_qkv, g_proj, g_gain, g_bias, g_pb, g_fb2, g_qvb, g_fb1, g_tab) = outs
    return (
        layer_out[None],
        grad_tokens.transpose(2, 0, 1, 3),
        g_gain,
        g_bias,
        g_qkv.transpose(0, 3, 1, 2),
        g_qvb,
        g_proj,
        g_pb,
        g_f1,
        g_fb1,
        g_f2,
        g_fb2,
        g_tab.transpose(1, 2, 0),
    )


def solution(mesh):
    return jax.shard_map(
        partial(on_device, mesh.shape["win"]),
        mesh=mesh,
        in_specs=(
            P("win", "tp", None, None),
            P("win", None, None),
            P("win", "tp", None, None),
            P(),
            P(),
            P(None, None, None, "tp"),
            P(None, None, "tp"),
            P(None, "tp", None),
            P(),
            P(None, None, "tp"),
            P(None, "tp"),
            P(None, "tp", None),
            P(),
            P(None, None, "tp"),
        ),
        out_specs=(
            P("win", "tp", None, None),
            P("win", "tp", None, None),
            P(),
            P(),
            P(None, None, None, "tp"),
            P(None, None, "tp"),
            P(None, "tp", None),
            P(),
            P(None, None, "tp"),
            P(None, "tp"),
            P(None, "tp", None),
            P(),
            P(None, None, "tp"),
        ),
        check_vma=False,
    )
```

```python
from functools import partial

import jax
import jax.numpy as jnp
import numpy as np
from jax import lax
from jax.experimental import pallas as pl
from jax.experimental.pallas import tpu as pltpu
from jax.sharding import PartitionSpec as P

C = 384
WIN = 7
SHIFT = 3
HD = 32
EPS = 1e-05
NEG = -1000000000.0
SCALE = HD**-0.5
F32 = jnp.float32
BF = jnp.bfloat16
SEG = 8
WROWS = WIN * SEG
WPAD = 64


def nn(a, b):
    return lax.dot_general(a, b, (((1,), (0,)), ((), ())), preferred_element_type=F32)


def nt(a, b):
    return lax.dot_general(a, b, (((1,), (1,)), ((), ())), preferred_element_type=F32)


def tn(a, b):
    return lax.dot_general(a, b, (((0,), (0,)), ((), ())), preferred_element_type=F32)


def norm_stats(x):
    mean = jnp.mean(x, -1, keepdims=True)
    cent = x - mean
    var = jnp.mean(cent * cent, -1, keepdims=True)
    rinv = lax.rsqrt(var + EPS)
    return cent * rinv, rinv


def norm_back(dz, xhat, rinv, gain):
    d = dz * gain
    return rinv * (
        d - jnp.mean(d, -1, keepdims=True) - xhat * jnp.mean(d * xhat, -1, keepdims=True)
    )


def tile_row(r, k, across):
    return (((r // WIN) * across + k) * WIN + r % WIN) * SEG


def zero_rows(n):
    return jnp.zeros((n, C), F32)


def head_mask():
    row = lax.broadcasted_iota(jnp.int32, (6 * WPAD, 6 * HD), 0) // WPAD
    col = lax.broadcasted_iota(jnp.int32, (6 * WPAD, 6 * HD), 1) // HD
    return (row == col).astype(BF)


def spread(x, mask):
    return jnp.concatenate([x] * 6, axis=0) * mask


def fold(o):
    lane = lax.broadcasted_iota(jnp.int32, (WPAD, 128), 1)

    def of(h, a, b):
        return o[WPAD * h : WPAD * (h + 1), a:b]

    one = jnp.where(lane < 96, of(2, 0, 128), of(3, 0, 128))
    one = jnp.where(lane < 64, of(1, 0, 128), one)
    one = jnp.where(lane < 32, of(0, 0, 128), one)
    two = jnp.where(lane[:, :64] < 32, of(4, 128, 192), of(5, 128, 192))
    return jnp.concatenate([one, two], axis=1)


def rows_at(i, n):
    return pl.ds(i * n, n)


def repeat(n, body, carry):
    for i in range(n):
        carry = body(i, carry)
    return carry


def iota(shape, dim):
    return lax.broadcasted_iota(jnp.int32, shape, dim)


def exact(a, b, ca, cb):
    return lax.dot_general(
        a,
        b,
        (((ca,), (cb,)), ((), ())),
        precision=lax.Precision.HIGHEST,
        preferred_element_type=F32,
    )


def offset_rows():
    return (12 - iota((16, 169), 0) == iota((16, 169), 1) // 13).astype(F32)


def offset_cols():
    return (iota((96, 169), 0) % 16 == iota((96, 169), 1) % 13).astype(F32)


def column_pick(kx):
    r = iota((96, 6 * WPAD), 0)
    c = iota((96, 6 * WPAD), 1)
    qx = c % 8
    return ((r // 16 == c // WPAD) & (r % 16 == qx - kx + WIN - 1) & (qx < WIN)).astype(BF)


def table_to_map(t, pick_ref, pos_ref):
    pos_ref[...] = jnp.zeros_like(pos_ref)
    group = (iota((8, 6 * WPAD), 1) % WPAD) // 8
    high = t.astype(BF)
    low = (t - high.astype(F32)).astype(BF)
    both = jnp.concatenate([high, low], axis=0)
    for kx in range(WIN):
        h = nn(both, pick_ref[kx])
        h = h[:16] + h[16:]
        g = jnp.zeros((8, 6 * WPAD), F32)
        for j in range(WIN):
            g = jnp.where(group == j, h[6 - j : 14 - j], g)
        for i in range(3):
            pos_ref[i, pl.ds(kx, 8, stride=8), :] = g[:, 128 * i : 128 * (i + 1)]


def map_to_table(pos_ref, pick_ref):
    group = (iota((16, 6 * WPAD), 1) % WPAD) // 8
    total = jnp.zeros((16, 96), F32)
    for kx in range(WIN):
        r = jnp.concatenate([pos_ref[i, pl.ds(kx, 8, stride=8), :] for i in range(3)], axis=1)
        h = jnp.zeros((16, 6 * WPAD), F32)
        for j in range(WIN):
            parts = [r, jnp.zeros((2 + j, 6 * WPAD), F32)]
            if j < 6:
                parts = [jnp.zeros((6 - j, 6 * WPAD), F32)] + parts
            h = jnp.where(group == j, jnp.concatenate(parts, axis=0), h)
        total = total + nt(h.astype(BF), pick_ref[kx])
    return total


def shift_in(tile, x_ref, rows, across):
    for r in range(rows):
        for k in range(across):
            a = tile(r + SHIFT, k)
            b = tile(r + SHIFT, (k + 1) % across)
            x_ref[pl.ds(tile_row(r, k, across), SEG), :] = jnp.concatenate(
                [a[SHIFT:WIN], b[:SHIFT], zero_rows(1)], axis=0
            )


def shift_out(tile, x_ref, rows, across):
    for r in range(rows):
        for k in range(across):
            a = tile(r - SHIFT, (k - 1) % across)
            b = tile(r - SHIFT, k)
            x_ref[pl.ds(tile_row(r, k, across), SEG), :] = jnp.concatenate(
                [a[WIN - SHIFT : WIN], b[: WIN - SHIFT], zero_rows(1)], axis=0
            )

EDGE_ROWS = 96
SMALL = 32


SMALL_ROWS = 24
SENT_ROWS = 8


def copies_of(pairs, sems):
    copies = [pltpu.make_async_copy(x, y, sems.at[n]) for n, (x, y) in enumerate(pairs)]
    for copy in copies:
        copy.start()
    return copies


def attn_copies(layer, par, qkvw_ref, projw_ref, a_ref):
    of_heads = pl.ds(pl.multiple_of(par * 96, 96), 96)
    pairs = [
        (qkvw_ref.at[layer, j, of_heads, :], a_ref.at[pl.ds(96 * j, 96), :]) for j in range(3)
    ]
    return pairs + [(projw_ref.at[layer, of_heads, :], a_ref.at[pl.ds(288, 96), :])]


def mlp_copies(layer, par, f1_ref, f2_ref, m_ref):
    of_units = pl.ds(pl.multiple_of(par * C, C), C)
    return [
        (f1_ref.at[layer, :, of_units], m_ref.at[pl.ds(0, C), :]),
        (f2_ref.at[layer, of_units, :], m_ref.at[pl.ds(C, C), :]),
    ]


def high_low(x):
    rows = []
    for r in range(4):
        rows.append(jnp.concatenate([x[4 * r + k : 4 * r + k + 1, 0:96] for k in range(4)], axis=1))
    rows.append(x[16:18])
    rows.append(jnp.concatenate([x[18:19, 0:192], x[19:20, 0:192]], axis=1))
    rows.append(zero_rows(1))
    x = jnp.concatenate(rows, axis=0)
    high = x.astype(BF).astype(F32)
    return jnp.concatenate([high, x - high], axis=0).astype(BF)


def pack_first_kernel(
    qkvw_ref, projw_ref, tab_ref, qvb_ref, fb1_ref,
    a0_ref, small_ref, tab_v, qvb_v, fb1_v, sems
):
    pairs = [(tab_ref, tab_v), (qvb_ref, qvb_v), (fb1_ref, fb1_v)]
    copies = copies_of(pairs + attn_copies(0, POSITION[0], qkvw_ref, projw_ref, a0_ref), sems)
    small_ref[...] = jnp.zeros_like(small_ref)
    for copy in copies[:3]:
        copy.wait()
    for layer in range(2):
        tab = tab_v[:, layer, :]
        wide = jnp.concatenate([jnp.broadcast_to(tab[h : h + 1], (16, 169)) for h in range(6)])
        small_ref[layer, 0:16, 0:96] = exact(offset_rows(), wide * offset_cols(), 1, 1)
        small_ref[layer, 16:17, :] = fb1_v[layer : layer + 1, 0:C]
        small_ref[layer, 17:18, :] = fb1_v[layer : layer + 1, C:]
        small_ref[layer, 18:20, 0:192] = qvb_v[layer]
    a0_ref[C:, :] = high_low(small_ref[0])
    for copy in copies[3:]:
        copy.wait()


def pack_kernel(
    qkvw_ref, projw_ref, f1_ref, f2_ref, cot_ref, small_ref, info_ref,
    m0_ref, a1_ref, m1_ref, edge_ref, cot_v, sems
):
    par = info_ref[0]
    pairs = [(cot_ref.at[pl.ds(0, SHIFT)], cot_v)]
    pairs += mlp_copies(0, par, f1_ref, f2_ref, m0_ref)
    pairs += attn_copies(1, par, qkvw_ref, projw_ref, a1_ref)
    pairs += mlp_copies(1, par, f1_ref, f2_ref, m1_ref)
    copies = copies_of(pairs, sems)
    a1_ref[C:, :] = high_low(small_ref[1])
    copies[0].wait()
    edge = [cot_v[r].astype(F32) for r in range(SHIFT)]
    n = EDGE_ROWS - SHIFT * cot_v.shape[1]
    edge_ref[...] = jnp.concatenate(edge + [zero_rows(n)], axis=0).astype(BF)
    for copy in copies[1:]:
        copy.wait()


def small_of(a_ref, small_ref):
    rows = a_ref[C : C + 2 * SENT_ROWS, :].astype(F32)
    x = rows[0:SENT_ROWS] + rows[SENT_ROWS:]
    small_ref[...] = jnp.zeros_like(small_ref)
    for r in range(4):
        for k in range(4):
            small_ref[4 * r + k : 4 * r + k + 1, 0:96] = x[r : r + 1, 96 * k : 96 * (k + 1)]
    small_ref[16:18, :] = x[4:6]
    small_ref[18:19, 0:192] = x[6:7, 0:192]
    small_ref[19:20, 0:192] = x[6:7, 192:384]


def edge_tile(edge, k, r):
    at = (k * SHIFT + r) * SEG
    return edge[at : at + SEG]


def edge_rows(ref, across, rows):
    tiles = [ref[pl.ds(tile_row(r, k, across), SEG), :] for k in range(across) for r in rows]
    return jnp.concatenate(tiles, axis=0).astype(BF)


def prep_kernel(layer, rows, across, *refs):
    (crop_ref, small_ref, info_ref) = refs[:3]
    if layer == 0:
        (lq_ref, lk_ref, pos_ref, pick_ref, c_ref) = refs[3:]
        for kx in range(WIN):
            pick_ref[kx] = column_pick(kx)
    else:
        (pick_ref, lq_ref, lk_ref, pos_ref, c_ref) = refs[3:]
    tp = info_ref[1]
    cols = across * WIN
    height = crop_ref.shape[2]
    table_to_map(small_ref[layer, 0:16, 0:96], pick_ref, pos_ref)
    c_ref[...] = jnp.zeros_like(c_ref)
    c_ref[0:cols, 0:height] = crop_ref[:, 0, :].astype(F32)
    crops = c_ref[...].astype(BF)
    row = iota((32, 128), 0)
    lane = iota((32, 128), 1)
    shift = SHIFT if layer == 1 else 0
    src = rows * tp + row + shift
    src = jnp.where(src >= height, src - height, src)
    grid = nt((src == lane).astype(BF), crops).astype(BF)
    labs = []
    for wc in range(across):
        qx = iota((128, 128), 1) % 8
        col = qx + (WIN * wc + shift)
        col = jnp.where(col >= cols, col - cols, col)
        pick = ((col == iota((128, 128), 0)) & (qx < WIN)).astype(BF)
        lab = nn(grid, pick)
        if layer == 1:
            g = rows * tp + row
            zr = (g >= height - WIN).astype(F32) + (g >= height - SHIFT).astype(F32)
            here = lane % 8 + WIN * wc
            zc = (here >= cols - WIN).astype(F32) + (here >= cols - SHIFT).astype(F32)
            lab = lab * 9.0 + zr * 3.0 + zc
        labs.append(lab)
    real = (iota((1, 128), 1) % 8 < WIN) & (iota((1, 128), 1) % WPAD < WROWS)
    for wr in range(rows // WIN):
        lines = []
        for wc in range(across):
            w = wr * across + wc
            mine = row == (lane % WPAD) // 8 + WIN * wr
            line = jnp.sum(jnp.where(mine, labs[wc], 0.0), 0, keepdims=True)
            line = jnp.where(real, line, -1.0)
            lq_ref[w : w + 1, :] = line
            lines.append(line)
        for wc in range(0, across, 2):
            w = wr * across + wc
            both = jnp.where(iota((1, 128), 1) < WPAD, lines[wc], lines[wc + 1])
            both = jnp.broadcast_to(both, (128, 128)).T
            lk_ref[w] = both[:WPAD]
            lk_ref[w + 1] = both[WPAD:]


def qkv_weight_of(half, j, layer, qkvw_ref, a_ref, b_ref):
    if half == 0:
        return qkvw_ref[layer, j]
    return jnp.concatenate([a_ref[96 * j : 96 * (j + 1)], b_ref[96 * j : 96 * (j + 1)]], axis=0)


def proj_weight_of(half, layer, projw_ref, a_ref, b_ref):
    if half == 0:
        return projw_ref[layer]
    return jnp.concatenate([a_ref[288:384], b_ref[288:384]], axis=0)


def norm_windows(layer, wins, x_ref, xn_ref, gain_ref, bias_ref):
    gain = gain_ref[layer, 0:1]
    bias = bias_ref[layer, 0:1]

    def four(i, carry):
        xhat, _ = norm_stats(x_ref[rows_at(i, 4 * WROWS), :])
        xn = xhat * gain + bias
        for n in range(4):
            part = jnp.concatenate(
                [xn[n * WROWS : (n + 1) * WROWS], zero_rows(WPAD - WROWS)], axis=0
            )
            xn_ref[rows_at(4 * i + n, WPAD), :] = part.astype(BF)
        return carry

    repeat(wins // 4, four, 0)


def project_half(xn_ref, qkv_ref, weight, qb, vb):
    n = xn_ref.shape[0]

    def part(i, carry):
        at = rows_at(i, n)
        xn = xn_ref[at, :]
        q = nt(xn, weight(0))
        k = nt(xn, weight(1))
        v = nt(xn, weight(2))
        qkv_ref[0, at, :] = ((q + qb) * SCALE).astype(BF)
        qkv_ref[1, at, :] = k.astype(BF)
        qkv_ref[2, at, :] = (v + vb).astype(BF)
        return carry

    repeat(1, part, 0)


def attend_forward(halves, wins, group, lq_ref, lk_ref, mask_ref):
    def body(i, carry):
        units = [(i * group + u, h) for u in range(group) for h in halves]
        scores = []
        for w, (qkv_ref, _, _, _) in units:
            at = rows_at(w, WPAD)
            scores.append(nt(qkv_ref[1, at, :], spread(qkv_ref[0, at, :], mask_ref[...])))
        probs = []
        for (w, (_, pos, p_ref, _)), s in zip(units, scores):
            same = lk_ref[w] == lq_ref[pl.ds(w, 1), :]
            same = jnp.concatenate([same] * 3, axis=1)
            s = jnp.where(same, s + jnp.concatenate([pos[n] for n in range(3)], axis=1), NEG)
            e = jnp.exp(s - jnp.max(s, 0, keepdims=True))
            p = (e * (1.0 / jnp.sum(e, 0, keepdims=True))).astype(BF)
            p_ref[w] = p
            probs.append(p)
        for (w, (qkv_ref, _, _, mix_ref)), p in zip(units, probs):
            at = rows_at(w, WPAD)
            mix_ref[at, :] = fold(tn(p, qkv_ref[2, at, :])).astype(BF)
        return carry

    repeat(wins // group, body, 0)


def add_branch(wins, mixes, weights, bias, x_ref, hid_ref):
    n = 8

    def part(i, carry):
        res = bias
        for m_ref, w in zip(mixes, weights):
            res = res + nn(m_ref[rows_at(i, n * WPAD), :], w)
        for k in range(n):
            to = rows_at(i * n + k, WROWS)
            hid_ref[to, :] = x_ref[to, :] + res[k * WPAD : k * WPAD + WROWS]
        return carry

    repeat(wins // n, part, 0)


def attn_own_kernel(rows, across, *refs):
    (tok_ref, gain_ref, bias_ref, pb_ref, qvb_ref, qkvw_ref, projw_ref) = refs[:7]
    (pos_ref, lq_ref, lk_ref) = refs[7:10]
    (xb_ref, xn_ref, hid_ref, qkv_ref, p_ref, mix_ref, mask_ref, x_ref) = refs[10:]
    wins = (rows // WIN) * across
    for r in range(rows):
        row = tok_ref[r].astype(F32)
        for k in range(across):
            x_ref[pl.ds(tile_row(r, k, across), SEG), :] = jnp.concatenate(
                [row[WIN * k : WIN * (k + 1)], zero_rows(1)], axis=0
            )
    xb_ref[...] = x_ref[...].astype(BF)
    mask_ref[...] = head_mask()
    norm_windows(0, wins, x_ref, xn_ref, gain_ref, bias_ref)
    project_half(
        xn_ref, qkv_ref, lambda j: qkvw_ref[0, j], qvb_ref[0, 0:1], qvb_ref[0, 1:2]
    )
    attend_forward(
        [(qkv_ref, pos_ref, p_ref, mix_ref)], wins, wins, lq_ref, lk_ref, mask_ref
    )
    add_branch(wins, [mix_ref], [projw_ref[0]], pb_ref[0:1], x_ref, hid_ref)


def attn_other_kernel(rows, across, *refs):
    (part_ref, xn_ref, a_ref, b_ref, lq_ref, lk_ref, pick_ref, info_ref) = refs[:8]
    (hid_ref, qkv_ref, p_ref, mix_ref, small_ref, mask_ref, pos_ref) = refs[8:]
    small_of(a_ref, small_ref)
    wins = (rows // WIN) * across
    mask_ref[...] = head_mask()
    bias = other_small(small_ref, info_ref[0], pick_ref, pos_ref)
    project_half(
        xn_ref,
        qkv_ref,
        lambda j: qkv_weight_of(1, j, 0, None, a_ref, b_ref),
        bias[0:1],
        bias[1:2],
    )
    attend_forward([(qkv_ref, pos_ref, p_ref, mix_ref)], wins, wins, lq_ref, lk_ref, mask_ref)
    add_branch(
        wins, [mix_ref], [proj_weight_of(1, 0, None, a_ref, b_ref)], 0.0, part_ref, hid_ref
    )


def other_small(small_ref, par, pick_ref, pos_ref):
    first = par == 0

    def swapped(v, n):
        return jnp.where(first, v, jnp.concatenate([v[:, n : 2 * n], v[:, :n]], axis=1))

    t = swapped(small_ref[0:16, 0:96], 48)
    table_to_map(t, pick_ref, pos_ref)
    return swapped(small_ref[18:20, 0:192], 96)


def norm_kernel(rows, across, *refs):
    (st_ref, halo_ref, gain_ref, bias_ref, qvb_ref, qkvw_ref) = refs[:6]
    (x_ref, xn_ref, qkv_ref) = refs[6:]

    def tile(r, k):
        if r < rows:
            return st_ref[pl.ds(tile_row(r, k, across), SEG), :]
        return edge_tile(halo, k, r - rows)

    halo = halo_ref[...].astype(F32)
    shift_in(tile, x_ref, rows, across)
    norm_windows(1, (rows // WIN) * across, x_ref, xn_ref, gain_ref, bias_ref)
    project_half(
        xn_ref, qkv_ref, lambda j: qkvw_ref[1, j], qvb_ref[1, 0:1], qvb_ref[1, 1:2]
    )


def attn_both_kernel(rows, across, *refs):
    (xn_ref, qkv0_ref, pos_ref, a_ref, b_ref) = refs[:5]
    (lq_ref, lk_ref, pick_ref, info_ref) = refs[5:9]
    (p0_ref, mix0_ref, qkv1_ref, p1_ref, mix1_ref, small_ref, mask_ref, pos1_ref) = refs[9:]
    wins = (rows // WIN) * across
    mask_ref[...] = head_mask()
    small_of(a_ref, small_ref)
    bias = other_small(small_ref, info_ref[0], pick_ref, pos1_ref)
    project_half(
        xn_ref,
        qkv1_ref,
        lambda j: qkv_weight_of(1, j, 1, None, a_ref, b_ref),
        bias[0:1],
        bias[1:2],
    )
    attend_forward(
        [(qkv0_ref, pos_ref, p0_ref, mix0_ref), (qkv1_ref, pos1_ref, p1_ref, mix1_ref)],
        wins,
        wins,
        lq_ref,
        lk_ref,
        mask_ref,
    )


def branch_kernel(wins, x_ref, mix0_ref, mix1_ref, projw_ref, a_ref, b_ref, pb_ref, hid_ref):
    add_branch(
        wins,
        [mix0_ref, mix1_ref],
        [projw_ref[1], proj_weight_of(1, 1, None, a_ref, b_ref)],
        pb_ref[1:2],
        x_ref,
        hid_ref,
    )


def up_weight(part, layer, base, f1_ref, a_ref, b_ref):
    if part == 0:
        return f1_ref[layer]
    return jnp.concatenate([a_ref[base : base + C], b_ref[base : base + C]], axis=1)


def down_weight(part, layer, base, f2_ref, a_ref, b_ref):
    if part == 0:
        return f2_ref[layer]
    return jnp.concatenate([a_ref[base + C : base + 2 * C], b_ref[base + C : base + 2 * C]], axis=0)


def up_biases(layer, par, fb1_ref, small_ref):
    own = fb1_ref[layer : layer + 1]
    one, two = small_ref[16:17], small_ref[17:18]
    first = par == 0
    return own, jnp.concatenate(
        [jnp.where(first, one, two), jnp.where(first, two, one)], axis=1
    )


def gelu_pair(u):
    phi = 0.5 + 0.5 * lax.erf(u * (2.0**-0.5))
    slope = phi + u * (jnp.exp(-0.5 * u * u) * (2.0 * np.pi) ** -0.5)
    return (u * phi).astype(BF), slope.astype(BF)


def mlp_own_kernel(hid_ref, gain_ref, bias_ref, fb1_ref, fb2_ref, f1_ref, f2_ref, st_ref, n2_ref, act_ref, gp_ref):
    h = hid_ref[...]
    xhat, _ = norm_stats(h)
    n2 = (xhat * gain_ref[0, 1:2] + bias_ref[0, 1:2]).astype(BF)
    n2_ref[...] = n2
    act, slope = gelu_pair(nn(n2, f1_ref[0]) + fb1_ref[0:1])
    for z in range(2):
        act_ref[z] = act[:, C * z : C * (z + 1)]
        gp_ref[z] = slope[:, C * z : C * (z + 1)]
    st_ref[...] = h + fb2_ref[0:1] + nn(act, f2_ref[0])


def mlp_other_kernel(
    across, part_ref, n2_ref, fb1_ref, small_ref, a_ref, b_ref, info_ref, st_ref, act_ref, gp_ref,
    edge_ref
):
    _, bias = up_biases(0, info_ref[0], fb1_ref, small_ref)
    act, slope = gelu_pair(nn(n2_ref[...], up_weight(1, 0, 0, None, a_ref, b_ref)) + bias)
    for z in range(2):
        act_ref[z] = act[:, C * z : C * (z + 1)]
        gp_ref[z] = slope[:, C * z : C * (z + 1)]
    st_ref[...] = part_ref[...] + nn(act, down_weight(1, 0, 0, None, a_ref, b_ref))
    edge_ref[...] = edge_rows(st_ref, across, range(SHIFT))


def quarter_of(par, slot, part):
    return (par ^ slot) if part == 0 else 2 + slot


BLOCKS = 2


def half_sums(du, ref):
    for z in range(2):
        ref[z : z + 1] += jnp.sum(du[z].astype(F32), 0, keepdims=True)


def mlp_own_both_kernel(rows, across, *refs):
    (cot_ref, edge_ref, hid_ref, gain_ref, bias_ref, fb1_ref, fb2_ref, f1_ref, f2_ref) = refs[:9]
    (g_ref, df_ref, n2_ref, st_ref, dz_ref, du_ref, act_ref, sum_ref, sf_ref) = refs[9:]
    layer = 1
    cols = across * WIN
    cot_edge = edge_ref[...].astype(F32)
    for r in range(rows):
        s = r + SHIFT
        if s < rows:
            row = cot_ref[s].astype(F32)
        else:
            row = cot_edge[(s - rows) * cols : (s - rows + 1) * cols]
        for k in range(across):
            a = WIN * k + SHIFT
            if k < across - 1:
                piece = [row[a : a + WIN]]
            else:
                piece = [row[a:], row[:SHIFT]]
            g_ref[pl.ds(tile_row(r, k, across), SEG), :] = jnp.concatenate(
                piece + [zero_rows(1)], axis=0
            )
    sum_ref[...] = jnp.zeros_like(sum_ref)
    sf_ref[...] = jnp.zeros_like(sf_ref)
    n = hid_ref.shape[0] // BLOCKS

    def block(i, carry):
        at = pl.ds(pl.multiple_of(i * n, n), n)
        h = hid_ref[at, :]
        xhat, _ = norm_stats(h)
        n2 = (xhat * gain_ref[layer, 1:2] + bias_ref[layer, 1:2]).astype(BF)
        n2_ref[at, :] = n2
        df = g_ref[at, :].astype(BF)
        df_ref[at, :] = df
        sf_ref[...] += jnp.sum(df.astype(F32), 0, keepdims=True)
        up = nn(n2, f1_ref[layer]) + fb1_ref[layer : layer + 1]
        grad = nt(df, f2_ref[layer])
        act, slope = gelu_pair(up)
        du = (grad * slope.astype(F32)).astype(BF)
        parts = [du[:, C * z : C * (z + 1)] for z in range(2)]
        for z in range(2):
            act_ref[z, at, :] = act[:, C * z : C * (z + 1)]
            du_ref[z, at, :] = parts[z]
        half_sums(parts, sum_ref)
        st_ref[at, :] = h + fb2_ref[layer : layer + 1] + nn(act, f2_ref[layer])
        dz_ref[at, :] = nt(du, f1_ref[layer])
        return carry

    lax.fori_loop(0, BLOCKS, block, 0)


def mlp_other_both_kernel(rows, across, *refs):
    (hid_ref, g_ref, df_ref, n2_ref, part_ref, dzp_ref, gain_ref, fb1_ref, small_ref) = refs[:9]
    (a_ref, b_ref, info_ref, sumo_ref, sf_ref) = refs[9:14]
    (st_ref, gh_ref, du_ref, act_ref, send_ref, sum_ref, sh_ref, edge_ref) = refs[14:]
    layer = 1
    par = info_ref[0]
    _, bias = up_biases(layer, par, fb1_ref, small_ref)
    w1 = up_weight(1, layer, 0, None, a_ref, b_ref)
    w2 = down_weight(1, layer, 0, None, a_ref, b_ref)
    sum_ref[0:2] = sumo_ref[...]
    sum_ref[2:4] = jnp.zeros((2, C), F32)
    sh_ref[0:2] = jnp.zeros((2, C), F32)
    sh_ref[2:3] = sf_ref[...]
    n = hid_ref.shape[0] // BLOCKS

    def block(i, carry):
        at = pl.ds(pl.multiple_of(i * n, n), n)
        up = nn(n2_ref[at, :], w1) + bias
        grad = nt(df_ref[at, :], w2)
        act, slope = gelu_pair(up)
        du = (grad * slope.astype(F32)).astype(BF)
        parts = [du[:, C * z : C * (z + 1)] for z in range(2)]
        for z in range(2):
            act_ref[z, at, :] = act[:, C * z : C * (z + 1)]
            du_ref[z, at, :] = parts[z]
        half_sums(parts, sum_ref.at[2:4])
        st_ref[at, :] = part_ref[at, :] + nn(act, w2)
        dz = dzp_ref[at, :] + nt(du, w1)
        xhat, rinv = norm_stats(hid_ref[at, :])
        sh_ref[0:1] += jnp.sum(dz * xhat, 0, keepdims=True)
        sh_ref[1:2] += jnp.sum(dz, 0, keepdims=True)
        gh_ref[at, :] = g_ref[at, :] + norm_back(dz, xhat, rinv, gain_ref[layer, 1:2])
        return carry

    lax.fori_loop(0, BLOCKS, block, 0)
    edge_ref[...] = edge_rows(st_ref, across, range(rows - SHIFT, rows))
    n2 = n2_ref[...]
    df = df_ref[...]
    send_ref[0:C, :] = tn(n2, du_ref[1]).astype(BF)
    send_ref[C:, :] = tn(act_ref[1], df).astype(BF)


def own_grads_kernel(n2_ref, df_ref, du_ref, act_ref, info_ref, keep_ref, send_ref):
    n2 = n2_ref[...]
    df = df_ref[...]
    for slot, ref in ((1, send_ref), (0, keep_ref)):
        q = info_ref[0] ^ slot
        ref[0:C, :] = tn(n2, du_ref[q]).astype(BF)
        ref[C:, :] = tn(act_ref[q], df).astype(BF)


def mlp_keep_kernel(n2_ref, df_ref, du_ref, act_ref, keep_ref):
    keep_ref[0:C, :] = tn(n2_ref[...], du_ref[0]).astype(BF)
    keep_ref[C:, :] = tn(act_ref[0], df_ref[...]).astype(BF)


def up_keep_kernel(n2_ref, du_ref, keep_ref):
    keep_ref[...] = tn(n2_ref[...], du_ref[0]).astype(BF)


def down_grad_kernel(rows, across, *refs):
    (gin_ref, halo_ref, act0_ref, act1_ref, info_ref, g_ref, df_ref, keep_ref, send_ref) = refs

    def tile(r, k):
        if r >= 0:
            return gin_ref[pl.ds(tile_row(r, k, across), SEG), :]
        return edge_tile(halo, k, r + SHIFT)

    halo = halo_ref[...].astype(F32)
    shift_out(tile, g_ref, rows, across)
    df = g_ref[...].astype(BF)
    df_ref[...] = df
    for slot, ref in ((1, send_ref), (0, keep_ref)):
        ref[1] = tn(act1_ref[slot], df).astype(BF)
        ref[0] = tn(act0_ref[info_ref[0] ^ slot], df).astype(BF)


def mlp_bwd_own_kernel(*refs):
    (df_ref, gp_ref, n2_ref, f1_ref, f2_ref, info_ref) = refs[:6]
    (dz_ref, sum_ref, keep_ref, send_ref, du_ref) = refs[6:]
    grad = nt(df_ref[...], f2_ref[0])
    parts = [
        (grad[:, C * z : C * (z + 1)] * gp_ref[z].astype(F32)).astype(BF) for z in range(2)
    ]
    for z in range(2):
        du_ref[z] = parts[z]
    sum_ref[...] = jnp.zeros_like(sum_ref)
    half_sums(parts, sum_ref)
    dz_ref[...] = nt(jnp.concatenate(parts, axis=1), f1_ref[0])
    n2 = n2_ref[...]
    for slot, ref in ((1, send_ref), (0, keep_ref)):
        ref[...] = tn(n2, du_ref[info_ref[0] ^ slot]).astype(BF)


def mlp_bwd_other_kernel(*refs):
    (g_ref, df_ref, hid_ref, n2_ref, gp_ref, dzp_ref, gain_ref, a_ref, b_ref, sumo_ref) = refs[:10]
    (gh_ref, du_ref, send_ref, sum_ref, sh_ref) = refs[10:]
    df = df_ref[...]
    grad = nt(df, down_weight(1, 0, 0, None, a_ref, b_ref))
    parts = [
        (grad[:, C * z : C * (z + 1)] * gp_ref[z].astype(F32)).astype(BF) for z in range(2)
    ]
    for z in range(2):
        du_ref[z] = parts[z]
    sum_ref[0:2] = sumo_ref[...]
    sum_ref[2:4] = jnp.zeros((2, C), F32)
    half_sums(parts, sum_ref.at[2:4])
    dz = dzp_ref[...] + nt(jnp.concatenate(parts, axis=1), up_weight(1, 0, 0, None, a_ref, b_ref))
    xhat, rinv = norm_stats(hid_ref[...])
    sh_ref[0:1] = jnp.sum(dz * xhat, 0, keepdims=True)
    sh_ref[1:2] = jnp.sum(dz, 0, keepdims=True)
    sh_ref[2:3] = jnp.sum(df.astype(F32), 0, keepdims=True)
    gh_ref[...] = g_ref[...] + norm_back(dz, xhat, rinv, gain_ref[0, 1:2])
    send_ref[...] = tn(n2_ref[...], du_ref[1]).astype(BF)


def window_grads(wins, gh_ref, da_ref):
    def four(i, s):
        g = gh_ref[rows_at(i, 4 * WROWS), :]
        for n in range(4):
            part = jnp.concatenate(
                [g[n * WROWS : (n + 1) * WROWS], zero_rows(WPAD - WROWS)], axis=0
            ).astype(BF)
            da_ref[rows_at(4 * i + n, WPAD), :] = part
            s = s + jnp.sum(part.astype(F32), 0, keepdims=True)
        return s

    return repeat(wins // 4, four, jnp.zeros((1, C), F32))


def attend_backward(halves, wins, group, mask_ref):
    def body(i, carry):
        units = [(i * group + u, h) for u in range(group) for h in halves]
        first = []
        for w, (qkv_ref, p_ref, do_ref, dqkv_ref, _) in units:
            at = rows_at(w, WPAD)
            do = spread(do_ref[at, :], mask_ref[...])
            first.append(nt(qkv_ref[2, at, :], do))
            dqkv_ref[2, at, :] = nn(p_ref[w], do).astype(BF)
        second = []
        for (w, (_, p_ref, _, _, acc_ref)), dp in zip(units, first):
            p = p_ref[w].astype(F32)
            ds = p * (dp - jnp.sum(p * dp, 0, keepdims=True))
            for n in range(3):
                acc_ref[n] += ds[:, 128 * n : 128 * (n + 1)]
            second.append(ds.astype(BF))
        for (w, (qkv_ref, _, _, dqkv_ref, _)), ds in zip(units, second):
            at = rows_at(w, WPAD)
            dqkv_ref[1, at, :] = nn(ds, spread(qkv_ref[0, at, :], mask_ref[...])).astype(BF)
            dqkv_ref[0, at, :] = fold(tn(ds, qkv_ref[1, at, :])).astype(BF)
        return carry

    repeat(wins // group, body, 0)


def half_grads(half, par, xn_ref, da_ref, mix_ref, dqkv_ref, row_ref, give):
    def put(value, at):
        if half == 0:
            row_ref[...] = value
            one = row_ref[pl.ds(pl.multiple_of(par * 96, 96), 96), :]
            two = row_ref[pl.ds(pl.multiple_of((1 - par) * 96, 96), 96), :]
        else:
            one, two = value[:96], value[96:]
        give(at, one.astype(BF), two.astype(BF))

    xn = xn_ref[...]
    for j in range(3):
        grad = tn(dqkv_ref[j], xn)
        put(grad * SCALE if j == 0 else grad, 96 * j)
    put(tn(mix_ref[...], da_ref[...]), 288)


def normed_grads(layer, wins, dqkvs, weights, gh_ref, x_ref, gain_ref, gx_ref):
    gain = gain_ref[layer, 0:1]
    n = 8

    def part(i, carry):
        sg, sb, sq = carry
        at = rows_at(i, n * WPAD)
        dn = nn(dqkvs[0][0, at, :], weights[0](0)) + nn(dqkvs[1][0, at, :], weights[1](0))
        dn = dn * SCALE
        for half in range(2):
            for j in (1, 2):
                dn = dn + nn(dqkvs[half][j, at, :], weights[half](j))
        new = []
        for half in range(2):
            for m, j in enumerate((0, 2)):
                new.append(
                    sq[half * 2 + m] + jnp.sum(dqkvs[half][j, at, :].astype(F32), 0, keepdims=True)
                )
        d = jnp.concatenate([dn[k * WPAD : k * WPAD + WROWS] for k in range(n)], axis=0)
        to = rows_at(i, n * WROWS)
        xhat, rinv = norm_stats(x_ref[to, :].astype(F32))
        sg = sg + jnp.sum(d * xhat, 0, keepdims=True)
        sb = sb + jnp.sum(d, 0, keepdims=True)
        gx_ref[to, :] = gh_ref[to, :] + norm_back(d, xhat, rinv, gain)
        return sg, sb, tuple(new)

    z = jnp.zeros((1, C), F32)
    zq = jnp.zeros((1, 6 * HD), F32)
    return repeat(wins // n, part, (z, z, (zq,) * 4))


def small_rows(ref, z, sq, fb1, table, shared):
    ref[...] = jnp.zeros_like(ref)
    if shared is not None:
        sg, sb, projb, sh_ref = shared
        ref[0:1] = sg
        ref[1:2] = sb
        ref[2:3] = projb
        ref[3:6] = sh_ref[...]
    ref[6:7] = fb1
    ref[7:8, 0:96] = sq[0][:, 96 * z : 96 * (z + 1)] * SCALE
    ref[7:8, 128:224] = sq[1][:, 96 * z : 96 * (z + 1)]
    ref[8:24, 0:48] = table[:, 48 * z : 48 * (z + 1)]


def mixed_grad_kernel(wins, gh_ref, projw_ref, a_ref, b_ref, da_ref, do_ref, pb_ref):
    pb_ref[...] = window_grads(wins, gh_ref, da_ref)
    for half in range(2):
        do_ref[half] = nt(da_ref[...], proj_weight_of(half, 1, projw_ref, a_ref, b_ref)).astype(BF)


def attn_bwd_kernel(rows, across, *refs):
    (gh_ref, x_ref, xn_ref, gain_ref, qkvw_ref, a_ref, b_ref, info_ref) = refs[:8]
    (fb1_ref, sh_ref, qkv0_ref, p0_ref, mix0_ref, qkv1_ref, p1_ref, mix1_ref, pick_ref) = refs[8:17]
    (da_ref, do_ref, pb_ref) = refs[17:20]
    (gin_ref, keep_ref, send_ref, edge_ref) = refs[20:24]
    (dqkv0_ref, dqkv1_ref, acc_ref, mask_ref, row_ref, sm_ref) = refs[24:]
    layer = 1
    par = info_ref[0]
    wins = (rows // WIN) * across
    mask_ref[...] = head_mask()
    acc_ref[...] = jnp.zeros_like(acc_ref)
    projb = pb_ref[...]
    attend_backward(
        [
            (qkv0_ref, p0_ref, do_ref.at[0], dqkv0_ref, acc_ref.at[0]),
            (qkv1_ref, p1_ref, do_ref.at[1], dqkv1_ref, acc_ref.at[1]),
        ],
        wins,
        wins,
        mask_ref,
    )
    for half, mix_ref, dqkv_ref in ((1, mix1_ref, dqkv1_ref), (0, mix0_ref, dqkv0_ref)):

        def give(at, one, two, half=half):
            keep_ref[half, at : at + 96, :] = one
            send_ref[half, at : at + 96, :] = two

        half_grads(half, par, xn_ref, da_ref, mix_ref, dqkv_ref, row_ref, give)
    weights = [
        lambda j, half=half: qkv_weight_of(half, j, layer, qkvw_ref, a_ref, b_ref)
        for half in range(2)
    ]
    sg, sb, sq = normed_grads(
        layer, wins, [dqkv0_ref, dqkv1_ref], weights, gh_ref, x_ref, gain_ref, gin_ref
    )
    edge_ref[...] = edge_rows(gin_ref, across, range(rows - SHIFT, rows))
    for half in range(2):
        table = map_to_table(acc_ref.at[half], pick_ref)
        for z in range(2):
            q = 2 * half + z
            small_rows(
                sm_ref.at[q], z, sq[2 * half : 2 * half + 2], fb1_ref[q : q + 1], table,
                (sg, sb, projb, sh_ref)
            )
    keep_ref[0, C:, :] = sm_ref[par].astype(BF)
    send_ref[0, C:, :] = sm_ref[1 - par].astype(BF)
    keep_ref[1, C:, :] = sm_ref[2].astype(BF)
    send_ref[1, C:, :] = sm_ref[3].astype(BF)


def column_sum(ref):
    return jnp.sum(ref[...].astype(F32), 0, keepdims=True)


def attn_bwd_heads_kernel(rows, across, *refs):
    (gh_ref, xn_ref, projw_ref, a_ref, b_ref, fb1_ref) = refs[:6]
    (qkv0_ref, p0_ref, qkv1_ref, p1_ref, mix1_ref, pick_ref) = refs[6:12]
    (da_ref, dqkv0_ref, acc0_ref, dqkv1_ref, pb_ref, keep_ref, send_ref) = refs[12:19]
    (do_ref, mask_ref, acc1_ref, sm_ref) = refs[19:]
    wins = (rows // WIN) * across
    mask_ref[...] = head_mask()
    acc0_ref[...] = jnp.zeros_like(acc0_ref)
    acc1_ref[...] = jnp.zeros_like(acc1_ref)
    pb_ref[...] = window_grads(wins, gh_ref, da_ref)
    da = da_ref[...]
    for half in range(2):
        do_ref[half] = nt(da, proj_weight_of(half, 0, projw_ref, a_ref, b_ref)).astype(BF)
    attend_backward(
        [
            (qkv1_ref, p1_ref, do_ref.at[1], dqkv1_ref, acc1_ref),
            (qkv0_ref, p0_ref, do_ref.at[0], dqkv0_ref, acc0_ref),
        ],
        wins,
        wins,
        mask_ref,
    )

    def give(at, one, two):
        keep_ref[at : at + 96, :] = one
        send_ref[at : at + 96, :] = two

    half_grads(1, None, xn_ref, da_ref, mix1_ref, dqkv1_ref, None, give)
    table = map_to_table(acc1_ref, pick_ref)
    sq = (column_sum(dqkv1_ref.at[0]), column_sum(dqkv1_ref.at[2]))
    for z, ref in ((0, keep_ref), (1, send_ref)):
        small_rows(sm_ref, z, sq, fb1_ref[2 + z : 3 + z], table, None)
        ref[C:, :] = sm_ref[...].astype(BF)


def attn_bwd_own_kernel(rows, across, *refs):
    (gh_ref, x_ref, xn_ref, gain_ref, qkvw_ref, a_ref, b_ref, info_ref) = refs[:8]
    (fb1_ref, sh_ref, da_ref, dqkv_ref, acc_ref, dqkv1_ref, pb_ref, mix_ref, pick_ref) = refs[8:17]
    (out_ref, keep_ref, send_ref) = refs[17:20]
    (gx_ref, row_ref, sm_ref) = refs[20:]
    par = info_ref[0]
    wins = (rows // WIN) * across

    def give(at, one, two):
        keep_ref[at : at + 96, :] = one
        send_ref[at : at + 96, :] = two

    half_grads(0, par, xn_ref, da_ref, mix_ref, dqkv_ref, row_ref, give)
    weights = [
        lambda j, half=half: qkv_weight_of(half, j, 0, qkvw_ref, a_ref, b_ref)
        for half in range(2)
    ]
    sg, sb, sq = normed_grads(
        0, wins, [dqkv_ref, dqkv1_ref], weights, gh_ref, x_ref, gain_ref, gx_ref
    )
    table = map_to_table(acc_ref, pick_ref)
    for z in range(2):
        small_rows(
            sm_ref.at[z], z, sq[0:2], fb1_ref[z : z + 1], table, (sg, sb, pb_ref[...], sh_ref)
        )
    keep_ref[C:, :] = sm_ref[par].astype(BF)
    send_ref[C:, :] = sm_ref[1 - par].astype(BF)
    for r in range(rows):
        parts = [gx_ref[pl.ds(tile_row(r, k, across), SEG), :][:WIN] for k in range(across)]
        out_ref[r, :, 0, :] = jnp.concatenate(parts, axis=0)


def pair_kernel(keep_ref, got_ref, own_ref, oth_ref):
    own_ref[...] = (keep_ref[0].astype(F32) + got_ref[0].astype(F32)).astype(BF)
    oth_ref[...] = (keep_ref[1].astype(F32) + got_ref[1].astype(F32)).astype(BF)


def combine_kernel(parts, bit, n_in, *refs):
    ins = refs[:n_in]
    info_ref = refs[n_in]
    outs = refs[n_in + 1 :]
    at = 0
    for rows, terms, split in parts:

        def total(first, n):
            acc = None
            for i, base in terms:
                x = ins[i][pl.ds(base + first, n), :].astype(F32)
                acc = x if acc is None else acc + x
            return acc.astype(BF)

        if bit is None or not split:
            whole = total(0, rows)
            for out in outs:
                out[at : at + rows, :] = whole
            at += rows
        else:
            n = rows // 2
            b = (info_ref[2] >> bit) & 1
            outs[0][at : at + n, :] = total(pl.multiple_of(b * n, n), n)
            outs[1][at : at + n, :] = total(pl.multiple_of((1 - b) * n, n), n)
            at += n


def close_kernel(halves, bit, mine_ref, got_ref, info_ref, out_ref, small_ref):
    join_kernel(halves, bit, mine_ref.at[0 : sum(halves)], got_ref, info_ref, out_ref)
    at = sum(halves)
    rest = (mine_ref[at:, :].astype(F32) + got_ref[at:, :].astype(F32)).astype(BF)
    n = rest.shape[0] - SMALL
    out_ref[2 * at :, :] = rest[:n]
    small_ref[...] = rest[n:]


def join_kernel(halves, bit, mine_ref, got_ref, info_ref, out_ref):
    b = (info_ref[2] >> bit) & 1
    at = 0
    for n in halves:
        for ref, place in ((mine_ref, b), (got_ref, 1 - b)):
            to = pl.multiple_of(2 * at + place * n, 16)
            out_ref[pl.ds(to, n), :] = ref[at : at + n, :]
        at += n
    if at < mine_ref.shape[0]:
        out_ref[2 * at :, :] = mine_ref[at:, :]


def out_kernel(rows, across, st_ref, halo_ref, o_ref):
    halo = halo_ref[C + SMALL :, :].astype(F32)
    for r in range(rows):
        parts = []
        for k in range(across):
            if r >= SHIFT:
                t = st_ref[pl.ds(tile_row(r - SHIFT, k, across), SEG), :]
            else:
                t = edge_tile(halo, k, r)
            parts.append(t[:WIN])
        last = parts[-1]
        parts = [last[WIN - SHIFT :]] + parts[:-1] + [last[: WIN - SHIFT]]
        o_ref[r] = jnp.concatenate(parts, axis=0).astype(BF)


def place_of(i, info_ref):
    return info_ref[0] ^ (i // 2), ((info_ref[2] >> 1) & 1) ^ (i % 2)


def put_up(pieces, base, info_ref, ref):
    n = C // 2
    for i in range(4):
        core, half = place_of(i, info_ref)
        rows = pl.ds(pl.multiple_of(half * n, n), n)
        cols = pl.ds(pl.multiple_of(core * C, C), C)
        ref[rows, cols] = pieces[i][base : base + n, :].astype(F32)


def put_down(pieces, base, info_ref, ref):
    n = C // 2
    for i in range(4):
        core, half = place_of(i, info_ref)
        rows = pl.ds(pl.multiple_of(core * C + half * n, n), n)
        ref[rows, :] = pieces[i][base : base + n, :].astype(F32)


def put_attn(pieces, base, info_ref, asm_ref, qkv_ref, proj_ref):
    n = C // 2
    for i in range(4):
        core, half = place_of(i, info_ref)
        rows = pl.ds(pl.multiple_of(half * n, n), n)
        asm_ref[core, rows, :] = pieces[i][base : base + n, :].astype(F32)
    for core in range(2):
        to = pl.ds(96 * core, 96)
        for j in range(3):
            qkv_ref[j, to, :] = asm_ref[core, 96 * j : 96 * (j + 1), :]
        proj_ref[to, :] = asm_ref[core, 288:384, :]


def final_second_kernel(*refs):
    pieces = refs[:4]
    (info_ref, f1_ref, f2_ref, qkv_ref, proj_ref) = refs[4:9]
    (up_ref, down_ref, asm_ref, q_ref, p_ref, sems) = refs[9:]
    put_up(pieces, 0, info_ref, up_ref)
    put_down(pieces, C // 2, info_ref, down_ref)
    put_attn(pieces, C, info_ref, asm_ref, q_ref, p_ref)
    outs = [f1_ref, f2_ref, qkv_ref, proj_ref]
    for copy in copies_of([(x, y.at[1]) for x, y in zip((up_ref, down_ref, q_ref, p_ref), outs)], sems):
        copy.wait()


def final_kernel(*refs):
    mlps, attns, smalls = refs[:4], refs[4:8], refs[8:10]
    (shared_ref, info_ref) = refs[10:12]
    (f1_ref, f2_ref, qkv_ref, proj_ref) = refs[16:20]
    (gain_ref, bias_ref, pb_ref, fb2_ref, qvb_ref, fb1_ref, tab_ref) = refs[20:27]
    (up_ref, down_ref, asm_ref, q_ref, p_ref, sm_ref, sems) = refs[27:]
    put_up(mlps, 0, info_ref, up_ref)
    copies = copies_of([(up_ref, f1_ref.at[0])], sems)
    put_down(mlps, C // 2, info_ref, down_ref)
    copies += copies_of([(down_ref, f2_ref.at[0])], sems.at[1:2])
    put_attn(attns, 0, info_ref, asm_ref, q_ref, p_ref)
    copies += copies_of([(q_ref, qkv_ref.at[0]), (p_ref, proj_ref.at[0])], sems.at[2:4])
    n = C // 2
    par = info_ref[0]
    for layer in range(2):
        for i in range(2):
            x = smalls[i][...] if layer == 1 else attns[2 * i][n:, :]
            sm_ref[par ^ i] = x.astype(F32)
        x, y = sm_ref[0], sm_ref[1]
        shared = x[0:6]
        if layer == 0:
            shared = sm_ref[par, 0:6, :] + shared_ref[0:6].astype(F32)
        gain_ref[layer, 0:1] = shared[0:1]
        gain_ref[layer, 1:2] = shared[3:4]
        bias_ref[layer, 0:1] = shared[1:2]
        bias_ref[layer, 1:2] = shared[4:5]
        pb_ref[layer : layer + 1] = shared[2:3]
        fb2_ref[layer : layer + 1] = shared[5:6]
        fb1_ref[layer : layer + 1, 0:C] = x[6:7]
        fb1_ref[layer : layer + 1, C:] = y[6:7]
        for k in range(2):
            qvb_ref[layer, k : k + 1, 0:96] = x[7:8, 128 * k : 128 * k + 96]
            qvb_ref[layer, k : k + 1, 96:192] = y[7:8, 128 * k : 128 * k + 96]
        t = jnp.concatenate([x[8:24, 0:48], y[8:24, 0:48]], axis=1)
        wide = tn(t.astype(BF), offset_rows().astype(BF)) * offset_cols()
        for h in range(6):
            tab_ref[h, layer : layer + 1, :] = jnp.sum(
                wide[16 * h : 16 * (h + 1)], 0, keepdims=True
            )
    for copy in copies:
        copy.wait()


VMEM = pl.BlockSpec(memory_space=pltpu.VMEM)
HBM = pl.BlockSpec(memory_space=pltpu.HBM)


class Position:
    def __getitem__(self, k):
        if k == 1:
            return lax.axis_index("tp")
        win = lax.axis_index("win")
        return win if k == 2 else lax.rem(win, 2)


POSITION = Position()


def call(kernel, name, us, limit, operands, outs, scratch=(), aliases=None):
    args = []
    specs = []
    at = [n for n, op in enumerate(operands) if op is POSITION]
    if at:
        (at,) = at
        inner = kernel

        def kernel(*refs):
            return inner(*refs[:at], POSITION, *refs[at:])

        operands = operands[:at] + operands[at + 1 :]
        aliases = {k - (k > at): v for k, v in (aliases or {}).items()}
    for op in operands:
        args.append(op[0] if isinstance(op, tuple) else op)
        specs.append(op[1] if isinstance(op, tuple) else VMEM)
    shapes = [jax.ShapeDtypeStruct(o[0], o[1]) for o in outs]
    return pl.pallas_call(
        kernel,
        name=name,
        in_specs=specs,
        out_specs=[o[2] if len(o) > 2 else VMEM for o in outs],
        input_output_aliases=aliases or {},
        out_shape=shapes,
        scratch_shapes=[s if not isinstance(s, tuple) else pltpu.VMEM(*s) for s in scratch],
        cost_estimate=pl.CostEstimate(
            flops=int(us * 1e10), bytes_accessed=1000000, transcendentals=0
        ),
        compiler_params=pltpu.CompilerParams(vmem_limit_bytes=limit * 2**20),
    )(*args)


def on_device(n_win, *args):
    (
        tokens,
        crop_ids,
        cotangent,
        norm_gain,
        norm_bias,
        qkv_weight,
        qv_bias,
        proj_weight,
        proj_bias,
        fc1_weight,
        fc1_bias,
        fc2_weight,
        fc2_bias,
        pos_table,
    ) = args
    rows, cols = tokens.shape[1:3]
    across = cols // WIN
    wins = (rows // WIN) * across
    ntok = wins * WROWS
    npad = wins * WPAD
    win = lax.axis_index("win")
    tp = lax.axis_index("tp")
    par = win % 2
    info = POSITION
    bits = n_win.bit_length() - 1
    assert n_win == 1 << bits and bits >= 3

    def to_tp(x, name):
        with jax.named_scope(name + "_tp"):
            return lax.ppermute(x, "tp", [(0, 1), (1, 0)])

    def to_win(x, bit, name):
        if bit >= bits:
            return jnp.zeros_like(x)
        with jax.named_scope("%s_win%d" % (name, bit)):
            return lax.ppermute(x, "win", [(i, i ^ (1 << bit)) for i in range(n_win)])

    def after(x, *others):
        return lax.optimization_barrier((x,) + others)[0]

    def combine(parts, bit, ins, name):
        total = sum(rows // 2 if split and bit is not None else rows for rows, _, split in parts)
        outs = [((total, C), BF)] * (1 if bit is None else 2)
        return call(
            partial(combine_kernel, parts, bit, len(ins)), name, 1, 4, tuple(ins) + (info,), outs
        )

    def join(halves, bit, mine, got, name):
        return call(
            partial(join_kernel, halves, bit), name, 1, 4, (mine, got, info),
            [((mine.shape[0] + sum(halves), C), BF)],
        )[0]

    qkv_t = qkv_weight.transpose(0, 2, 3, 1)
    table = pos_table.transpose(2, 0, 1)
    na = C + SMALL
    n = C // 2
    edge_b = ((across * SHIFT * SEG, C), BF)
    a0q, small = call(
        pack_first_kernel,
        "pack_first",
        0.1,
        60,
        tuple((x, HBM) for x in (qkv_t, proj_weight, table, qv_bias, fc1_bias)),
        [((C + 2 * SENT_ROWS, C), BF), ((2, SMALL_ROWS, C), F32)],
        [
            (table.shape, F32),
            (qv_bias.shape, F32),
            (fc1_bias.shape, F32),
            pltpu.SemaphoreType.DMA((7,)),
        ],
    )
    a0 = to_tp(a0q, "a0")
    m0q, a1q, m1q, cot_edge = call(
        pack_kernel,
        "pack",
        0.1,
        60,
        tuple((x, HBM) for x in (qkv_t, proj_weight, fc1_weight, fc2_weight, cotangent[0]))
        + (after(small, a0q), info),
        [
            ((2 * C, C), BF),
            ((C + 2 * SENT_ROWS, C), BF),
            ((2 * C, C), BF),
            ((EDGE_ROWS, C), BF),
        ],
        [((SHIFT, cols, C), BF), pltpu.SemaphoreType.DMA((9,))],
    )
    m0 = to_tp(m0q, "m0")
    crops = crop_ids.transpose(2, 0, 1)
    label_outs = [((wins, 128), F32), ((wins, WPAD, 128), F32), ((3, WPAD, 128), F32)]
    lq0, lk0, pos0, pick = call(
        partial(prep_kernel, 0, rows, across),
        "prep_0",
        0.1,
        8,
        (crops, after(small, m0q), info),
        label_outs + [((WIN, 96, 6 * WPAD), BF)],
        [((128, 128), F32)],
    )
    tiles = (rows // WIN, across, WIN, SEG, C)
    mask = ((6 * WPAD, 6 * HD), BF)
    half_outs = [((3, npad, 192), BF), ((wins, WPAD, 6 * WPAD), BF), ((npad, 192), BF)]
    tok_f = ((ntok, C), F32)
    tok_b = ((ntok, C), BF)
    hid_b = ((4, ntok, C), BF)
    other_scratch = [mask, ((3, WPAD, 128), F32)]

    x0, xn0, part, qkv00, p00, mix00 = call(
        partial(attn_own_kernel, rows, across),
        "attn_own_0",
        0.1,
        8,
        (tokens[0], norm_gain, norm_bias, proj_bias, qv_bias, qkv_t, proj_weight, pos0, lq0, lk0),
        [tok_b, ((npad, C), BF), tok_f] + half_outs,
        [mask, tok_f],
    )
    lq1, lk1, pos1 = call(
        partial(prep_kernel, 1, rows, across),
        "prep_1",
        0.1,
        8,
        (crops, after(small, part), info, pick),
        label_outs,
        [((128, 128), F32)],
    )
    a1 = to_tp(after(a1q, lq1), "a1")
    a0 = after(a0, lq1)
    a0s = to_win(a0, 0, "a0")
    hid0, qkv01, p01, mix01, small0 = call(
        partial(attn_other_kernel, rows, across),
        "attn_other_0",
        0.1,
        8,
        (part, xn0, a0, a0s, lq0, lk0, pick, info),
        [tok_f] + half_outs + [((SMALL_ROWS, C), F32)],
        other_scratch,
    )
    half_b = ((2, ntok, C), BF)
    st_own, n2f, act00, gp00 = call(
        mlp_own_kernel,
        "mlp_own_0",
        0.1,
        10,
        (hid0, norm_gain, norm_bias, fc1_bias, fc2_bias, fc1_weight, fc2_weight),
        [tok_f, tok_b, half_b, half_b],
    )
    m0 = after(m0, st_own)
    m0s = to_win(m0, 0, "m0")
    st0, act01, gp01, edge = call(
        partial(mlp_other_kernel, across),
        "mlp_other_0",
        3,
        10,
        (st_own, n2f, fc1_bias, small0, m0, m0s, info),
        [tok_f, half_b, half_b, edge_b],
    )
    halo = to_tp(edge, "edge0")
    a1 = after(a1, halo)
    a1s = to_win(a1, 0, "a1")
    cot_edge = to_tp(after(cot_edge, edge), "cot")
    m1 = to_tp(after(m1q, edge), "m1")
    x1, xn1, qkv10 = call(
        partial(norm_kernel, rows, across),
        "norm_1",
        2,
        6,
        (st0, halo, norm_gain, norm_bias, qv_bias, qkv_t),
        [tok_f, ((npad, C), BF), half_outs[0]],
    )
    p10, mix10, qkv11, p11, mix11, small1 = call(
        partial(attn_both_kernel, rows, across),
        "attn_fwd_1",
        10,
        9,
        (xn1, qkv10, pos1, a1, a1s, lq1, lk1, pick, info),
        half_outs[1:] + half_outs + [((SMALL_ROWS, C), F32)],
        other_scratch,
    )
    (hid1,) = call(
        partial(branch_kernel, wins),
        "branch_1",
        1,
        8,
        (x1, mix10, mix11, proj_weight, a1, a1s, proj_bias),
        [tok_f],
    )
    sums = [((4, C), F32), ((3, C), F32)]
    g1, df1, n21, st_own, dz_own, du10, act10, sum10, sf1 = call(
        partial(mlp_own_both_kernel, rows, across),
        "mlp_own_1",
        5,
        6,
        (cotangent[0], after(cot_edge, a1s), hid1, norm_gain, norm_bias, fc1_bias, fc2_bias)
        + (fc1_weight, fc2_weight),
        [tok_f, tok_b, tok_b, tok_f, tok_f, half_b, half_b, ((2, C), F32), ((1, C), F32)],
    )
    m1 = after(m1, dz_own)
    m1s = to_win(m1, 0, "m1")
    whole_q = ((2 * C, C), BF)
    keep_mo, send_mo = call(
        own_grads_kernel, "own_grads_1", 2, 4, (after(n21, m1), df1, du10, act10, info),
        [whole_q, whole_q],
    )
    mo_core = to_win(send_mo, 0, "gmo")
    st1, gh1, du11, act11, send_mx, gfb1, gsh1, out_edge = call(
        partial(mlp_other_both_kernel, rows, across),
        "mlp_other_1",
        6,
        7,
        (after(hid1, keep_mo), g1, df1, n21, st_own, dz_own, norm_gain, fc1_bias, small1, m1, m1s)
        + (info, sum10, sf1),
        [tok_f, tok_f, half_b, half_b, whole_q] + sums + [edge_b],
        aliases={1: 1, 4: 0},
    )

    def plus(x, y, name):
        return combine([(x.shape[0], [(0, 0), (1, 0)], True)], None, (x, y), name)[0]

    def pair(keep, got, name):
        shape = keep.shape[1:]
        return call(pair_kernel, name, 1, 4, (keep, got), [(shape, BF), (shape, BF)])

    mx_core = to_win(send_mx, 0, "gmx")
    (keep_mx,) = call(mlp_keep_kernel, "mlp_keep_1", 1, 4, (n21, df1, du11, act11), [whole_q])
    m1_oth = plus(keep_mx, after(mx_core, keep_mx), "m1_oth")
    m1_own = plus(keep_mo, after(mo_core, m1_oth), "m1_own")
    m1_t = to_tp(m1_oth, "gm1")
    da1, do1, pb1 = call(
        partial(mixed_grad_kernel, wins),
        "mixed_grad_1",
        0.1,
        4,
        (after(gh1, m1_own), proj_weight, a1, a1s),
        [((npad, C), BF), ((2, npad, 192), BF), ((1, C), F32)],
    )
    gin1, keep_a1, send_a1, edge = call(
        partial(attn_bwd_kernel, rows, across),
        "attn_bwd_1",
        14,
        8,
        (gh1, x1, xn1, norm_gain, qkv_t, a1, a1s, info)
        + (gfb1, gsh1, qkv10, p10, mix10, qkv11, p11, mix11, pick, da1, do1, pb1),
        [tok_f, ((2, na, C), BF), ((2, na, C), BF), edge_b],
        [
            ((3, npad, 192), BF),
            ((3, npad, 192), BF),
            ((2, 3, WPAD, 128), F32),
            mask,
            ((192, C), F32),
            ((4, SMALL, C), F32),
        ],
    )
    halo = to_tp(edge, "edge1")
    a1_core = to_win(after(send_a1, edge), 0, "ga1")
    m1_mine, m1_away = combine(
        [(C, [(0, 0), (1, 0)], True), (C, [(0, C), (1, C)], True)],
        1,
        (m1_own, after(m1_t, edge)),
        "m1_y",
    )
    m1_y = to_win(m1_away, 1, "gm1")
    a1_own, a1_oth = pair(keep_a1, after(a1_core, m1_away), "pair_a1")
    a1_t = to_tp(a1_oth, "ga1")
    g0, df0, keep_f2, send_f2 = call(
        partial(down_grad_kernel, rows, across),
        "down_grad_0",
        4,
        5,
        (gin1, after(halo, a1_oth), act00, act01, info),
        [tok_f, tok_b, ((2, C, C), BF), ((2, C, C), BF)],
    )
    f2_core = to_win(send_f2, 0, "gf2")
    quarter_b = ((C, C), BF)
    dz0, sum00, keep_fo, send_fo = call(
        mlp_bwd_own_kernel,
        "mlp_bwd_own_0",
        2,
        8,
        (df0, gp00, n2f, fc1_weight, fc2_weight, info),
        [tok_f, ((2, C), F32), quarter_b, quarter_b],
        [half_b],
    )
    fo_core = to_win(send_fo, 0, "gfo")
    m1_mine, m1_away = combine(
        [(n, [(0, 0), (1, 0)], True), (n, [(0, n), (1, n)], True)],
        2,
        (m1_mine, after(m1_y, dz0)),
        "m1_z",
    )
    m1_z = to_win(m1_away, 2, "gm1")
    f2_own, f2_oth = pair(keep_f2, after(f2_core, m1_away), "pair_f2")
    f2_t = to_tp(f2_oth, "gf2")
    a1_mine, a1_away = combine(
        [(C, [(0, 0), (1, 0)], True), (SMALL, [(0, C), (1, C)], False)],
        1,
        (a1_own, after(a1_t, f2_oth)),
        "a1_y",
    )
    a1_y = to_win(a1_away, 1, "ga1")
    gh0, du01, send_fx, gfb0, gsh0 = call(
        mlp_bwd_other_kernel,
        "mlp_bwd_other_0",
        3,
        8,
        (after(g0, a1_away), df0, hid0, n2f, gp01, dz0, norm_gain, m0, m0s, sum00),
        [tok_f, half_b, quarter_b] + sums,
    )
    fx_core = to_win(send_fx, 0, "gfx")
    (keep_fx,) = call(up_keep_kernel, "up_keep_0", 1, 4, (n2f, du01), [quarter_b])
    f1_oth = plus(keep_fx, after(fx_core, keep_fx), "f1_oth")
    f1_t = to_tp(f1_oth, "gf1")
    f1_own = plus(keep_fo, after(fo_core, f1_oth), "f1_own")
    (c1,) = combine(
        [(n, [(0, 0), (1, 0)], True), (n + SMALL, [(2, 0), (3, 0)], True)],
        None,
        (m1_mine, after(m1_z, f1_own), a1_mine, after(a1_y, f1_own)),
        "c1",
    )
    c1_b = to_win(c1, 3, "gc1")
    da, dqkv0, acc0, dqkv1, pb0, keep_o0, send_o0 = call(
        partial(attn_bwd_heads_kernel, rows, across),
        "attn_bwd_heads_0",
        8,
        8,
        (after(gh0, c1, f2_t), xn0, proj_weight, a0, a0s, gfb0)
        + (qkv00, p00, qkv01, p01, mix01, pick),
        [
            ((npad, C), BF),
            ((3, npad, 192), BF),
            ((3, WPAD, 128), F32),
            ((3, npad, 192), BF),
            ((1, C), F32),
            ((na, C), BF),
            ((na, C), BF),
        ],
        [((2, npad, 192), BF), mask, ((3, WPAD, 128), F32), ((SMALL, C), F32)],
    )
    o0_core = to_win(send_o0, 0, "go0")
    m0_mine, m0_away = combine(
        [(C, [(0, 0), (1, 0)], True), (C, [(2, 0), (3, 0)], True)],
        1,
        (f1_own, after(f1_t, send_o0), f2_own, f2_t),
        "m0_y",
    )
    m0_y = to_win(m0_away, 1, "gm0")
    (o0_sum,) = combine(
        [(na, [(0, 0), (1, 0)], True), (edge_b[0][0], [(2, 0)], True)],
        None,
        (keep_o0, after(o0_core, m0_away), out_edge),
        "o0",
    )
    o0_t = to_tp(o0_sum, "go0")
    c1 = plus(c1, after(c1_b, o0_sum), "c1_sum")
    for bit in range(4, bits):
        c1 = plus(c1, to_win(c1, bit, "gc1"), "c1_sum")
    c1_b = to_win(c1, 2, "gc1")
    grad_tokens, keep_a0, send_a0 = call(
        partial(attn_bwd_own_kernel, rows, across),
        "attn_bwd_own_0",
        9,
        7,
        (gh0, x0, xn0, norm_gain, qkv_t, a0, a0s, info)
        + (gfb0, gsh0, da, dqkv0, acc0, dqkv1, pb0, after(mix00, c1), pick),
        [((rows, cols, 1, C), F32), ((na, C), BF), ((na, C), BF)],
        [tok_f, ((192, C), F32), ((2, SMALL, C), F32)],
    )

    a0_core = to_win(send_a0, 0, "ga0")
    m0_mine, m0_away = combine(
        [(n, [(0, 0), (1, 0)], True), (n, [(0, n), (1, n)], True)],
        2,
        (m0_mine, after(m0_y, send_a0)),
        "m0_z",
    )
    m0_z = to_win(m0_away, 2, "gm0")
    a0_mine, a0_away = combine(
        [(C, [(0, 0), (1, 0), (2, 0)], True), (SMALL, [(0, C), (1, C), (2, C)], False)],
        1,
        (keep_a0, after(a0_core, m0_away), o0_t),
        "a0_y",
    )
    a0_y = to_win(a0_away, 1, "ga0")
    c1, c1_small = call(
        partial(close_kernel, [n // 2] * 2, 2), "c1_close", 1, 8, (c1, after(c1_b, a0_away), info),
        [((3 * n, C), BF), ((SMALL, C), BF)],
    )
    c1_back = to_win(c1, 1, "gc1_back")
    c1_sib = to_win(c1, 0, "gc1_mine")
    c1_small_sib = to_win(c1_small, 0, "gc1_small")
    m0 = plus(m0_mine, after(m0_z, c1), "m0_z2")
    m0_b = to_win(m0, 3, "gm0")
    a0 = plus(a0_mine, after(a0_y, m0), "a0_z")
    a0_z = to_win(a0, 2, "ga0")
    (layer_out,) = call(
        partial(out_kernel, rows, across), "layer_out", 1, 8, (after(st1, a0), o0_t),
        [((rows, cols, C), BF)],
    )
    m0 = plus(m0, after(m0_b, layer_out), "m0_sum")
    for bit in range(4, bits):
        m0 = plus(m0, to_win(m0, bit, "gm0"), "m0_sum")
    m0_b = to_win(m0, 2, "gm0_back")
    a0 = plus(a0, after(a0_z, m0), "a0_z2")
    a0_b = to_win(a0, 3, "ga0")
    c1_back = after(c1_back, a0)
    c1_pieces = (c1, c1_back, c1_sib, to_win(c1_back, 0, "gc1_theirs"))
    m0 = join([n // 2] * 2, 2, m0, after(m0_b, c1_back), "m0_join")
    m0_back = to_win(m0, 1, "gm0_back")
    m0_sib = to_win(m0, 0, "gm0_mine")
    c1_small_sib, c1_pieces = after((c1_small_sib, c1_pieces), m0)
    f1_shape, f2_shape = (2, C, 2 * C), (2, 2 * C, C)
    qkv_shape, proj_shape = (2, 3, 192, C), (2, 192, C)
    whole = [(f1_shape, F32, HBM), (f2_shape, F32, HBM), (qkv_shape, F32, HBM), (proj_shape, F32, HBM)]
    parts = [(x[0][1:], F32) for x in whole]
    attn_parts = [((2, C, C), F32)] + parts[2:]
    g_f1, g_f2, g_qkv, g_proj = call(
        final_second_kernel, "final_second", 1, 9, c1_pieces + (info,), whole,
        parts[:2] + attn_parts + [pltpu.SemaphoreType.DMA((4,))],
    )
    a0 = plus(a0, after(a0_b, g_f1), "a0_sum")
    for bit in range(4, bits):
        a0 = plus(a0, to_win(a0, bit, "ga0"), "a0_sum")
    a0_back = to_win(a0, 1, "ga0_back")
    a0_sib = to_win(a0, 0, "ga0_mine")
    shared = to_tp(a0[n : n + 16], "shared")
    m0_back = after(m0_back, a0_sib, shared)
    m0_pieces = (m0, m0_back, m0_sib, to_win(m0_back, 0, "gm0_theirs"))
    outs = call(
        final_kernel,
        "final",
        0.1,
        9,
        m0_pieces
        + (a0, a0_back, a0_sib, to_win(a0_back, 0, "ga0_theirs"), c1_small, c1_small_sib)
        + (shared, info, (g_f1, HBM), (g_f2, HBM), (g_qkv, HBM), (g_proj, HBM)),
        whole
        + [
            ((2, 2, C), F32),
            ((2, 2, C), F32),
            ((2, C), F32),
            ((2, C), F32),
            ((2, 2, 192), F32),
            ((2, 2 * C), F32),
            ((6, 2, 169), F32),
        ],
        parts[:2] + attn_parts + [((2, SMALL, C), F32), pltpu.SemaphoreType.DMA((4,))],
        aliases={12: 0, 13: 1, 14: 2, 15: 3},
    )
    (g_f1, g_f2, g_qkv, g_proj, g_gain, g_bias, g_pb, g_fb2, g_qvb, g_fb1, g_tab) = outs
    return (
        layer_out[None],
        grad_tokens.transpose(2, 0, 1, 3),
        g_gain,
        g_bias,
        g_qkv.transpose(0, 3, 1, 2),
        g_qvb,
        g_proj,
        g_pb,
        g_f1,
        g_fb1,
        g_f2,
        g_fb2,
        g_tab.transpose(1, 2, 0),
    )


def solution(mesh):
    return jax.shard_map(
        partial(on_device, mesh.shape["win"]),
        mesh=mesh,
        in_specs=(
            P("win", "tp", None, None),
            P("win", None, None),
            P("win", "tp", None, None),
            P(),
            P(),
            P(None, None, None, "tp"),
            P(None, None, "tp"),
            P(None, "tp", None),
            P(),
            P(None, None, "tp"),
            P(None, "tp"),
            P(None, "tp", None),
            P(),
            P(None, None, "tp"),
        ),
        out_specs=(
            P("win", "tp", None, None),
            P("win", "tp", None, None),
            P(),
            P(),
            P(None, None, None, "tp"),
            P(None, None, "tp"),
            P(None, "tp", None),
            P(),
            P(None, None, "tp"),
            P(None, "tp"),
            P(None, "tp", None),
            P(),
            P(None, None, "tp"),
        ),
        check_vma=False,
    )
```

```python
from functools import partial

import jax
import jax.numpy as jnp
import numpy as np
from jax import lax
from jax.experimental import pallas as pl
from jax.experimental.pallas import tpu as pltpu
from jax.sharding import PartitionSpec as P

C = 384
WIN = 7
SHIFT = 3
HD = 32
EPS = 1e-05
NEG = -1000000000.0
SCALE = HD**-0.5
F32 = jnp.float32
BF = jnp.bfloat16
SEG = 8
WROWS = WIN * SEG
WPAD = 64


def nn(a, b):
    return lax.dot_general(a, b, (((1,), (0,)), ((), ())), preferred_element_type=F32)


def nt(a, b):
    return lax.dot_general(a, b, (((1,), (1,)), ((), ())), preferred_element_type=F32)


def tn(a, b):
    return lax.dot_general(a, b, (((0,), (0,)), ((), ())), preferred_element_type=F32)


def norm_stats(x):
    mean = jnp.mean(x, -1, keepdims=True)
    cent = x - mean
    var = jnp.mean(cent * cent, -1, keepdims=True)
    rinv = lax.rsqrt(var + EPS)
    return cent * rinv, rinv


def norm_back(dz, xhat, rinv, gain):
    d = dz * gain
    return rinv * (
        d - jnp.mean(d, -1, keepdims=True) - xhat * jnp.mean(d * xhat, -1, keepdims=True)
    )


def tile_row(r, k, across):
    return (((r // WIN) * across + k) * WIN + r % WIN) * SEG


def zero_rows(n):
    return jnp.zeros((n, C), F32)


def head_mask():
    row = lax.broadcasted_iota(jnp.int32, (6 * WPAD, 6 * HD), 0) // WPAD
    col = lax.broadcasted_iota(jnp.int32, (6 * WPAD, 6 * HD), 1) // HD
    return (row == col).astype(BF)


def spread(x, mask):
    return jnp.concatenate([x] * 6, axis=0) * mask


def fold(o):
    lane = lax.broadcasted_iota(jnp.int32, (WPAD, 128), 1)

    def of(h, a, b):
        return o[WPAD * h : WPAD * (h + 1), a:b]

    one = jnp.where(lane < 96, of(2, 0, 128), of(3, 0, 128))
    one = jnp.where(lane < 64, of(1, 0, 128), one)
    one = jnp.where(lane < 32, of(0, 0, 128), one)
    two = jnp.where(lane[:, :64] < 32, of(4, 128, 192), of(5, 128, 192))
    return jnp.concatenate([one, two], axis=1)


def rows_at(i, n):
    return pl.ds(i * n, n)


def repeat(n, body, carry):
    for i in range(n):
        carry = body(i, carry)
    return carry


def iota(shape, dim):
    return lax.broadcasted_iota(jnp.int32, shape, dim)


def exact(a, b, ca, cb):
    return lax.dot_general(
        a,
        b,
        (((ca,), (cb,)), ((), ())),
        precision=lax.Precision.HIGHEST,
        preferred_element_type=F32,
    )


def offset_rows():
    return (12 - iota((16, 169), 0) == iota((16, 169), 1) // 13).astype(F32)


def offset_cols():
    return (iota((96, 169), 0) % 16 == iota((96, 169), 1) % 13).astype(F32)


def column_pick(kx):
    r = iota((96, 6 * WPAD), 0)
    c = iota((96, 6 * WPAD), 1)
    qx = c % 8
    return ((r // 16 == c // WPAD) & (r % 16 == qx - kx + WIN - 1) & (qx < WIN)).astype(BF)


def table_to_map(t, pick_ref, pos_ref):
    pos_ref[...] = jnp.zeros_like(pos_ref)
    group = (iota((8, 6 * WPAD), 1) % WPAD) // 8
    high = t.astype(BF)
    low = (t - high.astype(F32)).astype(BF)
    both = jnp.concatenate([high, low], axis=0)
    for kx in range(WIN):
        h = nn(both, pick_ref[kx])
        h = h[:16] + h[16:]
        g = jnp.zeros((8, 6 * WPAD), F32)
        for j in range(WIN):
            g = jnp.where(group == j, h[6 - j : 14 - j], g)
        for i in range(3):
            pos_ref[i, pl.ds(kx, 8, stride=8), :] = g[:, 128 * i : 128 * (i + 1)]


def map_to_table(pos_ref, pick_ref):
    group = (iota((16, 6 * WPAD), 1) % WPAD) // 8
    total = jnp.zeros((16, 96), F32)
    for kx in range(WIN):
        r = jnp.concatenate([pos_ref[i, pl.ds(kx, 8, stride=8), :] for i in range(3)], axis=1)
        h = jnp.zeros((16, 6 * WPAD), F32)
        for j in range(WIN):
            parts = [r, jnp.zeros((2 + j, 6 * WPAD), F32)]
            if j < 6:
                parts = [jnp.zeros((6 - j, 6 * WPAD), F32)] + parts
            h = jnp.where(group == j, jnp.concatenate(parts, axis=0), h)
        total = total + nt(h.astype(BF), pick_ref[kx])
    return total


def shift_in(tile, x_ref, rows, across):
    for r in range(rows):
        for k in range(across):
            a = tile(r + SHIFT, k)
            b = tile(r + SHIFT, (k + 1) % across)
            x_ref[pl.ds(tile_row(r, k, across), SEG), :] = jnp.concatenate(
                [a[SHIFT:WIN], b[:SHIFT], zero_rows(1)], axis=0
            )


def shift_out(tile, x_ref, rows, across):
    for r in range(rows):
        for k in range(across):
            a = tile(r - SHIFT, (k - 1) % across)
            b = tile(r - SHIFT, k)
            x_ref[pl.ds(tile_row(r, k, across), SEG), :] = jnp.concatenate(
                [a[WIN - SHIFT : WIN], b[: WIN - SHIFT], zero_rows(1)], axis=0
            )

EDGE_ROWS = 96
SMALL = 32


SMALL_ROWS = 24
SENT_ROWS = 8


def copies_of(pairs, sems):
    copies = [pltpu.make_async_copy(x, y, sems.at[n]) for n, (x, y) in enumerate(pairs)]
    for copy in copies:
        copy.start()
    return copies


def attn_copies(layer, par, qkvw_ref, projw_ref, a_ref):
    of_heads = pl.ds(pl.multiple_of(par * 96, 96), 96)
    pairs = [
        (qkvw_ref.at[layer, j, of_heads, :], a_ref.at[pl.ds(96 * j, 96), :]) for j in range(3)
    ]
    return pairs + [(projw_ref.at[layer, of_heads, :], a_ref.at[pl.ds(288, 96), :])]


def mlp_copies(layer, par, f1_ref, f2_ref, m_ref):
    of_units = pl.ds(pl.multiple_of(par * C, C), C)
    return [
        (f1_ref.at[layer, :, of_units], m_ref.at[pl.ds(0, C), :]),
        (f2_ref.at[layer, of_units, :], m_ref.at[pl.ds(C, C), :]),
    ]


def high_low(x):
    rows = []
    for r in range(4):
        rows.append(jnp.concatenate([x[4 * r + k : 4 * r + k + 1, 0:96] for k in range(4)], axis=1))
    rows.append(x[16:18])
    rows.append(jnp.concatenate([x[18:19, 0:192], x[19:20, 0:192]], axis=1))
    rows.append(zero_rows(1))
    x = jnp.concatenate(rows, axis=0)
    high = x.astype(BF).astype(F32)
    return jnp.concatenate([high, x - high], axis=0).astype(BF)


def pack_first_kernel(
    qkvw_ref, projw_ref, tab_ref, qvb_ref, fb1_ref,
    a0_ref, small_ref, tab_v, qvb_v, fb1_v, sems
):
    pairs = [(tab_ref, tab_v), (qvb_ref, qvb_v), (fb1_ref, fb1_v)]
    copies = copies_of(pairs + attn_copies(0, POSITION[0], qkvw_ref, projw_ref, a0_ref), sems)
    small_ref[...] = jnp.zeros_like(small_ref)
    for copy in copies[:3]:
        copy.wait()
    for layer in range(2):
        tab = tab_v[:, layer, :]
        wide = jnp.concatenate([jnp.broadcast_to(tab[h : h + 1], (16, 169)) for h in range(6)])
        small_ref[layer, 0:16, 0:96] = exact(offset_rows(), wide * offset_cols(), 1, 1)
        small_ref[layer, 16:17, :] = fb1_v[layer : layer + 1, 0:C]
        small_ref[layer, 17:18, :] = fb1_v[layer : layer + 1, C:]
        small_ref[layer, 18:20, 0:192] = qvb_v[layer]
    a0_ref[C:, :] = high_low(small_ref[0])
    for copy in copies[3:]:
        copy.wait()


def pack_kernel(
    qkvw_ref, projw_ref, f1_ref, f2_ref, cot_ref, small_ref, info_ref,
    m0_ref, a1_ref, m1_ref, edge_ref, cot_v, sems
):
    par = info_ref[0]
    pairs = [(cot_ref.at[pl.ds(0, SHIFT)], cot_v)]
    pairs += mlp_copies(0, par, f1_ref, f2_ref, m0_ref)
    pairs += attn_copies(1, par, qkvw_ref, projw_ref, a1_ref)
    pairs += mlp_copies(1, par, f1_ref, f2_ref, m1_ref)
    copies = copies_of(pairs, sems)
    a1_ref[C:, :] = high_low(small_ref[1])
    copies[0].wait()
    edge = [cot_v[r].astype(F32) for r in range(SHIFT)]
    n = EDGE_ROWS - SHIFT * cot_v.shape[1]
    edge_ref[...] = jnp.concatenate(edge + [zero_rows(n)], axis=0).astype(BF)
    for copy in copies[1:]:
        copy.wait()


def small_of(a_ref, small_ref):
    rows = a_ref[C : C + 2 * SENT_ROWS, :].astype(F32)
    x = rows[0:SENT_ROWS] + rows[SENT_ROWS:]
    small_ref[...] = jnp.zeros_like(small_ref)
    for r in range(4):
        for k in range(4):
            small_ref[4 * r + k : 4 * r + k + 1, 0:96] = x[r : r + 1, 96 * k : 96 * (k + 1)]
    small_ref[16:18, :] = x[4:6]
    small_ref[18:19, 0:192] = x[6:7, 0:192]
    small_ref[19:20, 0:192] = x[6:7, 192:384]


def edge_tile(edge, k, r):
    at = (k * SHIFT + r) * SEG
    return edge[at : at + SEG]


def edge_rows(ref, across, rows):
    tiles = [ref[pl.ds(tile_row(r, k, across), SEG), :] for k in range(across) for r in rows]
    return jnp.concatenate(tiles, axis=0).astype(BF)


def prep_kernel(layer, rows, across, *refs):
    (crop_ref, small_ref, info_ref) = refs[:3]
    if layer == 0:
        (lq_ref, lk_ref, pos_ref, pick_ref, c_ref) = refs[3:]
        for kx in range(WIN):
            pick_ref[kx] = column_pick(kx)
    else:
        (pick_ref, lq_ref, lk_ref, pos_ref, c_ref) = refs[3:]
    tp = info_ref[1]
    cols = across * WIN
    height = crop_ref.shape[2]
    table_to_map(small_ref[layer, 0:16, 0:96], pick_ref, pos_ref)
    c_ref[...] = jnp.zeros_like(c_ref)
    c_ref[0:cols, 0:height] = crop_ref[:, 0, :].astype(F32)
    crops = c_ref[...].astype(BF)
    row = iota((32, 128), 0)
    lane = iota((32, 128), 1)
    shift = SHIFT if layer == 1 else 0
    src = rows * tp + row + shift
    src = jnp.where(src >= height, src - height, src)
    grid = nt((src == lane).astype(BF), crops).astype(BF)
    labs = []
    for wc in range(across):
        qx = iota((128, 128), 1) % 8
        col = qx + (WIN * wc + shift)
        col = jnp.where(col >= cols, col - cols, col)
        pick = ((col == iota((128, 128), 0)) & (qx < WIN)).astype(BF)
        lab = nn(grid, pick)
        if layer == 1:
            g = rows * tp + row
            zr = (g >= height - WIN).astype(F32) + (g >= height - SHIFT).astype(F32)
            here = lane % 8 + WIN * wc
            zc = (here >= cols - WIN).astype(F32) + (here >= cols - SHIFT).astype(F32)
            lab = lab * 9.0 + zr * 3.0 + zc
        labs.append(lab)
    real = (iota((1, 128), 1) % 8 < WIN) & (iota((1, 128), 1) % WPAD < WROWS)
    for wr in range(rows // WIN):
        lines = []
        for wc in range(across):
            w = wr * across + wc
            mine = row == (lane % WPAD) // 8 + WIN * wr
            line = jnp.sum(jnp.where(mine, labs[wc], 0.0), 0, keepdims=True)
            line = jnp.where(real, line, -1.0)
            lq_ref[w : w + 1, :] = line
            lines.append(line)
        for wc in range(0, across, 2):
            w = wr * across + wc
            both = jnp.where(iota((1, 128), 1) < WPAD, lines[wc], lines[wc + 1])
            both = jnp.broadcast_to(both, (128, 128)).T
            lk_ref[w] = both[:WPAD]
            lk_ref[w + 1] = both[WPAD:]


def qkv_weight_of(half, j, layer, qkvw_ref, a_ref, b_ref):
    if half == 0:
        return qkvw_ref[layer, j]
    return jnp.concatenate([a_ref[96 * j : 96 * (j + 1)], b_ref[96 * j : 96 * (j + 1)]], axis=0)


def proj_weight_of(half, layer, projw_ref, a_ref, b_ref):
    if half == 0:
        return projw_ref[layer]
    return jnp.concatenate([a_ref[288:384], b_ref[288:384]], axis=0)


def norm_windows(layer, wins, x_ref, xn_ref, gain_ref, bias_ref):
    gain = gain_ref[layer, 0:1]
    bias = bias_ref[layer, 0:1]

    def four(i, carry):
        xhat, _ = norm_stats(x_ref[rows_at(i, 4 * WROWS), :])
        xn = xhat * gain + bias
        for n in range(4):
            part = jnp.concatenate(
                [xn[n * WROWS : (n + 1) * WROWS], zero_rows(WPAD - WROWS)], axis=0
            )
            xn_ref[rows_at(4 * i + n, WPAD), :] = part.astype(BF)
        return carry

    repeat(wins // 4, four, 0)


def project_half(xn_ref, qkv_ref, weight, qb, vb):
    n = xn_ref.shape[0]

    def part(i, carry):
        at = rows_at(i, n)
        xn = xn_ref[at, :]
        q = nt(xn, weight(0))
        k = nt(xn, weight(1))
        v = nt(xn, weight(2))
        qkv_ref[0, at, :] = ((q + qb) * SCALE).astype(BF)
        qkv_ref[1, at, :] = k.astype(BF)
        qkv_ref[2, at, :] = (v + vb).astype(BF)
        return carry

    repeat(1, part, 0)


def attend_forward(halves, wins, group, lq_ref, lk_ref, mask_ref):
    def body(i, carry):
        units = [(i * group + u, h) for u in range(group) for h in halves]
        scores = []
        for w, (qkv_ref, _, _, _) in units:
            at = rows_at(w, WPAD)
            scores.append(nt(qkv_ref[1, at, :], spread(qkv_ref[0, at, :], mask_ref[...])))
        probs = []
        for (w, (_, pos, p_ref, _)), s in zip(units, scores):
            same = lk_ref[w] == lq_ref[pl.ds(w, 1), :]
            same = jnp.concatenate([same] * 3, axis=1)
            s = jnp.where(same, s + jnp.concatenate([pos[n] for n in range(3)], axis=1), NEG)
            e = jnp.exp(s - jnp.max(s, 0, keepdims=True))
            p = (e * (1.0 / jnp.sum(e, 0, keepdims=True))).astype(BF)
            p_ref[w] = p
            probs.append(p)
        for (w, (qkv_ref, _, _, mix_ref)), p in zip(units, probs):
            at = rows_at(w, WPAD)
            mix_ref[at, :] = fold(tn(p, qkv_ref[2, at, :])).astype(BF)
        return carry

    repeat(wins // group, body, 0)


def add_branch(wins, mixes, weights, bias, x_ref, hid_ref):
    n = 8

    def part(i, carry):
        res = bias
        for m_ref, w in zip(mixes, weights):
            res = res + nn(m_ref[rows_at(i, n * WPAD), :], w)
        for k in range(n):
            to = rows_at(i * n + k, WROWS)
            hid_ref[to, :] = x_ref[to, :] + res[k * WPAD : k * WPAD + WROWS]
        return carry

    repeat(wins // n, part, 0)


def attn_own_kernel(rows, across, *refs):
    (tok_ref, gain_ref, bias_ref, pb_ref, qvb_ref, qkvw_ref, projw_ref) = refs[:7]
    (pos_ref, lq_ref, lk_ref) = refs[7:10]
    (xb_ref, xn_ref, hid_ref, qkv_ref, p_ref, mix_ref, mask_ref, x_ref) = refs[10:]
    wins = (rows // WIN) * across
    for r in range(rows):
        row = tok_ref[r].astype(F32)
        for k in range(across):
            x_ref[pl.ds(tile_row(r, k, across), SEG), :] = jnp.concatenate(
                [row[WIN * k : WIN * (k + 1)], zero_rows(1)], axis=0
            )
    xb_ref[...] = x_ref[...].astype(BF)
    mask_ref[...] = head_mask()
    norm_windows(0, wins, x_ref, xn_ref, gain_ref, bias_ref)
    project_half(
        xn_ref, qkv_ref, lambda j: qkvw_ref[0, j], qvb_ref[0, 0:1], qvb_ref[0, 1:2]
    )
    attend_forward(
        [(qkv_ref, pos_ref, p_ref, mix_ref)], wins, wins, lq_ref, lk_ref, mask_ref
    )
    add_branch(wins, [mix_ref], [projw_ref[0]], pb_ref[0:1], x_ref, hid_ref)


def attn_other_kernel(rows, across, *refs):
    (part_ref, xn_ref, a_ref, b_ref, lq_ref, lk_ref, pick_ref, info_ref) = refs[:8]
    (hid_ref, qkv_ref, p_ref, mix_ref, small_ref, mask_ref, pos_ref) = refs[8:]
    small_of(a_ref, small_ref)
    wins = (rows // WIN) * across
    mask_ref[...] = head_mask()
    bias = other_small(small_ref, info_ref[0], pick_ref, pos_ref)
    project_half(
        xn_ref,
        qkv_ref,
        lambda j: qkv_weight_of(1, j, 0, None, a_ref, b_ref),
        bias[0:1],
        bias[1:2],
    )
    attend_forward([(qkv_ref, pos_ref, p_ref, mix_ref)], wins, wins, lq_ref, lk_ref, mask_ref)
    add_branch(
        wins, [mix_ref], [proj_weight_of(1, 0, None, a_ref, b_ref)], 0.0, part_ref, hid_ref
    )


def other_small(small_ref, par, pick_ref, pos_ref):
    first = par == 0

    def swapped(v, n):
        return jnp.where(first, v, jnp.concatenate([v[:, n : 2 * n], v[:, :n]], axis=1))

    t = swapped(small_ref[0:16, 0:96], 48)
    table_to_map(t, pick_ref, pos_ref)
    return swapped(small_ref[18:20, 0:192], 96)


def norm_kernel(rows, across, *refs):
    (st_ref, halo_ref, gain_ref, bias_ref, qvb_ref, qkvw_ref) = refs[:6]
    (x_ref, xn_ref, qkv_ref) = refs[6:]

    def tile(r, k):
        if r < rows:
            return st_ref[pl.ds(tile_row(r, k, across), SEG), :]
        return edge_tile(halo, k, r - rows)

    halo = halo_ref[...].astype(F32)
    shift_in(tile, x_ref, rows, across)
    norm_windows(1, (rows // WIN) * across, x_ref, xn_ref, gain_ref, bias_ref)
    project_half(
        xn_ref, qkv_ref, lambda j: qkvw_ref[1, j], qvb_ref[1, 0:1], qvb_ref[1, 1:2]
    )


def attn_both_kernel(rows, across, *refs):
    (xn_ref, qkv0_ref, pos_ref, a_ref, b_ref, x_ref, projw_ref, pb_ref) = refs[:8]
    (lq_ref, lk_ref, pick_ref, info_ref) = refs[8:12]
    (hid_ref, p0_ref, mix0_out, qkv1_ref, p1_ref, mix1_out, small_ref) = refs[12:19]
    (mask_ref, pos1_ref, mix0_ref, mix1_ref, sems) = refs[19:]
    wins = (rows // WIN) * across
    mask_ref[...] = head_mask()
    small_of(a_ref, small_ref)
    bias = other_small(small_ref, info_ref[0], pick_ref, pos1_ref)
    project_half(
        xn_ref,
        qkv1_ref,
        lambda j: qkv_weight_of(1, j, 1, None, a_ref, b_ref),
        bias[0:1],
        bias[1:2],
    )
    attend_forward(
        [(qkv0_ref, pos_ref, p0_ref, mix0_ref), (qkv1_ref, pos1_ref, p1_ref, mix1_ref)],
        wins,
        wins,
        lq_ref,
        lk_ref,
        mask_ref,
    )
    copies = copies_of([(mix0_ref, mix0_out), (mix1_ref, mix1_out)], sems)
    add_branch(
        wins,
        [mix0_ref, mix1_ref],
        [projw_ref[1], proj_weight_of(1, 1, None, a_ref, b_ref)],
        pb_ref[1:2],
        x_ref,
        hid_ref,
    )
    for copy in copies:
        copy.wait()


def up_weight(part, layer, base, f1_ref, a_ref, b_ref):
    if part == 0:
        return f1_ref[layer]
    return jnp.concatenate([a_ref[base : base + C], b_ref[base : base + C]], axis=1)


def down_weight(part, layer, base, f2_ref, a_ref, b_ref):
    if part == 0:
        return f2_ref[layer]
    return jnp.concatenate([a_ref[base + C : base + 2 * C], b_ref[base + C : base + 2 * C]], axis=0)


def up_biases(layer, par, fb1_ref, small_ref):
    own = fb1_ref[layer : layer + 1]
    one, two = small_ref[16:17], small_ref[17:18]
    first = par == 0
    return own, jnp.concatenate(
        [jnp.where(first, one, two), jnp.where(first, two, one)], axis=1
    )


def gelu_pair(u):
    phi = 0.5 + 0.5 * lax.erf(u * (2.0**-0.5))
    slope = phi + u * (jnp.exp(-0.5 * u * u) * (2.0 * np.pi) ** -0.5)
    return (u * phi).astype(BF), slope.astype(BF)


def mlp_own_kernel(hid_ref, gain_ref, bias_ref, fb1_ref, fb2_ref, f1_ref, f2_ref, st_ref, n2_ref, act_ref, gp_ref):
    h = hid_ref[...]
    xhat, _ = norm_stats(h)
    n2 = (xhat * gain_ref[0, 1:2] + bias_ref[0, 1:2]).astype(BF)
    n2_ref[...] = n2
    act, slope = gelu_pair(nn(n2, f1_ref[0]) + fb1_ref[0:1])
    for z in range(2):
        act_ref[z] = act[:, C * z : C * (z + 1)]
        gp_ref[z] = slope[:, C * z : C * (z + 1)]
    st_ref[...] = h + fb2_ref[0:1] + nn(act, f2_ref[0])


def mlp_other_kernel(
    across, part_ref, n2_ref, fb1_ref, small_ref, a_ref, b_ref, info_ref, st_ref, act_ref, gp_ref,
    edge_ref
):
    _, bias = up_biases(0, info_ref[0], fb1_ref, small_ref)
    act, slope = gelu_pair(nn(n2_ref[...], up_weight(1, 0, 0, None, a_ref, b_ref)) + bias)
    for z in range(2):
        act_ref[z] = act[:, C * z : C * (z + 1)]
        gp_ref[z] = slope[:, C * z : C * (z + 1)]
    st_ref[...] = part_ref[...] + nn(act, down_weight(1, 0, 0, None, a_ref, b_ref))
    edge_ref[...] = edge_rows(st_ref, across, range(SHIFT))


def quarter_of(par, slot, part):
    return (par ^ slot) if part == 0 else 2 + slot


BLOCKS = 2


def half_sums(du, ref):
    for z in range(2):
        ref[z : z + 1] += jnp.sum(du[z].astype(F32), 0, keepdims=True)


def mlp_own_both_kernel(rows, across, *refs):
    (cot_ref, edge_ref, hid_ref, gain_ref, bias_ref, fb1_ref, fb2_ref, f1_ref, f2_ref) = refs[:9]
    (g_ref, df_ref, n2_ref, st_ref, dz_ref, du_ref, act_ref, sum_ref, sf_ref) = refs[9:]
    layer = 1
    cols = across * WIN
    cot_edge = edge_ref[...].astype(F32)
    for r in range(rows):
        s = r + SHIFT
        if s < rows:
            row = cot_ref[s].astype(F32)
        else:
            row = cot_edge[(s - rows) * cols : (s - rows + 1) * cols]
        for k in range(across):
            a = WIN * k + SHIFT
            if k < across - 1:
                piece = [row[a : a + WIN]]
            else:
                piece = [row[a:], row[:SHIFT]]
            g_ref[pl.ds(tile_row(r, k, across), SEG), :] = jnp.concatenate(
                piece + [zero_rows(1)], axis=0
            )
    sum_ref[...] = jnp.zeros_like(sum_ref)
    sf_ref[...] = jnp.zeros_like(sf_ref)
    n = hid_ref.shape[0] // BLOCKS

    def block(i, carry):
        at = pl.ds(pl.multiple_of(i * n, n), n)
        h = hid_ref[at, :]
        xhat, _ = norm_stats(h)
        n2 = (xhat * gain_ref[layer, 1:2] + bias_ref[layer, 1:2]).astype(BF)
        n2_ref[at, :] = n2
        df = g_ref[at, :].astype(BF)
        df_ref[at, :] = df
        sf_ref[...] += jnp.sum(df.astype(F32), 0, keepdims=True)
        up = nn(n2, f1_ref[layer]) + fb1_ref[layer : layer + 1]
        grad = nt(df, f2_ref[layer])
        act, slope = gelu_pair(up)
        du = (grad * slope.astype(F32)).astype(BF)
        parts = [du[:, C * z : C * (z + 1)] for z in range(2)]
        for z in range(2):
            act_ref[z, at, :] = act[:, C * z : C * (z + 1)]
            du_ref[z, at, :] = parts[z]
        half_sums(parts, sum_ref)
        st_ref[at, :] = h + fb2_ref[layer : layer + 1] + nn(act, f2_ref[layer])
        dz_ref[at, :] = nt(du, f1_ref[layer])
        return carry

    lax.fori_loop(0, BLOCKS, block, 0)


def mlp_other_both_kernel(rows, across, *refs):
    (hid_ref, g_ref, df_ref, n2_ref, part_ref, dzp_ref, gain_ref, fb1_ref, small_ref) = refs[:9]
    (a_ref, b_ref, info_ref, sumo_ref, sf_ref) = refs[9:14]
    (out_ref, gh_ref, du_ref, act_ref, send_ref, sum_ref, sh_ref, edge_ref, st_ref) = refs[14:]
    layer = 1
    par = info_ref[0]
    _, bias = up_biases(layer, par, fb1_ref, small_ref)
    w1 = up_weight(1, layer, 0, None, a_ref, b_ref)
    w2 = down_weight(1, layer, 0, None, a_ref, b_ref)
    sum_ref[0:2] = sumo_ref[...]
    sum_ref[2:4] = jnp.zeros((2, C), F32)
    sh_ref[0:2] = jnp.zeros((2, C), F32)
    sh_ref[2:3] = sf_ref[...]
    n = hid_ref.shape[0] // BLOCKS

    def block(i, carry):
        at = pl.ds(pl.multiple_of(i * n, n), n)
        up = nn(n2_ref[at, :], w1) + bias
        grad = nt(df_ref[at, :], w2)
        act, slope = gelu_pair(up)
        du = (grad * slope.astype(F32)).astype(BF)
        parts = [du[:, C * z : C * (z + 1)] for z in range(2)]
        for z in range(2):
            act_ref[z, at, :] = act[:, C * z : C * (z + 1)]
            du_ref[z, at, :] = parts[z]
        half_sums(parts, sum_ref.at[2:4])
        st_ref[at, :] = part_ref[at, :] + nn(act, w2)
        dz = dzp_ref[at, :] + nt(du, w1)
        xhat, rinv = norm_stats(hid_ref[at, :])
        sh_ref[0:1] += jnp.sum(dz * xhat, 0, keepdims=True)
        sh_ref[1:2] += jnp.sum(dz, 0, keepdims=True)
        gh_ref[at, :] = g_ref[at, :] + norm_back(dz, xhat, rinv, gain_ref[layer, 1:2])
        return carry

    lax.fori_loop(0, BLOCKS, block, 0)
    edge_ref[...] = edge_rows(st_ref, across, range(rows - SHIFT, rows))
    out_ref[...] = st_ref[...].astype(BF)
    n2 = n2_ref[...]
    df = df_ref[...]
    send_ref[0:C, :] = tn(n2, du_ref[1]).astype(BF)
    send_ref[C:, :] = tn(act_ref[1], df).astype(BF)


def own_grads_kernel(n2_ref, df_ref, du_ref, act_ref, info_ref, keep_ref, send_ref):
    n2 = n2_ref[...]
    df = df_ref[...]
    for slot, ref in ((1, send_ref), (0, keep_ref)):
        q = info_ref[0] ^ slot
        ref[0:C, :] = tn(n2, du_ref[q]).astype(BF)
        ref[C:, :] = tn(act_ref[q], df).astype(BF)


def mlp_keep_kernel(n2_ref, df_ref, du_ref, act_ref, keep_ref):
    keep_ref[0:C, :] = tn(n2_ref[...], du_ref[0]).astype(BF)
    keep_ref[C:, :] = tn(act_ref[0], df_ref[...]).astype(BF)


def up_keep_kernel(n2_ref, du_ref, keep_ref):
    keep_ref[...] = tn(n2_ref[...], du_ref[0]).astype(BF)


def down_grad_kernel(rows, across, *refs):
    (gin_ref, halo_ref, act0_ref, act1_ref, info_ref, g_ref, df_ref, keep_ref, send_ref) = refs

    def tile(r, k):
        if r >= 0:
            return gin_ref[pl.ds(tile_row(r, k, across), SEG), :]
        return edge_tile(halo, k, r + SHIFT)

    halo = halo_ref[...].astype(F32)
    shift_out(tile, g_ref, rows, across)
    df = g_ref[...].astype(BF)
    df_ref[...] = df
    for slot, ref in ((1, send_ref), (0, keep_ref)):
        ref[1] = tn(act1_ref[slot], df).astype(BF)
        ref[0] = tn(act0_ref[info_ref[0] ^ slot], df).astype(BF)


def mlp_bwd_own_kernel(*refs):
    (df_ref, gp_ref, n2_ref, f1_ref, f2_ref, info_ref) = refs[:6]
    (dz_ref, sum_ref, keep_ref, send_ref, du_ref) = refs[6:]
    grad = nt(df_ref[...], f2_ref[0])
    parts = [
        (grad[:, C * z : C * (z + 1)] * gp_ref[z].astype(F32)).astype(BF) for z in range(2)
    ]
    for z in range(2):
        du_ref[z] = parts[z]
    sum_ref[...] = jnp.zeros_like(sum_ref)
    half_sums(parts, sum_ref)
    dz_ref[...] = nt(jnp.concatenate(parts, axis=1), f1_ref[0])
    n2 = n2_ref[...]
    for slot, ref in ((1, send_ref), (0, keep_ref)):
        ref[...] = tn(n2, du_ref[info_ref[0] ^ slot]).astype(BF)


def mlp_bwd_other_kernel(*refs):
    (g_ref, df_ref, hid_ref, n2_ref, gp_ref, dzp_ref, gain_ref, a_ref, b_ref, sumo_ref) = refs[:10]
    (gh_ref, du_ref, send_ref, sum_ref, sh_ref) = refs[10:]
    df = df_ref[...]
    grad = nt(df, down_weight(1, 0, 0, None, a_ref, b_ref))
    parts = [
        (grad[:, C * z : C * (z + 1)] * gp_ref[z].astype(F32)).astype(BF) for z in range(2)
    ]
    for z in range(2):
        du_ref[z] = parts[z]
    sum_ref[0:2] = sumo_ref[...]
    sum_ref[2:4] = jnp.zeros((2, C), F32)
    half_sums(parts, sum_ref.at[2:4])
    dz = dzp_ref[...] + nt(jnp.concatenate(parts, axis=1), up_weight(1, 0, 0, None, a_ref, b_ref))
    xhat, rinv = norm_stats(hid_ref[...])
    sh_ref[0:1] = jnp.sum(dz * xhat, 0, keepdims=True)
    sh_ref[1:2] = jnp.sum(dz, 0, keepdims=True)
    sh_ref[2:3] = jnp.sum(df.astype(F32), 0, keepdims=True)
    gh_ref[...] = g_ref[...] + norm_back(dz, xhat, rinv, gain_ref[0, 1:2])
    send_ref[...] = tn(n2_ref[...], du_ref[1]).astype(BF)


def window_grads(wins, gh_ref, da_ref):
    def four(i, s):
        g = gh_ref[rows_at(i, 4 * WROWS), :]
        for n in range(4):
            part = jnp.concatenate(
                [g[n * WROWS : (n + 1) * WROWS], zero_rows(WPAD - WROWS)], axis=0
            ).astype(BF)
            da_ref[rows_at(4 * i + n, WPAD), :] = part
            s = s + jnp.sum(part.astype(F32), 0, keepdims=True)
        return s

    return repeat(wins // 4, four, jnp.zeros((1, C), F32))


def attend_backward(halves, wins, group, mask_ref):
    def body(i, carry):
        units = [(i * group + u, h) for u in range(group) for h in halves]
        first = []
        for w, (qkv_ref, p_ref, do_ref, dqkv_ref, _) in units:
            at = rows_at(w, WPAD)
            do = spread(do_ref[at, :], mask_ref[...])
            first.append(nt(qkv_ref[2, at, :], do))
            dqkv_ref[2, at, :] = nn(p_ref[w], do).astype(BF)
        second = []
        for (w, (_, p_ref, _, _, acc_ref)), dp in zip(units, first):
            p = p_ref[w].astype(F32)
            ds = p * (dp - jnp.sum(p * dp, 0, keepdims=True))
            for n in range(3):
                acc_ref[n] += ds[:, 128 * n : 128 * (n + 1)]
            second.append(ds.astype(BF))
        for (w, (qkv_ref, _, _, dqkv_ref, _)), ds in zip(units, second):
            at = rows_at(w, WPAD)
            dqkv_ref[1, at, :] = nn(ds, spread(qkv_ref[0, at, :], mask_ref[...])).astype(BF)
            dqkv_ref[0, at, :] = fold(tn(ds, qkv_ref[1, at, :])).astype(BF)
        return carry

    repeat(wins // group, body, 0)


def half_grads(half, par, xn_ref, da_ref, mix_ref, dqkv_ref, row_ref, give):
    def put(value, at):
        if half == 0:
            row_ref[...] = value
            one = row_ref[pl.ds(pl.multiple_of(par * 96, 96), 96), :]
            two = row_ref[pl.ds(pl.multiple_of((1 - par) * 96, 96), 96), :]
        else:
            one, two = value[:96], value[96:]
        give(at, one.astype(BF), two.astype(BF))

    xn = xn_ref[...]
    for j in range(3):
        grad = tn(dqkv_ref[j], xn)
        put(grad * SCALE if j == 0 else grad, 96 * j)
    put(tn(mix_ref[...], da_ref[...]), 288)


def normed_grads(layer, wins, dqkvs, weights, gh_ref, x_ref, gain_ref, gx_ref):
    gain = gain_ref[layer, 0:1]
    n = 8

    def part(i, carry):
        sg, sb, sq = carry
        at = rows_at(i, n * WPAD)
        dn = nn(dqkvs[0][0, at, :], weights[0](0)) + nn(dqkvs[1][0, at, :], weights[1](0))
        dn = dn * SCALE
        for half in range(2):
            for j in (1, 2):
                dn = dn + nn(dqkvs[half][j, at, :], weights[half](j))
        new = []
        for half in range(2):
            for m, j in enumerate((0, 2)):
                new.append(
                    sq[half * 2 + m] + jnp.sum(dqkvs[half][j, at, :].astype(F32), 0, keepdims=True)
                )
        d = jnp.concatenate([dn[k * WPAD : k * WPAD + WROWS] for k in range(n)], axis=0)
        to = rows_at(i, n * WROWS)
        xhat, rinv = norm_stats(x_ref[to, :].astype(F32))
        sg = sg + jnp.sum(d * xhat, 0, keepdims=True)
        sb = sb + jnp.sum(d, 0, keepdims=True)
        gx_ref[to, :] = gh_ref[to, :] + norm_back(d, xhat, rinv, gain)
        return sg, sb, tuple(new)

    z = jnp.zeros((1, C), F32)
    zq = jnp.zeros((1, 6 * HD), F32)
    return repeat(wins // n, part, (z, z, (zq,) * 4))


def small_rows(ref, z, sq, fb1, table, shared):
    ref[...] = jnp.zeros_like(ref)
    if shared is not None:
        sg, sb, projb, sh_ref = shared
        ref[0:1] = sg
        ref[1:2] = sb
        ref[2:3] = projb
        ref[3:6] = sh_ref[...]
    ref[6:7] = fb1
    ref[7:8, 0:96] = sq[0][:, 96 * z : 96 * (z + 1)] * SCALE
    ref[7:8, 128:224] = sq[1][:, 96 * z : 96 * (z + 1)]
    ref[8:24, 0:48] = table[:, 48 * z : 48 * (z + 1)]


def mixed_grad_kernel(wins, gh_ref, projw_ref, a_ref, b_ref, da_ref, do_ref, pb_ref):
    pb_ref[...] = window_grads(wins, gh_ref, da_ref)
    for half in range(2):
        do_ref[half] = nt(da_ref[...], proj_weight_of(half, 1, projw_ref, a_ref, b_ref)).astype(BF)


def attn_bwd_kernel(rows, across, *refs):
    (gh_ref, x_ref, xn_ref, gain_ref, qkvw_ref, a_ref, b_ref, info_ref) = refs[:8]
    (fb1_ref, sh_ref, qkv0_ref, p0_ref, mix0_ref, qkv1_ref, p1_ref, mix1_ref, pick_ref) = refs[8:17]
    (da_ref, do_ref, pb_ref) = refs[17:20]
    (gin_ref, keep_ref, send_ref, edge_ref) = refs[20:24]
    (dqkv0_ref, dqkv1_ref, acc_ref, mask_ref, row_ref, sm_ref) = refs[24:]
    layer = 1
    par = info_ref[0]
    wins = (rows // WIN) * across
    mask_ref[...] = head_mask()
    acc_ref[...] = jnp.zeros_like(acc_ref)
    projb = pb_ref[...]
    attend_backward(
        [
            (qkv0_ref, p0_ref, do_ref.at[0], dqkv0_ref, acc_ref.at[0]),
            (qkv1_ref, p1_ref, do_ref.at[1], dqkv1_ref, acc_ref.at[1]),
        ],
        wins,
        wins,
        mask_ref,
    )
    for half, mix_ref, dqkv_ref in ((1, mix1_ref, dqkv1_ref), (0, mix0_ref, dqkv0_ref)):

        def give(at, one, two, half=half):
            keep_ref[half, at : at + 96, :] = one
            send_ref[half, at : at + 96, :] = two

        half_grads(half, par, xn_ref, da_ref, mix_ref, dqkv_ref, row_ref, give)
    weights = [
        lambda j, half=half: qkv_weight_of(half, j, layer, qkvw_ref, a_ref, b_ref)
        for half in range(2)
    ]
    sg, sb, sq = normed_grads(
        layer, wins, [dqkv0_ref, dqkv1_ref], weights, gh_ref, x_ref, gain_ref, gin_ref
    )
    edge_ref[...] = edge_rows(gin_ref, across, range(rows - SHIFT, rows))
    for half in range(2):
        table = map_to_table(acc_ref.at[half], pick_ref)
        for z in range(2):
            q = 2 * half + z
            small_rows(
                sm_ref.at[q], z, sq[2 * half : 2 * half + 2], fb1_ref[q : q + 1], table,
                (sg, sb, projb, sh_ref)
            )
    keep_ref[0, C:, :] = sm_ref[par].astype(BF)
    send_ref[0, C:, :] = sm_ref[1 - par].astype(BF)
    keep_ref[1, C:, :] = sm_ref[2].astype(BF)
    send_ref[1, C:, :] = sm_ref[3].astype(BF)


def column_sum(ref):
    return jnp.sum(ref[...].astype(F32), 0, keepdims=True)


def attn_bwd_heads_kernel(rows, across, *refs):
    (gh_ref, xn_ref, projw_ref, a_ref, b_ref, fb1_ref) = refs[:6]
    (qkv0_ref, p0_ref, qkv1_ref, p1_ref, mix1_ref, pick_ref) = refs[6:12]
    (da_ref, dqkv0_ref, acc0_ref, dqkv1_ref, pb_ref, keep_ref, send_ref) = refs[12:19]
    (do_ref, mask_ref, acc1_ref, sm_ref) = refs[19:]
    wins = (rows // WIN) * across
    mask_ref[...] = head_mask()
    acc0_ref[...] = jnp.zeros_like(acc0_ref)
    acc1_ref[...] = jnp.zeros_like(acc1_ref)
    pb_ref[...] = window_grads(wins, gh_ref, da_ref)
    da = da_ref[...]
    for half in range(2):
        do_ref[half] = nt(da, proj_weight_of(half, 0, projw_ref, a_ref, b_ref)).astype(BF)
    attend_backward(
        [
            (qkv1_ref, p1_ref, do_ref.at[1], dqkv1_ref, acc1_ref),
            (qkv0_ref, p0_ref, do_ref.at[0], dqkv0_ref, acc0_ref),
        ],
        wins,
        wins,
        mask_ref,
    )

    def give(at, one, two):
        keep_ref[at : at + 96, :] = one
        send_ref[at : at + 96, :] = two

    half_grads(1, None, xn_ref, da_ref, mix1_ref, dqkv1_ref, None, give)
    table = map_to_table(acc1_ref, pick_ref)
    sq = (column_sum(dqkv1_ref.at[0]), column_sum(dqkv1_ref.at[2]))
    for z, ref in ((0, keep_ref), (1, send_ref)):
        small_rows(sm_ref, z, sq, fb1_ref[2 + z : 3 + z], table, None)
        ref[C:, :] = sm_ref[...].astype(BF)


def attn_bwd_own_kernel(rows, across, *refs):
    (gh_ref, x_ref, xn_ref, gain_ref, qkvw_ref, a_ref, b_ref, info_ref) = refs[:8]
    (fb1_ref, sh_ref, da_ref, dqkv_ref, acc_ref, dqkv1_ref, pb_ref, mix_ref, pick_ref) = refs[8:17]
    (out_ref, keep_ref, send_ref) = refs[17:20]
    (gx_ref, row_ref, sm_ref) = refs[20:]
    par = info_ref[0]
    wins = (rows // WIN) * across

    def give(at, one, two):
        keep_ref[at : at + 96, :] = one
        send_ref[at : at + 96, :] = two

    half_grads(0, par, xn_ref, da_ref, mix_ref, dqkv_ref, row_ref, give)
    weights = [
        lambda j, half=half: qkv_weight_of(half, j, 0, qkvw_ref, a_ref, b_ref)
        for half in range(2)
    ]
    sg, sb, sq = normed_grads(
        0, wins, [dqkv_ref, dqkv1_ref], weights, gh_ref, x_ref, gain_ref, gx_ref
    )
    table = map_to_table(acc_ref, pick_ref)
    for z in range(2):
        small_rows(
            sm_ref.at[z], z, sq[0:2], fb1_ref[z : z + 1], table, (sg, sb, pb_ref[...], sh_ref)
        )
    keep_ref[C:, :] = sm_ref[par].astype(BF)
    send_ref[C:, :] = sm_ref[1 - par].astype(BF)
    for r in range(rows):
        parts = [gx_ref[pl.ds(tile_row(r, k, across), SEG), :][:WIN] for k in range(across)]
        out_ref[r, :, 0, :] = jnp.concatenate(parts, axis=0)


def pair_kernel(keep_ref, got_ref, own_ref, oth_ref):
    own_ref[...] = (keep_ref[0].astype(F32) + got_ref[0].astype(F32)).astype(BF)
    oth_ref[...] = (keep_ref[1].astype(F32) + got_ref[1].astype(F32)).astype(BF)


def combine_kernel(parts, bit, n_in, *refs):
    ins = refs[:n_in]
    info_ref = refs[n_in]
    outs = refs[n_in + 1 :]
    at = 0
    for rows, terms, split in parts:

        def total(first, n):
            acc = None
            for i, base in terms:
                x = ins[i][pl.ds(base + first, n), :].astype(F32)
                acc = x if acc is None else acc + x
            return acc.astype(BF)

        if bit is None or not split:
            whole = total(0, rows)
            for out in outs:
                out[at : at + rows, :] = whole
            at += rows
        else:
            n = rows // 2
            b = (info_ref[2] >> bit) & 1
            outs[0][at : at + n, :] = total(pl.multiple_of(b * n, n), n)
            outs[1][at : at + n, :] = total(pl.multiple_of((1 - b) * n, n), n)
            at += n


def close_kernel(halves, bit, mine_ref, got_ref, info_ref, out_ref, small_ref):
    join_kernel(halves, bit, mine_ref.at[0 : sum(halves)], got_ref, info_ref, out_ref)
    at = sum(halves)
    rest = (mine_ref[at:, :].astype(F32) + got_ref[at:, :].astype(F32)).astype(BF)
    n = rest.shape[0] - SMALL
    out_ref[2 * at :, :] = rest[:n]
    small_ref[...] = rest[n:]


def join_kernel(halves, bit, mine_ref, got_ref, info_ref, out_ref):
    b = (info_ref[2] >> bit) & 1
    at = 0
    for n in halves:
        for ref, place in ((mine_ref, b), (got_ref, 1 - b)):
            to = pl.multiple_of(2 * at + place * n, 16)
            out_ref[pl.ds(to, n), :] = ref[at : at + n, :]
        at += n
    if at < mine_ref.shape[0]:
        out_ref[2 * at :, :] = mine_ref[at:, :]


def out_kernel(rows, across, in_ref, halo_ref, o_ref, st_ref):
    st_ref[...] = in_ref[...].astype(F32)
    halo = halo_ref[C + SMALL :, :].astype(F32)
    for r in range(rows):
        parts = []
        for k in range(across):
            if r >= SHIFT:
                t = st_ref[pl.ds(tile_row(r - SHIFT, k, across), SEG), :]
            else:
                t = edge_tile(halo, k, r)
            parts.append(t[:WIN])
        last = parts[-1]
        parts = [last[WIN - SHIFT :]] + parts[:-1] + [last[: WIN - SHIFT]]
        o_ref[r] = jnp.concatenate(parts, axis=0).astype(BF)


def place_of(i, info_ref):
    return info_ref[0] ^ (i // 2), ((info_ref[2] >> 1) & 1) ^ (i % 2)


def put_up(pieces, base, info_ref, ref):
    n = C // 2
    for i in range(4):
        core, half = place_of(i, info_ref)
        rows = pl.ds(pl.multiple_of(half * n, n), n)
        cols = pl.ds(pl.multiple_of(core * C, C), C)
        ref[rows, cols] = pieces[i][base : base + n, :].astype(F32)


def put_down(pieces, base, info_ref, ref):
    n = C // 2
    for i in range(4):
        core, half = place_of(i, info_ref)
        rows = pl.ds(pl.multiple_of(core * C + half * n, n), n)
        ref[rows, :] = pieces[i][base : base + n, :].astype(F32)


def put_attn(pieces, base, info_ref, asm_ref, qkv_ref, proj_ref):
    n = C // 2
    for i in range(4):
        core, half = place_of(i, info_ref)
        rows = pl.ds(pl.multiple_of(half * n, n), n)
        asm_ref[core, rows, :] = pieces[i][base : base + n, :].astype(F32)
    for core in range(2):
        to = pl.ds(96 * core, 96)
        for j in range(3):
            qkv_ref[j, to, :] = asm_ref[core, 96 * j : 96 * (j + 1), :]
        proj_ref[to, :] = asm_ref[core, 288:384, :]


def final_second_kernel(*refs):
    pieces = refs[:4]
    (info_ref, f1_ref, f2_ref, qkv_ref, proj_ref) = refs[4:9]
    (up_ref, down_ref, asm_ref, q_ref, p_ref, sems) = refs[9:]
    put_up(pieces, 0, info_ref, up_ref)
    put_down(pieces, C // 2, info_ref, down_ref)
    put_attn(pieces, C, info_ref, asm_ref, q_ref, p_ref)
    outs = [f1_ref, f2_ref, qkv_ref, proj_ref]
    for copy in copies_of([(x, y.at[1]) for x, y in zip((up_ref, down_ref, q_ref, p_ref), outs)], sems):
        copy.wait()


def final_kernel(*refs):
    mlps, attns, smalls = refs[:4], refs[4:8], refs[8:10]
    (shared_ref, info_ref) = refs[10:12]
    (f1_ref, f2_ref, qkv_ref, proj_ref) = refs[16:20]
    (gain_ref, bias_ref, pb_ref, fb2_ref, qvb_ref, fb1_ref, tab_ref) = refs[20:27]
    (up_ref, down_ref, asm_ref, q_ref, p_ref, sm_ref, sems) = refs[27:]
    put_up(mlps, 0, info_ref, up_ref)
    copies = copies_of([(up_ref, f1_ref.at[0])], sems)
    put_down(mlps, C // 2, info_ref, down_ref)
    copies += copies_of([(down_ref, f2_ref.at[0])], sems.at[1:2])
    put_attn(attns, 0, info_ref, asm_ref, q_ref, p_ref)
    copies += copies_of([(q_ref, qkv_ref.at[0]), (p_ref, proj_ref.at[0])], sems.at[2:4])
    n = C // 2
    par = info_ref[0]
    for layer in range(2):
        for i in range(2):
            x = smalls[i][...] if layer == 1 else attns[2 * i][n:, :]
            sm_ref[par ^ i] = x.astype(F32)
        x, y = sm_ref[0], sm_ref[1]
        shared = x[0:6]
        if layer == 0:
            shared = sm_ref[par, 0:6, :] + shared_ref[0:6].astype(F32)
        gain_ref[layer, 0:1] = shared[0:1]
        gain_ref[layer, 1:2] = shared[3:4]
        bias_ref[layer, 0:1] = shared[1:2]
        bias_ref[layer, 1:2] = shared[4:5]
        pb_ref[layer : layer + 1] = shared[2:3]
        fb2_ref[layer : layer + 1] = shared[5:6]
        fb1_ref[layer : layer + 1, 0:C] = x[6:7]
        fb1_ref[layer : layer + 1, C:] = y[6:7]
        for k in range(2):
            qvb_ref[layer, k : k + 1, 0:96] = x[7:8, 128 * k : 128 * k + 96]
            qvb_ref[layer, k : k + 1, 96:192] = y[7:8, 128 * k : 128 * k + 96]
        t = jnp.concatenate([x[8:24, 0:48], y[8:24, 0:48]], axis=1)
        wide = tn(t.astype(BF), offset_rows().astype(BF)) * offset_cols()
        for h in range(6):
            tab_ref[h, layer : layer + 1, :] = jnp.sum(
                wide[16 * h : 16 * (h + 1)], 0, keepdims=True
            )
    for copy in copies:
        copy.wait()


VMEM = pl.BlockSpec(memory_space=pltpu.VMEM)
HBM = pl.BlockSpec(memory_space=pltpu.HBM)


class Position:
    def __getitem__(self, k):
        if k == 1:
            return lax.axis_index("tp")
        win = lax.axis_index("win")
        return win if k == 2 else lax.rem(win, 2)


POSITION = Position()


def call(kernel, name, us, limit, operands, outs, scratch=(), aliases=None):
    args = []
    specs = []
    at = [n for n, op in enumerate(operands) if op is POSITION]
    if at:
        (at,) = at
        inner = kernel

        def kernel(*refs):
            return inner(*refs[:at], POSITION, *refs[at:])

        operands = operands[:at] + operands[at + 1 :]
        aliases = {k - (k > at): v for k, v in (aliases or {}).items()}
    for op in operands:
        args.append(op[0] if isinstance(op, tuple) else op)
        specs.append(op[1] if isinstance(op, tuple) else VMEM)
    shapes = [jax.ShapeDtypeStruct(o[0], o[1]) for o in outs]
    return pl.pallas_call(
        kernel,
        name=name,
        in_specs=specs,
        out_specs=[o[2] if len(o) > 2 else VMEM for o in outs],
        input_output_aliases=aliases or {},
        out_shape=shapes,
        scratch_shapes=[s if not isinstance(s, tuple) else pltpu.VMEM(*s) for s in scratch],
        cost_estimate=pl.CostEstimate(
            flops=int(us * 1e10), bytes_accessed=1000000, transcendentals=0
        ),
        compiler_params=pltpu.CompilerParams(vmem_limit_bytes=limit * 2**20),
    )(*args)


def on_device(n_win, *args):
    (
        tokens,
        crop_ids,
        cotangent,
        norm_gain,
        norm_bias,
        qkv_weight,
        qv_bias,
        proj_weight,
        proj_bias,
        fc1_weight,
        fc1_bias,
        fc2_weight,
        fc2_bias,
        pos_table,
    ) = args
    rows, cols = tokens.shape[1:3]
    across = cols // WIN
    wins = (rows // WIN) * across
    ntok = wins * WROWS
    npad = wins * WPAD
    win = lax.axis_index("win")
    tp = lax.axis_index("tp")
    par = win % 2
    info = POSITION
    bits = n_win.bit_length() - 1
    assert n_win == 1 << bits and bits >= 3

    def to_tp(x, name):
        with jax.named_scope(name + "_tp"):
            return lax.ppermute(x, "tp", [(0, 1), (1, 0)])

    def to_win(x, bit, name):
        if bit >= bits:
            return jnp.zeros_like(x)
        with jax.named_scope("%s_win%d" % (name, bit)):
            return lax.ppermute(x, "win", [(i, i ^ (1 << bit)) for i in range(n_win)])

    def after(x, *others):
        return lax.optimization_barrier((x,) + others)[0]

    def combine(parts, bit, ins, name):
        total = sum(rows // 2 if split and bit is not None else rows for rows, _, split in parts)
        outs = [((total, C), BF)] * (1 if bit is None else 2)
        return call(
            partial(combine_kernel, parts, bit, len(ins)), name, 1, 4, tuple(ins) + (info,), outs
        )

    def join(halves, bit, mine, got, name):
        return call(
            partial(join_kernel, halves, bit), name, 1, 4, (mine, got, info),
            [((mine.shape[0] + sum(halves), C), BF)],
        )[0]

    qkv_t = qkv_weight.transpose(0, 2, 3, 1)
    table = pos_table.transpose(2, 0, 1)
    na = C + SMALL
    n = C // 2
    edge_b = ((across * SHIFT * SEG, C), BF)
    a0q, small = call(
        pack_first_kernel,
        "pack_first",
        0.1,
        60,
        tuple((x, HBM) for x in (qkv_t, proj_weight, table, qv_bias, fc1_bias)),
        [((C + 2 * SENT_ROWS, C), BF), ((2, SMALL_ROWS, C), F32)],
        [
            (table.shape, F32),
            (qv_bias.shape, F32),
            (fc1_bias.shape, F32),
            pltpu.SemaphoreType.DMA((7,)),
        ],
    )
    a0 = to_tp(a0q, "a0")
    m0q, a1q, m1q, cot_edge = call(
        pack_kernel,
        "pack",
        0.1,
        60,
        tuple((x, HBM) for x in (qkv_t, proj_weight, fc1_weight, fc2_weight, cotangent[0]))
        + (after(small, a0q), info),
        [
            ((2 * C, C), BF),
            ((C + 2 * SENT_ROWS, C), BF),
            ((2 * C, C), BF),
            ((EDGE_ROWS, C), BF),
        ],
        [((SHIFT, cols, C), BF), pltpu.SemaphoreType.DMA((9,))],
    )
    m0 = to_tp(m0q, "m0")
    crops = crop_ids.transpose(2, 0, 1)
    label_outs = [((wins, 128), F32), ((wins, WPAD, 128), F32), ((3, WPAD, 128), F32)]
    lq0, lk0, pos0, pick = call(
        partial(prep_kernel, 0, rows, across),
        "prep_0",
        0.1,
        8,
        (crops, after(small, m0q), info),
        label_outs + [((WIN, 96, 6 * WPAD), BF)],
        [((128, 128), F32)],
    )
    tiles = (rows // WIN, across, WIN, SEG, C)
    mask = ((6 * WPAD, 6 * HD), BF)
    half_outs = [((3, npad, 192), BF), ((wins, WPAD, 6 * WPAD), BF), ((npad, 192), BF)]
    tok_f = ((ntok, C), F32)
    tok_b = ((ntok, C), BF)
    hid_b = ((4, ntok, C), BF)
    other_scratch = [mask, ((3, WPAD, 128), F32)]

    x0, xn0, part, qkv00, p00, mix00 = call(
        partial(attn_own_kernel, rows, across),
        "attn_own_0",
        0.1,
        8,
        (tokens[0], norm_gain, norm_bias, proj_bias, qv_bias, qkv_t, proj_weight, pos0, lq0, lk0),
        [tok_b, ((npad, C), BF), tok_f] + half_outs,
        [mask, tok_f],
    )
    lq1, lk1, pos1 = call(
        partial(prep_kernel, 1, rows, across),
        "prep_1",
        0.1,
        8,
        (crops, after(small, part), info, pick),
        label_outs,
        [((128, 128), F32)],
    )
    a1 = to_tp(after(a1q, lq1), "a1")
    a0 = after(a0, lq1)
    a0s = to_win(a0, 0, "a0")
    hid0, qkv01, p01, mix01, small0 = call(
        partial(attn_other_kernel, rows, across),
        "attn_other_0",
        0.1,
        8,
        (part, xn0, a0, a0s, lq0, lk0, pick, info),
        [tok_f] + half_outs + [((SMALL_ROWS, C), F32)],
        other_scratch,
    )
    half_b = ((2, ntok, C), BF)
    st_own, n2f, act00, gp00 = call(
        mlp_own_kernel,
        "mlp_own_0",
        0.1,
        10,
        (hid0, norm_gain, norm_bias, fc1_bias, fc2_bias, fc1_weight, fc2_weight),
        [tok_f, tok_b, half_b, half_b],
    )
    m0 = after(m0, st_own)
    m0s = to_win(m0, 0, "m0")
    st0, act01, gp01, edge = call(
        partial(mlp_other_kernel, across),
        "mlp_other_0",
        3,
        10,
        (st_own, n2f, fc1_bias, small0, m0, m0s, info),
        [tok_f, half_b, half_b, edge_b],
    )
    halo = to_tp(edge, "edge0")
    a1 = after(a1, halo)
    a1s = to_win(a1, 0, "a1")
    cot_edge = to_tp(after(cot_edge, edge), "cot")
    m1 = to_tp(after(m1q, edge), "m1")
    x1, xn1, qkv10 = call(
        partial(norm_kernel, rows, across),
        "norm_1",
        2,
        6,
        (st0, halo, norm_gain, norm_bias, qv_bias, qkv_t),
        [tok_f, ((npad, C), BF), half_outs[0]],
    )
    mix_out = half_outs[2] + (HBM,)
    hid1, p10, mix10, qkv11, p11, mix11, small1 = call(
        partial(attn_both_kernel, rows, across),
        "attn_fwd_1",
        10,
        12,
        (xn1, qkv10, pos1, a1, a1s, x1, proj_weight, proj_bias, lq1, lk1, pick, info),
        [tok_f, half_outs[1], mix_out] + half_outs[:2] + [mix_out, ((SMALL_ROWS, C), F32)],
        other_scratch + [half_outs[2], half_outs[2], pltpu.SemaphoreType.DMA((2,))],
    )
    sums = [((4, C), F32), ((3, C), F32)]
    g1, df1, n21, st_own, dz_own, du10, act10, sum10, sf1 = call(
        partial(mlp_own_both_kernel, rows, across),
        "mlp_own_1",
        5,
        6,
        (cotangent[0], after(cot_edge, a1s), hid1, norm_gain, norm_bias, fc1_bias, fc2_bias)
        + (fc1_weight, fc2_weight),
        [tok_f, tok_b, tok_b, tok_f, tok_f, half_b, half_b, ((2, C), F32), ((1, C), F32)],
    )
    m1 = after(m1, dz_own)
    m1s = to_win(m1, 0, "m1")
    whole_q = ((2 * C, C), BF)
    keep_mo, send_mo = call(
        own_grads_kernel, "own_grads_1", 2, 4, (after(n21, m1), df1, du10, act10, info),
        [whole_q, whole_q],
    )
    mo_core = to_win(send_mo, 0, "gmo")
    st1, gh1, du11, act11, send_mx, gfb1, gsh1, out_edge = call(
        partial(mlp_other_both_kernel, rows, across),
        "mlp_other_1",
        6,
        8,
        (after(hid1, keep_mo), g1, df1, n21, st_own, dz_own, norm_gain, fc1_bias, small1, m1, m1s)
        + (info, sum10, sf1),
        [tok_b, tok_f, half_b, half_b, whole_q] + sums + [edge_b],
        [tok_f],
        aliases={1: 1},
    )

    def plus(x, y, name):
        return combine([(x.shape[0], [(0, 0), (1, 0)], True)], None, (x, y), name)[0]

    def pair(keep, got, name):
        shape = keep.shape[1:]
        return call(pair_kernel, name, 1, 4, (keep, got), [(shape, BF), (shape, BF)])

    mx_core = to_win(send_mx, 0, "gmx")
    (keep_mx,) = call(mlp_keep_kernel, "mlp_keep_1", 1, 4, (n21, df1, du11, act11), [whole_q])
    m1_oth = plus(keep_mx, after(mx_core, keep_mx), "m1_oth")
    m1_own = plus(keep_mo, after(mo_core, m1_oth), "m1_own")
    m1_t = to_tp(m1_oth, "gm1")
    da1, do1, pb1 = call(
        partial(mixed_grad_kernel, wins),
        "mixed_grad_1",
        0.1,
        4,
        (after(gh1, m1_own), proj_weight, a1, a1s),
        [((npad, C), BF), ((2, npad, 192), BF), ((1, C), F32)],
    )
    gin1, keep_a1, send_a1, edge = call(
        partial(attn_bwd_kernel, rows, across),
        "attn_bwd_1",
        14,
        8,
        (gh1, x1, xn1, norm_gain, qkv_t, a1, a1s, info)
        + (gfb1, gsh1, qkv10, p10, mix10, qkv11, p11, mix11, pick, da1, do1, pb1),
        [tok_f, ((2, na, C), BF), ((2, na, C), BF), edge_b],
        [
            ((3, npad, 192), BF),
            ((3, npad, 192), BF),
            ((2, 3, WPAD, 128), F32),
            mask,
            ((192, C), F32),
            ((4, SMALL, C), F32),
        ],
    )
    halo = to_tp(edge, "edge1")
    a1_core = to_win(after(send_a1, edge), 0, "ga1")
    m1_mine, m1_away = combine(
        [(C, [(0, 0), (1, 0)], True), (C, [(0, C), (1, C)], True)],
        1,
        (m1_own, after(m1_t, edge)),
        "m1_y",
    )
    m1_y = to_win(m1_away, 1, "gm1")
    a1_own, a1_oth = pair(keep_a1, after(a1_core, m1_away), "pair_a1")
    a1_t = to_tp(a1_oth, "ga1")
    g0, df0, keep_f2, send_f2 = call(
        partial(down_grad_kernel, rows, across),
        "down_grad_0",
        4,
        5,
        (gin1, after(halo, a1_oth), act00, act01, info),
        [tok_f, tok_b, ((2, C, C), BF), ((2, C, C), BF)],
    )
    f2_core = to_win(send_f2, 0, "gf2")
    quarter_b = ((C, C), BF)
    dz0, sum00, keep_fo, send_fo = call(
        mlp_bwd_own_kernel,
        "mlp_bwd_own_0",
        2,
        8,
        (df0, gp00, n2f, fc1_weight, fc2_weight, info),
        [tok_f, ((2, C), F32), quarter_b, quarter_b],
        [half_b],
    )
    fo_core = to_win(send_fo, 0, "gfo")
    m1_mine, m1_away = combine(
        [(n, [(0, 0), (1, 0)], True), (n, [(0, n), (1, n)], True)],
        2,
        (m1_mine, after(m1_y, dz0)),
        "m1_z",
    )
    m1_z = to_win(m1_away, 2, "gm1")
    f2_own, f2_oth = pair(keep_f2, after(f2_core, m1_away), "pair_f2")
    f2_t = to_tp(f2_oth, "gf2")
    a1_mine, a1_away = combine(
        [(C, [(0, 0), (1, 0)], True), (SMALL, [(0, C), (1, C)], False)],
        1,
        (a1_own, after(a1_t, f2_oth)),
        "a1_y",
    )
    a1_y = to_win(a1_away, 1, "ga1")
    gh0, du01, send_fx, gfb0, gsh0 = call(
        mlp_bwd_other_kernel,
        "mlp_bwd_other_0",
        3,
        8,
        (after(g0, a1_away), df0, hid0, n2f, gp01, dz0, norm_gain, m0, m0s, sum00),
        [tok_f, half_b, quarter_b] + sums,
    )
    m1 = plus(m1_mine, after(m1_z, send_fx), "m1_z2")
    m1_b = to_win(m1, 3, "gm1")
    fx_core = to_win(send_fx, 0, "gfx")
    (keep_fx,) = call(up_keep_kernel, "up_keep_0", 1, 4, (n2f, du01), [quarter_b])
    f1_oth = plus(keep_fx, after(fx_core, keep_fx), "f1_oth")
    f1_t = to_tp(f1_oth, "gf1")
    f1_own = plus(keep_fo, after(fo_core, f1_oth), "f1_own")
    a1 = plus(a1_mine, after(a1_y, f1_own), "a1_z2")
    a1_b = to_win(a1, 3, "ga1")
    da, dqkv0, acc0, dqkv1, pb0, keep_o0, send_o0 = call(
        partial(attn_bwd_heads_kernel, rows, across),
        "attn_bwd_heads_0",
        8,
        8,
        (after(gh0, a1, f2_t), xn0, proj_weight, a0, a0s, gfb0)
        + (qkv00, p00, qkv01, p01, mix01, pick),
        [
            ((npad, C), BF),
            ((3, npad, 192), BF),
            ((3, WPAD, 128), F32),
            ((3, npad, 192), BF),
            ((1, C), F32),
            ((na, C), BF),
            ((na, C), BF),
        ],
        [((2, npad, 192), BF), mask, ((3, WPAD, 128), F32), ((SMALL, C), F32)],
    )
    o0_core = to_win(send_o0, 0, "go0")
    m0_mine, m0_away = combine(
        [(C, [(0, 0), (1, 0)], True), (C, [(2, 0), (3, 0)], True)],
        1,
        (f1_own, after(f1_t, send_o0), f2_own, f2_t),
        "m0_y",
    )
    m0_y = to_win(m0_away, 1, "gm0")
    (o0_sum,) = combine(
        [(na, [(0, 0), (1, 0)], True), (edge_b[0][0], [(2, 0)], True)],
        None,
        (keep_o0, after(o0_core, m0_away), out_edge),
        "o0",
    )
    o0_t = to_tp(o0_sum, "go0")
    (c1,) = combine(
        [(n, [(0, 0), (1, 0)], True), (n + SMALL, [(2, 0), (3, 0)], True)],
        None,
        (m1, after(m1_b, o0_sum), a1, after(a1_b, o0_sum)),
        "c1",
    )
    for bit in range(4, bits):
        c1 = plus(c1, to_win(c1, bit, "gc1"), "c1_sum")
    c1_b = to_win(c1, 2, "gc1")
    grad_tokens, keep_a0, send_a0 = call(
        partial(attn_bwd_own_kernel, rows, across),
        "attn_bwd_own_0",
        9,
        7,
        (gh0, x0, xn0, norm_gain, qkv_t, a0, a0s, info)
        + (gfb0, gsh0, da, dqkv0, acc0, dqkv1, pb0, after(mix00, c1), pick),
        [((rows, cols, 1, C), F32), ((na, C), BF), ((na, C), BF)],
        [tok_f, ((192, C), F32), ((2, SMALL, C), F32)],
    )

    a0_core = to_win(send_a0, 0, "ga0")
    m0_mine, m0_away = combine(
        [(n, [(0, 0), (1, 0)], True), (n, [(0, n), (1, n)], True)],
        2,
        (m0_mine, after(m0_y, send_a0)),
        "m0_z",
    )
    m0_z = to_win(m0_away, 2, "gm0")
    a0_mine, a0_away = combine(
        [(C, [(0, 0), (1, 0), (2, 0)], True), (SMALL, [(0, C), (1, C), (2, C)], False)],
        1,
        (keep_a0, after(a0_core, m0_away), o0_t),
        "a0_y",
    )
    a0_y = to_win(a0_away, 1, "ga0")
    c1, c1_small = call(
        partial(close_kernel, [n // 2] * 2, 2), "c1_close", 1, 8, (c1, after(c1_b, a0_away), info),
        [((3 * n, C), BF), ((SMALL, C), BF)],
    )
    c1_back = to_win(c1, 1, "gc1_back")
    c1_sib = to_win(c1, 0, "gc1_mine")
    c1_small_sib = to_win(c1_small, 0, "gc1_small")
    m0 = plus(m0_mine, after(m0_z, c1), "m0_z2")
    m0_b = to_win(m0, 3, "gm0")
    a0 = plus(a0_mine, after(a0_y, m0), "a0_z")
    a0_z = to_win(a0, 2, "ga0")
    (layer_out,) = call(
        partial(out_kernel, rows, across), "layer_out", 1, 8, (after(st1, a0), o0_t),
        [((rows, cols, C), BF)],
        [tok_f],
    )
    m0 = plus(m0, after(m0_b, layer_out), "m0_sum")
    for bit in range(4, bits):
        m0 = plus(m0, to_win(m0, bit, "gm0"), "m0_sum")
    m0_b = to_win(m0, 2, "gm0_back")
    a0 = plus(a0, after(a0_z, m0), "a0_z2")
    a0_b = to_win(a0, 3, "ga0")
    c1_back = after(c1_back, a0)
    c1_pieces = (c1, c1_back, c1_sib, to_win(c1_back, 0, "gc1_theirs"))
    m0 = join([n // 2] * 2, 2, m0, after(m0_b, c1_back), "m0_join")
    m0_back = to_win(m0, 1, "gm0_back")
    m0_sib = to_win(m0, 0, "gm0_mine")
    c1_small_sib, c1_pieces = after((c1_small_sib, c1_pieces), m0)
    f1_shape, f2_shape = (2, C, 2 * C), (2, 2 * C, C)
    qkv_shape, proj_shape = (2, 3, 192, C), (2, 192, C)
    whole = [(f1_shape, F32, HBM), (f2_shape, F32, HBM), (qkv_shape, F32, HBM), (proj_shape, F32, HBM)]
    parts = [(x[0][1:], F32) for x in whole]
    attn_parts = [((2, C, C), F32)] + parts[2:]
    g_f1, g_f2, g_qkv, g_proj = call(
        final_second_kernel, "final_second", 1, 9, c1_pieces + (info,), whole,
        parts[:2] + attn_parts + [pltpu.SemaphoreType.DMA((4,))],
    )
    a0 = plus(a0, after(a0_b, g_f1), "a0_sum")
    for bit in range(4, bits):
        a0 = plus(a0, to_win(a0, bit, "ga0"), "a0_sum")
    a0_back = to_win(a0, 1, "ga0_back")
    a0_sib = to_win(a0, 0, "ga0_mine")
    shared = to_tp(a0[n : n + 16], "shared")
    m0_back = after(m0_back, a0_sib, shared)
    m0_pieces = (m0, m0_back, m0_sib, to_win(m0_back, 0, "gm0_theirs"))
    outs = call(
        final_kernel,
        "final",
        0.1,
        9,
        m0_pieces
        + (a0, a0_back, a0_sib, to_win(a0_back, 0, "ga0_theirs"), c1_small, c1_small_sib)
        + (shared, info, (g_f1, HBM), (g_f2, HBM), (g_qkv, HBM), (g_proj, HBM)),
        whole
        + [
            ((2, 2, C), F32),
            ((2, 2, C), F32),
            ((2, C), F32),
            ((2, C), F32),
            ((2, 2, 192), F32),
            ((2, 2 * C), F32),
            ((6, 2, 169), F32),
        ],
        parts[:2] + attn_parts + [((2, SMALL, C), F32), pltpu.SemaphoreType.DMA((4,))],
        aliases={12: 0, 13: 1, 14: 2, 15: 3},
    )
    (g_f1, g_f2, g_qkv, g_proj, g_gain, g_bias, g_pb, g_fb2, g_qvb, g_fb1, g_tab) = outs
    return (
        layer_out[None],
        grad_tokens.transpose(2, 0, 1, 3),
        g_gain,
        g_bias,
        g_qkv.transpose(0, 3, 1, 2),
        g_qvb,
        g_proj,
        g_pb,
        g_f1,
        g_fb1,
        g_f2,
        g_fb2,
        g_tab.transpose(1, 2, 0),
    )


def solution(mesh):
    return jax.shard_map(
        partial(on_device, mesh.shape["win"]),
        mesh=mesh,
        in_specs=(
            P("win", "tp", None, None),
            P("win", None, None),
            P("win", "tp", None, None),
            P(),
            P(),
            P(None, None, None, "tp"),
            P(None, None, "tp"),
            P(None, "tp", None),
            P(),
            P(None, None, "tp"),
            P(None, "tp"),
            P(None, "tp", None),
            P(),
            P(None, None, "tp"),
        ),
        out_specs=(
            P("win", "tp", None, None),
            P("win", "tp", None, None),
            P(),
            P(),
            P(None, None, None, "tp"),
            P(None, None, "tp"),
            P(None, "tp", None),
            P(),
            P(None, None, "tp"),
            P(None, "tp"),
            P(None, "tp", None),
            P(),
            P(None, None, "tp"),
        ),
        check_vma=False,
    )
```

```python
from functools import partial

import jax
import jax.numpy as jnp
import numpy as np
from jax import lax
from jax.experimental import pallas as pl
from jax.experimental.pallas import tpu as pltpu
from jax.sharding import PartitionSpec as P

C = 384
WIN = 7
SHIFT = 3
HD = 32
EPS = 1e-05
NEG = -1000000000.0
SCALE = HD**-0.5
F32 = jnp.float32
BF = jnp.bfloat16
SEG = 8
WROWS = WIN * SEG
WPAD = 64


def nn(a, b):
    return lax.dot_general(a, b, (((1,), (0,)), ((), ())), preferred_element_type=F32)


def nt(a, b):
    return lax.dot_general(a, b, (((1,), (1,)), ((), ())), preferred_element_type=F32)


def tn(a, b):
    return lax.dot_general(a, b, (((0,), (0,)), ((), ())), preferred_element_type=F32)


def norm_stats(x):
    mean = jnp.mean(x, -1, keepdims=True)
    cent = x - mean
    var = jnp.mean(cent * cent, -1, keepdims=True)
    rinv = lax.rsqrt(var + EPS)
    return cent * rinv, rinv


def norm_back(dz, xhat, rinv, gain):
    d = dz * gain
    return rinv * (
        d - jnp.mean(d, -1, keepdims=True) - xhat * jnp.mean(d * xhat, -1, keepdims=True)
    )


def tile_row(r, k, across):
    return (((r // WIN) * across + k) * WIN + r % WIN) * SEG


def zero_rows(n):
    return jnp.zeros((n, C), F32)


def head_mask():
    row = lax.broadcasted_iota(jnp.int32, (6 * WPAD, 6 * HD), 0) // WPAD
    col = lax.broadcasted_iota(jnp.int32, (6 * WPAD, 6 * HD), 1) // HD
    return (row == col).astype(BF)


def spread(x, mask):
    return jnp.concatenate([x] * 6, axis=0) * mask


def fold(o):
    lane = lax.broadcasted_iota(jnp.int32, (WPAD, 128), 1)

    def of(h, a, b):
        return o[WPAD * h : WPAD * (h + 1), a:b]

    one = jnp.where(lane < 96, of(2, 0, 128), of(3, 0, 128))
    one = jnp.where(lane < 64, of(1, 0, 128), one)
    one = jnp.where(lane < 32, of(0, 0, 128), one)
    two = jnp.where(lane[:, :64] < 32, of(4, 128, 192), of(5, 128, 192))
    return jnp.concatenate([one, two], axis=1)


def rows_at(i, n):
    return pl.ds(i * n, n)


def repeat(n, body, carry):
    for i in range(n):
        carry = body(i, carry)
    return carry


def iota(shape, dim):
    return lax.broadcasted_iota(jnp.int32, shape, dim)


def exact(a, b, ca, cb):
    return lax.dot_general(
        a,
        b,
        (((ca,), (cb,)), ((), ())),
        precision=lax.Precision.HIGHEST,
        preferred_element_type=F32,
    )


def offset_rows():
    return (12 - iota((16, 169), 0) == iota((16, 169), 1) // 13).astype(F32)


def offset_cols():
    return (iota((96, 169), 0) % 16 == iota((96, 169), 1) % 13).astype(F32)


def column_pick(kx):
    r = iota((96, 6 * WPAD), 0)
    c = iota((96, 6 * WPAD), 1)
    qx = c % 8
    return ((r // 16 == c // WPAD) & (r % 16 == qx - kx + WIN - 1) & (qx < WIN)).astype(BF)


def table_to_map(t, pick_ref, pos_ref):
    pos_ref[...] = jnp.zeros_like(pos_ref)
    group = (iota((8, 6 * WPAD), 1) % WPAD) // 8
    high = t.astype(BF)
    low = (t - high.astype(F32)).astype(BF)
    both = jnp.concatenate([high, low], axis=0)
    for kx in range(WIN):
        h = nn(both, pick_ref[kx])
        h = h[:16] + h[16:]
        g = jnp.zeros((8, 6 * WPAD), F32)
        for j in range(WIN):
            g = jnp.where(group == j, h[6 - j : 14 - j], g)
        for i in range(3):
            pos_ref[i, pl.ds(kx, 8, stride=8), :] = g[:, 128 * i : 128 * (i + 1)]


def map_to_table(pos_ref, pick_ref):
    group = (iota((16, 6 * WPAD), 1) % WPAD) // 8
    total = jnp.zeros((16, 96), F32)
    for kx in range(WIN):
        r = jnp.concatenate([pos_ref[i, pl.ds(kx, 8, stride=8), :] for i in range(3)], axis=1)
        h = jnp.zeros((16, 6 * WPAD), F32)
        for j in range(WIN):
            parts = [r, jnp.zeros((2 + j, 6 * WPAD), F32)]
            if j < 6:
                parts = [jnp.zeros((6 - j, 6 * WPAD), F32)] + parts
            h = jnp.where(group == j, jnp.concatenate(parts, axis=0), h)
        total = total + nt(h.astype(BF), pick_ref[kx])
    return total


def shift_in(tile, x_ref, rows, across):
    for r in range(rows):
        for k in range(across):
            a = tile(r + SHIFT, k)
            b = tile(r + SHIFT, (k + 1) % across)
            x_ref[pl.ds(tile_row(r, k, across), SEG), :] = jnp.concatenate(
                [a[SHIFT:WIN], b[:SHIFT], zero_rows(1)], axis=0
            )


def shift_out(tile, x_ref, rows, across):
    for r in range(rows):
        for k in range(across):
            a = tile(r - SHIFT, (k - 1) % across)
            b = tile(r - SHIFT, k)
            x_ref[pl.ds(tile_row(r, k, across), SEG), :] = jnp.concatenate(
                [a[WIN - SHIFT : WIN], b[: WIN - SHIFT], zero_rows(1)], axis=0
            )

EDGE_ROWS = 96
SMALL = 32


SMALL_ROWS = 24
SENT_ROWS = 8


def copies_of(pairs, sems):
    copies = [pltpu.make_async_copy(x, y, sems.at[n]) for n, (x, y) in enumerate(pairs)]
    for copy in copies:
        copy.start()
    return copies


def attn_copies(layer, par, qkvw_ref, projw_ref, a_ref):
    of_heads = pl.ds(pl.multiple_of(par * 96, 96), 96)
    pairs = [
        (qkvw_ref.at[layer, j, of_heads, :], a_ref.at[pl.ds(96 * j, 96), :]) for j in range(3)
    ]
    return pairs + [(projw_ref.at[layer, of_heads, :], a_ref.at[pl.ds(288, 96), :])]


def mlp_copies(layer, par, f1_ref, f2_ref, m_ref):
    of_units = pl.ds(pl.multiple_of(par * C, C), C)
    return [
        (f1_ref.at[layer, :, of_units], m_ref.at[pl.ds(0, C), :]),
        (f2_ref.at[layer, of_units, :], m_ref.at[pl.ds(C, C), :]),
    ]


def high_low(x):
    rows = []
    for r in range(4):
        rows.append(jnp.concatenate([x[4 * r + k : 4 * r + k + 1, 0:96] for k in range(4)], axis=1))
    rows.append(x[16:18])
    rows.append(jnp.concatenate([x[18:19, 0:192], x[19:20, 0:192]], axis=1))
    rows.append(zero_rows(1))
    x = jnp.concatenate(rows, axis=0)
    high = x.astype(BF).astype(F32)
    return jnp.concatenate([high, x - high], axis=0).astype(BF)


def pack_first_kernel(
    qkvw_ref, projw_ref, tab_ref, qvb_ref, fb1_ref,
    a0_ref, small_ref, tab_v, qvb_v, fb1_v, sems
):
    pairs = [(tab_ref, tab_v), (qvb_ref, qvb_v), (fb1_ref, fb1_v)]
    copies = copies_of(pairs + attn_copies(0, POSITION[0], qkvw_ref, projw_ref, a0_ref), sems)
    small_ref[...] = jnp.zeros_like(small_ref)
    for copy in copies[:3]:
        copy.wait()
    for layer in range(2):
        tab = tab_v[:, layer, :]
        wide = jnp.concatenate([jnp.broadcast_to(tab[h : h + 1], (16, 169)) for h in range(6)])
        small_ref[layer, 0:16, 0:96] = exact(offset_rows(), wide * offset_cols(), 1, 1)
        small_ref[layer, 16:17, :] = fb1_v[layer : layer + 1, 0:C]
        small_ref[layer, 17:18, :] = fb1_v[layer : layer + 1, C:]
        small_ref[layer, 18:20, 0:192] = qvb_v[layer]
    a0_ref[C:, :] = high_low(small_ref[0])
    for copy in copies[3:]:
        copy.wait()


def pack_kernel(
    qkvw_ref, projw_ref, f1_ref, f2_ref, cot_ref, small_ref, info_ref,
    m0_ref, a1_ref, m1_ref, edge_ref, cot_v, sems
):
    par = info_ref[0]
    pairs = [(cot_ref.at[pl.ds(0, SHIFT)], cot_v)]
    pairs += mlp_copies(0, par, f1_ref, f2_ref, m0_ref)
    pairs += attn_copies(1, par, qkvw_ref, projw_ref, a1_ref)
    pairs += mlp_copies(1, par, f1_ref, f2_ref, m1_ref)
    copies = copies_of(pairs, sems)
    a1_ref[C:, :] = high_low(small_ref[1])
    copies[0].wait()
    edge = [cot_v[r].astype(F32) for r in range(SHIFT)]
    n = EDGE_ROWS - SHIFT * cot_v.shape[1]
    edge_ref[...] = jnp.concatenate(edge + [zero_rows(n)], axis=0).astype(BF)
    for copy in copies[1:]:
        copy.wait()


def small_of(a_ref, small_ref):
    rows = a_ref[C : C + 2 * SENT_ROWS, :].astype(F32)
    x = rows[0:SENT_ROWS] + rows[SENT_ROWS:]
    small_ref[...] = jnp.zeros_like(small_ref)
    for r in range(4):
        for k in range(4):
            small_ref[4 * r + k : 4 * r + k + 1, 0:96] = x[r : r + 1, 96 * k : 96 * (k + 1)]
    small_ref[16:18, :] = x[4:6]
    small_ref[18:19, 0:192] = x[6:7, 0:192]
    small_ref[19:20, 0:192] = x[6:7, 192:384]


def edge_tile(edge, k, r):
    at = (k * SHIFT + r) * SEG
    return edge[at : at + SEG]


def edge_rows(ref, across, rows):
    tiles = [ref[pl.ds(tile_row(r, k, across), SEG), :] for k in range(across) for r in rows]
    return jnp.concatenate(tiles, axis=0).astype(BF)


def prep_kernel(layer, rows, across, *refs):
    (crop_ref, small_ref, info_ref) = refs[:3]
    if layer == 0:
        (lq_ref, lk_ref, pos_ref, pick_ref, c_ref) = refs[3:]
        for kx in range(WIN):
            pick_ref[kx] = column_pick(kx)
    else:
        (pick_ref, lq_ref, lk_ref, pos_ref, c_ref) = refs[3:]
    tp = info_ref[1]
    cols = across * WIN
    height = crop_ref.shape[2]
    table_to_map(small_ref[layer, 0:16, 0:96], pick_ref, pos_ref)
    c_ref[...] = jnp.zeros_like(c_ref)
    c_ref[0:cols, 0:height] = crop_ref[:, 0, :].astype(F32)
    crops = c_ref[...].astype(BF)
    row = iota((32, 128), 0)
    lane = iota((32, 128), 1)
    shift = SHIFT if layer == 1 else 0
    src = rows * tp + row + shift
    src = jnp.where(src >= height, src - height, src)
    grid = nt((src == lane).astype(BF), crops).astype(BF)
    labs = []
    for wc in range(across):
        qx = iota((128, 128), 1) % 8
        col = qx + (WIN * wc + shift)
        col = jnp.where(col >= cols, col - cols, col)
        pick = ((col == iota((128, 128), 0)) & (qx < WIN)).astype(BF)
        lab = nn(grid, pick)
        if layer == 1:
            g = rows * tp + row
            zr = (g >= height - WIN).astype(F32) + (g >= height - SHIFT).astype(F32)
            here = lane % 8 + WIN * wc
            zc = (here >= cols - WIN).astype(F32) + (here >= cols - SHIFT).astype(F32)
            lab = lab * 9.0 + zr * 3.0 + zc
        labs.append(lab)
    real = (iota((1, 128), 1) % 8 < WIN) & (iota((1, 128), 1) % WPAD < WROWS)
    for wr in range(rows // WIN):
        lines = []
        for wc in range(across):
            w = wr * across + wc
            mine = row == (lane % WPAD) // 8 + WIN * wr
            line = jnp.sum(jnp.where(mine, labs[wc], 0.0), 0, keepdims=True)
            line = jnp.where(real, line, -1.0)
            lq_ref[w : w + 1, :] = line
            lines.append(line)
        for wc in range(0, across, 2):
            w = wr * across + wc
            both = jnp.where(iota((1, 128), 1) < WPAD, lines[wc], lines[wc + 1])
            both = jnp.broadcast_to(both, (128, 128)).T
            lk_ref[w] = both[:WPAD]
            lk_ref[w + 1] = both[WPAD:]


def qkv_weight_of(half, j, layer, qkvw_ref, a_ref, b_ref):
    if half == 0:
        return qkvw_ref[layer, j]
    return jnp.concatenate([a_ref[96 * j : 96 * (j + 1)], b_ref[96 * j : 96 * (j + 1)]], axis=0)


def proj_weight_of(half, layer, projw_ref, a_ref, b_ref):
    if half == 0:
        return projw_ref[layer]
    return jnp.concatenate([a_ref[288:384], b_ref[288:384]], axis=0)


def norm_windows(layer, wins, x_ref, xn_ref, gain_ref, bias_ref):
    gain = gain_ref[layer, 0:1]
    bias = bias_ref[layer, 0:1]

    def four(i, carry):
        xhat, _ = norm_stats(x_ref[rows_at(i, 4 * WROWS), :])
        xn = xhat * gain + bias
        for n in range(4):
            part = jnp.concatenate(
                [xn[n * WROWS : (n + 1) * WROWS], zero_rows(WPAD - WROWS)], axis=0
            )
            xn_ref[rows_at(4 * i + n, WPAD), :] = part.astype(BF)
        return carry

    repeat(wins // 4, four, 0)


def project_half(xn_ref, qkv_ref, weight, qb, vb):
    n = xn_ref.shape[0]

    def part(i, carry):
        at = rows_at(i, n)
        xn = xn_ref[at, :]
        q = nt(xn, weight(0))
        k = nt(xn, weight(1))
        v = nt(xn, weight(2))
        qkv_ref[0, at, :] = ((q + qb) * SCALE).astype(BF)
        qkv_ref[1, at, :] = k.astype(BF)
        qkv_ref[2, at, :] = (v + vb).astype(BF)
        return carry

    repeat(1, part, 0)


def attend_forward(halves, wins, group, lq_ref, lk_ref, mask_ref):
    def body(i, carry):
        units = [(i * group + u, h) for u in range(group) for h in halves]
        scores = []
        for w, (qkv_ref, _, _, _) in units:
            at = rows_at(w, WPAD)
            scores.append(nt(qkv_ref[1, at, :], spread(qkv_ref[0, at, :], mask_ref[...])))
        probs = []
        for (w, (_, pos, p_ref, _)), s in zip(units, scores):
            same = lk_ref[w] == lq_ref[pl.ds(w, 1), :]
            same = jnp.concatenate([same] * 3, axis=1)
            s = jnp.where(same, s + jnp.concatenate([pos[n] for n in range(3)], axis=1), NEG)
            e = jnp.exp(s - jnp.max(s, 0, keepdims=True))
            p = (e * (1.0 / jnp.sum(e, 0, keepdims=True))).astype(BF)
            p_ref[w] = p
            probs.append(p)
        for (w, (qkv_ref, _, _, mix_ref)), p in zip(units, probs):
            at = rows_at(w, WPAD)
            mix_ref[at, :] = fold(tn(p, qkv_ref[2, at, :])).astype(BF)
        return carry

    repeat(wins // group, body, 0)


def add_branch(wins, mixes, weights, bias, x_ref, hid_ref):
    n = 8

    def part(i, carry):
        res = bias
        for m_ref, w in zip(mixes, weights):
            res = res + nn(m_ref[rows_at(i, n * WPAD), :], w)
        for k in range(n):
            to = rows_at(i * n + k, WROWS)
            hid_ref[to, :] = x_ref[to, :] + res[k * WPAD : k * WPAD + WROWS]
        return carry

    repeat(wins // n, part, 0)


def attn_own_kernel(rows, across, *refs):
    (tok_ref, gain_ref, bias_ref, pb_ref, qvb_ref, qkvw_ref, projw_ref) = refs[:7]
    (pos_ref, lq_ref, lk_ref) = refs[7:10]
    (xb_ref, xn_ref, hid_ref, qkv_ref, p_ref, mix_ref, mask_ref, x_ref) = refs[10:]
    wins = (rows // WIN) * across
    for r in range(rows):
        row = tok_ref[r].astype(F32)
        for k in range(across):
            x_ref[pl.ds(tile_row(r, k, across), SEG), :] = jnp.concatenate(
                [row[WIN * k : WIN * (k + 1)], zero_rows(1)], axis=0
            )
    xb_ref[...] = x_ref[...].astype(BF)
    mask_ref[...] = head_mask()
    norm_windows(0, wins, x_ref, xn_ref, gain_ref, bias_ref)
    project_half(
        xn_ref, qkv_ref, lambda j: qkvw_ref[0, j], qvb_ref[0, 0:1], qvb_ref[0, 1:2]
    )
    attend_forward(
        [(qkv_ref, pos_ref, p_ref, mix_ref)], wins, wins, lq_ref, lk_ref, mask_ref
    )
    add_branch(wins, [mix_ref], [projw_ref[0]], pb_ref[0:1], x_ref, hid_ref)


def attn_other_kernel(rows, across, *refs):
    (part_ref, xn_ref, a_ref, b_ref, lq_ref, lk_ref, pick_ref, info_ref) = refs[:8]
    (hid_ref, qkv_ref, p_ref, mix_ref, small_ref, mask_ref, pos_ref) = refs[8:]
    small_of(a_ref, small_ref)
    wins = (rows // WIN) * across
    mask_ref[...] = head_mask()
    bias = other_small(small_ref, info_ref[0], pick_ref, pos_ref)
    project_half(
        xn_ref,
        qkv_ref,
        lambda j: qkv_weight_of(1, j, 0, None, a_ref, b_ref),
        bias[0:1],
        bias[1:2],
    )
    attend_forward([(qkv_ref, pos_ref, p_ref, mix_ref)], wins, wins, lq_ref, lk_ref, mask_ref)
    add_branch(
        wins, [mix_ref], [proj_weight_of(1, 0, None, a_ref, b_ref)], 0.0, part_ref, hid_ref
    )


def other_small(small_ref, par, pick_ref, pos_ref):
    first = par == 0

    def swapped(v, n):
        return jnp.where(first, v, jnp.concatenate([v[:, n : 2 * n], v[:, :n]], axis=1))

    t = swapped(small_ref[0:16, 0:96], 48)
    table_to_map(t, pick_ref, pos_ref)
    return swapped(small_ref[18:20, 0:192], 96)


def norm_kernel(rows, across, *refs):
    (st_ref, halo_ref, gain_ref, bias_ref, qvb_ref, qkvw_ref) = refs[:6]
    (x_ref, xn_ref, qkv_ref) = refs[6:]

    def tile(r, k):
        if r < rows:
            return st_ref[pl.ds(tile_row(r, k, across), SEG), :]
        return edge_tile(halo, k, r - rows)

    halo = halo_ref[...].astype(F32)
    shift_in(tile, x_ref, rows, across)
    norm_windows(1, (rows // WIN) * across, x_ref, xn_ref, gain_ref, bias_ref)
    project_half(
        xn_ref, qkv_ref, lambda j: qkvw_ref[1, j], qvb_ref[1, 0:1], qvb_ref[1, 1:2]
    )


def attn_both_kernel(rows, across, *refs):
    (xn_ref, qkv0_ref, pos_ref, a_ref, b_ref, x_ref, projw_ref, pb_ref) = refs[:8]
    (lq_ref, lk_ref, pick_ref, info_ref) = refs[8:12]
    (hid_ref, p0_ref, mix0_out, qkv1_ref, p1_ref, mix1_out, small_ref) = refs[12:19]
    (mask_ref, pos1_ref, mix0_ref, mix1_ref, sems) = refs[19:]
    wins = (rows // WIN) * across
    mask_ref[...] = head_mask()
    small_of(a_ref, small_ref)
    bias = other_small(small_ref, info_ref[0], pick_ref, pos1_ref)
    project_half(
        xn_ref,
        qkv1_ref,
        lambda j: qkv_weight_of(1, j, 1, None, a_ref, b_ref),
        bias[0:1],
        bias[1:2],
    )
    attend_forward(
        [(qkv0_ref, pos_ref, p0_ref, mix0_ref), (qkv1_ref, pos1_ref, p1_ref, mix1_ref)],
        wins,
        wins,
        lq_ref,
        lk_ref,
        mask_ref,
    )
    copies = copies_of([(mix0_ref, mix0_out), (mix1_ref, mix1_out)], sems)
    add_branch(
        wins,
        [mix0_ref, mix1_ref],
        [projw_ref[1], proj_weight_of(1, 1, None, a_ref, b_ref)],
        pb_ref[1:2],
        x_ref,
        hid_ref,
    )
    for copy in copies:
        copy.wait()


def up_weight(part, layer, base, f1_ref, a_ref, b_ref):
    if part == 0:
        return f1_ref[layer]
    return jnp.concatenate([a_ref[base : base + C], b_ref[base : base + C]], axis=1)


def down_weight(part, layer, base, f2_ref, a_ref, b_ref):
    if part == 0:
        return f2_ref[layer]
    return jnp.concatenate([a_ref[base + C : base + 2 * C], b_ref[base + C : base + 2 * C]], axis=0)


def up_biases(layer, par, fb1_ref, small_ref):
    own = fb1_ref[layer : layer + 1]
    one, two = small_ref[16:17], small_ref[17:18]
    first = par == 0
    return own, jnp.concatenate(
        [jnp.where(first, one, two), jnp.where(first, two, one)], axis=1
    )


def gelu_pair(u):
    phi = 0.5 + 0.5 * lax.erf(u * (2.0**-0.5))
    slope = phi + u * (jnp.exp(-0.5 * u * u) * (2.0 * np.pi) ** -0.5)
    return (u * phi).astype(BF), slope.astype(BF)


def mlp_own_kernel(hid_ref, gain_ref, bias_ref, fb1_ref, fb2_ref, f1_ref, f2_ref, st_ref, n2_ref, act_ref, gp_ref):
    h = hid_ref[...]
    xhat, _ = norm_stats(h)
    n2 = (xhat * gain_ref[0, 1:2] + bias_ref[0, 1:2]).astype(BF)
    n2_ref[...] = n2
    act, slope = gelu_pair(nn(n2, f1_ref[0]) + fb1_ref[0:1])
    for z in range(2):
        act_ref[z] = act[:, C * z : C * (z + 1)]
        gp_ref[z] = slope[:, C * z : C * (z + 1)]
    st_ref[...] = h + fb2_ref[0:1] + nn(act, f2_ref[0])


def mlp_other_kernel(
    across, part_ref, n2_ref, fb1_ref, small_ref, a_ref, b_ref, info_ref, st_ref, act_ref, gp_ref,
    edge_ref
):
    _, bias = up_biases(0, info_ref[0], fb1_ref, small_ref)
    act, slope = gelu_pair(nn(n2_ref[...], up_weight(1, 0, 0, None, a_ref, b_ref)) + bias)
    for z in range(2):
        act_ref[z] = act[:, C * z : C * (z + 1)]
        gp_ref[z] = slope[:, C * z : C * (z + 1)]
    st_ref[...] = part_ref[...] + nn(act, down_weight(1, 0, 0, None, a_ref, b_ref))
    edge_ref[...] = edge_rows(st_ref, across, range(SHIFT))


def quarter_of(par, slot, part):
    return (par ^ slot) if part == 0 else 2 + slot


BLOCKS = 2


def half_sums(du, ref):
    for z in range(2):
        ref[z : z + 1] += jnp.sum(du[z].astype(F32), 0, keepdims=True)


def mlp_own_both_kernel(rows, across, *refs):
    (cot_ref, edge_ref, hid_ref, gain_ref, bias_ref, fb1_ref, fb2_ref, f1_ref, f2_ref) = refs[:9]
    (g_ref, df_ref, n2_ref, st_ref, dz_ref, du_ref, act_ref, sum_ref, sf_ref) = refs[9:]
    layer = 1
    cols = across * WIN
    cot_edge = edge_ref[...].astype(F32)
    for r in range(rows):
        s = r + SHIFT
        if s < rows:
            row = cot_ref[s].astype(F32)
        else:
            row = cot_edge[(s - rows) * cols : (s - rows + 1) * cols]
        for k in range(across):
            a = WIN * k + SHIFT
            if k < across - 1:
                piece = [row[a : a + WIN]]
            else:
                piece = [row[a:], row[:SHIFT]]
            g_ref[pl.ds(tile_row(r, k, across), SEG), :] = jnp.concatenate(
                piece + [zero_rows(1)], axis=0
            )
    sum_ref[...] = jnp.zeros_like(sum_ref)
    sf_ref[...] = jnp.zeros_like(sf_ref)
    n = hid_ref.shape[0] // BLOCKS

    def block(i, carry):
        at = pl.ds(pl.multiple_of(i * n, n), n)
        h = hid_ref[at, :]
        xhat, _ = norm_stats(h)
        n2 = (xhat * gain_ref[layer, 1:2] + bias_ref[layer, 1:2]).astype(BF)
        n2_ref[at, :] = n2
        df = g_ref[at, :].astype(BF)
        df_ref[at, :] = df
        sf_ref[...] += jnp.sum(df.astype(F32), 0, keepdims=True)
        up = nn(n2, f1_ref[layer]) + fb1_ref[layer : layer + 1]
        grad = nt(df, f2_ref[layer])
        act, slope = gelu_pair(up)
        du = (grad * slope.astype(F32)).astype(BF)
        parts = [du[:, C * z : C * (z + 1)] for z in range(2)]
        for z in range(2):
            act_ref[z, at, :] = act[:, C * z : C * (z + 1)]
            du_ref[z, at, :] = parts[z]
        half_sums(parts, sum_ref)
        st_ref[at, :] = h + fb2_ref[layer : layer + 1] + nn(act, f2_ref[layer])
        dz_ref[at, :] = nt(du, f1_ref[layer])
        return carry

    lax.fori_loop(0, BLOCKS, block, 0)


def mlp_other_both_kernel(rows, across, *refs):
    (hid_ref, g_ref, df_ref, n2_ref, part_ref, dzp_ref, gain_ref, fb1_ref, small_ref) = refs[:9]
    (a_ref, b_ref, info_ref, sumo_ref, sf_ref) = refs[9:14]
    (out_ref, gh_ref, du_ref, act_ref, send_ref, sum_ref, sh_ref, edge_ref, st_ref) = refs[14:]
    layer = 1
    par = info_ref[0]
    _, bias = up_biases(layer, par, fb1_ref, small_ref)
    w1 = up_weight(1, layer, 0, None, a_ref, b_ref)
    w2 = down_weight(1, layer, 0, None, a_ref, b_ref)
    sum_ref[0:2] = sumo_ref[...]
    sum_ref[2:4] = jnp.zeros((2, C), F32)
    sh_ref[0:2] = jnp.zeros((2, C), F32)
    sh_ref[2:3] = sf_ref[...]
    n = hid_ref.shape[0] // BLOCKS

    def block(i, carry):
        at = pl.ds(pl.multiple_of(i * n, n), n)
        up = nn(n2_ref[at, :], w1) + bias
        grad = nt(df_ref[at, :], w2)
        act, slope = gelu_pair(up)
        du = (grad * slope.astype(F32)).astype(BF)
        parts = [du[:, C * z : C * (z + 1)] for z in range(2)]
        for z in range(2):
            act_ref[z, at, :] = act[:, C * z : C * (z + 1)]
            du_ref[z, at, :] = parts[z]
        half_sums(parts, sum_ref.at[2:4])
        st_ref[at, :] = part_ref[at, :] + nn(act, w2)
        dz = dzp_ref[at, :] + nt(du, w1)
        xhat, rinv = norm_stats(hid_ref[at, :])
        sh_ref[0:1] += jnp.sum(dz * xhat, 0, keepdims=True)
        sh_ref[1:2] += jnp.sum(dz, 0, keepdims=True)
        gh_ref[at, :] = g_ref[at, :] + norm_back(dz, xhat, rinv, gain_ref[layer, 1:2])
        return carry

    lax.fori_loop(0, BLOCKS, block, 0)
    edge_ref[...] = edge_rows(st_ref, across, range(rows - SHIFT, rows))
    out_ref[...] = st_ref[...].astype(BF)
    n2 = n2_ref[...]
    df = df_ref[...]
    send_ref[0:C, :] = tn(n2, du_ref[1]).astype(BF)
    send_ref[C:, :] = tn(act_ref[1], df).astype(BF)


def own_grads_kernel(n2_ref, df_ref, du_ref, act_ref, info_ref, keep_ref, send_ref):
    n2 = n2_ref[...]
    df = df_ref[...]
    for slot, ref in ((1, send_ref), (0, keep_ref)):
        q = info_ref[0] ^ slot
        ref[0:C, :] = tn(n2, du_ref[q]).astype(BF)
        ref[C:, :] = tn(act_ref[q], df).astype(BF)


def mlp_keep_kernel(n2_ref, df_ref, du_ref, act_ref, keep_ref):
    keep_ref[0:C, :] = tn(n2_ref[...], du_ref[0]).astype(BF)
    keep_ref[C:, :] = tn(act_ref[0], df_ref[...]).astype(BF)


def up_keep_kernel(n2_ref, du_ref, keep_ref):
    keep_ref[...] = tn(n2_ref[...], du_ref[0]).astype(BF)


def down_grad_kernel(rows, across, *refs):
    (gin_ref, halo_ref, act0_ref, act1_ref, info_ref, g_ref, df_ref, keep_ref, send_ref) = refs

    def tile(r, k):
        if r >= 0:
            return gin_ref[pl.ds(tile_row(r, k, across), SEG), :]
        return edge_tile(halo, k, r + SHIFT)

    halo = halo_ref[...].astype(F32)
    shift_out(tile, g_ref, rows, across)
    df = g_ref[...].astype(BF)
    df_ref[...] = df
    for slot, ref in ((1, send_ref), (0, keep_ref)):
        ref[1] = tn(act1_ref[slot], df).astype(BF)
        ref[0] = tn(act0_ref[info_ref[0] ^ slot], df).astype(BF)


def mlp_bwd_own_kernel(*refs):
    (df_ref, gp_ref, n2_ref, f1_ref, f2_ref, info_ref) = refs[:6]
    (dz_ref, sum_ref, keep_ref, send_ref, du_ref) = refs[6:]
    grad = nt(df_ref[...], f2_ref[0])
    parts = [
        (grad[:, C * z : C * (z + 1)] * gp_ref[z].astype(F32)).astype(BF) for z in range(2)
    ]
    for z in range(2):
        du_ref[z] = parts[z]
    sum_ref[...] = jnp.zeros_like(sum_ref)
    half_sums(parts, sum_ref)
    dz_ref[...] = nt(jnp.concatenate(parts, axis=1), f1_ref[0])
    n2 = n2_ref[...]
    for slot, ref in ((1, send_ref), (0, keep_ref)):
        ref[...] = tn(n2, du_ref[info_ref[0] ^ slot]).astype(BF)


def mlp_bwd_other_kernel(*refs):
    (g_ref, df_ref, hid_ref, n2_ref, gp_ref, dzp_ref, gain_ref, a_ref, b_ref, sumo_ref) = refs[:10]
    (gh_ref, du_ref, send_ref, sum_ref, sh_ref) = refs[10:]
    df = df_ref[...]
    grad = nt(df, down_weight(1, 0, 0, None, a_ref, b_ref))
    parts = [
        (grad[:, C * z : C * (z + 1)] * gp_ref[z].astype(F32)).astype(BF) for z in range(2)
    ]
    for z in range(2):
        du_ref[z] = parts[z]
    sum_ref[0:2] = sumo_ref[...]
    sum_ref[2:4] = jnp.zeros((2, C), F32)
    half_sums(parts, sum_ref.at[2:4])
    dz = dzp_ref[...] + nt(jnp.concatenate(parts, axis=1), up_weight(1, 0, 0, None, a_ref, b_ref))
    xhat, rinv = norm_stats(hid_ref[...])
    sh_ref[0:1] = jnp.sum(dz * xhat, 0, keepdims=True)
    sh_ref[1:2] = jnp.sum(dz, 0, keepdims=True)
    sh_ref[2:3] = jnp.sum(df.astype(F32), 0, keepdims=True)
    gh_ref[...] = g_ref[...] + norm_back(dz, xhat, rinv, gain_ref[0, 1:2])
    send_ref[...] = tn(n2_ref[...], du_ref[1]).astype(BF)


def window_grads(wins, gh_ref, da_ref):
    def four(i, s):
        g = gh_ref[rows_at(i, 4 * WROWS), :]
        for n in range(4):
            part = jnp.concatenate(
                [g[n * WROWS : (n + 1) * WROWS], zero_rows(WPAD - WROWS)], axis=0
            ).astype(BF)
            da_ref[rows_at(4 * i + n, WPAD), :] = part
            s = s + jnp.sum(part.astype(F32), 0, keepdims=True)
        return s

    return repeat(wins // 4, four, jnp.zeros((1, C), F32))


def attend_backward(halves, wins, group, mask_ref):
    def body(i, carry):
        units = [(i * group + u, h) for u in range(group) for h in halves]
        first = []
        for w, (qkv_ref, p_ref, do_ref, dqkv_ref, _) in units:
            at = rows_at(w, WPAD)
            do = spread(do_ref[at, :], mask_ref[...])
            first.append(nt(qkv_ref[2, at, :], do))
            dqkv_ref[2, at, :] = nn(p_ref[w], do).astype(BF)
        second = []
        for (w, (_, p_ref, _, _, acc_ref)), dp in zip(units, first):
            p = p_ref[w].astype(F32)
            ds = p * (dp - jnp.sum(p * dp, 0, keepdims=True))
            for n in range(3):
                acc_ref[n] += ds[:, 128 * n : 128 * (n + 1)]
            second.append(ds.astype(BF))
        for (w, (qkv_ref, _, _, dqkv_ref, _)), ds in zip(units, second):
            at = rows_at(w, WPAD)
            dqkv_ref[1, at, :] = nn(ds, spread(qkv_ref[0, at, :], mask_ref[...])).astype(BF)
            dqkv_ref[0, at, :] = fold(tn(ds, qkv_ref[1, at, :])).astype(BF)
        return carry

    repeat(wins // group, body, 0)


def half_grads(half, par, xn_ref, da_ref, mix_ref, dqkv_ref, row_ref, give):
    def put(value, at):
        if half == 0:
            row_ref[...] = value
            one = row_ref[pl.ds(pl.multiple_of(par * 96, 96), 96), :]
            two = row_ref[pl.ds(pl.multiple_of((1 - par) * 96, 96), 96), :]
        else:
            one, two = value[:96], value[96:]
        give(at, one.astype(BF), two.astype(BF))

    xn = xn_ref[...]
    for j in range(3):
        grad = tn(dqkv_ref[j], xn)
        put(grad * SCALE if j == 0 else grad, 96 * j)
    put(tn(mix_ref[...], da_ref[...]), 288)


def normed_grads(layer, wins, dqkvs, weights, gh_ref, x_ref, gain_ref, gx_ref):
    gain = gain_ref[layer, 0:1]
    n = 8

    def part(i, carry):
        sg, sb, sq = carry
        at = rows_at(i, n * WPAD)
        dn = nn(dqkvs[0][0, at, :], weights[0](0)) + nn(dqkvs[1][0, at, :], weights[1](0))
        dn = dn * SCALE
        for half in range(2):
            for j in (1, 2):
                dn = dn + nn(dqkvs[half][j, at, :], weights[half](j))
        new = []
        for half in range(2):
            for m, j in enumerate((0, 2)):
                new.append(
                    sq[half * 2 + m] + jnp.sum(dqkvs[half][j, at, :].astype(F32), 0, keepdims=True)
                )
        d = jnp.concatenate([dn[k * WPAD : k * WPAD + WROWS] for k in range(n)], axis=0)
        to = rows_at(i, n * WROWS)
        xhat, rinv = norm_stats(x_ref[to, :].astype(F32))
        sg = sg + jnp.sum(d * xhat, 0, keepdims=True)
        sb = sb + jnp.sum(d, 0, keepdims=True)
        gx_ref[to, :] = gh_ref[to, :] + norm_back(d, xhat, rinv, gain)
        return sg, sb, tuple(new)

    z = jnp.zeros((1, C), F32)
    zq = jnp.zeros((1, 6 * HD), F32)
    return repeat(wins // n, part, (z, z, (zq,) * 4))


def small_rows(ref, z, sq, fb1, table, shared):
    ref[...] = jnp.zeros_like(ref)
    if shared is not None:
        sg, sb, projb, sh_ref = shared
        ref[0:1] = sg
        ref[1:2] = sb
        ref[2:3] = projb
        ref[3:6] = sh_ref[...]
    ref[6:7] = fb1
    ref[7:8, 0:96] = sq[0][:, 96 * z : 96 * (z + 1)] * SCALE
    ref[7:8, 128:224] = sq[1][:, 96 * z : 96 * (z + 1)]
    ref[8:24, 0:48] = table[:, 48 * z : 48 * (z + 1)]


def mixed_grad_kernel(wins, gh_ref, projw_ref, a_ref, b_ref, da_ref, do_ref, pb_ref):
    pb_ref[...] = window_grads(wins, gh_ref, da_ref)
    for half in range(2):
        do_ref[half] = nt(da_ref[...], proj_weight_of(half, 1, projw_ref, a_ref, b_ref)).astype(BF)


def attn_bwd_kernel(rows, across, *refs):
    (gh_ref, x_ref, xn_ref, gain_ref, qkvw_ref, a_ref, b_ref, info_ref) = refs[:8]
    (fb1_ref, sh_ref, qkv0_ref, p0_ref, mix0_ref, qkv1_ref, p1_ref, mix1_ref, pick_ref) = refs[8:17]
    (da_ref, do_ref, pb_ref) = refs[17:20]
    (gin_ref, keep_ref, send_ref, edge_ref) = refs[20:24]
    (dqkv0_ref, dqkv1_ref, acc_ref, mask_ref, row_ref, sm_ref) = refs[24:]
    layer = 1
    par = info_ref[0]
    wins = (rows // WIN) * across
    mask_ref[...] = head_mask()
    acc_ref[...] = jnp.zeros_like(acc_ref)
    projb = pb_ref[...]
    attend_backward(
        [
            (qkv0_ref, p0_ref, do_ref.at[0], dqkv0_ref, acc_ref.at[0]),
            (qkv1_ref, p1_ref, do_ref.at[1], dqkv1_ref, acc_ref.at[1]),
        ],
        wins,
        wins,
        mask_ref,
    )
    for half, mix_ref, dqkv_ref in ((1, mix1_ref, dqkv1_ref), (0, mix0_ref, dqkv0_ref)):

        def give(at, one, two, half=half):
            keep_ref[half, at : at + 96, :] = one
            send_ref[half, at : at + 96, :] = two

        half_grads(half, par, xn_ref, da_ref, mix_ref, dqkv_ref, row_ref, give)
    weights = [
        lambda j, half=half: qkv_weight_of(half, j, layer, qkvw_ref, a_ref, b_ref)
        for half in range(2)
    ]
    sg, sb, sq = normed_grads(
        layer, wins, [dqkv0_ref, dqkv1_ref], weights, gh_ref, x_ref, gain_ref, gin_ref
    )
    edge_ref[...] = edge_rows(gin_ref, across, range(rows - SHIFT, rows))
    for half in range(2):
        table = map_to_table(acc_ref.at[half], pick_ref)
        for z in range(2):
            q = 2 * half + z
            small_rows(
                sm_ref.at[q], z, sq[2 * half : 2 * half + 2], fb1_ref[q : q + 1], table,
                (sg, sb, projb, sh_ref)
            )
    keep_ref[0, C:, :] = sm_ref[par].astype(BF)
    send_ref[0, C:, :] = sm_ref[1 - par].astype(BF)
    keep_ref[1, C:, :] = sm_ref[2].astype(BF)
    send_ref[1, C:, :] = sm_ref[3].astype(BF)


def column_sum(ref):
    return jnp.sum(ref[...].astype(F32), 0, keepdims=True)


def attn_bwd_heads_kernel(rows, across, *refs):
    (gh_ref, xn_ref, projw_ref, a_ref, b_ref, fb1_ref) = refs[:6]
    (qkv0_ref, p0_ref, qkv1_ref, p1_ref, mix1_ref, pick_ref) = refs[6:12]
    (da_ref, dqkv0_ref, acc0_ref, dqkv1_ref, pb_ref, keep_ref, send_ref) = refs[12:19]
    (do_ref, mask_ref, acc1_ref, sm_ref) = refs[19:]
    wins = (rows // WIN) * across
    mask_ref[...] = head_mask()
    acc0_ref[...] = jnp.zeros_like(acc0_ref)
    acc1_ref[...] = jnp.zeros_like(acc1_ref)
    pb_ref[...] = window_grads(wins, gh_ref, da_ref)
    da = da_ref[...]
    for half in range(2):
        do_ref[half] = nt(da, proj_weight_of(half, 0, projw_ref, a_ref, b_ref)).astype(BF)
    attend_backward(
        [
            (qkv1_ref, p1_ref, do_ref.at[1], dqkv1_ref, acc1_ref),
            (qkv0_ref, p0_ref, do_ref.at[0], dqkv0_ref, acc0_ref),
        ],
        wins,
        wins,
        mask_ref,
    )

    def give(at, one, two):
        keep_ref[at : at + 96, :] = one
        send_ref[at : at + 96, :] = two

    half_grads(1, None, xn_ref, da_ref, mix1_ref, dqkv1_ref, None, give)
    table = map_to_table(acc1_ref, pick_ref)
    sq = (column_sum(dqkv1_ref.at[0]), column_sum(dqkv1_ref.at[2]))
    for z, ref in ((0, keep_ref), (1, send_ref)):
        small_rows(sm_ref, z, sq, fb1_ref[2 + z : 3 + z], table, None)
        ref[C:, :] = sm_ref[...].astype(BF)


def attn_bwd_own_kernel(rows, across, *refs):
    (gh_ref, x_ref, xn_ref, gain_ref, qkvw_ref, a_ref, b_ref, info_ref) = refs[:8]
    (fb1_ref, sh_ref, da_ref, dqkv_ref, acc_ref, dqkv1_ref, pb_ref, mix_ref, pick_ref) = refs[8:17]
    (out_ref, keep_ref, send_ref) = refs[17:20]
    (gx_ref, row_ref, sm_ref) = refs[20:]
    par = info_ref[0]
    wins = (rows // WIN) * across

    def give(at, one, two):
        keep_ref[at : at + 96, :] = one
        send_ref[at : at + 96, :] = two

    half_grads(0, par, xn_ref, da_ref, mix_ref, dqkv_ref, row_ref, give)
    weights = [
        lambda j, half=half: qkv_weight_of(half, j, 0, qkvw_ref, a_ref, b_ref)
        for half in range(2)
    ]
    sg, sb, sq = normed_grads(
        0, wins, [dqkv_ref, dqkv1_ref], weights, gh_ref, x_ref, gain_ref, gx_ref
    )
    table = map_to_table(acc_ref, pick_ref)
    for z in range(2):
        small_rows(
            sm_ref.at[z], z, sq[0:2], fb1_ref[z : z + 1], table, (sg, sb, pb_ref[...], sh_ref)
        )
    keep_ref[C:, :] = sm_ref[par].astype(BF)
    send_ref[C:, :] = sm_ref[1 - par].astype(BF)
    for r in range(rows):
        parts = [gx_ref[pl.ds(tile_row(r, k, across), SEG), :][:WIN] for k in range(across)]
        out_ref[r, :, 0, :] = jnp.concatenate(parts, axis=0)


def pair_kernel(keep_ref, got_ref, own_ref, oth_ref):
    own_ref[...] = (keep_ref[0].astype(F32) + got_ref[0].astype(F32)).astype(BF)
    oth_ref[...] = (keep_ref[1].astype(F32) + got_ref[1].astype(F32)).astype(BF)


def combine_kernel(parts, bit, n_in, *refs):
    ins = refs[:n_in]
    info_ref = refs[n_in]
    outs = refs[n_in + 1 :]
    at = 0
    for rows, terms, split in parts:

        def total(first, n):
            acc = None
            for i, base in terms:
                x = ins[i][pl.ds(base + first, n), :].astype(F32)
                acc = x if acc is None else acc + x
            return acc.astype(BF)

        if bit is None or not split:
            whole = total(0, rows)
            for out in outs:
                out[at : at + rows, :] = whole
            at += rows
        else:
            n = rows // 2
            b = (info_ref[2] >> bit) & 1
            outs[0][at : at + n, :] = total(pl.multiple_of(b * n, n), n)
            outs[1][at : at + n, :] = total(pl.multiple_of((1 - b) * n, n), n)
            at += n


def close_kernel(halves, bit, mine_ref, got_ref, info_ref, out_ref, small_ref):
    join_kernel(halves, bit, mine_ref.at[0 : sum(halves)], got_ref, info_ref, out_ref)
    at = sum(halves)
    rest = (mine_ref[at:, :].astype(F32) + got_ref[at:, :].astype(F32)).astype(BF)
    n = rest.shape[0] - SMALL
    out_ref[2 * at :, :] = rest[:n]
    small_ref[...] = rest[n:]


def join_kernel(halves, bit, mine_ref, got_ref, info_ref, out_ref):
    b = (info_ref[2] >> bit) & 1
    at = 0
    for n in halves:
        for ref, place in ((mine_ref, b), (got_ref, 1 - b)):
            to = pl.multiple_of(2 * at + place * n, 16)
            out_ref[pl.ds(to, n), :] = ref[at : at + n, :]
        at += n
    if at < mine_ref.shape[0]:
        out_ref[2 * at :, :] = mine_ref[at:, :]


def out_kernel(rows, across, in_ref, halo_ref, o_ref, st_ref):
    st_ref[...] = in_ref[...].astype(F32)
    halo = halo_ref[C + SMALL :, :].astype(F32)
    for r in range(rows):
        parts = []
        for k in range(across):
            if r >= SHIFT:
                t = st_ref[pl.ds(tile_row(r - SHIFT, k, across), SEG), :]
            else:
                t = edge_tile(halo, k, r)
            parts.append(t[:WIN])
        last = parts[-1]
        parts = [last[WIN - SHIFT :]] + parts[:-1] + [last[: WIN - SHIFT]]
        o_ref[r] = jnp.concatenate(parts, axis=0).astype(BF)


def place_of(i, info_ref):
    return info_ref[0] ^ (i // 2), ((info_ref[2] >> 1) & 1) ^ (i % 2)


def put_up(pieces, base, info_ref, ref):
    n = C // 2
    for i in range(4):
        core, half = place_of(i, info_ref)
        rows = pl.ds(pl.multiple_of(half * n, n), n)
        cols = pl.ds(pl.multiple_of(core * C, C), C)
        ref[rows, cols] = pieces[i][base : base + n, :].astype(F32)


def put_down(pieces, base, info_ref, ref):
    n = C // 2
    for i in range(4):
        core, half = place_of(i, info_ref)
        rows = pl.ds(pl.multiple_of(core * C + half * n, n), n)
        ref[rows, :] = pieces[i][base : base + n, :].astype(F32)


def put_attn(pieces, base, info_ref, asm_ref, qkv_ref, proj_ref):
    n = C // 2
    for i in range(4):
        core, half = place_of(i, info_ref)
        rows = pl.ds(pl.multiple_of(half * n, n), n)
        asm_ref[core, rows, :] = pieces[i][base : base + n, :].astype(F32)
    for core in range(2):
        to = pl.ds(96 * core, 96)
        for j in range(3):
            qkv_ref[j, to, :] = asm_ref[core, 96 * j : 96 * (j + 1), :]
        proj_ref[to, :] = asm_ref[core, 288:384, :]


def final_second_kernel(*refs):
    pieces = refs[:4]
    (info_ref, f1_ref, f2_ref, qkv_ref, proj_ref) = refs[4:9]
    (up_ref, down_ref, asm_ref, q_ref, p_ref, sems) = refs[9:]
    put_up(pieces, 0, info_ref, up_ref)
    put_down(pieces, C // 2, info_ref, down_ref)
    put_attn(pieces, C, info_ref, asm_ref, q_ref, p_ref)
    outs = [f1_ref, f2_ref, qkv_ref, proj_ref]
    for copy in copies_of([(x, y.at[1]) for x, y in zip((up_ref, down_ref, q_ref, p_ref), outs)], sems):
        copy.wait()


def final_kernel(*refs):
    mlps, attns, smalls = refs[:4], refs[4:8], refs[8:10]
    (shared_ref, info_ref) = refs[10:12]
    (f1_ref, f2_ref, qkv_ref, proj_ref) = refs[16:20]
    (gain_ref, bias_ref, pb_ref, fb2_ref, qvb_ref, fb1_ref, tab_ref) = refs[20:27]
    (up_ref, down_ref, asm_ref, q_ref, p_ref, sm_ref, sems) = refs[27:]
    put_up(mlps, 0, info_ref, up_ref)
    copies = copies_of([(up_ref, f1_ref.at[0])], sems)
    put_down(mlps, C // 2, info_ref, down_ref)
    copies += copies_of([(down_ref, f2_ref.at[0])], sems.at[1:2])
    put_attn(attns, 0, info_ref, asm_ref, q_ref, p_ref)
    copies += copies_of([(q_ref, qkv_ref.at[0]), (p_ref, proj_ref.at[0])], sems.at[2:4])
    n = C // 2
    par = info_ref[0]
    for layer in range(2):
        for i in range(2):
            x = smalls[i][...] if layer == 1 else attns[2 * i][n:, :]
            sm_ref[par ^ i] = x.astype(F32)
        x, y = sm_ref[0], sm_ref[1]
        shared = x[0:6]
        if layer == 0:
            shared = sm_ref[par, 0:6, :] + shared_ref[0:6].astype(F32)
        gain_ref[layer, 0:1] = shared[0:1]
        gain_ref[layer, 1:2] = shared[3:4]
        bias_ref[layer, 0:1] = shared[1:2]
        bias_ref[layer, 1:2] = shared[4:5]
        pb_ref[layer : layer + 1] = shared[2:3]
        fb2_ref[layer : layer + 1] = shared[5:6]
        fb1_ref[layer : layer + 1, 0:C] = x[6:7]
        fb1_ref[layer : layer + 1, C:] = y[6:7]
        for k in range(2):
            qvb_ref[layer, k : k + 1, 0:96] = x[7:8, 128 * k : 128 * k + 96]
            qvb_ref[layer, k : k + 1, 96:192] = y[7:8, 128 * k : 128 * k + 96]
        t = jnp.concatenate([x[8:24, 0:48], y[8:24, 0:48]], axis=1)
        wide = tn(t.astype(BF), offset_rows().astype(BF)) * offset_cols()
        for h in range(6):
            tab_ref[h, layer : layer + 1, :] = jnp.sum(
                wide[16 * h : 16 * (h + 1)], 0, keepdims=True
            )
    for copy in copies:
        copy.wait()


VMEM = pl.BlockSpec(memory_space=pltpu.VMEM)
HBM = pl.BlockSpec(memory_space=pltpu.HBM)


class Position:
    def __getitem__(self, k):
        if k == 1:
            return lax.axis_index("tp")
        win = lax.axis_index("win")
        return win if k == 2 else lax.rem(win, 2)


POSITION = Position()


def call(kernel, name, us, limit, operands, outs, scratch=(), aliases=None):
    args = []
    specs = []
    at = [n for n, op in enumerate(operands) if op is POSITION]
    if at:
        (at,) = at
        inner = kernel

        def kernel(*refs):
            return inner(*refs[:at], POSITION, *refs[at:])

        operands = operands[:at] + operands[at + 1 :]
        aliases = {k - (k > at): v for k, v in (aliases or {}).items()}
    for op in operands:
        args.append(op[0] if isinstance(op, tuple) else op)
        specs.append(op[1] if isinstance(op, tuple) else VMEM)
    shapes = [jax.ShapeDtypeStruct(o[0], o[1]) for o in outs]
    return pl.pallas_call(
        kernel,
        name=name,
        in_specs=specs,
        out_specs=[o[2] if len(o) > 2 else VMEM for o in outs],
        input_output_aliases=aliases or {},
        out_shape=shapes,
        scratch_shapes=[s if not isinstance(s, tuple) else pltpu.VMEM(*s) for s in scratch],
        cost_estimate=pl.CostEstimate(
            flops=int(us * 7e9), bytes_accessed=1000000, transcendentals=0
        ),
        compiler_params=pltpu.CompilerParams(vmem_limit_bytes=limit * 2**20),
    )(*args)


def on_device(n_win, *args):
    (
        tokens,
        crop_ids,
        cotangent,
        norm_gain,
        norm_bias,
        qkv_weight,
        qv_bias,
        proj_weight,
        proj_bias,
        fc1_weight,
        fc1_bias,
        fc2_weight,
        fc2_bias,
        pos_table,
    ) = args
    rows, cols = tokens.shape[1:3]
    across = cols // WIN
    wins = (rows // WIN) * across
    ntok = wins * WROWS
    npad = wins * WPAD
    win = lax.axis_index("win")
    tp = lax.axis_index("tp")
    par = win % 2
    info = POSITION
    bits = n_win.bit_length() - 1
    assert n_win == 1 << bits and bits >= 3

    def to_tp(x, name):
        with jax.named_scope(name + "_tp"):
            return lax.ppermute(x, "tp", [(0, 1), (1, 0)])

    def to_win(x, bit, name):
        if bit >= bits:
            return jnp.zeros_like(x)
        with jax.named_scope("%s_win%d" % (name, bit)):
            return lax.ppermute(x, "win", [(i, i ^ (1 << bit)) for i in range(n_win)])

    def after(x, *others):
        return lax.optimization_barrier((x,) + others)[0]

    def combine(parts, bit, ins, name):
        total = sum(rows // 2 if split and bit is not None else rows for rows, _, split in parts)
        outs = [((total, C), BF)] * (1 if bit is None else 2)
        return call(
            partial(combine_kernel, parts, bit, len(ins)), name, 1, 4, tuple(ins) + (info,), outs
        )

    def join(halves, bit, mine, got, name):
        return call(
            partial(join_kernel, halves, bit), name, 1, 4, (mine, got, info),
            [((mine.shape[0] + sum(halves), C), BF)],
        )[0]

    qkv_t = qkv_weight.transpose(0, 2, 3, 1)
    table = pos_table.transpose(2, 0, 1)
    na = C + SMALL
    n = C // 2
    edge_b = ((across * SHIFT * SEG, C), BF)
    a0q, small = call(
        pack_first_kernel,
        "pack_first",
        0.1,
        60,
        tuple((x, HBM) for x in (qkv_t, proj_weight, table, qv_bias, fc1_bias)),
        [((C + 2 * SENT_ROWS, C), BF), ((2, SMALL_ROWS, C), F32)],
        [
            (table.shape, F32),
            (qv_bias.shape, F32),
            (fc1_bias.shape, F32),
            pltpu.SemaphoreType.DMA((7,)),
        ],
    )
    a0 = to_tp(a0q, "a0")
    m0q, a1q, m1q, cot_edge = call(
        pack_kernel,
        "pack",
        0.1,
        60,
        tuple((x, HBM) for x in (qkv_t, proj_weight, fc1_weight, fc2_weight, cotangent[0]))
        + (after(small, a0q), info),
        [
            ((2 * C, C), BF),
            ((C + 2 * SENT_ROWS, C), BF),
            ((2 * C, C), BF),
            ((EDGE_ROWS, C), BF),
        ],
        [((SHIFT, cols, C), BF), pltpu.SemaphoreType.DMA((9,))],
    )
    m0 = to_tp(m0q, "m0")
    crops = crop_ids.transpose(2, 0, 1)
    label_outs = [((wins, 128), F32), ((wins, WPAD, 128), F32), ((3, WPAD, 128), F32)]
    lq0, lk0, pos0, pick = call(
        partial(prep_kernel, 0, rows, across),
        "prep_0",
        0.1,
        8,
        (crops, after(small, m0q), info),
        label_outs + [((WIN, 96, 6 * WPAD), BF)],
        [((128, 128), F32)],
    )
    tiles = (rows // WIN, across, WIN, SEG, C)
    mask = ((6 * WPAD, 6 * HD), BF)
    half_outs = [((3, npad, 192), BF), ((wins, WPAD, 6 * WPAD), BF), ((npad, 192), BF)]
    tok_f = ((ntok, C), F32)
    tok_b = ((ntok, C), BF)
    hid_b = ((4, ntok, C), BF)
    other_scratch = [mask, ((3, WPAD, 128), F32)]

    x0, xn0, part, qkv00, p00, mix00 = call(
        partial(attn_own_kernel, rows, across),
        "attn_own_0",
        0.1,
        8,
        (tokens[0], norm_gain, norm_bias, proj_bias, qv_bias, qkv_t, proj_weight, pos0, lq0, lk0),
        [tok_b, ((npad, C), BF), tok_f] + half_outs,
        [mask, tok_f],
    )
    lq1, lk1, pos1 = call(
        partial(prep_kernel, 1, rows, across),
        "prep_1",
        0.1,
        8,
        (crops, after(small, part), info, pick),
        label_outs,
        [((128, 128), F32)],
    )
    a1 = to_tp(after(a1q, lq1), "a1")
    a0 = after(a0, lq1)
    a0s = to_win(a0, 0, "a0")
    hid0, qkv01, p01, mix01, small0 = call(
        partial(attn_other_kernel, rows, across),
        "attn_other_0",
        0.1,
        8,
        (part, xn0, a0, a0s, lq0, lk0, pick, info),
        [tok_f] + half_outs + [((SMALL_ROWS, C), F32)],
        other_scratch,
    )
    half_b = ((2, ntok, C), BF)
    st_own, n2f, act00, gp00 = call(
        mlp_own_kernel,
        "mlp_own_0",
        0.1,
        10,
        (hid0, norm_gain, norm_bias, fc1_bias, fc2_bias, fc1_weight, fc2_weight),
        [tok_f, tok_b, half_b, half_b],
    )
    m0 = after(m0, st_own)
    m0s = to_win(m0, 0, "m0")
    st0, act01, gp01, edge = call(
        partial(mlp_other_kernel, across),
        "mlp_other_0",
        3,
        10,
        (st_own, n2f, fc1_bias, small0, m0, m0s, info),
        [tok_f, half_b, half_b, edge_b],
    )
    halo = to_tp(edge, "edge0")
    a1 = after(a1, halo)
    a1s = to_win(a1, 0, "a1")
    cot_edge = to_tp(after(cot_edge, edge), "cot")
    m1 = to_tp(after(m1q, edge), "m1")
    x1, xn1, qkv10 = call(
        partial(norm_kernel, rows, across),
        "norm_1",
        2,
        6,
        (st0, halo, norm_gain, norm_bias, qv_bias, qkv_t),
        [tok_f, ((npad, C), BF), half_outs[0]],
    )
    mix_out = half_outs[2] + (HBM,)
    hid1, p10, mix10, qkv11, p11, mix11, small1 = call(
        partial(attn_both_kernel, rows, across),
        "attn_fwd_1",
        10,
        12,
        (xn1, qkv10, pos1, a1, a1s, x1, proj_weight, proj_bias, lq1, lk1, pick, info),
        [tok_f, half_outs[1], mix_out] + half_outs[:2] + [mix_out, ((SMALL_ROWS, C), F32)],
        other_scratch + [half_outs[2], half_outs[2], pltpu.SemaphoreType.DMA((2,))],
    )
    sums = [((4, C), F32), ((3, C), F32)]
    g1, df1, n21, st_own, dz_own, du10, act10, sum10, sf1 = call(
        partial(mlp_own_both_kernel, rows, across),
        "mlp_own_1",
        5,
        6,
        (cotangent[0], after(cot_edge, a1s), hid1, norm_gain, norm_bias, fc1_bias, fc2_bias)
        + (fc1_weight, fc2_weight),
        [tok_f, tok_b, tok_b, tok_f, tok_f, half_b, half_b, ((2, C), F32), ((1, C), F32)],
    )
    m1 = after(m1, dz_own)
    m1s = to_win(m1, 0, "m1")
    whole_q = ((2 * C, C), BF)
    keep_mo, send_mo = call(
        own_grads_kernel, "own_grads_1", 2, 4, (after(n21, m1), df1, du10, act10, info),
        [whole_q, whole_q],
    )
    mo_core = to_win(send_mo, 0, "gmo")
    st1, gh1, du11, act11, send_mx, gfb1, gsh1, out_edge = call(
        partial(mlp_other_both_kernel, rows, across),
        "mlp_other_1",
        6,
        8,
        (after(hid1, keep_mo), g1, df1, n21, st_own, dz_own, norm_gain, fc1_bias, small1, m1, m1s)
        + (info, sum10, sf1),
        [tok_b, tok_f, half_b, half_b, whole_q] + sums + [edge_b],
        [tok_f],
        aliases={1: 1},
    )

    def plus(x, y, name):
        return combine([(x.shape[0], [(0, 0), (1, 0)], True)], None, (x, y), name)[0]

    def pair(keep, got, name):
        shape = keep.shape[1:]
        return call(pair_kernel, name, 1, 4, (keep, got), [(shape, BF), (shape, BF)])

    mx_core = to_win(send_mx, 0, "gmx")
    (keep_mx,) = call(mlp_keep_kernel, "mlp_keep_1", 1, 4, (n21, df1, du11, act11), [whole_q])
    m1_oth = plus(keep_mx, after(mx_core, keep_mx), "m1_oth")
    m1_own = plus(keep_mo, after(mo_core, m1_oth), "m1_own")
    m1_t = to_tp(m1_oth, "gm1")
    da1, do1, pb1 = call(
        partial(mixed_grad_kernel, wins),
        "mixed_grad_1",
        0.1,
        4,
        (after(gh1, m1_own), proj_weight, a1, a1s),
        [((npad, C), BF), ((2, npad, 192), BF), ((1, C), F32)],
    )
    gin1, keep_a1, send_a1, edge = call(
        partial(attn_bwd_kernel, rows, across),
        "attn_bwd_1",
        14,
        8,
        (gh1, x1, xn1, norm_gain, qkv_t, a1, a1s, info)
        + (gfb1, gsh1, qkv10, p10, mix10, qkv11, p11, mix11, pick, da1, do1, pb1),
        [tok_f, ((2, na, C), BF), ((2, na, C), BF), edge_b],
        [
            ((3, npad, 192), BF),
            ((3, npad, 192), BF),
            ((2, 3, WPAD, 128), F32),
            mask,
            ((192, C), F32),
            ((4, SMALL, C), F32),
        ],
    )
    halo = to_tp(edge, "edge1")
    a1_core = to_win(after(send_a1, edge), 0, "ga1")
    m1_mine, m1_away = combine(
        [(C, [(0, 0), (1, 0)], True), (C, [(0, C), (1, C)], True)],
        1,
        (m1_own, after(m1_t, edge)),
        "m1_y",
    )
    m1_y = to_win(m1_away, 1, "gm1")
    a1_own, a1_oth = pair(keep_a1, after(a1_core, m1_away), "pair_a1")
    a1_t = to_tp(a1_oth, "ga1")
    g0, df0, keep_f2, send_f2 = call(
        partial(down_grad_kernel, rows, across),
        "down_grad_0",
        4,
        5,
        (gin1, after(halo, a1_oth), act00, act01, info),
        [tok_f, tok_b, ((2, C, C), BF), ((2, C, C), BF)],
    )
    f2_core = to_win(send_f2, 0, "gf2")
    quarter_b = ((C, C), BF)
    dz0, sum00, keep_fo, send_fo = call(
        mlp_bwd_own_kernel,
        "mlp_bwd_own_0",
        2,
        8,
        (df0, gp00, n2f, fc1_weight, fc2_weight, info),
        [tok_f, ((2, C), F32), quarter_b, quarter_b],
        [half_b],
    )
    fo_core = to_win(send_fo, 0, "gfo")
    m1_mine, m1_away = combine(
        [(n, [(0, 0), (1, 0)], True), (n, [(0, n), (1, n)], True)],
        2,
        (m1_mine, after(m1_y, dz0)),
        "m1_z",
    )
    m1_z = to_win(m1_away, 2, "gm1")
    f2_own, f2_oth = pair(keep_f2, after(f2_core, m1_away), "pair_f2")
    f2_t = to_tp(f2_oth, "gf2")
    a1_mine, a1_away = combine(
        [(C, [(0, 0), (1, 0)], True), (SMALL, [(0, C), (1, C)], False)],
        1,
        (a1_own, after(a1_t, f2_oth)),
        "a1_y",
    )
    a1_y = to_win(a1_away, 1, "ga1")
    gh0, du01, send_fx, gfb0, gsh0 = call(
        mlp_bwd_other_kernel,
        "mlp_bwd_other_0",
        3,
        8,
        (after(g0, a1_away), df0, hid0, n2f, gp01, dz0, norm_gain, m0, m0s, sum00),
        [tok_f, half_b, quarter_b] + sums,
    )
    m1 = plus(m1_mine, after(m1_z, send_fx), "m1_z2")
    m1_b = to_win(m1, 3, "gm1")
    fx_core = to_win(send_fx, 0, "gfx")
    (keep_fx,) = call(up_keep_kernel, "up_keep_0", 1, 4, (n2f, du01), [quarter_b])
    f1_oth = plus(keep_fx, after(fx_core, keep_fx), "f1_oth")
    f1_t = to_tp(f1_oth, "gf1")
    f1_own = plus(keep_fo, after(fo_core, f1_oth), "f1_own")
    a1 = plus(a1_mine, after(a1_y, f1_own), "a1_z2")
    a1_b = to_win(a1, 3, "ga1")
    da, dqkv0, acc0, dqkv1, pb0, keep_o0, send_o0 = call(
        partial(attn_bwd_heads_kernel, rows, across),
        "attn_bwd_heads_0",
        8,
        8,
        (after(gh0, a1, f2_t), xn0, proj_weight, a0, a0s, gfb0)
        + (qkv00, p00, qkv01, p01, mix01, pick),
        [
            ((npad, C), BF),
            ((3, npad, 192), BF),
            ((3, WPAD, 128), F32),
            ((3, npad, 192), BF),
            ((1, C), F32),
            ((na, C), BF),
            ((na, C), BF),
        ],
        [((2, npad, 192), BF), mask, ((3, WPAD, 128), F32), ((SMALL, C), F32)],
    )
    o0_core = to_win(send_o0, 0, "go0")
    m0_mine, m0_away = combine(
        [(C, [(0, 0), (1, 0)], True), (C, [(2, 0), (3, 0)], True)],
        1,
        (f1_own, after(f1_t, send_o0), f2_own, f2_t),
        "m0_y",
    )
    m0_y = to_win(m0_away, 1, "gm0")
    (o0_sum,) = combine(
        [(na, [(0, 0), (1, 0)], True), (edge_b[0][0], [(2, 0)], True)],
        None,
        (keep_o0, after(o0_core, m0_away), out_edge),
        "o0",
    )
    o0_t = to_tp(o0_sum, "go0")
    (c1,) = combine(
        [(n, [(0, 0), (1, 0)], True), (n + SMALL, [(2, 0), (3, 0)], True)],
        None,
        (m1, after(m1_b, o0_sum), a1, after(a1_b, o0_sum)),
        "c1",
    )
    for bit in range(4, bits):
        c1 = plus(c1, to_win(c1, bit, "gc1"), "c1_sum")
    c1_b = to_win(c1, 2, "gc1")
    grad_tokens, keep_a0, send_a0 = call(
        partial(attn_bwd_own_kernel, rows, across),
        "attn_bwd_own_0",
        9,
        7,
        (gh0, x0, xn0, norm_gain, qkv_t, a0, a0s, info)
        + (gfb0, gsh0, da, dqkv0, acc0, dqkv1, pb0, after(mix00, c1), pick),
        [((rows, cols, 1, C), F32), ((na, C), BF), ((na, C), BF)],
        [tok_f, ((192, C), F32), ((2, SMALL, C), F32)],
    )

    a0_core = to_win(send_a0, 0, "ga0")
    m0_mine, m0_away = combine(
        [(n, [(0, 0), (1, 0)], True), (n, [(0, n), (1, n)], True)],
        2,
        (m0_mine, after(m0_y, send_a0)),
        "m0_z",
    )
    m0_z = to_win(m0_away, 2, "gm0")
    a0_mine, a0_away = combine(
        [(C, [(0, 0), (1, 0), (2, 0)], True), (SMALL, [(0, C), (1, C), (2, C)], False)],
        1,
        (keep_a0, after(a0_core, m0_away), o0_t),
        "a0_y",
    )
    a0_y = to_win(a0_away, 1, "ga0")
    c1, c1_small = call(
        partial(close_kernel, [n // 2] * 2, 2), "c1_close", 1, 8, (c1, after(c1_b, a0_away), info),
        [((3 * n, C), BF), ((SMALL, C), BF)],
    )
    c1_back = to_win(c1, 1, "gc1_back")
    c1_sib = to_win(c1, 0, "gc1_mine")
    c1_small_sib = to_win(c1_small, 0, "gc1_small")
    m0 = plus(m0_mine, after(m0_z, c1), "m0_z2")
    m0_b = to_win(m0, 3, "gm0")
    a0 = plus(a0_mine, after(a0_y, m0), "a0_z")
    a0_z = to_win(a0, 2, "ga0")
    (layer_out,) = call(
        partial(out_kernel, rows, across), "layer_out", 1, 8, (after(st1, a0), o0_t),
        [((rows, cols, C), BF)],
        [tok_f],
    )
    m0 = plus(m0, after(m0_b, layer_out), "m0_sum")
    for bit in range(4, bits):
        m0 = plus(m0, to_win(m0, bit, "gm0"), "m0_sum")
    m0_b = to_win(m0, 2, "gm0_back")
    a0 = plus(a0, after(a0_z, m0), "a0_z2")
    a0_b = to_win(a0, 3, "ga0")
    c1_back = after(c1_back, a0)
    c1_pieces = (c1, c1_back, c1_sib, to_win(c1_back, 0, "gc1_theirs"))
    m0 = join([n // 2] * 2, 2, m0, after(m0_b, c1_back), "m0_join")
    m0_back = to_win(m0, 1, "gm0_back")
    m0_sib = to_win(m0, 0, "gm0_mine")
    c1_small_sib, c1_pieces = after((c1_small_sib, c1_pieces), m0)
    f1_shape, f2_shape = (2, C, 2 * C), (2, 2 * C, C)
    qkv_shape, proj_shape = (2, 3, 192, C), (2, 192, C)
    whole = [(f1_shape, F32, HBM), (f2_shape, F32, HBM), (qkv_shape, F32, HBM), (proj_shape, F32, HBM)]
    parts = [(x[0][1:], F32) for x in whole]
    attn_parts = [((2, C, C), F32)] + parts[2:]
    g_f1, g_f2, g_qkv, g_proj = call(
        final_second_kernel, "final_second", 1, 9, c1_pieces + (info,), whole,
        parts[:2] + attn_parts + [pltpu.SemaphoreType.DMA((4,))],
    )
    a0 = plus(a0, after(a0_b, g_f1), "a0_sum")
    for bit in range(4, bits):
        a0 = plus(a0, to_win(a0, bit, "ga0"), "a0_sum")
    a0_back = to_win(a0, 1, "ga0_back")
    a0_sib = to_win(a0, 0, "ga0_mine")
    shared = to_tp(a0[n : n + 16], "shared")
    m0_back = after(m0_back, a0_sib, shared)
    m0_pieces = (m0, m0_back, m0_sib, to_win(m0_back, 0, "gm0_theirs"))
    outs = call(
        final_kernel,
        "final",
        0.1,
        9,
        m0_pieces
        + (a0, a0_back, a0_sib, to_win(a0_back, 0, "ga0_theirs"), c1_small, c1_small_sib)
        + (shared, info, (g_f1, HBM), (g_f2, HBM), (g_qkv, HBM), (g_proj, HBM)),
        whole
        + [
            ((2, 2, C), F32),
            ((2, 2, C), F32),
            ((2, C), F32),
            ((2, C), F32),
            ((2, 2, 192), F32),
            ((2, 2 * C), F32),
            ((6, 2, 169), F32),
        ],
        parts[:2] + attn_parts + [((2, SMALL, C), F32), pltpu.SemaphoreType.DMA((4,))],
        aliases={12: 0, 13: 1, 14: 2, 15: 3},
    )
    (g_f1, g_f2, g_qkv, g_proj, g_gain, g_bias, g_pb, g_fb2, g_qvb, g_fb1, g_tab) = outs
    return (
        layer_out[None],
        grad_tokens.transpose(2, 0, 1, 3),
        g_gain,
        g_bias,
        g_qkv.transpose(0, 3, 1, 2),
        g_qvb,
        g_proj,
        g_pb,
        g_f1,
        g_fb1,
        g_f2,
        g_fb2,
        g_tab.transpose(1, 2, 0),
    )


def solution(mesh):
    return jax.shard_map(
        partial(on_device, mesh.shape["win"]),
        mesh=mesh,
        in_specs=(
            P("win", "tp", None, None),
            P("win", None, None),
            P("win", "tp", None, None),
            P(),
            P(),
            P(None, None, None, "tp"),
            P(None, None, "tp"),
            P(None, "tp", None),
            P(),
            P(None, None, "tp"),
            P(None, "tp"),
            P(None, "tp", None),
            P(),
            P(None, None, "tp"),
        ),
        out_specs=(
            P("win", "tp", None, None),
            P("win", "tp", None, None),
            P(),
            P(),
            P(None, None, None, "tp"),
            P(None, None, "tp"),
            P(None, "tp", None),
            P(),
            P(None, None, "tp"),
            P(None, "tp"),
            P(None, "tp", None),
            P(),
            P(None, None, "tp"),
        ),
        check_vma=False,
    )
```

```python
from functools import partial

import jax
import jax.numpy as jnp
import numpy as np
from jax import lax
from jax.experimental import pallas as pl
from jax.experimental.pallas import tpu as pltpu
from jax.sharding import PartitionSpec as P

C = 384
WIN = 7
SHIFT = 3
HD = 32
EPS = 1e-05
NEG = -1000000000.0
SCALE = HD**-0.5
F32 = jnp.float32
BF = jnp.bfloat16
SEG = 8
WROWS = WIN * SEG
WPAD = 64


def nn(a, b):
    return lax.dot_general(a, b, (((1,), (0,)), ((), ())), preferred_element_type=F32)


def nt(a, b):
    return lax.dot_general(a, b, (((1,), (1,)), ((), ())), preferred_element_type=F32)


def tn(a, b):
    return lax.dot_general(a, b, (((0,), (0,)), ((), ())), preferred_element_type=F32)


def norm_stats(x):
    mean = jnp.mean(x, -1, keepdims=True)
    cent = x - mean
    var = jnp.mean(cent * cent, -1, keepdims=True)
    rinv = lax.rsqrt(var + EPS)
    return cent * rinv, rinv


def norm_back(dz, xhat, rinv, gain):
    d = dz * gain
    return rinv * (
        d - jnp.mean(d, -1, keepdims=True) - xhat * jnp.mean(d * xhat, -1, keepdims=True)
    )


def tile_row(r, k, across):
    return (((r // WIN) * across + k) * WIN + r % WIN) * SEG


def zero_rows(n):
    return jnp.zeros((n, C), F32)


def head_mask():
    row = lax.broadcasted_iota(jnp.int32, (6 * WPAD, 6 * HD), 0) // WPAD
    col = lax.broadcasted_iota(jnp.int32, (6 * WPAD, 6 * HD), 1) // HD
    return (row == col).astype(BF)


def spread(x, mask):
    return jnp.concatenate([x] * 6, axis=0) * mask


def fold(o):
    lane = lax.broadcasted_iota(jnp.int32, (WPAD, 128), 1)

    def of(h, a, b):
        return o[WPAD * h : WPAD * (h + 1), a:b]

    one = jnp.where(lane < 96, of(2, 0, 128), of(3, 0, 128))
    one = jnp.where(lane < 64, of(1, 0, 128), one)
    one = jnp.where(lane < 32, of(0, 0, 128), one)
    two = jnp.where(lane[:, :64] < 32, of(4, 128, 192), of(5, 128, 192))
    return jnp.concatenate([one, two], axis=1)


def rows_at(i, n):
    return pl.ds(i * n, n)


def repeat(n, body, carry):
    for i in range(n):
        carry = body(i, carry)
    return carry


def iota(shape, dim):
    return lax.broadcasted_iota(jnp.int32, shape, dim)


def exact(a, b, ca, cb):
    return lax.dot_general(
        a,
        b,
        (((ca,), (cb,)), ((), ())),
        precision=lax.Precision.HIGHEST,
        preferred_element_type=F32,
    )


def offset_rows():
    return (12 - iota((16, 169), 0) == iota((16, 169), 1) // 13).astype(F32)


def offset_cols():
    return (iota((96, 169), 0) % 16 == iota((96, 169), 1) % 13).astype(F32)


def column_pick(kx):
    r = iota((96, 6 * WPAD), 0)
    c = iota((96, 6 * WPAD), 1)
    qx = c % 8
    return ((r // 16 == c // WPAD) & (r % 16 == qx - kx + WIN - 1) & (qx < WIN)).astype(BF)


def table_to_map(t, pick_ref, pos_ref):
    pos_ref[...] = jnp.zeros_like(pos_ref)
    group = (iota((8, 6 * WPAD), 1) % WPAD) // 8
    high = t.astype(BF)
    low = (t - high.astype(F32)).astype(BF)
    both = jnp.concatenate([high, low], axis=0)
    for kx in range(WIN):
        h = nn(both, pick_ref[kx])
        h = h[:16] + h[16:]
        g = jnp.zeros((8, 6 * WPAD), F32)
        for j in range(WIN):
            g = jnp.where(group == j, h[6 - j : 14 - j], g)
        for i in range(3):
            pos_ref[i, pl.ds(kx, 8, stride=8), :] = g[:, 128 * i : 128 * (i + 1)]


def map_to_table(pos_ref, pick_ref):
    group = (iota((16, 6 * WPAD), 1) % WPAD) // 8
    total = jnp.zeros((16, 96), F32)
    for kx in range(WIN):
        r = jnp.concatenate([pos_ref[i, pl.ds(kx, 8, stride=8), :] for i in range(3)], axis=1)
        h = jnp.zeros((16, 6 * WPAD), F32)
        for j in range(WIN):
            parts = [r, jnp.zeros((2 + j, 6 * WPAD), F32)]
            if j < 6:
                parts = [jnp.zeros((6 - j, 6 * WPAD), F32)] + parts
            h = jnp.where(group == j, jnp.concatenate(parts, axis=0), h)
        total = total + nt(h.astype(BF), pick_ref[kx])
    return total


def shift_in(tile, x_ref, rows, across):
    for r in range(rows):
        for k in range(across):
            a = tile(r + SHIFT, k)
            b = tile(r + SHIFT, (k + 1) % across)
            x_ref[pl.ds(tile_row(r, k, across), SEG), :] = jnp.concatenate(
                [a[SHIFT:WIN], b[:SHIFT], zero_rows(1)], axis=0
            )


def shift_out(tile, x_ref, rows, across):
    for r in range(rows):
        for k in range(across):
            a = tile(r - SHIFT, (k - 1) % across)
            b = tile(r - SHIFT, k)
            x_ref[pl.ds(tile_row(r, k, across), SEG), :] = jnp.concatenate(
                [a[WIN - SHIFT : WIN], b[: WIN - SHIFT], zero_rows(1)], axis=0
            )

EDGE_ROWS = 96
SMALL = 16


SMALL_ROWS = 24
SENT_ROWS = 8


def copies_of(pairs, sems):
    copies = [pltpu.make_async_copy(x, y, sems.at[n]) for n, (x, y) in enumerate(pairs)]
    for copy in copies:
        copy.start()
    return copies


def attn_copies(layer, par, qkvw_ref, projw_ref, a_ref):
    of_heads = pl.ds(pl.multiple_of(par * 96, 96), 96)
    pairs = [
        (qkvw_ref.at[layer, j, of_heads, :], a_ref.at[pl.ds(96 * j, 96), :]) for j in range(3)
    ]
    return pairs + [(projw_ref.at[layer, of_heads, :], a_ref.at[pl.ds(288, 96), :])]


def mlp_copies(layer, par, f1_ref, f2_ref, m_ref):
    of_units = pl.ds(pl.multiple_of(par * C, C), C)
    return [
        (f1_ref.at[layer, :, of_units], m_ref.at[pl.ds(0, C), :]),
        (f2_ref.at[layer, of_units, :], m_ref.at[pl.ds(C, C), :]),
    ]


def high_low(x):
    rows = []
    for r in range(4):
        rows.append(jnp.concatenate([x[4 * r + k : 4 * r + k + 1, 0:96] for k in range(4)], axis=1))
    rows.append(x[16:18])
    rows.append(jnp.concatenate([x[18:19, 0:192], x[19:20, 0:192]], axis=1))
    rows.append(zero_rows(1))
    x = jnp.concatenate(rows, axis=0)
    high = x.astype(BF).astype(F32)
    return jnp.concatenate([high, x - high], axis=0).astype(BF)


def pack_first_kernel(
    qkvw_ref, projw_ref, tab_ref, qvb_ref, fb1_ref,
    a0_ref, small_ref, tab_v, qvb_v, fb1_v, sems
):
    pairs = [(tab_ref, tab_v), (qvb_ref, qvb_v), (fb1_ref, fb1_v)]
    copies = copies_of(pairs + attn_copies(0, POSITION[0], qkvw_ref, projw_ref, a0_ref), sems)
    small_ref[...] = jnp.zeros_like(small_ref)
    for copy in copies[:3]:
        copy.wait()
    for layer in range(2):
        tab = tab_v[:, layer, :]
        wide = jnp.concatenate([jnp.broadcast_to(tab[h : h + 1], (16, 169)) for h in range(6)])
        small_ref[layer, 0:16, 0:96] = exact(offset_rows(), wide * offset_cols(), 1, 1)
        small_ref[layer, 16:17, :] = fb1_v[layer : layer + 1, 0:C]
        small_ref[layer, 17:18, :] = fb1_v[layer : layer + 1, C:]
        small_ref[layer, 18:20, 0:192] = qvb_v[layer]
    a0_ref[C:, :] = high_low(small_ref[0])
    for copy in copies[3:]:
        copy.wait()


def pack_kernel(
    qkvw_ref, projw_ref, f1_ref, f2_ref, cot_ref, small_ref, info_ref,
    m0_ref, a1_ref, m1_ref, edge_ref, cot_v, sems
):
    par = info_ref[0]
    pairs = [(cot_ref.at[pl.ds(0, SHIFT)], cot_v)]
    pairs += mlp_copies(0, par, f1_ref, f2_ref, m0_ref)
    pairs += attn_copies(1, par, qkvw_ref, projw_ref, a1_ref)
    pairs += mlp_copies(1, par, f1_ref, f2_ref, m1_ref)
    copies = copies_of(pairs, sems)
    a1_ref[C:, :] = high_low(small_ref[1])
    copies[0].wait()
    edge = [cot_v[r].astype(F32) for r in range(SHIFT)]
    n = EDGE_ROWS - SHIFT * cot_v.shape[1]
    edge_ref[...] = jnp.concatenate(edge + [zero_rows(n)], axis=0).astype(BF)
    for copy in copies[1:]:
        copy.wait()


def small_of(a_ref, small_ref):
    rows = a_ref[C : C + 2 * SENT_ROWS, :].astype(F32)
    x = rows[0:SENT_ROWS] + rows[SENT_ROWS:]
    small_ref[...] = jnp.zeros_like(small_ref)
    for r in range(4):
        for k in range(4):
            small_ref[4 * r + k : 4 * r + k + 1, 0:96] = x[r : r + 1, 96 * k : 96 * (k + 1)]
    small_ref[16:18, :] = x[4:6]
    small_ref[18:19, 0:192] = x[6:7, 0:192]
    small_ref[19:20, 0:192] = x[6:7, 192:384]


def edge_tile(edge, k, r):
    at = (k * SHIFT + r) * SEG
    return edge[at : at + SEG]


def edge_rows(ref, across, rows):
    tiles = [ref[pl.ds(tile_row(r, k, across), SEG), :] for k in range(across) for r in rows]
    return jnp.concatenate(tiles, axis=0).astype(BF)


def prep_kernel(layer, rows, across, *refs):
    (crop_ref, small_ref, info_ref) = refs[:3]
    if layer == 0:
        (lq_ref, lk_ref, pos_ref, pick_ref, c_ref) = refs[3:]
        for kx in range(WIN):
            pick_ref[kx] = column_pick(kx)
    else:
        (pick_ref, lq_ref, lk_ref, pos_ref, c_ref) = refs[3:]
    tp = info_ref[1]
    cols = across * WIN
    height = crop_ref.shape[2]
    table_to_map(small_ref[layer, 0:16, 0:96], pick_ref, pos_ref)
    c_ref[...] = jnp.zeros_like(c_ref)
    c_ref[0:cols, 0:height] = crop_ref[:, 0, :].astype(F32)
    crops = c_ref[...].astype(BF)
    row = iota((32, 128), 0)
    lane = iota((32, 128), 1)
    shift = SHIFT if layer == 1 else 0
    src = rows * tp + row + shift
    src = jnp.where(src >= height, src - height, src)
    grid = nt((src == lane).astype(BF), crops).astype(BF)
    labs = []
    for wc in range(across):
        qx = iota((128, 128), 1) % 8
        col = qx + (WIN * wc + shift)
        col = jnp.where(col >= cols, col - cols, col)
        pick = ((col == iota((128, 128), 0)) & (qx < WIN)).astype(BF)
        lab = nn(grid, pick)
        if layer == 1:
            g = rows * tp + row
            zr = (g >= height - WIN).astype(F32) + (g >= height - SHIFT).astype(F32)
            here = lane % 8 + WIN * wc
            zc = (here >= cols - WIN).astype(F32) + (here >= cols - SHIFT).astype(F32)
            lab = lab * 9.0 + zr * 3.0 + zc
        labs.append(lab)
    real = (iota((1, 128), 1) % 8 < WIN) & (iota((1, 128), 1) % WPAD < WROWS)
    for wr in range(rows // WIN):
        lines = []
        for wc in range(across):
            w = wr * across + wc
            mine = row == (lane % WPAD) // 8 + WIN * wr
            line = jnp.sum(jnp.where(mine, labs[wc], 0.0), 0, keepdims=True)
            line = jnp.where(real, line, -1.0)
            lq_ref[w : w + 1, :] = line
            lines.append(line)
        for wc in range(0, across, 2):
            w = wr * across + wc
            both = jnp.where(iota((1, 128), 1) < WPAD, lines[wc], lines[wc + 1])
            both = jnp.broadcast_to(both, (128, 128)).T
            lk_ref[w] = both[:WPAD]
            lk_ref[w + 1] = both[WPAD:]


def qkv_weight_of(half, j, layer, qkvw_ref, a_ref, b_ref):
    if half == 0:
        return qkvw_ref[layer, j]
    return jnp.concatenate([a_ref[96 * j : 96 * (j + 1)], b_ref[96 * j : 96 * (j + 1)]], axis=0)


def proj_weight_of(half, layer, projw_ref, a_ref, b_ref):
    if half == 0:
        return projw_ref[layer]
    return jnp.concatenate([a_ref[288:384], b_ref[288:384]], axis=0)


def norm_windows(layer, wins, x_ref, xn_ref, gain_ref, bias_ref):
    gain = gain_ref[layer, 0:1]
    bias = bias_ref[layer, 0:1]

    def four(i, carry):
        xhat, _ = norm_stats(x_ref[rows_at(i, 4 * WROWS), :])
        xn = xhat * gain + bias
        for n in range(4):
            part = jnp.concatenate(
                [xn[n * WROWS : (n + 1) * WROWS], zero_rows(WPAD - WROWS)], axis=0
            )
            xn_ref[rows_at(4 * i + n, WPAD), :] = part.astype(BF)
        return carry

    repeat(wins // 4, four, 0)


def project_half(xn_ref, qkv_ref, weight, qb, vb):
    n = xn_ref.shape[0]

    def part(i, carry):
        at = rows_at(i, n)
        xn = xn_ref[at, :]
        q = nt(xn, weight(0))
        k = nt(xn, weight(1))
        v = nt(xn, weight(2))
        qkv_ref[0, at, :] = ((q + qb) * SCALE).astype(BF)
        qkv_ref[1, at, :] = k.astype(BF)
        qkv_ref[2, at, :] = (v + vb).astype(BF)
        return carry

    repeat(1, part, 0)


def attend_forward(halves, wins, group, lq_ref, lk_ref, mask_ref):
    def body(i, carry):
        units = [(i * group + u, h) for u in range(group) for h in halves]
        scores = []
        for w, (qkv_ref, _, _, _) in units:
            at = rows_at(w, WPAD)
            scores.append(nt(qkv_ref[1, at, :], spread(qkv_ref[0, at, :], mask_ref[...])))
        probs = []
        for (w, (_, pos, p_ref, _)), s in zip(units, scores):
            same = lk_ref[w] == lq_ref[pl.ds(w, 1), :]
            same = jnp.concatenate([same] * 3, axis=1)
            s = jnp.where(same, s + jnp.concatenate([pos[n] for n in range(3)], axis=1), NEG)
            e = jnp.exp(s - jnp.max(s, 0, keepdims=True))
            p = (e * (1.0 / jnp.sum(e, 0, keepdims=True))).astype(BF)
            p_ref[w] = p
            probs.append(p)
        for (w, (qkv_ref, _, _, mix_ref)), p in zip(units, probs):
            at = rows_at(w, WPAD)
            mix_ref[at, :] = fold(tn(p, qkv_ref[2, at, :])).astype(BF)
        return carry

    repeat(wins // group, body, 0)


def add_branch(wins, mixes, weights, bias, x_ref, hid_ref):
    n = 8

    def part(i, carry):
        res = bias
        for m_ref, w in zip(mixes, weights):
            res = res + nn(m_ref[rows_at(i, n * WPAD), :], w)
        for k in range(n):
            to = rows_at(i * n + k, WROWS)
            hid_ref[to, :] = x_ref[to, :] + res[k * WPAD : k * WPAD + WROWS]
        return carry

    repeat(wins // n, part, 0)


def attn_own_kernel(rows, across, *refs):
    (tok_ref, gain_ref, bias_ref, pb_ref, qvb_ref, qkvw_ref, projw_ref) = refs[:7]
    (pos_ref, lq_ref, lk_ref) = refs[7:10]
    (xb_ref, xn_ref, hid_ref, qkv_ref, p_ref, mix_ref, mask_ref, x_ref) = refs[10:]
    wins = (rows // WIN) * across
    for r in range(rows):
        row = tok_ref[r].astype(F32)
        for k in range(across):
            x_ref[pl.ds(tile_row(r, k, across), SEG), :] = jnp.concatenate(
                [row[WIN * k : WIN * (k + 1)], zero_rows(1)], axis=0
            )
    xb_ref[...] = x_ref[...].astype(BF)
    mask_ref[...] = head_mask()
    norm_windows(0, wins, x_ref, xn_ref, gain_ref, bias_ref)
    project_half(
        xn_ref, qkv_ref, lambda j: qkvw_ref[0, j], qvb_ref[0, 0:1], qvb_ref[0, 1:2]
    )
    attend_forward(
        [(qkv_ref, pos_ref, p_ref, mix_ref)], wins, wins, lq_ref, lk_ref, mask_ref
    )
    add_branch(wins, [mix_ref], [projw_ref[0]], pb_ref[0:1], x_ref, hid_ref)


def attn_other_kernel(rows, across, *refs):
    (part_ref, xn_ref, a_ref, b_ref, lq_ref, lk_ref, pick_ref, info_ref) = refs[:8]
    (hid_ref, qkv_ref, p_ref, mix_ref, small_ref, mask_ref, pos_ref) = refs[8:]
    small_of(a_ref, small_ref)
    wins = (rows // WIN) * across
    mask_ref[...] = head_mask()
    bias = other_small(small_ref, info_ref[0], pick_ref, pos_ref)
    project_half(
        xn_ref,
        qkv_ref,
        lambda j: qkv_weight_of(1, j, 0, None, a_ref, b_ref),
        bias[0:1],
        bias[1:2],
    )
    attend_forward([(qkv_ref, pos_ref, p_ref, mix_ref)], wins, wins, lq_ref, lk_ref, mask_ref)
    add_branch(
        wins, [mix_ref], [proj_weight_of(1, 0, None, a_ref, b_ref)], 0.0, part_ref, hid_ref
    )


def other_small(small_ref, par, pick_ref, pos_ref):
    first = par == 0

    def swapped(v, n):
        return jnp.where(first, v, jnp.concatenate([v[:, n : 2 * n], v[:, :n]], axis=1))

    t = swapped(small_ref[0:16, 0:96], 48)
    table_to_map(t, pick_ref, pos_ref)
    return swapped(small_ref[18:20, 0:192], 96)


def norm_kernel(rows, across, *refs):
    (st_ref, halo_ref, gain_ref, bias_ref, qvb_ref, qkvw_ref) = refs[:6]
    (x_ref, xn_ref, qkv_ref) = refs[6:]

    def tile(r, k):
        if r < rows:
            return st_ref[pl.ds(tile_row(r, k, across), SEG), :]
        return edge_tile(halo, k, r - rows)

    halo = halo_ref[...].astype(F32)
    shift_in(tile, x_ref, rows, across)
    norm_windows(1, (rows // WIN) * across, x_ref, xn_ref, gain_ref, bias_ref)
    project_half(
        xn_ref, qkv_ref, lambda j: qkvw_ref[1, j], qvb_ref[1, 0:1], qvb_ref[1, 1:2]
    )


def attn_both_kernel(rows, across, *refs):
    (xn_ref, qkv0_ref, pos_ref, a_ref, b_ref, x_ref, projw_ref, pb_ref) = refs[:8]
    (lq_ref, lk_ref, pick_ref, info_ref) = refs[8:12]
    (hid_ref, p0_ref, mix0_out, qkv1_ref, p1_ref, mix1_out, small_ref) = refs[12:19]
    (mask_ref, pos1_ref, mix0_ref, mix1_ref, sems) = refs[19:]
    wins = (rows // WIN) * across
    mask_ref[...] = head_mask()
    small_of(a_ref, small_ref)
    bias = other_small(small_ref, info_ref[0], pick_ref, pos1_ref)
    project_half(
        xn_ref,
        qkv1_ref,
        lambda j: qkv_weight_of(1, j, 1, None, a_ref, b_ref),
        bias[0:1],
        bias[1:2],
    )
    attend_forward(
        [(qkv0_ref, pos_ref, p0_ref, mix0_ref), (qkv1_ref, pos1_ref, p1_ref, mix1_ref)],
        wins,
        wins,
        lq_ref,
        lk_ref,
        mask_ref,
    )
    copies = copies_of([(mix0_ref, mix0_out), (mix1_ref, mix1_out)], sems)
    add_branch(
        wins,
        [mix0_ref, mix1_ref],
        [projw_ref[1], proj_weight_of(1, 1, None, a_ref, b_ref)],
        pb_ref[1:2],
        x_ref,
        hid_ref,
    )
    for copy in copies:
        copy.wait()


def up_weight(part, layer, base, f1_ref, a_ref, b_ref):
    if part == 0:
        return f1_ref[layer]
    return jnp.concatenate([a_ref[base : base + C], b_ref[base : base + C]], axis=1)


def down_weight(part, layer, base, f2_ref, a_ref, b_ref):
    if part == 0:
        return f2_ref[layer]
    return jnp.concatenate([a_ref[base + C : base + 2 * C], b_ref[base + C : base + 2 * C]], axis=0)


def up_biases(layer, par, fb1_ref, small_ref):
    own = fb1_ref[layer : layer + 1]
    one, two = small_ref[16:17], small_ref[17:18]
    first = par == 0
    return own, jnp.concatenate(
        [jnp.where(first, one, two), jnp.where(first, two, one)], axis=1
    )


def gelu_pair(u):
    phi = 0.5 + 0.5 * lax.erf(u * (2.0**-0.5))
    slope = phi + u * (jnp.exp(-0.5 * u * u) * (2.0 * np.pi) ** -0.5)
    return (u * phi).astype(BF), slope.astype(BF)


def mlp_own_kernel(hid_ref, gain_ref, bias_ref, fb1_ref, fb2_ref, f1_ref, f2_ref, st_ref, n2_ref, act_ref, gp_ref):
    h = hid_ref[...]
    xhat, _ = norm_stats(h)
    n2 = (xhat * gain_ref[0, 1:2] + bias_ref[0, 1:2]).astype(BF)
    n2_ref[...] = n2
    act, slope = gelu_pair(nn(n2, f1_ref[0]) + fb1_ref[0:1])
    for z in range(2):
        act_ref[z] = act[:, C * z : C * (z + 1)]
        gp_ref[z] = slope[:, C * z : C * (z + 1)]
    st_ref[...] = h + fb2_ref[0:1] + nn(act, f2_ref[0])


def mlp_other_kernel(
    across, part_ref, n2_ref, fb1_ref, small_ref, a_ref, b_ref, info_ref, st_ref, act_ref, gp_ref,
    edge_ref
):
    _, bias = up_biases(0, info_ref[0], fb1_ref, small_ref)
    act, slope = gelu_pair(nn(n2_ref[...], up_weight(1, 0, 0, None, a_ref, b_ref)) + bias)
    for z in range(2):
        act_ref[z] = act[:, C * z : C * (z + 1)]
        gp_ref[z] = slope[:, C * z : C * (z + 1)]
    st_ref[...] = part_ref[...] + nn(act, down_weight(1, 0, 0, None, a_ref, b_ref))
    edge_ref[...] = edge_rows(st_ref, across, range(SHIFT))


def quarter_of(par, slot, part):
    return (par ^ slot) if part == 0 else 2 + slot


BLOCKS = 1


def half_sums(du, ref):
    for z in range(2):
        ref[z : z + 1] += jnp.sum(du[z].astype(F32), 0, keepdims=True)


def mlp_own_both_kernel(rows, across, *refs):
    (cot_ref, edge_ref, hid_ref, gain_ref, bias_ref, fb1_ref, fb2_ref, f1_ref, f2_ref) = refs[:9]
    (g_ref, df_ref, n2_ref, st_ref, dz_ref, du_ref, act_ref, sum_ref, sf_ref) = refs[9:]
    layer = 1
    cols = across * WIN
    cot_edge = edge_ref[...].astype(F32)
    for r in range(rows):
        s = r + SHIFT
        if s < rows:
            row = cot_ref[s].astype(F32)
        else:
            row = cot_edge[(s - rows) * cols : (s - rows + 1) * cols]
        for k in range(across):
            a = WIN * k + SHIFT
            if k < across - 1:
                piece = [row[a : a + WIN]]
            else:
                piece = [row[a:], row[:SHIFT]]
            g_ref[pl.ds(tile_row(r, k, across), SEG), :] = jnp.concatenate(
                piece + [zero_rows(1)], axis=0
            )
    sum_ref[...] = jnp.zeros_like(sum_ref)
    sf_ref[...] = jnp.zeros_like(sf_ref)
    n = hid_ref.shape[0] // BLOCKS

    def block(i, carry):
        at = pl.ds(pl.multiple_of(i * n, n), n)
        h = hid_ref[at, :]
        xhat, _ = norm_stats(h)
        n2 = (xhat * gain_ref[layer, 1:2] + bias_ref[layer, 1:2]).astype(BF)
        n2_ref[at, :] = n2
        df = g_ref[at, :].astype(BF)
        df_ref[at, :] = df
        sf_ref[...] += jnp.sum(df.astype(F32), 0, keepdims=True)
        up = nn(n2, f1_ref[layer]) + fb1_ref[layer : layer + 1]
        grad = nt(df, f2_ref[layer])
        act, slope = gelu_pair(up)
        du = (grad * slope.astype(F32)).astype(BF)
        parts = [du[:, C * z : C * (z + 1)] for z in range(2)]
        for z in range(2):
            act_ref[z, at, :] = act[:, C * z : C * (z + 1)]
            du_ref[z, at, :] = parts[z]
        half_sums(parts, sum_ref)
        st_ref[at, :] = h + fb2_ref[layer : layer + 1] + nn(act, f2_ref[layer])
        dz_ref[at, :] = nt(du, f1_ref[layer])
        return carry

    lax.fori_loop(0, BLOCKS, block, 0)


def mlp_other_both_kernel(rows, across, *refs):
    (hid_ref, g_ref, df_ref, n2_ref, part_ref, dzp_ref, gain_ref, fb1_ref, small_ref) = refs[:9]
    (a_ref, b_ref, info_ref, sumo_ref, sf_ref) = refs[9:14]
    (out_ref, gh_ref, du_ref, act_ref, send_ref, sum_ref, sh_ref, edge_ref, st_ref) = refs[14:]
    layer = 1
    par = info_ref[0]
    _, bias = up_biases(layer, par, fb1_ref, small_ref)
    w1 = up_weight(1, layer, 0, None, a_ref, b_ref)
    w2 = down_weight(1, layer, 0, None, a_ref, b_ref)
    sum_ref[0:2] = sumo_ref[...]
    sum_ref[2:4] = jnp.zeros((2, C), F32)
    sh_ref[0:2] = jnp.zeros((2, C), F32)
    sh_ref[2:3] = sf_ref[...]
    n = hid_ref.shape[0] // BLOCKS

    def block(i, carry):
        at = pl.ds(pl.multiple_of(i * n, n), n)
        up = nn(n2_ref[at, :], w1) + bias
        grad = nt(df_ref[at, :], w2)
        act, slope = gelu_pair(up)
        du = (grad * slope.astype(F32)).astype(BF)
        parts = [du[:, C * z : C * (z + 1)] for z in range(2)]
        for z in range(2):
            act_ref[z, at, :] = act[:, C * z : C * (z + 1)]
            du_ref[z, at, :] = parts[z]
        half_sums(parts, sum_ref.at[2:4])
        st_ref[at, :] = part_ref[at, :] + nn(act, w2)
        dz = dzp_ref[at, :] + nt(du, w1)
        xhat, rinv = norm_stats(hid_ref[at, :])
        sh_ref[0:1] += jnp.sum(dz * xhat, 0, keepdims=True)
        sh_ref[1:2] += jnp.sum(dz, 0, keepdims=True)
        gh_ref[at, :] = g_ref[at, :] + norm_back(dz, xhat, rinv, gain_ref[layer, 1:2])
        return carry

    lax.fori_loop(0, BLOCKS, block, 0)
    edge_ref[...] = edge_rows(st_ref, across, range(rows - SHIFT, rows))
    out_ref[...] = st_ref[...].astype(BF)
    n2 = n2_ref[...]
    df = df_ref[...]
    send_ref[0:C, :] = tn(n2, du_ref[1]).astype(BF)
    send_ref[C:, :] = tn(act_ref[1], df).astype(BF)


def own_grads_kernel(n2_ref, df_ref, du_ref, act_ref, info_ref, keep_ref, send_ref):
    n2 = n2_ref[...]
    df = df_ref[...]
    for slot, ref in ((1, send_ref), (0, keep_ref)):
        q = info_ref[0] ^ slot
        ref[0:C, :] = tn(n2, du_ref[q]).astype(BF)
        ref[C:, :] = tn(act_ref[q], df).astype(BF)


def mlp_keep_kernel(n2_ref, df_ref, du_ref, act_ref, keep_ref):
    keep_ref[0:C, :] = tn(n2_ref[...], du_ref[0]).astype(BF)
    keep_ref[C:, :] = tn(act_ref[0], df_ref[...]).astype(BF)


def up_keep_kernel(n2_ref, du_ref, keep_ref):
    keep_ref[...] = tn(n2_ref[...], du_ref[0]).astype(BF)


def down_grad_kernel(rows, across, *refs):
    (gin_ref, halo_ref, act0_ref, act1_ref, info_ref, g_ref, df_ref, keep_ref, send_ref) = refs

    def tile(r, k):
        if r >= 0:
            return gin_ref[pl.ds(tile_row(r, k, across), SEG), :]
        return edge_tile(halo, k, r + SHIFT)

    halo = halo_ref[...].astype(F32)
    shift_out(tile, g_ref, rows, across)
    df = g_ref[...].astype(BF)
    df_ref[...] = df
    for slot, ref in ((1, send_ref), (0, keep_ref)):
        ref[1] = tn(act1_ref[slot], df).astype(BF)
        ref[0] = tn(act0_ref[info_ref[0] ^ slot], df).astype(BF)


def mlp_bwd_own_kernel(*refs):
    (df_ref, gp_ref, n2_ref, f1_ref, f2_ref, info_ref) = refs[:6]
    (dz_ref, sum_ref, keep_ref, send_ref, du_ref) = refs[6:]
    grad = nt(df_ref[...], f2_ref[0])
    parts = [
        (grad[:, C * z : C * (z + 1)] * gp_ref[z].astype(F32)).astype(BF) for z in range(2)
    ]
    for z in range(2):
        du_ref[z] = parts[z]
    sum_ref[...] = jnp.zeros_like(sum_ref)
    half_sums(parts, sum_ref)
    dz_ref[...] = nt(jnp.concatenate(parts, axis=1), f1_ref[0])
    n2 = n2_ref[...]
    for slot, ref in ((1, send_ref), (0, keep_ref)):
        ref[...] = tn(n2, du_ref[info_ref[0] ^ slot]).astype(BF)


def mlp_bwd_other_kernel(*refs):
    (g_ref, df_ref, hid_ref, n2_ref, gp_ref, dzp_ref, gain_ref, a_ref, b_ref, sumo_ref) = refs[:10]
    (gh_ref, du_ref, send_ref, sum_ref, sh_ref) = refs[10:]
    df = df_ref[...]
    grad = nt(df, down_weight(1, 0, 0, None, a_ref, b_ref))
    parts = [
        (grad[:, C * z : C * (z + 1)] * gp_ref[z].astype(F32)).astype(BF) for z in range(2)
    ]
    for z in range(2):
        du_ref[z] = parts[z]
    sum_ref[0:2] = sumo_ref[...]
    sum_ref[2:4] = jnp.zeros((2, C), F32)
    half_sums(parts, sum_ref.at[2:4])
    dz = dzp_ref[...] + nt(jnp.concatenate(parts, axis=1), up_weight(1, 0, 0, None, a_ref, b_ref))
    xhat, rinv = norm_stats(hid_ref[...])
    sh_ref[0:1] = jnp.sum(dz * xhat, 0, keepdims=True)
    sh_ref[1:2] = jnp.sum(dz, 0, keepdims=True)
    sh_ref[2:3] = jnp.sum(df.astype(F32), 0, keepdims=True)
    gh_ref[...] = g_ref[...] + norm_back(dz, xhat, rinv, gain_ref[0, 1:2])
    send_ref[...] = tn(n2_ref[...], du_ref[1]).astype(BF)


def window_grads(wins, gh_ref, da_ref):
    def four(i, s):
        g = gh_ref[rows_at(i, 4 * WROWS), :]
        for n in range(4):
            part = jnp.concatenate(
                [g[n * WROWS : (n + 1) * WROWS], zero_rows(WPAD - WROWS)], axis=0
            ).astype(BF)
            da_ref[rows_at(4 * i + n, WPAD), :] = part
            s = s + jnp.sum(part.astype(F32), 0, keepdims=True)
        return s

    return repeat(wins // 4, four, jnp.zeros((1, C), F32))


def attend_backward(halves, wins, group, mask_ref):
    def body(i, carry):
        units = [(i * group + u, h) for u in range(group) for h in halves]
        first = []
        for w, (qkv_ref, p_ref, do_ref, dqkv_ref, _) in units:
            at = rows_at(w, WPAD)
            do = spread(do_ref[at, :], mask_ref[...])
            first.append(nt(qkv_ref[2, at, :], do))
            dqkv_ref[2, at, :] = nn(p_ref[w], do).astype(BF)
        second = []
        for (w, (_, p_ref, _, _, acc_ref)), dp in zip(units, first):
            p = p_ref[w].astype(F32)
            ds = p * (dp - jnp.sum(p * dp, 0, keepdims=True))
            for n in range(3):
                acc_ref[n] += ds[:, 128 * n : 128 * (n + 1)]
            second.append(ds.astype(BF))
        for (w, (qkv_ref, _, _, dqkv_ref, _)), ds in zip(units, second):
            at = rows_at(w, WPAD)
            dqkv_ref[1, at, :] = nn(ds, spread(qkv_ref[0, at, :], mask_ref[...])).astype(BF)
            dqkv_ref[0, at, :] = fold(tn(ds, qkv_ref[1, at, :])).astype(BF)
        return carry

    repeat(wins // group, body, 0)


def half_grads(half, par, xn_ref, da_ref, mix_ref, dqkv_ref, row_ref, give):
    def put(value, at):
        if half == 0:
            row_ref[...] = value
            one = row_ref[pl.ds(pl.multiple_of(par * 96, 96), 96), :]
            two = row_ref[pl.ds(pl.multiple_of((1 - par) * 96, 96), 96), :]
        else:
            one, two = value[:96], value[96:]
        give(at, one.astype(BF), two.astype(BF))

    xn = xn_ref[...]
    for j in range(3):
        grad = tn(dqkv_ref[j], xn)
        put(grad * SCALE if j == 0 else grad, 96 * j)
    put(tn(mix_ref[...], da_ref[...]), 288)


def normed_grads(layer, wins, dqkvs, weights, gh_ref, x_ref, gain_ref, gx_ref):
    gain = gain_ref[layer, 0:1]
    n = 8

    def part(i, carry):
        sg, sb, sq = carry
        at = rows_at(i, n * WPAD)
        dn = nn(dqkvs[0][0, at, :], weights[0](0)) + nn(dqkvs[1][0, at, :], weights[1](0))
        dn = dn * SCALE
        for half in range(2):
            for j in (1, 2):
                dn = dn + nn(dqkvs[half][j, at, :], weights[half](j))
        new = []
        for half in range(2):
            for m, j in enumerate((0, 2)):
                new.append(
                    sq[half * 2 + m] + jnp.sum(dqkvs[half][j, at, :].astype(F32), 0, keepdims=True)
                )
        d = jnp.concatenate([dn[k * WPAD : k * WPAD + WROWS] for k in range(n)], axis=0)
        to = rows_at(i, n * WROWS)
        xhat, rinv = norm_stats(x_ref[to, :].astype(F32))
        sg = sg + jnp.sum(d * xhat, 0, keepdims=True)
        sb = sb + jnp.sum(d, 0, keepdims=True)
        gx_ref[to, :] = gh_ref[to, :] + norm_back(d, xhat, rinv, gain)
        return sg, sb, tuple(new)

    z = jnp.zeros((1, C), F32)
    zq = jnp.zeros((1, 6 * HD), F32)
    return repeat(wins // n, part, (z, z, (zq,) * 4))


def small_rows(ref, z, sq, fb1, table, shared):
    ref[...] = jnp.zeros_like(ref)
    if shared is not None:
        sg, sb, projb, sh_ref = shared
        ref[0:1] = sg
        ref[1:2] = sb
        ref[2:3] = projb
        ref[3:6] = sh_ref[...]
    ref[6:7] = fb1
    ref[7:8, 0:96] = sq[0][:, 96 * z : 96 * (z + 1)] * SCALE
    ref[7:8, 128:224] = sq[1][:, 96 * z : 96 * (z + 1)]
    part = table[:, 48 * z : 48 * (z + 1)]
    for r in range(2):
        ref[8 + r : 9 + r, :] = jnp.concatenate(
            [part[8 * r + k : 8 * r + k + 1] for k in range(8)], axis=1
        )


def mixed_grad_kernel(wins, gh_ref, projw_ref, a_ref, b_ref, da_ref, do_ref, pb_ref):
    pb_ref[...] = window_grads(wins, gh_ref, da_ref)
    for half in range(2):
        do_ref[half] = nt(da_ref[...], proj_weight_of(half, 1, projw_ref, a_ref, b_ref)).astype(BF)


def attn_bwd_kernel(rows, across, *refs):
    (gh_ref, x_ref, xn_ref, gain_ref, qkvw_ref, a_ref, b_ref, info_ref) = refs[:8]
    (fb1_ref, sh_ref, qkv0_ref, p0_ref, mix0_ref, qkv1_ref, p1_ref, mix1_ref, pick_ref) = refs[8:17]
    (da_ref, do_ref, pb_ref) = refs[17:20]
    (gin_ref, keep_ref, send_ref, edge_ref) = refs[20:24]
    (dqkv0_ref, dqkv1_ref, acc_ref, mask_ref, row_ref, sm_ref) = refs[24:]
    layer = 1
    par = info_ref[0]
    wins = (rows // WIN) * across
    mask_ref[...] = head_mask()
    acc_ref[...] = jnp.zeros_like(acc_ref)
    projb = pb_ref[...]
    attend_backward(
        [
            (qkv0_ref, p0_ref, do_ref.at[0], dqkv0_ref, acc_ref.at[0]),
            (qkv1_ref, p1_ref, do_ref.at[1], dqkv1_ref, acc_ref.at[1]),
        ],
        wins,
        wins,
        mask_ref,
    )
    for half, mix_ref, dqkv_ref in ((1, mix1_ref, dqkv1_ref), (0, mix0_ref, dqkv0_ref)):

        def give(at, one, two, half=half):
            keep_ref[half, at : at + 96, :] = one
            send_ref[half, at : at + 96, :] = two

        half_grads(half, par, xn_ref, da_ref, mix_ref, dqkv_ref, row_ref, give)
    weights = [
        lambda j, half=half: qkv_weight_of(half, j, layer, qkvw_ref, a_ref, b_ref)
        for half in range(2)
    ]
    sg, sb, sq = normed_grads(
        layer, wins, [dqkv0_ref, dqkv1_ref], weights, gh_ref, x_ref, gain_ref, gin_ref
    )
    edge_ref[...] = edge_rows(gin_ref, across, range(rows - SHIFT, rows))
    for half in range(2):
        table = map_to_table(acc_ref.at[half], pick_ref)
        for z in range(2):
            q = 2 * half + z
            small_rows(
                sm_ref.at[q], z, sq[2 * half : 2 * half + 2], fb1_ref[q : q + 1], table,
                (sg, sb, projb, sh_ref)
            )
    keep_ref[0, C:, :] = sm_ref[par].astype(BF)
    send_ref[0, C:, :] = sm_ref[1 - par].astype(BF)
    keep_ref[1, C:, :] = sm_ref[2].astype(BF)
    send_ref[1, C:, :] = sm_ref[3].astype(BF)


def column_sum(ref):
    return jnp.sum(ref[...].astype(F32), 0, keepdims=True)


def attn_bwd_heads_kernel(rows, across, *refs):
    (gh_ref, xn_ref, projw_ref, a_ref, b_ref, fb1_ref) = refs[:6]
    (qkv0_ref, p0_ref, qkv1_ref, p1_ref, mix1_ref, pick_ref) = refs[6:12]
    (da_ref, dqkv0_ref, acc0_ref, dqkv1_ref, pb_ref, keep_ref, send_ref) = refs[12:19]
    (do_ref, mask_ref, acc1_ref, sm_ref) = refs[19:]
    wins = (rows // WIN) * across
    mask_ref[...] = head_mask()
    acc0_ref[...] = jnp.zeros_like(acc0_ref)
    acc1_ref[...] = jnp.zeros_like(acc1_ref)
    pb_ref[...] = window_grads(wins, gh_ref, da_ref)
    da = da_ref[...]
    for half in range(2):
        do_ref[half] = nt(da, proj_weight_of(half, 0, projw_ref, a_ref, b_ref)).astype(BF)
    attend_backward(
        [
            (qkv1_ref, p1_ref, do_ref.at[1], dqkv1_ref, acc1_ref),
            (qkv0_ref, p0_ref, do_ref.at[0], dqkv0_ref, acc0_ref),
        ],
        wins,
        wins,
        mask_ref,
    )

    def give(at, one, two):
        keep_ref[at : at + 96, :] = one
        send_ref[at : at + 96, :] = two

    half_grads(1, None, xn_ref, da_ref, mix1_ref, dqkv1_ref, None, give)
    table = map_to_table(acc1_ref, pick_ref)
    sq = (column_sum(dqkv1_ref.at[0]), column_sum(dqkv1_ref.at[2]))
    for z, ref in ((0, keep_ref), (1, send_ref)):
        small_rows(sm_ref, z, sq, fb1_ref[2 + z : 3 + z], table, None)
        ref[C:, :] = sm_ref[...].astype(BF)


def attn_bwd_own_kernel(rows, across, *refs):
    (gh_ref, x_ref, xn_ref, gain_ref, qkvw_ref, a_ref, b_ref, info_ref) = refs[:8]
    (fb1_ref, sh_ref, da_ref, dqkv_ref, acc_ref, dqkv1_ref, pb_ref, mix_ref, pick_ref) = refs[8:17]
    (out_ref, keep_ref, send_ref) = refs[17:20]
    (gx_ref, row_ref, sm_ref) = refs[20:]
    par = info_ref[0]
    wins = (rows // WIN) * across

    def give(at, one, two):
        keep_ref[at : at + 96, :] = one
        send_ref[at : at + 96, :] = two

    half_grads(0, par, xn_ref, da_ref, mix_ref, dqkv_ref, row_ref, give)
    weights = [
        lambda j, half=half: qkv_weight_of(half, j, 0, qkvw_ref, a_ref, b_ref)
        for half in range(2)
    ]
    sg, sb, sq = normed_grads(
        0, wins, [dqkv_ref, dqkv1_ref], weights, gh_ref, x_ref, gain_ref, gx_ref
    )
    table = map_to_table(acc_ref, pick_ref)
    for z in range(2):
        small_rows(
            sm_ref.at[z], z, sq[0:2], fb1_ref[z : z + 1], table, (sg, sb, pb_ref[...], sh_ref)
        )
    keep_ref[C:, :] = sm_ref[par].astype(BF)
    send_ref[C:, :] = sm_ref[1 - par].astype(BF)
    for r in range(rows):
        parts = [gx_ref[pl.ds(tile_row(r, k, across), SEG), :][:WIN] for k in range(across)]
        out_ref[r, :, 0, :] = jnp.concatenate(parts, axis=0)


def pair_kernel(keep_ref, got_ref, own_ref, oth_ref):
    own_ref[...] = (keep_ref[0].astype(F32) + got_ref[0].astype(F32)).astype(BF)
    oth_ref[...] = (keep_ref[1].astype(F32) + got_ref[1].astype(F32)).astype(BF)


def combine_kernel(parts, bit, n_in, *refs):
    ins = refs[:n_in]
    info_ref = refs[n_in]
    outs = refs[n_in + 1 :]
    at = 0
    for rows, terms, split in parts:

        def total(first, n):
            acc = None
            for i, base in terms:
                x = ins[i][pl.ds(base + first, n), :].astype(F32)
                acc = x if acc is None else acc + x
            return acc.astype(BF)

        if bit is None or not split:
            whole = total(0, rows)
            for out in outs:
                out[at : at + rows, :] = whole
            at += rows
        else:
            n = rows // 2
            b = (info_ref[2] >> bit) & 1
            outs[0][at : at + n, :] = total(pl.multiple_of(b * n, n), n)
            outs[1][at : at + n, :] = total(pl.multiple_of((1 - b) * n, n), n)
            at += n


def close_kernel(halves, bit, mine_ref, got_ref, info_ref, out_ref, small_ref):
    join_kernel(halves, bit, mine_ref.at[0 : sum(halves)], got_ref, info_ref, out_ref)
    at = sum(halves)
    rest = (mine_ref[at:, :].astype(F32) + got_ref[at:, :].astype(F32)).astype(BF)
    n = rest.shape[0] - SMALL
    out_ref[2 * at :, :] = rest[:n]
    small_ref[...] = rest[n:]


def join_kernel(halves, bit, mine_ref, got_ref, info_ref, out_ref):
    b = (info_ref[2] >> bit) & 1
    at = 0
    for n in halves:
        for ref, place in ((mine_ref, b), (got_ref, 1 - b)):
            to = pl.multiple_of(2 * at + place * n, 16)
            out_ref[pl.ds(to, n), :] = ref[at : at + n, :]
        at += n
    if at < mine_ref.shape[0]:
        out_ref[2 * at :, :] = mine_ref[at:, :]


def out_kernel(rows, across, in_ref, halo_ref, o_ref, st_ref):
    st_ref[...] = in_ref[...].astype(F32)
    halo = halo_ref[C + SMALL :, :].astype(F32)
    for r in range(rows):
        parts = []
        for k in range(across):
            if r >= SHIFT:
                t = st_ref[pl.ds(tile_row(r - SHIFT, k, across), SEG), :]
            else:
                t = edge_tile(halo, k, r)
            parts.append(t[:WIN])
        last = parts[-1]
        parts = [last[WIN - SHIFT :]] + parts[:-1] + [last[: WIN - SHIFT]]
        o_ref[r] = jnp.concatenate(parts, axis=0).astype(BF)


def place_of(i, info_ref):
    return info_ref[0] ^ (i // 2), ((info_ref[2] >> 1) & 1) ^ (i % 2)


def put_up(pieces, base, info_ref, ref):
    n = C // 2
    for i in range(4):
        core, half = place_of(i, info_ref)
        rows = pl.ds(pl.multiple_of(half * n, n), n)
        cols = pl.ds(pl.multiple_of(core * C, C), C)
        ref[rows, cols] = pieces[i][base : base + n, :].astype(F32)


def put_down(pieces, base, info_ref, ref):
    n = C // 2
    for i in range(4):
        core, half = place_of(i, info_ref)
        rows = pl.ds(pl.multiple_of(core * C + half * n, n), n)
        ref[rows, :] = pieces[i][base : base + n, :].astype(F32)


def put_attn(pieces, base, info_ref, asm_ref, qkv_ref, proj_ref):
    n = C // 2
    for i in range(4):
        core, half = place_of(i, info_ref)
        rows = pl.ds(pl.multiple_of(half * n, n), n)
        asm_ref[core, rows, :] = pieces[i][base : base + n, :].astype(F32)
    for core in range(2):
        to = pl.ds(96 * core, 96)
        for j in range(3):
            qkv_ref[j, to, :] = asm_ref[core, 96 * j : 96 * (j + 1), :]
        proj_ref[to, :] = asm_ref[core, 288:384, :]


def final_second_kernel(*refs):
    pieces = refs[:4]
    (info_ref, f1_ref, f2_ref, qkv_ref, proj_ref) = refs[4:9]
    (up_ref, down_ref, asm_ref, q_ref, p_ref, sems) = refs[9:]
    put_up(pieces, 0, info_ref, up_ref)
    put_down(pieces, C // 2, info_ref, down_ref)
    put_attn(pieces, C, info_ref, asm_ref, q_ref, p_ref)
    outs = [f1_ref, f2_ref, qkv_ref, proj_ref]
    for copy in copies_of([(x, y.at[1]) for x, y in zip((up_ref, down_ref, q_ref, p_ref), outs)], sems):
        copy.wait()


def final_kernel(*refs):
    mlps, attns, smalls = refs[:4], refs[4:8], refs[8:10]
    (shared_ref, info_ref) = refs[10:12]
    (f1_ref, f2_ref, qkv_ref, proj_ref) = refs[16:20]
    (gain_ref, bias_ref, pb_ref, fb2_ref, qvb_ref, fb1_ref, tab_ref) = refs[20:27]
    (up_ref, down_ref, asm_ref, q_ref, p_ref, sm_ref, sems) = refs[27:]
    put_up(mlps, 0, info_ref, up_ref)
    copies = copies_of([(up_ref, f1_ref.at[0])], sems)
    put_down(mlps, C // 2, info_ref, down_ref)
    copies += copies_of([(down_ref, f2_ref.at[0])], sems.at[1:2])
    put_attn(attns, 0, info_ref, asm_ref, q_ref, p_ref)
    copies += copies_of([(q_ref, qkv_ref.at[0]), (p_ref, proj_ref.at[0])], sems.at[2:4])
    n = C // 2
    par = info_ref[0]
    for layer in range(2):
        for i in range(2):
            x = smalls[i][...] if layer == 1 else attns[2 * i][n:, :]
            sm_ref[par ^ i] = x.astype(F32)
        x, y = sm_ref[0], sm_ref[1]
        shared = x[0:6]
        if layer == 0:
            shared = sm_ref[par, 0:6, :] + shared_ref[0:6].astype(F32)
        gain_ref[layer, 0:1] = shared[0:1]
        gain_ref[layer, 1:2] = shared[3:4]
        bias_ref[layer, 0:1] = shared[1:2]
        bias_ref[layer, 1:2] = shared[4:5]
        pb_ref[layer : layer + 1] = shared[2:3]
        fb2_ref[layer : layer + 1] = shared[5:6]
        fb1_ref[layer : layer + 1, 0:C] = x[6:7]
        fb1_ref[layer : layer + 1, C:] = y[6:7]
        for k in range(2):
            qvb_ref[layer, k : k + 1, 0:96] = x[7:8, 128 * k : 128 * k + 96]
            qvb_ref[layer, k : k + 1, 96:192] = y[7:8, 128 * k : 128 * k + 96]
        t = jnp.concatenate(
            [
                jnp.concatenate(
                    [v[8 + r : 9 + r, 48 * k : 48 * (k + 1)] for r in range(2) for k in range(8)],
                    axis=0,
                )
                for v in (x, y)
            ],
            axis=1,
        )
        wide = tn(t.astype(BF), offset_rows().astype(BF)) * offset_cols()
        for h in range(6):
            tab_ref[h, layer : layer + 1, :] = jnp.sum(
                wide[16 * h : 16 * (h + 1)], 0, keepdims=True
            )
    for copy in copies:
        copy.wait()


VMEM = pl.BlockSpec(memory_space=pltpu.VMEM)
HBM = pl.BlockSpec(memory_space=pltpu.HBM)


class Position:
    def __getitem__(self, k):
        if k == 1:
            return lax.axis_index("tp")
        win = lax.axis_index("win")
        return win if k == 2 else lax.rem(win, 2)


POSITION = Position()


def call(kernel, name, us, limit, operands, outs, scratch=(), aliases=None):
    args = []
    specs = []
    at = [n for n, op in enumerate(operands) if op is POSITION]
    if at:
        (at,) = at
        inner = kernel

        def kernel(*refs):
            return inner(*refs[:at], POSITION, *refs[at:])

        operands = operands[:at] + operands[at + 1 :]
        aliases = {k - (k > at): v for k, v in (aliases or {}).items()}
    for op in operands:
        args.append(op[0] if isinstance(op, tuple) else op)
        specs.append(op[1] if isinstance(op, tuple) else VMEM)
    shapes = [jax.ShapeDtypeStruct(o[0], o[1]) for o in outs]
    return pl.pallas_call(
        kernel,
        name=name,
        in_specs=specs,
        out_specs=[o[2] if len(o) > 2 else VMEM for o in outs],
        input_output_aliases=aliases or {},
        out_shape=shapes,
        scratch_shapes=[s if not isinstance(s, tuple) else pltpu.VMEM(*s) for s in scratch],
        cost_estimate=pl.CostEstimate(
            flops=int(us * 7e9), bytes_accessed=1000000, transcendentals=0
        ),
        compiler_params=pltpu.CompilerParams(vmem_limit_bytes=limit * 2**20),
    )(*args)


def on_device(n_win, *args):
    (
        tokens,
        crop_ids,
        cotangent,
        norm_gain,
        norm_bias,
        qkv_weight,
        qv_bias,
        proj_weight,
        proj_bias,
        fc1_weight,
        fc1_bias,
        fc2_weight,
        fc2_bias,
        pos_table,
    ) = args
    rows, cols = tokens.shape[1:3]
    across = cols // WIN
    wins = (rows // WIN) * across
    ntok = wins * WROWS
    npad = wins * WPAD
    win = lax.axis_index("win")
    tp = lax.axis_index("tp")
    par = win % 2
    info = POSITION
    bits = n_win.bit_length() - 1
    assert n_win == 1 << bits and bits >= 3

    def to_tp(x, name):
        with jax.named_scope(name + "_tp"):
            return lax.ppermute(x, "tp", [(0, 1), (1, 0)])

    def to_win(x, bit, name):
        if bit >= bits:
            return jnp.zeros_like(x)
        with jax.named_scope("%s_win%d" % (name, bit)):
            return lax.ppermute(x, "win", [(i, i ^ (1 << bit)) for i in range(n_win)])

    def after(x, *others):
        return lax.optimization_barrier((x,) + others)[0]

    def combine(parts, bit, ins, name):
        total = sum(rows // 2 if split and bit is not None else rows for rows, _, split in parts)
        outs = [((total, C), BF)] * (1 if bit is None else 2)
        return call(
            partial(combine_kernel, parts, bit, len(ins)), name, 1, 4, tuple(ins) + (info,), outs
        )

    def join(halves, bit, mine, got, name):
        return call(
            partial(join_kernel, halves, bit), name, 1, 4, (mine, got, info),
            [((mine.shape[0] + sum(halves), C), BF)],
        )[0]

    qkv_t = qkv_weight.transpose(0, 2, 3, 1)
    table = pos_table.transpose(2, 0, 1)
    na = C + SMALL
    n = C // 2
    edge_b = ((across * SHIFT * SEG, C), BF)
    a0q, small = call(
        pack_first_kernel,
        "pack_first",
        0.1,
        60,
        tuple((x, HBM) for x in (qkv_t, proj_weight, table, qv_bias, fc1_bias)),
        [((C + 2 * SENT_ROWS, C), BF), ((2, SMALL_ROWS, C), F32)],
        [
            (table.shape, F32),
            (qv_bias.shape, F32),
            (fc1_bias.shape, F32),
            pltpu.SemaphoreType.DMA((7,)),
        ],
    )
    a0 = to_tp(a0q, "a0")
    m0q, a1q, m1q, cot_edge = call(
        pack_kernel,
        "pack",
        0.1,
        60,
        tuple((x, HBM) for x in (qkv_t, proj_weight, fc1_weight, fc2_weight, cotangent[0]))
        + (after(small, a0q), info),
        [
            ((2 * C, C), BF),
            ((C + 2 * SENT_ROWS, C), BF),
            ((2 * C, C), BF),
            ((EDGE_ROWS, C), BF),
        ],
        [((SHIFT, cols, C), BF), pltpu.SemaphoreType.DMA((9,))],
    )
    m0 = to_tp(m0q, "m0")
    crops = crop_ids.transpose(2, 0, 1)
    label_outs = [((wins, 128), F32), ((wins, WPAD, 128), F32), ((3, WPAD, 128), F32)]
    lq0, lk0, pos0, pick = call(
        partial(prep_kernel, 0, rows, across),
        "prep_0",
        0.1,
        8,
        (crops, after(small, m0q), info),
        label_outs + [((WIN, 96, 6 * WPAD), BF)],
        [((128, 128), F32)],
    )
    tiles = (rows // WIN, across, WIN, SEG, C)
    mask = ((6 * WPAD, 6 * HD), BF)
    half_outs = [((3, npad, 192), BF), ((wins, WPAD, 6 * WPAD), BF), ((npad, 192), BF)]
    tok_f = ((ntok, C), F32)
    tok_b = ((ntok, C), BF)
    hid_b = ((4, ntok, C), BF)
    other_scratch = [mask, ((3, WPAD, 128), F32)]

    x0, xn0, part, qkv00, p00, mix00 = call(
        partial(attn_own_kernel, rows, across),
        "attn_own_0",
        0.1,
        8,
        (tokens[0], norm_gain, norm_bias, proj_bias, qv_bias, qkv_t, proj_weight, pos0, lq0, lk0),
        [tok_b, ((npad, C), BF), tok_f] + half_outs,
        [mask, tok_f],
    )
    lq1, lk1, pos1 = call(
        partial(prep_kernel, 1, rows, across),
        "prep_1",
        0.1,
        8,
        (crops, after(small, part), info, pick),
        label_outs,
        [((128, 128), F32)],
    )
    a1 = to_tp(after(a1q, lq1), "a1")
    a0 = after(a0, lq1)
    a0s = to_win(a0, 0, "a0")
    hid0, qkv01, p01, mix01, small0 = call(
        partial(attn_other_kernel, rows, across),
        "attn_other_0",
        0.1,
        8,
        (part, xn0, a0, a0s, lq0, lk0, pick, info),
        [tok_f] + half_outs + [((SMALL_ROWS, C), F32)],
        other_scratch,
    )
    half_b = ((2, ntok, C), BF)
    st_own, n2f, act00, gp00 = call(
        mlp_own_kernel,
        "mlp_own_0",
        0.1,
        10,
        (hid0, norm_gain, norm_bias, fc1_bias, fc2_bias, fc1_weight, fc2_weight),
        [tok_f, tok_b, half_b, half_b],
    )
    m0 = after(m0, st_own)
    m0s = to_win(m0, 0, "m0")
    st0, act01, gp01, edge = call(
        partial(mlp_other_kernel, across),
        "mlp_other_0",
        3,
        10,
        (st_own, n2f, fc1_bias, small0, m0, m0s, info),
        [tok_f, half_b, half_b, edge_b],
    )
    halo = to_tp(edge, "edge0")
    a1 = after(a1, halo)
    a1s = to_win(a1, 0, "a1")
    cot_edge = to_tp(after(cot_edge, edge), "cot")
    m1 = to_tp(after(m1q, edge), "m1")
    x1, xn1, qkv10 = call(
        partial(norm_kernel, rows, across),
        "norm_1",
        2,
        6,
        (st0, halo, norm_gain, norm_bias, qv_bias, qkv_t),
        [tok_f, ((npad, C), BF), half_outs[0]],
    )
    mix_out = half_outs[2] + (HBM,)
    hid1, p10, mix10, qkv11, p11, mix11, small1 = call(
        partial(attn_both_kernel, rows, across),
        "attn_fwd_1",
        10,
        12,
        (xn1, qkv10, pos1, a1, a1s, x1, proj_weight, proj_bias, lq1, lk1, pick, info),
        [tok_f, half_outs[1], mix_out] + half_outs[:2] + [mix_out, ((SMALL_ROWS, C), F32)],
        other_scratch + [half_outs[2], half_outs[2], pltpu.SemaphoreType.DMA((2,))],
    )
    sums = [((4, C), F32), ((3, C), F32)]
    g1, df1, n21, st_own, dz_own, du10, act10, sum10, sf1 = call(
        partial(mlp_own_both_kernel, rows, across),
        "mlp_own_1",
        5,
        11,
        (cotangent[0], after(cot_edge, a1s), hid1, norm_gain, norm_bias, fc1_bias, fc2_bias)
        + (fc1_weight, fc2_weight),
        [tok_f, tok_b, tok_b, tok_f, tok_f, half_b, half_b, ((2, C), F32), ((1, C), F32)],
    )
    m1 = after(m1, dz_own)
    m1s = to_win(m1, 0, "m1")
    whole_q = ((2 * C, C), BF)
    keep_mo, send_mo = call(
        own_grads_kernel, "own_grads_1", 2, 4, (after(n21, m1), df1, du10, act10, info),
        [whole_q, whole_q],
    )
    mo_core = to_win(send_mo, 0, "gmo")
    st1, gh1, du11, act11, send_mx, gfb1, gsh1, out_edge = call(
        partial(mlp_other_both_kernel, rows, across),
        "mlp_other_1",
        6,
        12,
        (after(hid1, keep_mo), g1, df1, n21, st_own, dz_own, norm_gain, fc1_bias, small1, m1, m1s)
        + (info, sum10, sf1),
        [tok_b, tok_f, half_b, half_b, whole_q] + sums + [edge_b],
        [tok_f],
        aliases={1: 1},
    )

    def plus(x, y, name):
        return combine([(x.shape[0], [(0, 0), (1, 0)], True)], None, (x, y), name)[0]

    def pair(keep, got, name):
        shape = keep.shape[1:]
        return call(pair_kernel, name, 1, 4, (keep, got), [(shape, BF), (shape, BF)])

    mx_core = to_win(send_mx, 0, "gmx")
    (keep_mx,) = call(mlp_keep_kernel, "mlp_keep_1", 1, 4, (n21, df1, du11, act11), [whole_q])
    m1_oth = plus(keep_mx, after(mx_core, keep_mx), "m1_oth")
    m1_own = plus(keep_mo, after(mo_core, m1_oth), "m1_own")
    m1_t = to_tp(m1_oth, "gm1")
    da1, do1, pb1 = call(
        partial(mixed_grad_kernel, wins),
        "mixed_grad_1",
        0.1,
        4,
        (after(gh1, m1_own), proj_weight, a1, a1s),
        [((npad, C), BF), ((2, npad, 192), BF), ((1, C), F32)],
    )
    gin1, keep_a1, send_a1, edge = call(
        partial(attn_bwd_kernel, rows, across),
        "attn_bwd_1",
        14,
        8,
        (gh1, x1, xn1, norm_gain, qkv_t, a1, a1s, info)
        + (gfb1, gsh1, qkv10, p10, mix10, qkv11, p11, mix11, pick, da1, do1, pb1),
        [tok_f, ((2, na, C), BF), ((2, na, C), BF), edge_b],
        [
            ((3, npad, 192), BF),
            ((3, npad, 192), BF),
            ((2, 3, WPAD, 128), F32),
            mask,
            ((192, C), F32),
            ((4, SMALL, C), F32),
        ],
    )
    halo = to_tp(edge, "edge1")
    a1_core = to_win(after(send_a1, edge), 0, "ga1")
    m1_mine, m1_away = combine(
        [(C, [(0, 0), (1, 0)], True), (C, [(0, C), (1, C)], True)],
        1,
        (m1_own, after(m1_t, edge)),
        "m1_y",
    )
    m1_y = to_win(m1_away, 1, "gm1")
    a1_own, a1_oth = pair(keep_a1, after(a1_core, m1_away), "pair_a1")
    a1_t = to_tp(a1_oth, "ga1")
    g0, df0, keep_f2, send_f2 = call(
        partial(down_grad_kernel, rows, across),
        "down_grad_0",
        4,
        5,
        (gin1, after(halo, a1_oth), act00, act01, info),
        [tok_f, tok_b, ((2, C, C), BF), ((2, C, C), BF)],
    )
    f2_core = to_win(send_f2, 0, "gf2")
    quarter_b = ((C, C), BF)
    dz0, sum00, keep_fo, send_fo = call(
        mlp_bwd_own_kernel,
        "mlp_bwd_own_0",
        2,
        8,
        (df0, gp00, n2f, fc1_weight, fc2_weight, info),
        [tok_f, ((2, C), F32), quarter_b, quarter_b],
        [half_b],
    )
    fo_core = to_win(send_fo, 0, "gfo")
    m1_mine, m1_away = combine(
        [(n, [(0, 0), (1, 0)], True), (n, [(0, n), (1, n)], True)],
        2,
        (m1_mine, after(m1_y, dz0)),
        "m1_z",
    )
    m1_z = to_win(m1_away, 2, "gm1")
    f2_own, f2_oth = pair(keep_f2, after(f2_core, m1_away), "pair_f2")
    f2_t = to_tp(f2_oth, "gf2")
    a1_mine, a1_away = combine(
        [(C, [(0, 0), (1, 0)], True), (SMALL, [(0, C), (1, C)], False)],
        1,
        (a1_own, after(a1_t, f2_oth)),
        "a1_y",
    )
    a1_y = to_win(a1_away, 1, "ga1")
    gh0, du01, send_fx, gfb0, gsh0 = call(
        mlp_bwd_other_kernel,
        "mlp_bwd_other_0",
        3,
        8,
        (after(g0, a1_away), df0, hid0, n2f, gp01, dz0, norm_gain, m0, m0s, sum00),
        [tok_f, half_b, quarter_b] + sums,
    )
    m1 = plus(m1_mine, after(m1_z, send_fx), "m1_z2")
    m1_b = to_win(m1, 3, "gm1")
    fx_core = to_win(send_fx, 0, "gfx")
    (keep_fx,) = call(up_keep_kernel, "up_keep_0", 1, 4, (n2f, du01), [quarter_b])
    f1_oth = plus(keep_fx, after(fx_core, keep_fx), "f1_oth")
    f1_t = to_tp(f1_oth, "gf1")
    f1_own = plus(keep_fo, after(fo_core, f1_oth), "f1_own")
    a1 = plus(a1_mine, after(a1_y, f1_own), "a1_z2")
    a1_b = to_win(a1, 3, "ga1")
    da, dqkv0, acc0, dqkv1, pb0, keep_o0, send_o0 = call(
        partial(attn_bwd_heads_kernel, rows, across),
        "attn_bwd_heads_0",
        8,
        8,
        (after(gh0, a1, f2_t), xn0, proj_weight, a0, a0s, gfb0)
        + (qkv00, p00, qkv01, p01, mix01, pick),
        [
            ((npad, C), BF),
            ((3, npad, 192), BF),
            ((3, WPAD, 128), F32),
            ((3, npad, 192), BF),
            ((1, C), F32),
            ((na, C), BF),
            ((na, C), BF),
        ],
        [((2, npad, 192), BF), mask, ((3, WPAD, 128), F32), ((SMALL, C), F32)],
    )
    o0_core = to_win(send_o0, 0, "go0")
    m0_mine, m0_away = combine(
        [(C, [(0, 0), (1, 0)], True), (C, [(2, 0), (3, 0)], True)],
        1,
        (f1_own, after(f1_t, send_o0), f2_own, f2_t),
        "m0_y",
    )
    m0_y = to_win(m0_away, 1, "gm0")
    (o0_sum,) = combine(
        [(na, [(0, 0), (1, 0)], True), (edge_b[0][0], [(2, 0)], True)],
        None,
        (keep_o0, after(o0_core, m0_away), out_edge),
        "o0",
    )
    o0_t = to_tp(o0_sum, "go0")
    (c1,) = combine(
        [(n, [(0, 0), (1, 0)], True), (n + SMALL, [(2, 0), (3, 0)], True)],
        None,
        (m1, after(m1_b, o0_sum), a1, after(a1_b, o0_sum)),
        "c1",
    )
    for bit in range(4, bits):
        c1 = plus(c1, to_win(c1, bit, "gc1"), "c1_sum")
    c1_b = to_win(c1, 2, "gc1")
    grad_tokens, keep_a0, send_a0 = call(
        partial(attn_bwd_own_kernel, rows, across),
        "attn_bwd_own_0",
        9,
        7,
        (gh0, x0, xn0, norm_gain, qkv_t, a0, a0s, info)
        + (gfb0, gsh0, da, dqkv0, acc0, dqkv1, pb0, after(mix00, c1), pick),
        [((rows, cols, 1, C), F32), ((na, C), BF), ((na, C), BF)],
        [tok_f, ((192, C), F32), ((2, SMALL, C), F32)],
    )

    a0_core = to_win(send_a0, 0, "ga0")
    m0_mine, m0_away = combine(
        [(n, [(0, 0), (1, 0)], True), (n, [(0, n), (1, n)], True)],
        2,
        (m0_mine, after(m0_y, send_a0)),
        "m0_z",
    )
    m0_z = to_win(m0_away, 2, "gm0")
    a0_mine, a0_away = combine(
        [(C, [(0, 0), (1, 0), (2, 0)], True), (SMALL, [(0, C), (1, C), (2, C)], False)],
        1,
        (keep_a0, after(a0_core, m0_away), o0_t),
        "a0_y",
    )
    a0_y = to_win(a0_away, 1, "ga0")
    c1, c1_small = call(
        partial(close_kernel, [n // 2] * 2, 2), "c1_close", 1, 8, (c1, after(c1_b, a0_away), info),
        [((3 * n, C), BF), ((SMALL, C), BF)],
    )
    c1_back = to_win(c1, 1, "gc1_back")
    c1_sib = to_win(c1, 0, "gc1_mine")
    c1_small_sib = to_win(c1_small, 0, "gc1_small")
    m0 = plus(m0_mine, after(m0_z, c1), "m0_z2")
    m0_b = to_win(m0, 3, "gm0")
    a0 = plus(a0_mine, after(a0_y, m0), "a0_z")
    a0_z = to_win(a0, 2, "ga0")
    (layer_out,) = call(
        partial(out_kernel, rows, across), "layer_out", 1, 8, (after(st1, a0), o0_t),
        [((rows, cols, C), BF)],
        [tok_f],
    )
    m0 = plus(m0, after(m0_b, layer_out), "m0_sum")
    for bit in range(4, bits):
        m0 = plus(m0, to_win(m0, bit, "gm0"), "m0_sum")
    m0_b = to_win(m0, 2, "gm0_back")
    a0 = plus(a0, after(a0_z, m0), "a0_z2")
    a0_b = to_win(a0, 3, "ga0")
    c1_back = after(c1_back, a0)
    c1_pieces = (c1, c1_back, c1_sib, to_win(c1_back, 0, "gc1_theirs"))
    m0 = join([n // 2] * 2, 2, m0, after(m0_b, c1_back), "m0_join")
    m0_back = to_win(m0, 1, "gm0_back")
    m0_sib = to_win(m0, 0, "gm0_mine")
    c1_small_sib, c1_pieces = after((c1_small_sib, c1_pieces), m0)
    f1_shape, f2_shape = (2, C, 2 * C), (2, 2 * C, C)
    qkv_shape, proj_shape = (2, 3, 192, C), (2, 192, C)
    whole = [(f1_shape, F32, HBM), (f2_shape, F32, HBM), (qkv_shape, F32, HBM), (proj_shape, F32, HBM)]
    parts = [(x[0][1:], F32) for x in whole]
    attn_parts = [((2, C, C), F32)] + parts[2:]
    g_f1, g_f2, g_qkv, g_proj = call(
        final_second_kernel, "final_second", 1, 9, c1_pieces + (info,), whole,
        parts[:2] + attn_parts + [pltpu.SemaphoreType.DMA((4,))],
    )
    a0 = plus(a0, after(a0_b, g_f1), "a0_sum")
    for bit in range(4, bits):
        a0 = plus(a0, to_win(a0, bit, "ga0"), "a0_sum")
    a0_back = to_win(a0, 1, "ga0_back")
    a0_sib = to_win(a0, 0, "ga0_mine")
    shared = to_tp(a0[n : n + 16], "shared")
    m0_back = after(m0_back, a0_sib, shared)
    m0_pieces = (m0, m0_back, m0_sib, to_win(m0_back, 0, "gm0_theirs"))
    outs = call(
        final_kernel,
        "final",
        0.1,
        9,
        m0_pieces
        + (a0, a0_back, a0_sib, to_win(a0_back, 0, "ga0_theirs"), c1_small, c1_small_sib)
        + (shared, info, (g_f1, HBM), (g_f2, HBM), (g_qkv, HBM), (g_proj, HBM)),
        whole
        + [
            ((2, 2, C), F32),
            ((2, 2, C), F32),
            ((2, C), F32),
            ((2, C), F32),
            ((2, 2, 192), F32),
            ((2, 2 * C), F32),
            ((6, 2, 169), F32),
        ],
        parts[:2] + attn_parts + [((2, SMALL, C), F32), pltpu.SemaphoreType.DMA((4,))],
        aliases={12: 0, 13: 1, 14: 2, 15: 3},
    )
    (g_f1, g_f2, g_qkv, g_proj, g_gain, g_bias, g_pb, g_fb2, g_qvb, g_fb1, g_tab) = outs
    return (
        layer_out[None],
        grad_tokens.transpose(2, 0, 1, 3),
        g_gain,
        g_bias,
        g_qkv.transpose(0, 3, 1, 2),
        g_qvb,
        g_proj,
        g_pb,
        g_f1,
        g_fb1,
        g_f2,
        g_fb2,
        g_tab.transpose(1, 2, 0),
    )


def solution(mesh):
    return jax.shard_map(
        partial(on_device, mesh.shape["win"]),
        mesh=mesh,
        in_specs=(
            P("win", "tp", None, None),
            P("win", None, None),
            P("win", "tp", None, None),
            P(),
            P(),
            P(None, None, None, "tp"),
            P(None, None, "tp"),
            P(None, "tp", None),
            P(),
            P(None, None, "tp"),
            P(None, "tp"),
            P(None, "tp", None),
            P(),
            P(None, None, "tp"),
        ),
        out_specs=(
            P("win", "tp", None, None),
            P("win", "tp", None, None),
            P(),
            P(),
            P(None, None, None, "tp"),
            P(None, None, "tp"),
            P(None, "tp", None),
            P(),
            P(None, None, "tp"),
            P(None, "tp"),
            P(None, "tp", None),
            P(),
            P(None, None, "tp"),
        ),
        check_vma=False,
    )
```

```python
from functools import partial

import jax
import jax.numpy as jnp
import numpy as np
from jax import lax
from jax.experimental import pallas as pl
from jax.experimental.pallas import tpu as pltpu
from jax.sharding import PartitionSpec as P

C = 384
WIN = 7
SHIFT = 3
HD = 32
EPS = 1e-05
NEG = -1000000000.0
SCALE = HD**-0.5
F32 = jnp.float32
BF = jnp.bfloat16
SEG = 8
WROWS = WIN * SEG
WPAD = 64


def nn(a, b):
    return lax.dot_general(a, b, (((1,), (0,)), ((), ())), preferred_element_type=F32)


def nt(a, b):
    return lax.dot_general(a, b, (((1,), (1,)), ((), ())), preferred_element_type=F32)


def tn(a, b):
    return lax.dot_general(a, b, (((0,), (0,)), ((), ())), preferred_element_type=F32)


def norm_stats(x):
    mean = jnp.mean(x, -1, keepdims=True)
    cent = x - mean
    var = jnp.mean(cent * cent, -1, keepdims=True)
    rinv = lax.rsqrt(var + EPS)
    return cent * rinv, rinv


def norm_back(dz, xhat, rinv, gain):
    d = dz * gain
    return rinv * (
        d - jnp.mean(d, -1, keepdims=True) - xhat * jnp.mean(d * xhat, -1, keepdims=True)
    )


def tile_row(r, k, across):
    return (((r // WIN) * across + k) * WIN + r % WIN) * SEG


def zero_rows(n):
    return jnp.zeros((n, C), F32)


def head_mask():
    row = lax.broadcasted_iota(jnp.int32, (6 * WPAD, 6 * HD), 0) // WPAD
    col = lax.broadcasted_iota(jnp.int32, (6 * WPAD, 6 * HD), 1) // HD
    return (row == col).astype(BF)


def spread(x, mask):
    return jnp.concatenate([x] * 6, axis=0) * mask


def fold(o):
    lane = lax.broadcasted_iota(jnp.int32, (WPAD, 128), 1)

    def of(h, a, b):
        return o[WPAD * h : WPAD * (h + 1), a:b]

    one = jnp.where(lane < 96, of(2, 0, 128), of(3, 0, 128))
    one = jnp.where(lane < 64, of(1, 0, 128), one)
    one = jnp.where(lane < 32, of(0, 0, 128), one)
    two = jnp.where(lane[:, :64] < 32, of(4, 128, 192), of(5, 128, 192))
    return jnp.concatenate([one, two], axis=1)


def rows_at(i, n):
    return pl.ds(i * n, n)


def repeat(n, body, carry):
    for i in range(n):
        carry = body(i, carry)
    return carry


def iota(shape, dim):
    return lax.broadcasted_iota(jnp.int32, shape, dim)


def exact(a, b, ca, cb):
    return lax.dot_general(
        a,
        b,
        (((ca,), (cb,)), ((), ())),
        precision=lax.Precision.HIGHEST,
        preferred_element_type=F32,
    )


def offset_rows():
    return (12 - iota((16, 169), 0) == iota((16, 169), 1) // 13).astype(F32)


def offset_cols():
    return (iota((96, 169), 0) % 16 == iota((96, 169), 1) % 13).astype(F32)


def column_pick(kx):
    r = iota((96, 6 * WPAD), 0)
    c = iota((96, 6 * WPAD), 1)
    qx = c % 8
    return ((r // 16 == c // WPAD) & (r % 16 == qx - kx + WIN - 1) & (qx < WIN)).astype(BF)


def table_to_map(t, pick_ref, pos_ref):
    pos_ref[...] = jnp.zeros_like(pos_ref)
    group = (iota((8, 6 * WPAD), 1) % WPAD) // 8
    high = t.astype(BF)
    low = (t - high.astype(F32)).astype(BF)
    both = jnp.concatenate([high, low], axis=0)
    for kx in range(WIN):
        h = nn(both, pick_ref[kx])
        h = h[:16] + h[16:]
        g = jnp.zeros((8, 6 * WPAD), F32)
        for j in range(WIN):
            g = jnp.where(group == j, h[6 - j : 14 - j], g)
        for i in range(3):
            pos_ref[i, pl.ds(kx, 8, stride=8), :] = g[:, 128 * i : 128 * (i + 1)]


def map_to_table(pos_ref, pick_ref):
    group = (iota((16, 6 * WPAD), 1) % WPAD) // 8
    total = jnp.zeros((16, 96), F32)
    for kx in range(WIN):
        r = jnp.concatenate([pos_ref[i, pl.ds(kx, 8, stride=8), :] for i in range(3)], axis=1)
        h = jnp.zeros((16, 6 * WPAD), F32)
        for j in range(WIN):
            parts = [r, jnp.zeros((2 + j, 6 * WPAD), F32)]
            if j < 6:
                parts = [jnp.zeros((6 - j, 6 * WPAD), F32)] + parts
            h = jnp.where(group == j, jnp.concatenate(parts, axis=0), h)
        total = total + nt(h.astype(BF), pick_ref[kx])
    return total


def shift_in(tile, x_ref, rows, across):
    for r in range(rows):
        for k in range(across):
            a = tile(r + SHIFT, k)
            b = tile(r + SHIFT, (k + 1) % across)
            x_ref[pl.ds(tile_row(r, k, across), SEG), :] = jnp.concatenate(
                [a[SHIFT:WIN], b[:SHIFT], zero_rows(1)], axis=0
            )


def shift_out(tile, x_ref, rows, across):
    for r in range(rows):
        for k in range(across):
            a = tile(r - SHIFT, (k - 1) % across)
            b = tile(r - SHIFT, k)
            x_ref[pl.ds(tile_row(r, k, across), SEG), :] = jnp.concatenate(
                [a[WIN - SHIFT : WIN], b[: WIN - SHIFT], zero_rows(1)], axis=0
            )

EDGE_ROWS = 96
SMALL = 16


SMALL_ROWS = 24
SENT_ROWS = 8


def copies_of(pairs, sems):
    copies = [pltpu.make_async_copy(x, y, sems.at[n]) for n, (x, y) in enumerate(pairs)]
    for copy in copies:
        copy.start()
    return copies


def attn_copies(layer, par, qkvw_ref, projw_ref, a_ref):
    of_heads = pl.ds(pl.multiple_of(par * 96, 96), 96)
    pairs = [
        (qkvw_ref.at[layer, j, of_heads, :], a_ref.at[pl.ds(96 * j, 96), :]) for j in range(3)
    ]
    return pairs + [(projw_ref.at[layer, of_heads, :], a_ref.at[pl.ds(288, 96), :])]


def mlp_copies(layer, par, f1_ref, f2_ref, m_ref):
    of_units = pl.ds(pl.multiple_of(par * C, C), C)
    return [
        (f1_ref.at[layer, :, of_units], m_ref.at[pl.ds(0, C), :]),
        (f2_ref.at[layer, of_units, :], m_ref.at[pl.ds(C, C), :]),
    ]


def high_low(x):
    rows = []
    for r in range(4):
        rows.append(jnp.concatenate([x[4 * r + k : 4 * r + k + 1, 0:96] for k in range(4)], axis=1))
    rows.append(x[16:18])
    rows.append(jnp.concatenate([x[18:19, 0:192], x[19:20, 0:192]], axis=1))
    rows.append(zero_rows(1))
    x = jnp.concatenate(rows, axis=0)
    high = x.astype(BF).astype(F32)
    return jnp.concatenate([high, x - high], axis=0).astype(BF)


def pack_first_kernel(
    qkvw_ref, projw_ref, tab_ref, qvb_ref, fb1_ref,
    a0_ref, small_ref, tab_v, qvb_v, fb1_v, sems
):
    pairs = [(tab_ref, tab_v), (qvb_ref, qvb_v), (fb1_ref, fb1_v)]
    copies = copies_of(pairs + attn_copies(0, POSITION[0], qkvw_ref, projw_ref, a0_ref), sems)
    small_ref[...] = jnp.zeros_like(small_ref)
    for copy in copies[:3]:
        copy.wait()
    for layer in range(2):
        tab = tab_v[:, layer, :]
        wide = jnp.concatenate([jnp.broadcast_to(tab[h : h + 1], (16, 169)) for h in range(6)])
        small_ref[layer, 0:16, 0:96] = exact(offset_rows(), wide * offset_cols(), 1, 1)
        small_ref[layer, 16:17, :] = fb1_v[layer : layer + 1, 0:C]
        small_ref[layer, 17:18, :] = fb1_v[layer : layer + 1, C:]
        small_ref[layer, 18:20, 0:192] = qvb_v[layer]
    a0_ref[C:, :] = high_low(small_ref[0])
    for copy in copies[3:]:
        copy.wait()


def pack_kernel(
    qkvw_ref, projw_ref, f1_ref, f2_ref, cot_ref, small_ref, info_ref,
    m0_ref, a1_ref, m1_ref, edge_ref, cot_v, sems
):
    par = info_ref[0]
    pairs = [(cot_ref.at[pl.ds(0, SHIFT)], cot_v)]
    pairs += mlp_copies(0, par, f1_ref, f2_ref, m0_ref)
    pairs += attn_copies(1, par, qkvw_ref, projw_ref, a1_ref)
    pairs += mlp_copies(1, par, f1_ref, f2_ref, m1_ref)
    copies = copies_of(pairs, sems)
    a1_ref[C:, :] = high_low(small_ref[1])
    copies[0].wait()
    edge = [cot_v[r].astype(F32) for r in range(SHIFT)]
    n = EDGE_ROWS - SHIFT * cot_v.shape[1]
    edge_ref[...] = jnp.concatenate(edge + [zero_rows(n)], axis=0).astype(BF)
    for copy in copies[1:]:
        copy.wait()


def small_of(a_ref, small_ref):
    rows = a_ref[C : C + 2 * SENT_ROWS, :].astype(F32)
    x = rows[0:SENT_ROWS] + rows[SENT_ROWS:]
    small_ref[...] = jnp.zeros_like(small_ref)
    for r in range(4):
        for k in range(4):
            small_ref[4 * r + k : 4 * r + k + 1, 0:96] = x[r : r + 1, 96 * k : 96 * (k + 1)]
    small_ref[16:18, :] = x[4:6]
    small_ref[18:19, 0:192] = x[6:7, 0:192]
    small_ref[19:20, 0:192] = x[6:7, 192:384]


def edge_tile(edge, k, r):
    at = (k * SHIFT + r) * SEG
    return edge[at : at + SEG]


def edge_rows(ref, across, rows):
    tiles = [ref[pl.ds(tile_row(r, k, across), SEG), :] for k in range(across) for r in rows]
    return jnp.concatenate(tiles, axis=0).astype(BF)


def prep_kernel(layer, rows, across, *refs):
    (crop_ref, small_ref, info_ref) = refs[:3]
    if layer == 0:
        (lq_ref, lk_ref, pos_ref, pick_ref, c_ref) = refs[3:]
        for kx in range(WIN):
            pick_ref[kx] = column_pick(kx)
    else:
        (pick_ref, lq_ref, lk_ref, pos_ref, c_ref) = refs[3:]
    tp = info_ref[1]
    cols = across * WIN
    height = crop_ref.shape[2]
    table_to_map(small_ref[layer, 0:16, 0:96], pick_ref, pos_ref)
    c_ref[...] = jnp.zeros_like(c_ref)
    c_ref[0:cols, 0:height] = crop_ref[:, 0, :].astype(F32)
    crops = c_ref[...].astype(BF)
    row = iota((32, 128), 0)
    lane = iota((32, 128), 1)
    shift = SHIFT if layer == 1 else 0
    src = rows * tp + row + shift
    src = jnp.where(src >= height, src - height, src)
    grid = nt((src == lane).astype(BF), crops).astype(BF)
    labs = []
    for wc in range(across):
        qx = iota((128, 128), 1) % 8
        col = qx + (WIN * wc + shift)
        col = jnp.where(col >= cols, col - cols, col)
        pick = ((col == iota((128, 128), 0)) & (qx < WIN)).astype(BF)
        lab = nn(grid, pick)
        if layer == 1:
            g = rows * tp + row
            zr = (g >= height - WIN).astype(F32) + (g >= height - SHIFT).astype(F32)
            here = lane % 8 + WIN * wc
            zc = (here >= cols - WIN).astype(F32) + (here >= cols - SHIFT).astype(F32)
            lab = lab * 9.0 + zr * 3.0 + zc
        labs.append(lab)
    real = (iota((1, 128), 1) % 8 < WIN) & (iota((1, 128), 1) % WPAD < WROWS)
    for wr in range(rows // WIN):
        lines = []
        for wc in range(across):
            w = wr * across + wc
            mine = row == (lane % WPAD) // 8 + WIN * wr
            line = jnp.sum(jnp.where(mine, labs[wc], 0.0), 0, keepdims=True)
            line = jnp.where(real, line, -1.0)
            lq_ref[w : w + 1, :] = line
            lines.append(line)
        for wc in range(0, across, 2):
            w = wr * across + wc
            both = jnp.where(iota((1, 128), 1) < WPAD, lines[wc], lines[wc + 1])
            both = jnp.broadcast_to(both, (128, 128)).T
            lk_ref[w] = both[:WPAD]
            lk_ref[w + 1] = both[WPAD:]


def qkv_weight_of(half, j, layer, qkvw_ref, a_ref, b_ref):
    if half == 0:
        return qkvw_ref[layer, j]
    return jnp.concatenate([a_ref[96 * j : 96 * (j + 1)], b_ref[96 * j : 96 * (j + 1)]], axis=0)


def proj_weight_of(half, layer, projw_ref, a_ref, b_ref):
    if half == 0:
        return projw_ref[layer]
    return jnp.concatenate([a_ref[288:384], b_ref[288:384]], axis=0)


def norm_windows(layer, wins, x_ref, xn_ref, gain_ref, bias_ref):
    gain = gain_ref[layer, 0:1]
    bias = bias_ref[layer, 0:1]

    def four(i, carry):
        xhat, _ = norm_stats(x_ref[rows_at(i, 4 * WROWS), :])
        xn = xhat * gain + bias
        for n in range(4):
            part = jnp.concatenate(
                [xn[n * WROWS : (n + 1) * WROWS], zero_rows(WPAD - WROWS)], axis=0
            )
            xn_ref[rows_at(4 * i + n, WPAD), :] = part.astype(BF)
        return carry

    repeat(wins // 4, four, 0)


def project_half(xn_ref, qkv_ref, weight, qb, vb):
    n = xn_ref.shape[0]

    def part(i, carry):
        at = rows_at(i, n)
        xn = xn_ref[at, :]
        q = nt(xn, weight(0))
        k = nt(xn, weight(1))
        v = nt(xn, weight(2))
        qkv_ref[0, at, :] = ((q + qb) * SCALE).astype(BF)
        qkv_ref[1, at, :] = k.astype(BF)
        qkv_ref[2, at, :] = (v + vb).astype(BF)
        return carry

    repeat(1, part, 0)


def attend_forward(halves, wins, group, lq_ref, lk_ref, mask_ref):
    def body(i, carry):
        units = [(i * group + u, h) for u in range(group) for h in halves]
        scores = []
        for w, (qkv_ref, _, _, _) in units:
            at = rows_at(w, WPAD)
            scores.append(nt(qkv_ref[1, at, :], spread(qkv_ref[0, at, :], mask_ref[...])))
        probs = []
        for (w, (_, pos, p_ref, _)), s in zip(units, scores):
            same = lk_ref[w] == lq_ref[pl.ds(w, 1), :]
            same = jnp.concatenate([same] * 3, axis=1)
            s = jnp.where(same, s + jnp.concatenate([pos[n] for n in range(3)], axis=1), NEG)
            e = jnp.exp(s - jnp.max(s, 0, keepdims=True))
            p = (e * (1.0 / jnp.sum(e, 0, keepdims=True))).astype(BF)
            p_ref[w] = p
            probs.append(p)
        for (w, (qkv_ref, _, _, mix_ref)), p in zip(units, probs):
            at = rows_at(w, WPAD)
            mix_ref[at, :] = fold(tn(p, qkv_ref[2, at, :])).astype(BF)
        return carry

    repeat(wins // group, body, 0)


def add_branch(wins, mixes, weights, bias, x_ref, hid_ref):
    n = 8

    def part(i, carry):
        res = bias
        for m_ref, w in zip(mixes, weights):
            res = res + nn(m_ref[rows_at(i, n * WPAD), :], w)
        for k in range(n):
            to = rows_at(i * n + k, WROWS)
            hid_ref[to, :] = x_ref[to, :] + res[k * WPAD : k * WPAD + WROWS]
        return carry

    repeat(wins // n, part, 0)


def attn_own_kernel(rows, across, *refs):
    (tok_ref, gain_ref, bias_ref, pb_ref, qvb_ref, qkvw_ref, projw_ref) = refs[:7]
    (pos_ref, lq_ref, lk_ref) = refs[7:10]
    (xb_ref, xn_ref, hid_ref, qkv_ref, p_ref, mix_ref, mask_ref, x_ref) = refs[10:]
    wins = (rows // WIN) * across
    for r in range(rows):
        row = tok_ref[r].astype(F32)
        for k in range(across):
            x_ref[pl.ds(tile_row(r, k, across), SEG), :] = jnp.concatenate(
                [row[WIN * k : WIN * (k + 1)], zero_rows(1)], axis=0
            )
    xb_ref[...] = x_ref[...].astype(BF)
    mask_ref[...] = head_mask()
    norm_windows(0, wins, x_ref, xn_ref, gain_ref, bias_ref)
    project_half(
        xn_ref, qkv_ref, lambda j: qkvw_ref[0, j], qvb_ref[0, 0:1], qvb_ref[0, 1:2]
    )
    attend_forward(
        [(qkv_ref, pos_ref, p_ref, mix_ref)], wins, wins, lq_ref, lk_ref, mask_ref
    )
    add_branch(wins, [mix_ref], [projw_ref[0]], pb_ref[0:1], x_ref, hid_ref)


def attn_other_kernel(rows, across, *refs):
    (part_ref, xn_ref, a_ref, b_ref, lq_ref, lk_ref, pick_ref, info_ref) = refs[:8]
    (hid_ref, qkv_ref, p_ref, mix_ref, small_ref, mask_ref, pos_ref) = refs[8:]
    small_of(a_ref, small_ref)
    wins = (rows // WIN) * across
    mask_ref[...] = head_mask()
    bias = other_small(small_ref, info_ref[0], pick_ref, pos_ref)
    project_half(
        xn_ref,
        qkv_ref,
        lambda j: qkv_weight_of(1, j, 0, None, a_ref, b_ref),
        bias[0:1],
        bias[1:2],
    )
    attend_forward([(qkv_ref, pos_ref, p_ref, mix_ref)], wins, wins, lq_ref, lk_ref, mask_ref)
    add_branch(
        wins, [mix_ref], [proj_weight_of(1, 0, None, a_ref, b_ref)], 0.0, part_ref, hid_ref
    )


def other_small(small_ref, par, pick_ref, pos_ref):
    first = par == 0

    def swapped(v, n):
        return jnp.where(first, v, jnp.concatenate([v[:, n : 2 * n], v[:, :n]], axis=1))

    t = swapped(small_ref[0:16, 0:96], 48)
    table_to_map(t, pick_ref, pos_ref)
    return swapped(small_ref[18:20, 0:192], 96)


def norm_kernel(rows, across, *refs):
    (st_ref, halo_ref, gain_ref, bias_ref, qvb_ref, qkvw_ref) = refs[:6]
    (x_ref, xn_ref, qkv_ref) = refs[6:]

    def tile(r, k):
        if r < rows:
            return st_ref[pl.ds(tile_row(r, k, across), SEG), :]
        return edge_tile(halo, k, r - rows)

    halo = halo_ref[...].astype(F32)
    shift_in(tile, x_ref, rows, across)
    norm_windows(1, (rows // WIN) * across, x_ref, xn_ref, gain_ref, bias_ref)
    project_half(
        xn_ref, qkv_ref, lambda j: qkvw_ref[1, j], qvb_ref[1, 0:1], qvb_ref[1, 1:2]
    )


def attn_both_kernel(rows, across, *refs):
    (xn_ref, qkv0_ref, pos_ref, a_ref, b_ref, x_ref, projw_ref, pb_ref) = refs[:8]
    (lq_ref, lk_ref, pick_ref, info_ref) = refs[8:12]
    (hid_ref, p0_ref, mix0_out, qkv1_ref, p1_ref, mix1_out, small_ref) = refs[12:19]
    (mask_ref, pos1_ref, mix0_ref, mix1_ref, sems) = refs[19:]
    wins = (rows // WIN) * across
    mask_ref[...] = head_mask()
    small_of(a_ref, small_ref)
    bias = other_small(small_ref, info_ref[0], pick_ref, pos1_ref)
    project_half(
        xn_ref,
        qkv1_ref,
        lambda j: qkv_weight_of(1, j, 1, None, a_ref, b_ref),
        bias[0:1],
        bias[1:2],
    )
    attend_forward(
        [(qkv0_ref, pos_ref, p0_ref, mix0_ref), (qkv1_ref, pos1_ref, p1_ref, mix1_ref)],
        wins,
        wins,
        lq_ref,
        lk_ref,
        mask_ref,
    )
    copies = copies_of([(mix0_ref, mix0_out), (mix1_ref, mix1_out)], sems)
    add_branch(
        wins,
        [mix0_ref, mix1_ref],
        [projw_ref[1], proj_weight_of(1, 1, None, a_ref, b_ref)],
        pb_ref[1:2],
        x_ref,
        hid_ref,
    )
    for copy in copies:
        copy.wait()


def up_weight(part, layer, base, f1_ref, a_ref, b_ref):
    if part == 0:
        return f1_ref[layer]
    return jnp.concatenate([a_ref[base : base + C], b_ref[base : base + C]], axis=1)


def down_weight(part, layer, base, f2_ref, a_ref, b_ref):
    if part == 0:
        return f2_ref[layer]
    return jnp.concatenate([a_ref[base + C : base + 2 * C], b_ref[base + C : base + 2 * C]], axis=0)


def up_biases(layer, par, fb1_ref, small_ref):
    own = fb1_ref[layer : layer + 1]
    one, two = small_ref[16:17], small_ref[17:18]
    first = par == 0
    return own, jnp.concatenate(
        [jnp.where(first, one, two), jnp.where(first, two, one)], axis=1
    )


def gelu_pair(u):
    phi = 0.5 + 0.5 * lax.erf(u * (2.0**-0.5))
    slope = phi + u * (jnp.exp(-0.5 * u * u) * (2.0 * np.pi) ** -0.5)
    return (u * phi).astype(BF), slope.astype(BF)


def mlp_own_kernel(hid_ref, gain_ref, bias_ref, fb1_ref, fb2_ref, f1_ref, f2_ref, st_ref, n2_ref, act_ref, gp_ref):
    h = hid_ref[...]
    xhat, _ = norm_stats(h)
    n2 = (xhat * gain_ref[0, 1:2] + bias_ref[0, 1:2]).astype(BF)
    n2_ref[...] = n2
    act, slope = gelu_pair(nn(n2, f1_ref[0]) + fb1_ref[0:1])
    for z in range(2):
        act_ref[z] = act[:, C * z : C * (z + 1)]
        gp_ref[z] = slope[:, C * z : C * (z + 1)]
    st_ref[...] = h + fb2_ref[0:1] + nn(act, f2_ref[0])


def mlp_other_kernel(
    across, part_ref, n2_ref, fb1_ref, small_ref, a_ref, b_ref, info_ref, st_ref, act_ref, gp_ref,
    edge_ref
):
    _, bias = up_biases(0, info_ref[0], fb1_ref, small_ref)
    act, slope = gelu_pair(nn(n2_ref[...], up_weight(1, 0, 0, None, a_ref, b_ref)) + bias)
    for z in range(2):
        act_ref[z] = act[:, C * z : C * (z + 1)]
        gp_ref[z] = slope[:, C * z : C * (z + 1)]
    st_ref[...] = part_ref[...] + nn(act, down_weight(1, 0, 0, None, a_ref, b_ref))
    edge_ref[...] = edge_rows(st_ref, across, range(SHIFT))


def quarter_of(par, slot, part):
    return (par ^ slot) if part == 0 else 2 + slot


BLOCKS = 1


def half_sums(du, ref):
    for z in range(2):
        ref[z : z + 1] += jnp.sum(du[z].astype(F32), 0, keepdims=True)


def mlp_own_both_kernel(rows, across, *refs):
    (cot_ref, edge_ref, hid_ref, gain_ref, bias_ref, fb1_ref, fb2_ref, f1_ref, f2_ref) = refs[:9]
    (g_ref, df_ref, n2_ref, st_ref, dz_ref, du_ref, act_ref, sum_ref, sf_ref) = refs[9:]
    layer = 1
    cols = across * WIN
    cot_edge = edge_ref[...].astype(F32)
    for r in range(rows):
        s = r + SHIFT
        if s < rows:
            row = cot_ref[s].astype(F32)
        else:
            row = cot_edge[(s - rows) * cols : (s - rows + 1) * cols]
        for k in range(across):
            a = WIN * k + SHIFT
            if k < across - 1:
                piece = [row[a : a + WIN]]
            else:
                piece = [row[a:], row[:SHIFT]]
            g_ref[pl.ds(tile_row(r, k, across), SEG), :] = jnp.concatenate(
                piece + [zero_rows(1)], axis=0
            )
    sum_ref[...] = jnp.zeros_like(sum_ref)
    sf_ref[...] = jnp.zeros_like(sf_ref)
    n = hid_ref.shape[0] // BLOCKS

    def block(i, carry):
        at = pl.ds(pl.multiple_of(i * n, n), n)
        h = hid_ref[at, :]
        xhat, _ = norm_stats(h)
        n2 = (xhat * gain_ref[layer, 1:2] + bias_ref[layer, 1:2]).astype(BF)
        n2_ref[at, :] = n2
        df = g_ref[at, :].astype(BF)
        df_ref[at, :] = df
        sf_ref[...] += jnp.sum(df.astype(F32), 0, keepdims=True)
        up = nn(n2, f1_ref[layer]) + fb1_ref[layer : layer + 1]
        grad = nt(df, f2_ref[layer])
        act, slope = gelu_pair(up)
        du = (grad * slope.astype(F32)).astype(BF)
        parts = [du[:, C * z : C * (z + 1)] for z in range(2)]
        for z in range(2):
            act_ref[z, at, :] = act[:, C * z : C * (z + 1)]
            du_ref[z, at, :] = parts[z]
        half_sums(parts, sum_ref)
        st_ref[at, :] = h + fb2_ref[layer : layer + 1] + nn(act, f2_ref[layer])
        dz_ref[at, :] = nt(du, f1_ref[layer])
        return carry

    lax.fori_loop(0, BLOCKS, block, 0)


def mlp_other_both_kernel(rows, across, *refs):
    (hid_ref, g_ref, df_ref, n2_ref, part_ref, dzp_ref, gain_ref, fb1_ref, small_ref) = refs[:9]
    (a_ref, b_ref, info_ref, sumo_ref, sf_ref) = refs[9:14]
    (out_ref, gh_ref, du_ref, act_ref, send_ref, sum_ref, sh_ref, edge_ref, st_ref) = refs[14:]
    layer = 1
    par = info_ref[0]
    _, bias = up_biases(layer, par, fb1_ref, small_ref)
    w1 = up_weight(1, layer, 0, None, a_ref, b_ref)
    w2 = down_weight(1, layer, 0, None, a_ref, b_ref)
    sum_ref[0:2] = sumo_ref[...]
    sum_ref[2:4] = jnp.zeros((2, C), F32)
    sh_ref[0:2] = jnp.zeros((2, C), F32)
    sh_ref[2:3] = sf_ref[...]
    n = hid_ref.shape[0] // BLOCKS

    def block(i, carry):
        at = pl.ds(pl.multiple_of(i * n, n), n)
        up = nn(n2_ref[at, :], w1) + bias
        grad = nt(df_ref[at, :], w2)
        act, slope = gelu_pair(up)
        du = (grad * slope.astype(F32)).astype(BF)
        parts = [du[:, C * z : C * (z + 1)] for z in range(2)]
        for z in range(2):
            act_ref[z, at, :] = act[:, C * z : C * (z + 1)]
            du_ref[z, at, :] = parts[z]
        half_sums(parts, sum_ref.at[2:4])
        st_ref[at, :] = part_ref[at, :] + nn(act, w2)
        dz = dzp_ref[at, :] + nt(du, w1)
        xhat, rinv = norm_stats(hid_ref[at, :])
        sh_ref[0:1] += jnp.sum(dz * xhat, 0, keepdims=True)
        sh_ref[1:2] += jnp.sum(dz, 0, keepdims=True)
        gh_ref[at, :] = g_ref[at, :] + norm_back(dz, xhat, rinv, gain_ref[layer, 1:2])
        return carry

    lax.fori_loop(0, BLOCKS, block, 0)
    edge_ref[...] = edge_rows(st_ref, across, range(rows - SHIFT, rows))
    out_ref[...] = st_ref[...].astype(BF)
    n2 = n2_ref[...]
    df = df_ref[...]
    send_ref[0:C, :] = tn(n2, du_ref[1]).astype(BF)
    send_ref[C:, :] = tn(act_ref[1], df).astype(BF)


def own_grads_kernel(n2_ref, df_ref, du_ref, act_ref, info_ref, keep_ref, send_ref):
    n2 = n2_ref[...]
    df = df_ref[...]
    for slot, ref in ((1, send_ref), (0, keep_ref)):
        q = info_ref[0] ^ slot
        ref[0:C, :] = tn(n2, du_ref[q]).astype(BF)
        ref[C:, :] = tn(act_ref[q], df).astype(BF)


def mlp_keep_kernel(n2_ref, df_ref, du_ref, act_ref, keep_ref):
    keep_ref[0:C, :] = tn(n2_ref[...], du_ref[0]).astype(BF)
    keep_ref[C:, :] = tn(act_ref[0], df_ref[...]).astype(BF)


def up_keep_kernel(n2_ref, du_ref, keep_ref):
    keep_ref[...] = tn(n2_ref[...], du_ref[0]).astype(BF)


def down_grad_kernel(rows, across, *refs):
    (gin_ref, halo_ref, act0_ref, act1_ref, info_ref, g_ref, df_ref, keep_ref, send_ref) = refs

    def tile(r, k):
        if r >= 0:
            return gin_ref[pl.ds(tile_row(r, k, across), SEG), :]
        return edge_tile(halo, k, r + SHIFT)

    halo = halo_ref[...].astype(F32)
    shift_out(tile, g_ref, rows, across)
    df = g_ref[...].astype(BF)
    df_ref[...] = df
    for slot, ref in ((1, send_ref), (0, keep_ref)):
        ref[1] = tn(act1_ref[slot], df).astype(BF)
        ref[0] = tn(act0_ref[info_ref[0] ^ slot], df).astype(BF)


def mlp_bwd_own_kernel(*refs):
    (df_ref, gp_ref, n2_ref, f1_ref, f2_ref, info_ref) = refs[:6]
    (dz_ref, sum_ref, keep_ref, send_ref, du_ref) = refs[6:]
    grad = nt(df_ref[...], f2_ref[0])
    parts = [
        (grad[:, C * z : C * (z + 1)] * gp_ref[z].astype(F32)).astype(BF) for z in range(2)
    ]
    for z in range(2):
        du_ref[z] = parts[z]
    sum_ref[...] = jnp.zeros_like(sum_ref)
    half_sums(parts, sum_ref)
    dz_ref[...] = nt(jnp.concatenate(parts, axis=1), f1_ref[0])
    n2 = n2_ref[...]
    for slot, ref in ((1, send_ref), (0, keep_ref)):
        ref[...] = tn(n2, du_ref[info_ref[0] ^ slot]).astype(BF)


def mlp_bwd_other_kernel(*refs):
    (g_ref, df_ref, hid_ref, n2_ref, gp_ref, dzp_ref, gain_ref, a_ref, b_ref, sumo_ref) = refs[:10]
    (gh_ref, du_ref, send_ref, sum_ref, sh_ref) = refs[10:]
    df = df_ref[...]
    grad = nt(df, down_weight(1, 0, 0, None, a_ref, b_ref))
    parts = [
        (grad[:, C * z : C * (z + 1)] * gp_ref[z].astype(F32)).astype(BF) for z in range(2)
    ]
    for z in range(2):
        du_ref[z] = parts[z]
    sum_ref[0:2] = sumo_ref[...]
    sum_ref[2:4] = jnp.zeros((2, C), F32)
    half_sums(parts, sum_ref.at[2:4])
    dz = dzp_ref[...] + nt(jnp.concatenate(parts, axis=1), up_weight(1, 0, 0, None, a_ref, b_ref))
    xhat, rinv = norm_stats(hid_ref[...])
    sh_ref[0:1] = jnp.sum(dz * xhat, 0, keepdims=True)
    sh_ref[1:2] = jnp.sum(dz, 0, keepdims=True)
    sh_ref[2:3] = jnp.sum(df.astype(F32), 0, keepdims=True)
    gh_ref[...] = g_ref[...] + norm_back(dz, xhat, rinv, gain_ref[0, 1:2])
    send_ref[...] = tn(n2_ref[...], du_ref[1]).astype(BF)


def window_grads(wins, gh_ref, da_ref):
    def four(i, s):
        g = gh_ref[rows_at(i, 4 * WROWS), :]
        for n in range(4):
            part = jnp.concatenate(
                [g[n * WROWS : (n + 1) * WROWS], zero_rows(WPAD - WROWS)], axis=0
            ).astype(BF)
            da_ref[rows_at(4 * i + n, WPAD), :] = part
            s = s + jnp.sum(part.astype(F32), 0, keepdims=True)
        return s

    return repeat(wins // 4, four, jnp.zeros((1, C), F32))


def attend_backward(halves, wins, group, mask_ref):
    def body(i, carry):
        units = [(i * group + u, h) for u in range(group) for h in halves]
        first = []
        for w, (qkv_ref, p_ref, do_ref, dqkv_ref, _) in units:
            at = rows_at(w, WPAD)
            do = spread(do_ref[at, :], mask_ref[...])
            first.append(nt(qkv_ref[2, at, :], do))
            dqkv_ref[2, at, :] = nn(p_ref[w], do).astype(BF)
        second = []
        for (w, (_, p_ref, _, _, acc_ref)), dp in zip(units, first):
            p = p_ref[w].astype(F32)
            ds = p * (dp - jnp.sum(p * dp, 0, keepdims=True))
            for n in range(3):
                acc_ref[n] += ds[:, 128 * n : 128 * (n + 1)]
            second.append(ds.astype(BF))
        for (w, (qkv_ref, _, _, dqkv_ref, _)), ds in zip(units, second):
            at = rows_at(w, WPAD)
            dqkv_ref[1, at, :] = nn(ds, spread(qkv_ref[0, at, :], mask_ref[...])).astype(BF)
            dqkv_ref[0, at, :] = fold(tn(ds, qkv_ref[1, at, :])).astype(BF)
        return carry

    repeat(wins // group, body, 0)


def half_grads(half, par, xn_ref, da_ref, mix_ref, dqkv_ref, row_ref, give):
    def put(value, at):
        if half == 0:
            row_ref[...] = value
            one = row_ref[pl.ds(pl.multiple_of(par * 96, 96), 96), :]
            two = row_ref[pl.ds(pl.multiple_of((1 - par) * 96, 96), 96), :]
        else:
            one, two = value[:96], value[96:]
        give(at, one.astype(BF), two.astype(BF))

    xn = xn_ref[...]
    for j in range(3):
        grad = tn(dqkv_ref[j], xn)
        put(grad * SCALE if j == 0 else grad, 96 * j)
    put(tn(mix_ref[...], da_ref[...]), 288)


def normed_grads(layer, wins, dqkvs, weights, gh_ref, x_ref, gain_ref, gx_ref):
    gain = gain_ref[layer, 0:1]
    n = 8

    def part(i, carry):
        sg, sb, sq = carry
        at = rows_at(i, n * WPAD)
        dn = nn(dqkvs[0][0, at, :], weights[0](0)) + nn(dqkvs[1][0, at, :], weights[1](0))
        dn = dn * SCALE
        for half in range(2):
            for j in (1, 2):
                dn = dn + nn(dqkvs[half][j, at, :], weights[half](j))
        new = []
        for half in range(2):
            for m, j in enumerate((0, 2)):
                new.append(
                    sq[half * 2 + m] + jnp.sum(dqkvs[half][j, at, :].astype(F32), 0, keepdims=True)
                )
        d = jnp.concatenate([dn[k * WPAD : k * WPAD + WROWS] for k in range(n)], axis=0)
        to = rows_at(i, n * WROWS)
        xhat, rinv = norm_stats(x_ref[to, :].astype(F32))
        sg = sg + jnp.sum(d * xhat, 0, keepdims=True)
        sb = sb + jnp.sum(d, 0, keepdims=True)
        gx_ref[to, :] = gh_ref[to, :] + norm_back(d, xhat, rinv, gain)
        return sg, sb, tuple(new)

    z = jnp.zeros((1, C), F32)
    zq = jnp.zeros((1, 6 * HD), F32)
    return repeat(wins // n, part, (z, z, (zq,) * 4))


def small_rows(ref, z, sq, fb1, table, shared):
    ref[...] = jnp.zeros_like(ref)
    if shared is not None:
        sg, sb, projb, sh_ref = shared
        ref[0:1] = sg
        ref[1:2] = sb
        ref[2:3] = projb
        ref[3:6] = sh_ref[...]
    ref[6:7] = fb1
    ref[7:8, 0:96] = sq[0][:, 96 * z : 96 * (z + 1)] * SCALE
    ref[7:8, 128:224] = sq[1][:, 96 * z : 96 * (z + 1)]
    part = table[:, 48 * z : 48 * (z + 1)]
    for r in range(2):
        ref[8 + r : 9 + r, :] = jnp.concatenate(
            [part[8 * r + k : 8 * r + k + 1] for k in range(8)], axis=1
        )


def mixed_grad_kernel(wins, gh_ref, projw_ref, a_ref, b_ref, da_ref, do_ref, pb_ref):
    pb_ref[...] = window_grads(wins, gh_ref, da_ref)
    for half in range(2):
        do_ref[half] = nt(da_ref[...], proj_weight_of(half, 1, projw_ref, a_ref, b_ref)).astype(BF)


def attn_bwd_kernel(rows, across, *refs):
    (gh_ref, x_ref, xn_ref, gain_ref, qkvw_ref, a_ref, b_ref, info_ref) = refs[:8]
    (fb1_ref, sh_ref, qkv0_ref, p0_ref, mix0_ref, qkv1_ref, p1_ref, mix1_ref, pick_ref) = refs[8:17]
    (da_ref, do_ref, pb_ref) = refs[17:20]
    (gin_ref, keep_ref, send_ref, edge_ref) = refs[20:24]
    (dqkv0_ref, dqkv1_ref, acc_ref, mask_ref, row_ref, sm_ref) = refs[24:]
    layer = 1
    par = info_ref[0]
    wins = (rows // WIN) * across
    mask_ref[...] = head_mask()
    acc_ref[...] = jnp.zeros_like(acc_ref)
    projb = pb_ref[...]
    attend_backward(
        [
            (qkv0_ref, p0_ref, do_ref.at[0], dqkv0_ref, acc_ref.at[0]),
            (qkv1_ref, p1_ref, do_ref.at[1], dqkv1_ref, acc_ref.at[1]),
        ],
        wins,
        wins,
        mask_ref,
    )
    for half, mix_ref, dqkv_ref in ((1, mix1_ref, dqkv1_ref), (0, mix0_ref, dqkv0_ref)):

        def give(at, one, two, half=half):
            keep_ref[half, at : at + 96, :] = one
            send_ref[half, at : at + 96, :] = two

        half_grads(half, par, xn_ref, da_ref, mix_ref, dqkv_ref, row_ref, give)
    weights = [
        lambda j, half=half: qkv_weight_of(half, j, layer, qkvw_ref, a_ref, b_ref)
        for half in range(2)
    ]
    sg, sb, sq = normed_grads(
        layer, wins, [dqkv0_ref, dqkv1_ref], weights, gh_ref, x_ref, gain_ref, gin_ref
    )
    edge_ref[...] = edge_rows(gin_ref, across, range(rows - SHIFT, rows))
    for half in range(2):
        table = map_to_table(acc_ref.at[half], pick_ref)
        for z in range(2):
            q = 2 * half + z
            small_rows(
                sm_ref.at[q], z, sq[2 * half : 2 * half + 2], fb1_ref[q : q + 1], table,
                (sg, sb, projb, sh_ref)
            )
    keep_ref[0, C:, :] = sm_ref[par].astype(BF)
    send_ref[0, C:, :] = sm_ref[1 - par].astype(BF)
    keep_ref[1, C:, :] = sm_ref[2].astype(BF)
    send_ref[1, C:, :] = sm_ref[3].astype(BF)


def column_sum(ref):
    return jnp.sum(ref[...].astype(F32), 0, keepdims=True)


def attn_bwd_heads_kernel(rows, across, *refs):
    (gh_ref, xn_ref, projw_ref, a_ref, b_ref, fb1_ref) = refs[:6]
    (qkv0_ref, p0_ref, qkv1_ref, p1_ref, mix1_ref, pick_ref) = refs[6:12]
    (da_ref, dqkv0_ref, acc0_ref, dqkv1_ref, pb_ref, keep_ref, send_ref) = refs[12:19]
    (do_ref, mask_ref, acc1_ref, sm_ref) = refs[19:]
    wins = (rows // WIN) * across
    mask_ref[...] = head_mask()
    acc0_ref[...] = jnp.zeros_like(acc0_ref)
    acc1_ref[...] = jnp.zeros_like(acc1_ref)
    pb_ref[...] = window_grads(wins, gh_ref, da_ref)
    da = da_ref[...]
    for half in range(2):
        do_ref[half] = nt(da, proj_weight_of(half, 0, projw_ref, a_ref, b_ref)).astype(BF)
    attend_backward(
        [
            (qkv1_ref, p1_ref, do_ref.at[1], dqkv1_ref, acc1_ref),
            (qkv0_ref, p0_ref, do_ref.at[0], dqkv0_ref, acc0_ref),
        ],
        wins,
        wins,
        mask_ref,
    )

    def give(at, one, two):
        keep_ref[at : at + 96, :] = one
        send_ref[at : at + 96, :] = two

    half_grads(1, None, xn_ref, da_ref, mix1_ref, dqkv1_ref, None, give)
    table = map_to_table(acc1_ref, pick_ref)
    sq = (column_sum(dqkv1_ref.at[0]), column_sum(dqkv1_ref.at[2]))
    for z, ref in ((0, keep_ref), (1, send_ref)):
        small_rows(sm_ref, z, sq, fb1_ref[2 + z : 3 + z], table, None)
        ref[C:, :] = sm_ref[...].astype(BF)


def attn_bwd_own_kernel(rows, across, *refs):
    (gh_ref, x_ref, xn_ref, gain_ref, qkvw_ref, a_ref, b_ref, info_ref) = refs[:8]
    (fb1_ref, sh_ref, da_ref, dqkv_ref, acc_ref, dqkv1_ref, pb_ref, mix_ref, pick_ref) = refs[8:17]
    (out_ref, keep_ref, send_ref) = refs[17:20]
    (gx_ref, row_ref, sm_ref) = refs[20:]
    par = info_ref[0]
    wins = (rows // WIN) * across

    def give(at, one, two):
        keep_ref[at : at + 96, :] = one
        send_ref[at : at + 96, :] = two

    half_grads(0, par, xn_ref, da_ref, mix_ref, dqkv_ref, row_ref, give)
    weights = [
        lambda j, half=half: qkv_weight_of(half, j, 0, qkvw_ref, a_ref, b_ref)
        for half in range(2)
    ]
    sg, sb, sq = normed_grads(
        0, wins, [dqkv_ref, dqkv1_ref], weights, gh_ref, x_ref, gain_ref, gx_ref
    )
    table = map_to_table(acc_ref, pick_ref)
    for z in range(2):
        small_rows(
            sm_ref.at[z], z, sq[0:2], fb1_ref[z : z + 1], table, (sg, sb, pb_ref[...], sh_ref)
        )
    keep_ref[C:, :] = sm_ref[par].astype(BF)
    send_ref[C:, :] = sm_ref[1 - par].astype(BF)
    for r in range(rows):
        parts = [gx_ref[pl.ds(tile_row(r, k, across), SEG), :][:WIN] for k in range(across)]
        out_ref[r, :, 0, :] = jnp.concatenate(parts, axis=0)


def pair_kernel(keep_ref, got_ref, own_ref, oth_ref):
    own_ref[...] = (keep_ref[0].astype(F32) + got_ref[0].astype(F32)).astype(BF)
    oth_ref[...] = (keep_ref[1].astype(F32) + got_ref[1].astype(F32)).astype(BF)


def combine_kernel(parts, bit, n_in, *refs):
    ins = refs[:n_in]
    info_ref = refs[n_in]
    outs = refs[n_in + 1 :]
    at = 0
    for rows, terms, split in parts:

        def total(first, n):
            acc = None
            for i, base in terms:
                x = ins[i][pl.ds(base + first, n), :].astype(F32)
                acc = x if acc is None else acc + x
            return acc.astype(BF)

        if bit is None or not split:
            whole = total(0, rows)
            for out in outs:
                out[at : at + rows, :] = whole
            at += rows
        else:
            n = rows // 2
            b = (info_ref[2] >> bit) & 1
            outs[0][at : at + n, :] = total(pl.multiple_of(b * n, n), n)
            outs[1][at : at + n, :] = total(pl.multiple_of((1 - b) * n, n), n)
            at += n


def close_kernel(halves, bit, mine_ref, got_ref, info_ref, out_ref, small_ref):
    join_kernel(halves, bit, mine_ref.at[0 : sum(halves)], got_ref, info_ref, out_ref)
    at = sum(halves)
    rest = (mine_ref[at:, :].astype(F32) + got_ref[at:, :].astype(F32)).astype(BF)
    n = rest.shape[0] - SMALL
    out_ref[2 * at :, :] = rest[:n]
    small_ref[...] = rest[n:]


def join_kernel(halves, bit, mine_ref, got_ref, info_ref, out_ref):
    b = (info_ref[2] >> bit) & 1
    at = 0
    for n in halves:
        for ref, place in ((mine_ref, b), (got_ref, 1 - b)):
            to = pl.multiple_of(2 * at + place * n, 16)
            out_ref[pl.ds(to, n), :] = ref[at : at + n, :]
        at += n
    if at < mine_ref.shape[0]:
        out_ref[2 * at :, :] = mine_ref[at:, :]


def out_kernel(rows, across, in_ref, halo_ref, o_ref, st_ref):
    st_ref[...] = in_ref[...].astype(F32)
    halo = halo_ref[C:, :].astype(F32)
    for r in range(rows):
        parts = []
        for k in range(across):
            if r >= SHIFT:
                t = st_ref[pl.ds(tile_row(r - SHIFT, k, across), SEG), :]
            else:
                t = edge_tile(halo, k, r)
            parts.append(t[:WIN])
        last = parts[-1]
        parts = [last[WIN - SHIFT :]] + parts[:-1] + [last[: WIN - SHIFT]]
        o_ref[r] = jnp.concatenate(parts, axis=0).astype(BF)


def place_of(i, info_ref):
    return info_ref[0] ^ (i // 2), ((info_ref[2] >> 1) & 1) ^ (i % 2)


def put_up(pieces, base, info_ref, ref):
    n = C // 2
    for i in range(4):
        core, half = place_of(i, info_ref)
        rows = pl.ds(pl.multiple_of(half * n, n), n)
        cols = pl.ds(pl.multiple_of(core * C, C), C)
        ref[rows, cols] = pieces[i][base : base + n, :].astype(F32)


def put_down(pieces, base, info_ref, ref):
    n = C // 2
    for i in range(4):
        core, half = place_of(i, info_ref)
        rows = pl.ds(pl.multiple_of(core * C + half * n, n), n)
        ref[rows, :] = pieces[i][base : base + n, :].astype(F32)


def put_attn(pieces, base, info_ref, asm_ref, qkv_ref, proj_ref):
    n = C // 2
    for i in range(4):
        core, half = place_of(i, info_ref)
        rows = pl.ds(pl.multiple_of(half * n, n), n)
        asm_ref[core, rows, :] = pieces[i][base : base + n, :].astype(F32)
    for core in range(2):
        to = pl.ds(96 * core, 96)
        for j in range(3):
            qkv_ref[j, to, :] = asm_ref[core, 96 * j : 96 * (j + 1), :]
        proj_ref[to, :] = asm_ref[core, 288:384, :]


def final_second_kernel(*refs):
    pieces = refs[:4]
    (info_ref, f1_ref, f2_ref, qkv_ref, proj_ref) = refs[4:9]
    (up_ref, down_ref, asm_ref, q_ref, p_ref, sems) = refs[9:]
    put_up(pieces, 0, info_ref, up_ref)
    put_down(pieces, C // 2, info_ref, down_ref)
    put_attn(pieces, C, info_ref, asm_ref, q_ref, p_ref)
    outs = [f1_ref, f2_ref, qkv_ref, proj_ref]
    for copy in copies_of([(x, y.at[1]) for x, y in zip((up_ref, down_ref, q_ref, p_ref), outs)], sems):
        copy.wait()


def final_kernel(*refs):
    mlps, attns, smalls = refs[:4], refs[4:8], refs[8:10]
    (shared_ref, info_ref) = refs[10:12]
    (f1_ref, f2_ref, qkv_ref, proj_ref) = refs[16:20]
    (gain_ref, bias_ref, pb_ref, fb2_ref, qvb_ref, fb1_ref, tab_ref) = refs[20:27]
    (up_ref, down_ref, asm_ref, q_ref, p_ref, sm_ref, sems) = refs[27:]
    put_up(mlps, 0, info_ref, up_ref)
    copies = copies_of([(up_ref, f1_ref.at[0])], sems)
    put_down(mlps, C // 2, info_ref, down_ref)
    copies += copies_of([(down_ref, f2_ref.at[0])], sems.at[1:2])
    put_attn(attns, 0, info_ref, asm_ref, q_ref, p_ref)
    copies += copies_of([(q_ref, qkv_ref.at[0]), (p_ref, proj_ref.at[0])], sems.at[2:4])
    n = C // 2
    par = info_ref[0]
    for layer in range(2):
        for i in range(2):
            x = smalls[i][...] if layer == 1 else attns[2 * i][n:, :]
            sm_ref[par ^ i] = x.astype(F32)
        x, y = sm_ref[0], sm_ref[1]
        shared = x[0:6]
        if layer == 0:
            shared = sm_ref[par, 0:6, :] + shared_ref[0:6].astype(F32)
        gain_ref[layer, 0:1] = shared[0:1]
        gain_ref[layer, 1:2] = shared[3:4]
        bias_ref[layer, 0:1] = shared[1:2]
        bias_ref[layer, 1:2] = shared[4:5]
        pb_ref[layer : layer + 1] = shared[2:3]
        fb2_ref[layer : layer + 1] = shared[5:6]
        fb1_ref[layer : layer + 1, 0:C] = x[6:7]
        fb1_ref[layer : layer + 1, C:] = y[6:7]
        for k in range(2):
            qvb_ref[layer, k : k + 1, 0:96] = x[7:8, 128 * k : 128 * k + 96]
            qvb_ref[layer, k : k + 1, 96:192] = y[7:8, 128 * k : 128 * k + 96]
        t = jnp.concatenate(
            [
                jnp.concatenate(
                    [v[8 + r : 9 + r, 48 * k : 48 * (k + 1)] for r in range(2) for k in range(8)],
                    axis=0,
                )
                for v in (x, y)
            ],
            axis=1,
        )
        wide = tn(t.astype(BF), offset_rows().astype(BF)) * offset_cols()
        for h in range(6):
            tab_ref[h, layer : layer + 1, :] = jnp.sum(
                wide[16 * h : 16 * (h + 1)], 0, keepdims=True
            )
    for copy in copies:
        copy.wait()


VMEM = pl.BlockSpec(memory_space=pltpu.VMEM)
HBM = pl.BlockSpec(memory_space=pltpu.HBM)


class Position:
    def __getitem__(self, k):
        if k == 1:
            return lax.axis_index("tp")
        win = lax.axis_index("win")
        return win if k == 2 else lax.rem(win, 2)


POSITION = Position()


def call(kernel, name, us, limit, operands, outs, scratch=(), aliases=None):
    args = []
    specs = []
    at = [n for n, op in enumerate(operands) if op is POSITION]
    if at:
        (at,) = at
        inner = kernel

        def kernel(*refs):
            return inner(*refs[:at], POSITION, *refs[at:])

        operands = operands[:at] + operands[at + 1 :]
        aliases = {k - (k > at): v for k, v in (aliases or {}).items()}
    for op in operands:
        args.append(op[0] if isinstance(op, tuple) else op)
        specs.append(op[1] if isinstance(op, tuple) else VMEM)
    shapes = [jax.ShapeDtypeStruct(o[0], o[1]) for o in outs]
    return pl.pallas_call(
        kernel,
        name=name,
        in_specs=specs,
        out_specs=[o[2] if len(o) > 2 else VMEM for o in outs],
        input_output_aliases=aliases or {},
        out_shape=shapes,
        scratch_shapes=[s if not isinstance(s, tuple) else pltpu.VMEM(*s) for s in scratch],
        cost_estimate=pl.CostEstimate(
            flops=int(us * 5e9), bytes_accessed=1000000, transcendentals=0
        ),
        compiler_params=pltpu.CompilerParams(vmem_limit_bytes=limit * 2**20),
    )(*args)


def on_device(n_win, *args):
    (
        tokens,
        crop_ids,
        cotangent,
        norm_gain,
        norm_bias,
        qkv_weight,
        qv_bias,
        proj_weight,
        proj_bias,
        fc1_weight,
        fc1_bias,
        fc2_weight,
        fc2_bias,
        pos_table,
    ) = args
    rows, cols = tokens.shape[1:3]
    across = cols // WIN
    wins = (rows // WIN) * across
    ntok = wins * WROWS
    npad = wins * WPAD
    win = lax.axis_index("win")
    tp = lax.axis_index("tp")
    par = win % 2
    info = POSITION
    bits = n_win.bit_length() - 1
    assert n_win == 1 << bits and bits >= 3

    def to_tp(x, name):
        with jax.named_scope(name + "_tp"):
            return lax.ppermute(x, "tp", [(0, 1), (1, 0)])

    def to_win(x, bit, name):
        if bit >= bits:
            return jnp.zeros_like(x)
        with jax.named_scope("%s_win%d" % (name, bit)):
            return lax.ppermute(x, "win", [(i, i ^ (1 << bit)) for i in range(n_win)])

    def after(x, *others):
        return lax.optimization_barrier((x,) + others)[0]

    def combine(parts, bit, ins, name):
        total = sum(rows // 2 if split and bit is not None else rows for rows, _, split in parts)
        outs = [((total, C), BF)] * (1 if bit is None else 2)
        return call(
            partial(combine_kernel, parts, bit, len(ins)), name, 1, 4, tuple(ins) + (info,), outs
        )

    def join(halves, bit, mine, got, name):
        return call(
            partial(join_kernel, halves, bit), name, 1, 4, (mine, got, info),
            [((mine.shape[0] + sum(halves), C), BF)],
        )[0]

    qkv_t = qkv_weight.transpose(0, 2, 3, 1)
    table = pos_table.transpose(2, 0, 1)
    na = C + SMALL
    n = C // 2
    edge_b = ((across * SHIFT * SEG, C), BF)
    a0q, small = call(
        pack_first_kernel,
        "pack_first",
        0.1,
        60,
        tuple((x, HBM) for x in (qkv_t, proj_weight, table, qv_bias, fc1_bias)),
        [((C + 2 * SENT_ROWS, C), BF), ((2, SMALL_ROWS, C), F32)],
        [
            (table.shape, F32),
            (qv_bias.shape, F32),
            (fc1_bias.shape, F32),
            pltpu.SemaphoreType.DMA((7,)),
        ],
    )
    a0 = to_tp(a0q, "a0")
    m0q, a1q, m1q, cot_edge = call(
        pack_kernel,
        "pack",
        0.1,
        60,
        tuple((x, HBM) for x in (qkv_t, proj_weight, fc1_weight, fc2_weight, cotangent[0]))
        + (after(small, a0q), info),
        [
            ((2 * C, C), BF),
            ((C + 2 * SENT_ROWS, C), BF),
            ((2 * C, C), BF),
            ((EDGE_ROWS, C), BF),
        ],
        [((SHIFT, cols, C), BF), pltpu.SemaphoreType.DMA((9,))],
    )
    m0 = to_tp(m0q, "m0")
    crops = crop_ids.transpose(2, 0, 1)
    label_outs = [((wins, 128), F32), ((wins, WPAD, 128), F32), ((3, WPAD, 128), F32)]
    lq0, lk0, pos0, pick = call(
        partial(prep_kernel, 0, rows, across),
        "prep_0",
        0.1,
        8,
        (crops, after(small, m0q), info),
        label_outs + [((WIN, 96, 6 * WPAD), BF)],
        [((128, 128), F32)],
    )
    tiles = (rows // WIN, across, WIN, SEG, C)
    mask = ((6 * WPAD, 6 * HD), BF)
    half_outs = [((3, npad, 192), BF), ((wins, WPAD, 6 * WPAD), BF), ((npad, 192), BF)]
    tok_f = ((ntok, C), F32)
    tok_b = ((ntok, C), BF)
    hid_b = ((4, ntok, C), BF)
    other_scratch = [mask, ((3, WPAD, 128), F32)]

    x0, xn0, part, qkv00, p00, mix00 = call(
        partial(attn_own_kernel, rows, across),
        "attn_own_0",
        0.1,
        8,
        (tokens[0], norm_gain, norm_bias, proj_bias, qv_bias, qkv_t, proj_weight, pos0, lq0, lk0),
        [tok_b, ((npad, C), BF), tok_f] + half_outs,
        [mask, tok_f],
    )
    lq1, lk1, pos1 = call(
        partial(prep_kernel, 1, rows, across),
        "prep_1",
        0.1,
        8,
        (crops, after(small, part), info, pick),
        label_outs,
        [((128, 128), F32)],
    )
    a1 = to_tp(after(a1q, lq1), "a1")
    a0 = after(a0, lq1)
    a0s = to_win(a0, 0, "a0")
    hid0, qkv01, p01, mix01, small0 = call(
        partial(attn_other_kernel, rows, across),
        "attn_other_0",
        0.1,
        8,
        (part, xn0, a0, a0s, lq0, lk0, pick, info),
        [tok_f] + half_outs + [((SMALL_ROWS, C), F32)],
        other_scratch,
    )
    half_b = ((2, ntok, C), BF)
    st_own, n2f, act00, gp00 = call(
        mlp_own_kernel,
        "mlp_own_0",
        0.1,
        10,
        (hid0, norm_gain, norm_bias, fc1_bias, fc2_bias, fc1_weight, fc2_weight),
        [tok_f, tok_b, half_b, half_b],
    )
    m0 = after(m0, st_own)
    m0s = to_win(m0, 0, "m0")
    st0, act01, gp01, edge = call(
        partial(mlp_other_kernel, across),
        "mlp_other_0",
        3,
        10,
        (st_own, n2f, fc1_bias, small0, m0, m0s, info),
        [tok_f, half_b, half_b, edge_b],
    )
    halo = to_tp(edge, "edge0")
    a1 = after(a1, halo)
    a1s = to_win(a1, 0, "a1")
    cot_edge = to_tp(after(cot_edge, edge), "cot")
    m1 = to_tp(after(m1q, edge), "m1")
    x1, xn1, qkv10 = call(
        partial(norm_kernel, rows, across),
        "norm_1",
        2,
        6,
        (st0, halo, norm_gain, norm_bias, qv_bias, qkv_t),
        [tok_f, ((npad, C), BF), half_outs[0]],
    )
    mix_out = half_outs[2] + (HBM,)
    hid1, p10, mix10, qkv11, p11, mix11, small1 = call(
        partial(attn_both_kernel, rows, across),
        "attn_fwd_1",
        10,
        12,
        (xn1, qkv10, pos1, a1, a1s, x1, proj_weight, proj_bias, lq1, lk1, pick, info),
        [tok_f, half_outs[1], mix_out] + half_outs[:2] + [mix_out, ((SMALL_ROWS, C), F32)],
        other_scratch + [half_outs[2], half_outs[2], pltpu.SemaphoreType.DMA((2,))],
    )
    sums = [((4, C), F32), ((3, C), F32)]
    g1, df1, n21, st_own, dz_own, du10, act10, sum10, sf1 = call(
        partial(mlp_own_both_kernel, rows, across),
        "mlp_own_1",
        5,
        11,
        (cotangent[0], after(cot_edge, a1s), hid1, norm_gain, norm_bias, fc1_bias, fc2_bias)
        + (fc1_weight, fc2_weight),
        [tok_f, tok_b, tok_b, tok_f, tok_f, half_b, half_b, ((2, C), F32), ((1, C), F32)],
    )
    m1 = after(m1, dz_own)
    m1s = to_win(m1, 0, "m1")
    whole_q = ((2 * C, C), BF)
    keep_mo, send_mo = call(
        own_grads_kernel, "own_grads_1", 2, 4, (after(n21, m1), df1, du10, act10, info),
        [whole_q, whole_q],
    )
    mo_core = to_win(send_mo, 0, "gmo")
    st1, gh1, du11, act11, send_mx, gfb1, gsh1, out_edge = call(
        partial(mlp_other_both_kernel, rows, across),
        "mlp_other_1",
        6,
        12,
        (after(hid1, keep_mo), g1, df1, n21, st_own, dz_own, norm_gain, fc1_bias, small1, m1, m1s)
        + (info, sum10, sf1),
        [tok_b, tok_f, half_b, half_b, whole_q] + sums + [edge_b],
        [tok_f],
        aliases={1: 1},
    )

    def plus(x, y, name):
        return combine([(x.shape[0], [(0, 0), (1, 0)], True)], None, (x, y), name)[0]

    def pair(keep, got, name):
        shape = keep.shape[1:]
        return call(pair_kernel, name, 1, 4, (keep, got), [(shape, BF), (shape, BF)])

    mx_core = to_win(send_mx, 0, "gmx")
    (keep_mx,) = call(mlp_keep_kernel, "mlp_keep_1", 1, 4, (n21, df1, du11, act11), [whole_q])
    m1_oth = plus(keep_mx, after(mx_core, keep_mx), "m1_oth")
    m1_own = plus(keep_mo, after(mo_core, m1_oth), "m1_own")
    m1_t = to_tp(m1_oth, "gm1")
    da1, do1, pb1 = call(
        partial(mixed_grad_kernel, wins),
        "mixed_grad_1",
        0.1,
        4,
        (after(gh1, m1_own), proj_weight, a1, a1s),
        [((npad, C), BF), ((2, npad, 192), BF), ((1, C), F32)],
    )
    gin1, keep_a1, send_a1, edge = call(
        partial(attn_bwd_kernel, rows, across),
        "attn_bwd_1",
        14,
        8,
        (gh1, x1, xn1, norm_gain, qkv_t, a1, a1s, info)
        + (gfb1, gsh1, qkv10, p10, mix10, qkv11, p11, mix11, pick, da1, do1, pb1),
        [tok_f, ((2, na, C), BF), ((2, na, C), BF), edge_b],
        [
            ((3, npad, 192), BF),
            ((3, npad, 192), BF),
            ((2, 3, WPAD, 128), F32),
            mask,
            ((192, C), F32),
            ((4, SMALL, C), F32),
        ],
    )
    halo = to_tp(edge, "edge1")
    a1_core = to_win(after(send_a1, edge), 0, "ga1")
    m1_mine, m1_away = combine(
        [(C, [(0, 0), (1, 0)], True), (C, [(0, C), (1, C)], True)],
        1,
        (m1_own, after(m1_t, edge)),
        "m1_y",
    )
    m1_y = to_win(m1_away, 1, "gm1")
    a1_own, a1_oth = pair(keep_a1, after(a1_core, m1_away), "pair_a1")
    a1_t = to_tp(a1_oth, "ga1")
    g0, df0, keep_f2, send_f2 = call(
        partial(down_grad_kernel, rows, across),
        "down_grad_0",
        4,
        5,
        (gin1, after(halo, a1_oth), act00, act01, info),
        [tok_f, tok_b, ((2, C, C), BF), ((2, C, C), BF)],
    )
    f2_core = to_win(send_f2, 0, "gf2")
    quarter_b = ((C, C), BF)
    dz0, sum00, keep_fo, send_fo = call(
        mlp_bwd_own_kernel,
        "mlp_bwd_own_0",
        2,
        8,
        (df0, gp00, n2f, fc1_weight, fc2_weight, info),
        [tok_f, ((2, C), F32), quarter_b, quarter_b],
        [half_b],
    )
    fo_core = to_win(send_fo, 0, "gfo")
    m1_mine, m1_away = combine(
        [(n, [(0, 0), (1, 0)], True), (n, [(0, n), (1, n)], True)],
        2,
        (m1_mine, after(m1_y, dz0)),
        "m1_z",
    )
    m1_z = to_win(m1_away, 2, "gm1")
    f2_own, f2_oth = pair(keep_f2, after(f2_core, m1_away), "pair_f2")
    f2_t = to_tp(f2_oth, "gf2")
    a1_mine, a1_away = combine(
        [(C, [(0, 0), (1, 0)], True), (SMALL, [(0, C), (1, C)], False)],
        1,
        (a1_own, after(a1_t, f2_oth)),
        "a1_y",
    )
    a1_y = to_win(a1_away, 1, "ga1")
    gh0, du01, send_fx, gfb0, gsh0 = call(
        mlp_bwd_other_kernel,
        "mlp_bwd_other_0",
        3,
        8,
        (after(g0, a1_away), df0, hid0, n2f, gp01, dz0, norm_gain, m0, m0s, sum00),
        [tok_f, half_b, quarter_b] + sums,
    )
    m1 = plus(m1_mine, after(m1_z, send_fx), "m1_z2")
    m1_b = to_win(m1, 3, "gm1")
    fx_core = to_win(send_fx, 0, "gfx")
    (keep_fx,) = call(up_keep_kernel, "up_keep_0", 1, 4, (n2f, du01), [quarter_b])
    (f1_oth,) = combine(
        [(C, [(0, 0), (1, 0)], True), (edge_b[0][0], [(2, 0)], True)],
        None,
        (keep_fx, after(fx_core, keep_fx), out_edge),
        "f1_oth",
    )
    f1_t = to_tp(f1_oth, "gf1")
    f1_own = plus(keep_fo, after(fo_core, f1_oth), "f1_own")
    a1 = plus(a1_mine, after(a1_y, f1_own), "a1_z2")
    a1_b = to_win(a1, 3, "ga1")
    da, dqkv0, acc0, dqkv1, pb0, keep_o0, send_o0 = call(
        partial(attn_bwd_heads_kernel, rows, across),
        "attn_bwd_heads_0",
        8,
        8,
        (after(gh0, a1, f2_t), xn0, proj_weight, a0, a0s, gfb0)
        + (qkv00, p00, qkv01, p01, mix01, pick),
        [
            ((npad, C), BF),
            ((3, npad, 192), BF),
            ((3, WPAD, 128), F32),
            ((3, npad, 192), BF),
            ((1, C), F32),
            ((na, C), BF),
            ((na, C), BF),
        ],
        [((2, npad, 192), BF), mask, ((3, WPAD, 128), F32), ((SMALL, C), F32)],
    )
    o0_core = to_win(send_o0, 0, "go0")
    m0_mine, m0_away = combine(
        [(C, [(0, 0), (1, 0)], True), (C, [(2, 0), (3, 0)], True)],
        1,
        (f1_own, after(f1_t, send_o0), f2_own, f2_t),
        "m0_y",
    )
    m0_y = to_win(m0_away, 1, "gm0")
    o0_sum = plus(keep_o0, after(o0_core, m0_away), "o0")
    o0_t = to_tp(o0_sum, "go0")
    (c1,) = combine(
        [(n, [(0, 0), (1, 0)], True), (n + SMALL, [(2, 0), (3, 0)], True)],
        None,
        (m1, after(m1_b, o0_sum), a1, after(a1_b, o0_sum)),
        "c1",
    )
    for bit in range(4, bits):
        c1 = plus(c1, to_win(c1, bit, "gc1"), "c1_sum")
    c1_b = to_win(c1, 2, "gc1")
    grad_tokens, keep_a0, send_a0 = call(
        partial(attn_bwd_own_kernel, rows, across),
        "attn_bwd_own_0",
        9,
        7,
        (gh0, x0, xn0, norm_gain, qkv_t, a0, a0s, info)
        + (gfb0, gsh0, da, dqkv0, acc0, dqkv1, pb0, after(mix00, c1), pick),
        [((rows, cols, 1, C), F32), ((na, C), BF), ((na, C), BF)],
        [tok_f, ((192, C), F32), ((2, SMALL, C), F32)],
    )

    a0_core = to_win(send_a0, 0, "ga0")
    m0_mine, m0_away = combine(
        [(n, [(0, 0), (1, 0)], True), (n, [(0, n), (1, n)], True)],
        2,
        (m0_mine, after(m0_y, send_a0)),
        "m0_z",
    )
    m0_z = to_win(m0_away, 2, "gm0")
    a0_mine, a0_away = combine(
        [(C, [(0, 0), (1, 0), (2, 0)], True), (SMALL, [(0, C), (1, C), (2, C)], False)],
        1,
        (keep_a0, after(a0_core, m0_away), o0_t),
        "a0_y",
    )
    a0_y = to_win(a0_away, 1, "ga0")
    c1, c1_small = call(
        partial(close_kernel, [n // 2] * 2, 2), "c1_close", 1, 8, (c1, after(c1_b, a0_away), info),
        [((3 * n, C), BF), ((SMALL, C), BF)],
    )
    c1_back = to_win(c1, 1, "gc1_back")
    c1_sib = to_win(c1, 0, "gc1_mine")
    c1_small_sib = to_win(c1_small, 0, "gc1_small")
    m0 = plus(m0_mine, after(m0_z, c1), "m0_z2")
    m0_b = to_win(m0, 3, "gm0")
    a0 = plus(a0_mine, after(a0_y, m0), "a0_z")
    a0_z = to_win(a0, 2, "ga0")
    (layer_out,) = call(
        partial(out_kernel, rows, across), "layer_out", 1, 8, (after(st1, a0), f1_t),
        [((rows, cols, C), BF)],
        [tok_f],
    )
    m0 = plus(m0, after(m0_b, layer_out), "m0_sum")
    for bit in range(4, bits):
        m0 = plus(m0, to_win(m0, bit, "gm0"), "m0_sum")
    m0_b = to_win(m0, 2, "gm0_back")
    a0 = plus(a0, after(a0_z, m0), "a0_z2")
    a0_b = to_win(a0, 3, "ga0")
    c1_back = after(c1_back, a0)
    c1_pieces = (c1, c1_back, c1_sib, to_win(c1_back, 0, "gc1_theirs"))
    m0 = join([n // 2] * 2, 2, m0, after(m0_b, c1_back), "m0_join")
    m0_back = to_win(m0, 1, "gm0_back")
    m0_sib = to_win(m0, 0, "gm0_mine")
    c1_small_sib, c1_pieces = after((c1_small_sib, c1_pieces), m0)
    f1_shape, f2_shape = (2, C, 2 * C), (2, 2 * C, C)
    qkv_shape, proj_shape = (2, 3, 192, C), (2, 192, C)
    whole = [(f1_shape, F32, HBM), (f2_shape, F32, HBM), (qkv_shape, F32, HBM), (proj_shape, F32, HBM)]
    parts = [(x[0][1:], F32) for x in whole]
    attn_parts = [((2, C, C), F32)] + parts[2:]
    g_f1, g_f2, g_qkv, g_proj = call(
        final_second_kernel, "final_second", 1, 9, c1_pieces + (info,), whole,
        parts[:2] + attn_parts + [pltpu.SemaphoreType.DMA((4,))],
    )
    a0 = plus(a0, after(a0_b, g_f1), "a0_sum")
    for bit in range(4, bits):
        a0 = plus(a0, to_win(a0, bit, "ga0"), "a0_sum")
    a0_back = to_win(a0, 1, "ga0_back")
    a0_sib = to_win(a0, 0, "ga0_mine")
    shared = to_tp(a0[n : n + 16], "shared")
    m0_back = after(m0_back, a0_sib, shared)
    m0_pieces = (m0, m0_back, m0_sib, to_win(m0_back, 0, "gm0_theirs"))
    outs = call(
        final_kernel,
        "final",
        0.1,
        9,
        m0_pieces
        + (a0, a0_back, a0_sib, to_win(a0_back, 0, "ga0_theirs"), c1_small, c1_small_sib)
        + (shared, info, (g_f1, HBM), (g_f2, HBM), (g_qkv, HBM), (g_proj, HBM)),
        whole
        + [
            ((2, 2, C), F32),
            ((2, 2, C), F32),
            ((2, C), F32),
            ((2, C), F32),
            ((2, 2, 192), F32),
            ((2, 2 * C), F32),
            ((6, 2, 169), F32),
        ],
        parts[:2] + attn_parts + [((2, SMALL, C), F32), pltpu.SemaphoreType.DMA((4,))],
        aliases={12: 0, 13: 1, 14: 2, 15: 3},
    )
    (g_f1, g_f2, g_qkv, g_proj, g_gain, g_bias, g_pb, g_fb2, g_qvb, g_fb1, g_tab) = outs
    return (
        layer_out[None],
        grad_tokens.transpose(2, 0, 1, 3),
        g_gain,
        g_bias,
        g_qkv.transpose(0, 3, 1, 2),
        g_qvb,
        g_proj,
        g_pb,
        g_f1,
        g_fb1,
        g_f2,
        g_fb2,
        g_tab.transpose(1, 2, 0),
    )


def solution(mesh):
    return jax.shard_map(
        partial(on_device, mesh.shape["win"]),
        mesh=mesh,
        in_specs=(
            P("win", "tp", None, None),
            P("win", None, None),
            P("win", "tp", None, None),
            P(),
            P(),
            P(None, None, None, "tp"),
            P(None, None, "tp"),
            P(None, "tp", None),
            P(),
            P(None, None, "tp"),
            P(None, "tp"),
            P(None, "tp", None),
            P(),
            P(None, None, "tp"),
        ),
        out_specs=(
            P("win", "tp", None, None),
            P("win", "tp", None, None),
            P(),
            P(),
            P(None, None, None, "tp"),
            P(None, None, "tp"),
            P(None, "tp", None),
            P(),
            P(None, None, "tp"),
            P(None, "tp"),
            P(None, "tp", None),
            P(),
            P(None, None, "tp"),
        ),
        check_vma=False,
    )
```
